32 devices in a mesh: rep: 1, seq: 8 (over z, y), head: 2 (over x), sub: 2 (over core).
Axes of the slice: x: 2, y: 2, z: 4, core: 2. Of those that a mesh axis runs over, the one named last changes fastest.
Arguments:
- head_query_rows: bfloat16 [2048, 2048], P(('rep', 'seq', 'sub'), 'head'), may hold values from -6 to 6, as said below
- head_key_rows: bfloat16 [2048, 2048], P(('rep', 'seq', 'sub'), 'head'), may hold values from -6 to 6, as said below
- head_value_rows: bfloat16 [2048, 2048], P(('rep', 'seq', 'sub'), 'head'), may hold values from -6 to 6
- output_gradient: bfloat16 [2048, 4096], P(('rep', 'seq', 'sub'), 'head'), may hold values from -6 to 6
- output_matrix: bfloat16 [2048, 4096], P('head', 'sub'), may hold values from -0.125 to 0.125
- adapter_down_weight: bfloat16 [2048, 16], P('head'), may hold values from -0.125 to 0.125
- adapter_up_weight: bfloat16 [16, 4096], replicated, may hold values from -0.09375 to 0.09375
Outputs:
- query_gradient: bfloat16 [2048, 2048], P(('rep', 'seq', 'sub'), 'head')
- key_gradient: bfloat16 [2048, 2048], P(('rep', 'seq', 'sub'), 'head')
- value_gradient: bfloat16 [2048, 2048], P(('rep', 'seq', 'sub'), 'head')
- adapter_down_gradient: float32 [2048, 16], P(('rep', 'head'))
- adapter_up_gradient: float32 [16, 4096], P('rep', 'head')
The draws below stay inside these ranges and needn't reach their ends.
Inputs may be any that keep to these rules, and one draw needn't show every extreme that they name: `head_query_rows`: entries of the queries are real values within the range. `head_key_rows`: entries of the keys are real values within the range.
All inputs are finite; a program needn't handle non-finite values.
Results may differ from the reference program's by a relative error of at most 0.029.
Values may be sent and summed in bfloat16 or wider, within the bound.
No kernel may reach another device: no remote copies, remote signals or barrier semaphores. Data moves between devices by JAX's collectives and lax.ppermute only.
A program may use at most 64 MiB of HBM per device.

```python
import jax
import jax.numpy as jnp
from jax import lax

HD = 128
HEADS = 16
MODEL_WIDTH = 4096
LOW_RANK = 16
GROUP = 2048
TOK_DEV = 128
SEQ = 2048
HEAD_FEATURES = 2048


def paired_rows(key):
    base = jax.random.fold_in(key, 11)
    streams = jax.random.split(base, 2)
    shape = (SEQ, HEAD_FEATURES)
    query_raw = jnp.clip(jax.random.normal(streams[0], shape, jnp.float32), -6.0, 6.0)
    key_raw = jnp.clip(jax.random.normal(streams[1], shape, jnp.float32), -6.0, 6.0)
    return (query_raw, key_raw)


def draw_head_query_rows(key, part):
    return paired_rows(key)[0].astype(jnp.bfloat16)


def draw_head_key_rows(key, part):
    return paired_rows(key)[1].astype(jnp.bfloat16)


def level_of(stream_key, extent, cuts, least, largest):
    gain, own = 1.0, jax.random.fold_in(stream_key, 6)
    for dim, blocks in cuts:
        steps = jnp.exp(jax.random.uniform(jax.random.fold_in(own, dim), (blocks,), jnp.float32, least / len(cuts), largest / len(cuts)))
        gain = gain * jnp.repeat(steps, extent[dim] // blocks).reshape([-1 if axis == dim else 1 for axis in range(len(extent))])
    return gain


def noise(rng, extent, spread, limit, cuts=(), held_as=jnp.bfloat16):
    entries = jax.random.normal(rng, extent, jnp.float32) * spread
    if len(cuts) > 0:
        entries = level_of(rng, extent, cuts, -0.22, 0.18) * entries
    return jnp.clip(entries, min=-limit, max=limit).astype(held_as)


def setup_inputs(seed: int = 0, part: int = 0) -> dict:
    streams_of = jax.random.split(jax.random.key(seed), 8)
    part_splits = jax.random.split(jax.random.fold_in(streams_of[7], part), 8)
    return {
        "head_query_rows": draw_head_query_rows(jax.random.fold_in(jax.random.fold_in(streams_of[7], part), 71), part),
        "head_key_rows": draw_head_key_rows(jax.random.fold_in(jax.random.fold_in(streams_of[7], part), 71), part),
        "head_value_rows": noise(part_splits[2], (SEQ, HEAD_FEATURES), 1.0, 6.0, ((0, 16), (1, 2))),
        "output_gradient": noise(part_splits[3], (SEQ, MODEL_WIDTH), 1.0, 6.0, ((0, 16), (1, 2))),
        "output_matrix": noise(streams_of[4], (HEAD_FEATURES, MODEL_WIDTH), HEAD_FEATURES ** -0.5, 0.125, ((0, 2), (1, 2))),
        "adapter_down_weight": noise(streams_of[5], (HEAD_FEATURES, LOW_RANK), HEAD_FEATURES ** -0.5, 0.125, ((0, 2),)),
        "adapter_up_weight": noise(streams_of[6], (LOW_RANK, MODEL_WIDTH), MODEL_WIDTH ** -0.5, 0.09375),
    }


def exact_dot(left, right):
    return jnp.dot(left.astype(jnp.float32), right.astype(jnp.float32), precision=lax.Precision.HIGHEST)


def group_pass(pieces):
    query_g, key_g, value_g, dout_g = pieces
    inverse = HD ** -0.5
    row_idx = lax.broadcasted_iota(jnp.int32, (GROUP, GROUP), 0)
    col_idx = lax.broadcasted_iota(jnp.int32, (GROUP, GROUP), 1)
    visible = col_idx <= row_idx
    scores = exact_dot(query_g, key_g.T) * inverse
    scores = jnp.where(visible, scores, -jnp.inf)
    highest = jnp.max(scores, axis=1, keepdims=True)
    powers = jnp.exp(scores - highest)
    prob = powers / jnp.sum(powers, axis=1, keepdims=True)
    prob_lo = prob.astype(jnp.bfloat16)
    attn_g = exact_dot(prob_lo, value_g).astype(jnp.bfloat16)
    dprob = exact_dot(dout_g, value_g.T)
    delta = jnp.sum(prob * dprob, axis=1, keepdims=True)
    dscore = (prob * (dprob - delta) * inverse).astype(jnp.bfloat16)
    grad_q = exact_dot(dscore, key_g).astype(jnp.bfloat16)
    blocks = GROUP // TOK_DEV
    score_grad_blocks = dscore.reshape(blocks, TOK_DEV, GROUP).astype(jnp.float32)
    query_tiles = query_g.reshape(blocks, TOK_DEV, HD).astype(jnp.float32)
    key_partials = jnp.einsum("srz,srj->szj", score_grad_blocks, query_tiles, precision=lax.Precision.HIGHEST)
    key_partials = lax.optimization_barrier(key_partials.astype(jnp.bfloat16)).astype(jnp.float32)
    grad_k = jnp.sum(key_partials, axis=0).astype(jnp.bfloat16)
    probability_blocks = prob_lo.reshape(blocks, TOK_DEV, GROUP).astype(jnp.float32)
    output_grad_blocks = dout_g.reshape(blocks, TOK_DEV, HD).astype(jnp.float32)
    value_partials = jnp.einsum("srz,srj->szj", probability_blocks, output_grad_blocks, precision=lax.Precision.HIGHEST)
    value_partials = lax.optimization_barrier(value_partials.astype(jnp.bfloat16)).astype(jnp.float32)
    grad_v = jnp.sum(value_partials, axis=0).astype(jnp.bfloat16)
    return attn_g, grad_q, grad_k, grad_v


def heads_pass(query_h, key_h, value_h, dout_h, roll_by):
    count = query_h.shape[0]

    def prepare(tensor):
        return jnp.roll(tensor, -roll_by, axis=1).reshape(count * (SEQ // GROUP), GROUP, HD)

    results = lax.map(group_pass, (prepare(query_h), prepare(key_h), prepare(value_h), prepare(dout_h)))

    def restore(tensor):
        return jnp.roll(tensor.reshape(count, SEQ, HD), roll_by, axis=1)

    return tuple(restore(result) for result in results)


def split_heads(tensor):
    return tensor.reshape(SEQ, HEADS, HD).transpose(1, 0, 2)


def join_heads(tensor):
    return tensor.transpose(1, 0, 2).reshape(SEQ, HEAD_FEATURES)


def reference(head_query_rows, head_key_rows, head_value_rows, output_gradient, output_matrix, adapter_down_weight, adapter_up_weight):
    adapter_upward = exact_dot(output_gradient, adapter_up_weight.T)
    projected_output = exact_dot(output_gradient, output_matrix.T)
    adapter_backward = exact_dot(adapter_upward, adapter_down_weight.T)
    attention_gradient = (projected_output + 2.0 * adapter_backward).astype(jnp.bfloat16)
    per_head = [split_heads(tensor) for tensor in (head_query_rows, head_key_rows, head_value_rows, attention_gradient)]
    half_heads = HEADS // 2
    plain_heads = heads_pass(*[tensor[:half_heads] for tensor in per_head], 0)
    moved_heads = heads_pass(*[tensor[half_heads:] for tensor in per_head], GROUP // 2)
    joined = [join_heads(jnp.concatenate((first, second), axis=0)) for first, second in zip(plain_heads, moved_heads)]
    attention_output, query_gradient, key_gradient, value_gradient = joined
    adapter_middle = exact_dot(attention_output, adapter_down_weight)
    adapter_down_gradient = 2.0 * exact_dot(attention_output.T, adapter_upward)
    adapter_up_gradient = 2.0 * exact_dot(adapter_middle.T, output_gradient)
    return query_gradient, key_gradient, value_gradient, adapter_down_gradient, adapter_up_gradient
```

```python
import functools
import math

import jax
import jax.numpy as jnp
from jax import lax
from jax.experimental import pallas as pl
from jax.experimental.pallas import tpu as pltpu
from jax.sharding import PartitionSpec as P

HD = 128
GROUP = 2048
TILE = 256
HIDDEN = -1e30
SCALE = HD ** (-0.5)
LOG2_SCALE = SCALE * math.log2(math.e)


def dot_nt(left, right):
    return lax.dot_general(
        left, right, (((1,), (1,)), ((), ())), preferred_element_type=jnp.float32
    )


def dot_nn(left, right):
    return jnp.dot(left, right, preferred_element_type=jnp.float32)


def rows_of(ref, blocks, first, count):
    return ref[0:blocks, first : first + count, :].reshape(blocks * count, HD)


def scores_of(sub, keys_own, keys_other, queries, tok):
    def tail_hidden(scores, visible):
        head = scores.shape[0] - TILE
        tail = jnp.where(visible, scores[head:], HIDDEN)
        return tail if head == 0 else jnp.concatenate((scores[:head], tail), axis=0)

    key_at = lax.broadcasted_iota(jnp.int32, (TILE, TILE), 0)
    query_at = lax.broadcasted_iota(jnp.int32, (TILE, TILE), 1)
    own = tail_hidden(dot_nt(keys_own, queries), key_at <= query_at)
    other = tail_hidden(
        dot_nt(keys_other, queries), key_at // tok < query_at // tok + sub
    )
    return own, other


def forward_kernel(tok, sub_ref, own_ref, other_ref, down_t_ref, attn_ref, mid_ref, stat_ref):
    blocks = own_ref.shape[0]
    step = TILE // tok
    sub = sub_ref[0]
    values_own_t = rows_of(own_ref, blocks, 2 * tok, tok).T
    values_other_t = rows_of(other_ref, blocks, tok, tok).T
    for tile in range(blocks // step):
        upto = (tile + 1) * step
        width = upto * tok
        at = tile * TILE
        queries = own_ref[tile * step : upto, 0:tok, :].reshape(TILE, HD)
        own, other = scores_of(
            sub, rows_of(own_ref, upto, tok, tok), rows_of(other_ref, upto, 0, tok), queries, tok
        )
        highest = jnp.maximum(
            jnp.max(own, axis=0, keepdims=True), jnp.max(other, axis=0, keepdims=True)
        )
        own = jnp.exp2((own - highest) * LOG2_SCALE)
        other = jnp.exp2((other - highest) * LOG2_SCALE)
        inverse = 1.0 / (
            jnp.sum(own, axis=0, keepdims=True) + jnp.sum(other, axis=0, keepdims=True)
        )
        attn = dot_nn(values_own_t[:, :width], own.astype(jnp.bfloat16)) + dot_nn(
            values_other_t[:, :width], other.astype(jnp.bfloat16)
        )
        attn = (attn * inverse).astype(jnp.bfloat16)
        attn_ref[:, at : at + TILE] = attn
        mid_ref[:, at : at + TILE] = dot_nn(down_t_ref[...], attn)
        stat_ref[0:1, at : at + TILE] = highest
        stat_ref[1:2, at : at + TILE] = inverse


def backward_kernel(
    tok,
    sub_ref,
    own_ref,
    other_ref,
    dout_ref,
    attn_ref,
    lora_ref,
    stat_ref,
    dq_ref,
    dk_own_ref,
    dv_own_ref,
    pair_other_ref,
    down_grad_ref,
    dk_own,
    dv_own,
    dk_other,
    dv_other,
):
    blocks = own_ref.shape[0]
    step = TILE // tok
    sub = sub_ref[0]
    keys_own_t = rows_of(own_ref, blocks, tok, tok).T
    keys_other_t = rows_of(other_ref, blocks, 0, tok).T
    tiles = blocks // step
    for tile in reversed(range(tiles)):
        upto = (tile + 1) * step
        width = upto * tok
        at = tile * TILE
        queries = own_ref[tile * step : upto, 0:tok, :].reshape(TILE, HD)
        douts = dout_ref[tile * step : upto, 0:tok, :].reshape(TILE, HD)
        highest = stat_ref[0:1, at : at + TILE]
        inverse = stat_ref[1:2, at : at + TILE]
        own, other = scores_of(
            sub, rows_of(own_ref, upto, tok, tok), rows_of(other_ref, upto, 0, tok), queries, tok
        )
        own = jnp.exp2((own - highest) * LOG2_SCALE) * inverse
        other = jnp.exp2((other - highest) * LOG2_SCALE) * inverse
        dprob_own = dot_nt(rows_of(own_ref, upto, 2 * tok, tok), douts)
        dprob_other = dot_nt(rows_of(other_ref, upto, tok, tok), douts)
        delta = jnp.sum(own * dprob_own, axis=0, keepdims=True) + jnp.sum(
            other * dprob_other, axis=0, keepdims=True
        )
        ds_own = (own * (dprob_own - delta) * SCALE).astype(jnp.bfloat16)
        ds_other = (other * (dprob_other - delta) * SCALE).astype(jnp.bfloat16)
        dq = dot_nn(keys_own_t[:, :width], ds_own) + dot_nn(keys_other_t[:, :width], ds_other)
        dq_ref[tile * step : upto] = dq.T.astype(jnp.bfloat16).reshape(step, tok, HD)
        terms = (
            (dk_own, dot_nn(ds_own, queries)),
            (dk_other, dot_nn(ds_other, queries)),
            (dv_own, dot_nn(own.astype(jnp.bfloat16), douts)),
            (dv_other, dot_nn(other.astype(jnp.bfloat16), douts)),
        )
        for total, term in terms:
            if tile == tiles - 1:
                total[...] = term
            else:
                total[0:width] += term
    shape = (blocks, tok, HD)
    dk_own_ref[...] = dk_own[...].reshape(shape)
    dv_own_ref[...] = dv_own[...].reshape(shape)
    pair_other_ref[:, 0:tok, :] = dk_other[...].astype(jnp.bfloat16).reshape(shape)
    pair_other_ref[:, tok : 2 * tok, :] = dv_other[...].astype(jnp.bfloat16).reshape(shape)
    low_rank = lora_ref.shape[0]
    down_grad_ref[...] = 2.0 * dot_nt(lora_ref[...], attn_ref[...])


def call_kernel(body, outs, scratch, flops, exps, *operands):
    in_bytes = sum(x.size * x.dtype.itemsize for x in operands)
    out_bytes = sum(x.size * x.dtype.itemsize for x in outs)
    specs = [pl.BlockSpec(memory_space=pltpu.SMEM)]
    specs += [pl.BlockSpec(memory_space=pltpu.VMEM)] * (len(operands) - 1)
    return pl.pallas_call(
        body,
        out_shape=outs,
        in_specs=specs,
        out_specs=[pl.BlockSpec(memory_space=pltpu.VMEM)] * len(outs),
        scratch_shapes=scratch,
        compiler_params=pltpu.CompilerParams(vmem_limit_bytes=48 * 1024 * 1024),
        cost_estimate=pl.CostEstimate(
            flops=flops, bytes_accessed=in_bytes + out_bytes, transcendentals=exps
        ),
    )(*operands)


def shape_of(shape, dtype):
    return jax.ShapeDtypeStruct(shape, dtype)


def on_device(
    sizes,
    head_query_rows,
    head_key_rows,
    head_value_rows,
    output_gradient,
    output_matrix,
    adapter_down_weight,
    adapter_up_weight,
):
    seqs, heads, subs = sizes
    tok, feats = head_query_rows.shape
    cols = output_gradient.shape[1]
    low_rank = adapter_up_weight.shape[0]
    local_heads = feats // HD
    block_rows = tok * subs
    ranks = GROUP // block_rows
    copies = ranks // local_heads
    shift_blocks = GROUP // 2 // block_rows

    seq = lax.axis_index("seq")
    head = lax.axis_index("head")
    sub = lax.axis_index("sub")
    shift = jnp.where(head >= heads // 2, shift_blocks, 0)
    rank = (seq - shift + seqs) % ranks
    my_head = rank // copies

    groups = []
    for at_head in range(heads):
        moved = shift_blocks if at_head >= heads // 2 else 0
        for first in range(0, seqs, ranks):
            groups.append(
                [((first + moved + i) % seqs) * heads + at_head for i in range(ranks)]
            )

    def exchange(parts):
        return lax.all_to_all(
            parts, ("seq", "head"), 0, 0, axis_index_groups=groups, tiled=True
        )

    def by_head(rows):
        parts = rows.reshape(tok, local_heads, HD).transpose(1, 0, 2)
        return parts if copies == 1 else jnp.repeat(parts, copies, axis=0)

    def from_heads(parts):
        return parts[::copies].transpose(1, 0, 2).reshape(tok, feats)

    def swap(value):
        if subs == 1:
            return value
        return lax.ppermute(value, "sub", [(0, 1), (1, 0)])

    chunks = heads // subs
    pieces = []
    for k in range(heads):
        pairs = []
        for src_head in range(heads):
            for src_sub in range(subs):
                j = (src_head % chunks) * subs + src_sub
                dst = ((j + k) % heads) * subs + src_head // chunks
                pairs.append((src_head * subs + src_sub, dst))
        pieces.append(lax.ppermute(output_gradient, ("head", "sub"), pairs))

    sent = jnp.concatenate(
        [by_head(head_query_rows), by_head(head_key_rows), by_head(head_value_rows)], axis=1
    )
    own = exchange(sent)
    other = swap(own[:, tok:])

    up_half = lax.dynamic_slice_in_dim(adapter_up_weight, sub * chunks * cols, chunks * cols, 1)
    if chunks == 1:
        both = jnp.concatenate(pieces, axis=0)
        lora_all = dot_nt(both, up_half)
        grad_all = dot_nt(both, output_matrix)
        grad_all += 2.0 * dot_nt(lora_all.astype(jnp.bfloat16), adapter_down_weight)
        grads = [grad_all[k * tok : (k + 1) * tok] for k in range(heads)]
        loras = [lora_all[k * tok : (k + 1) * tok] for k in range(heads)]
    else:
        grads, loras = [], []
        for k in range(heads):
            at = (((head - k + heads) % heads) // subs) * cols
            lora = dot_nt(pieces[k], lax.dynamic_slice_in_dim(up_half, at, cols, 1))
            grad = dot_nt(pieces[k], lax.dynamic_slice_in_dim(output_matrix, at, cols, 1))
            grads.append(grad + 2.0 * dot_nt(lora.astype(jnp.bfloat16), adapter_down_weight))
            loras.append(lora)

    def terms_for(which, terms):
        total = None
        for k in range(heads):
            mine = ((head - k + heads) % heads) % subs == which
            term = jnp.where(mine, terms[k], 0.0)
            total = term if total is None else total + term
        return total

    packed = [jnp.concatenate((g, l), axis=1) for g, l in zip(grads, loras)]
    received = swap(terms_for(1 - sub, packed).astype(jnp.bfloat16))
    packed_own = terms_for(sub, packed) + received.astype(jnp.float32)
    attention_gradient = packed_own[:, :feats].astype(jnp.bfloat16)
    lora_up = packed_own[:, feats:]

    sub_arg = jnp.full((1,), sub, jnp.int32)
    down_head = lax.dynamic_slice_in_dim(adapter_down_weight, my_head * HD, HD, 0)
    rows = ranks * tok
    pair_count = rows * (rows + TILE)
    attn_t, mid_t, stats = call_kernel(
        functools.partial(forward_kernel, tok),
        [
            shape_of((HD, rows), jnp.bfloat16),
            shape_of((low_rank, rows), jnp.float32),
            shape_of((8, rows), jnp.float32),
        ],
        [],
        4 * pair_count * HD,
        pair_count,
        sub_arg,
        own,
        other,
        down_head.T,
    )

    lora_rows = jnp.broadcast_to(lora_up.astype(jnp.bfloat16).T, (ranks, low_rank, tok))
    mid_rows = mid_t.reshape(low_rank, ranks, tok).transpose(1, 0, 2).astype(jnp.bfloat16)
    arrived = exchange(
        jnp.concatenate([by_head(attention_gradient), lora_rows, mid_rows], axis=1)
    )
    lora_t = arrived[:, tok : tok + low_rank].transpose(1, 0, 2).reshape(low_rank, rows)
    middle_t = jnp.sum(arrived[::copies, tok + low_rank :].astype(jnp.float32), axis=0)
    middle_sum = middle_t
    for k in range(1, heads):
        middle_sum += lax.ppermute(
            middle_t, "head", [(i, (i + k) % heads) for i in range(heads)]
        )
    up_part = 2.0 * dot_nn(middle_sum.astype(jnp.bfloat16), output_gradient)

    dq, dk_own, dv_own, pair_other, down_part = call_kernel(
        functools.partial(backward_kernel, tok),
        [
            shape_of((ranks, tok, HD), jnp.bfloat16),
            shape_of((ranks, tok, HD), jnp.float32),
            shape_of((ranks, tok, HD), jnp.float32),
            shape_of((ranks, 2 * tok, HD), jnp.bfloat16),
            shape_of((low_rank, HD), jnp.float32),
        ],
        [pltpu.VMEM((rows, HD), jnp.float32)] * 4,
        10 * pair_count * HD,
        pair_count,
        sub_arg,
        own,
        other,
        arrived[:, :tok],
        attn_t,
        lora_t,
        stats,
    )
    pair_received = swap(pair_other).astype(jnp.float32)
    dk = (dk_own + pair_received[:, :tok]).astype(jnp.bfloat16)
    dv = (dv_own + pair_received[:, tok:]).astype(jnp.bfloat16)
    back = exchange(jnp.concatenate([dq, dk, dv], axis=1))
    query_gradient = from_heads(back[:, :tok])
    key_gradient = from_heads(back[:, tok : 2 * tok])
    value_gradient = from_heads(back[:, 2 * tok :])

    peers = seqs * subs
    width = cols // peers
    scattered = lax.all_to_all(
        up_part.reshape(low_rank, peers, width).transpose(1, 0, 2), ("seq", "sub"), 0, 0, tiled=True
    )
    up_piece = jnp.sum(scattered, axis=0)
    mine = jnp.concatenate((down_part, up_piece), axis=1)
    everyone = lax.all_to_all(
        jnp.broadcast_to(mine, (peers,) + mine.shape), ("seq", "sub"), 0, 0, tiled=True
    )
    up_gradient = everyone[:, :, HD:].transpose(1, 0, 2).reshape(low_rank, cols)
    down_terms = jnp.sum(everyone[:, :, :HD].reshape(seqs, subs, low_rank, HD), axis=1)
    down_terms = jnp.where(
        head >= heads // 2, jnp.roll(down_terms, -shift_blocks, axis=0), down_terms
    )
    down_terms = jnp.sum(down_terms.reshape(seqs // ranks, ranks, low_rank, HD), axis=0)
    down_gradient = down_terms[::copies].transpose(0, 2, 1).reshape(feats, low_rank)
    return (query_gradient, key_gradient, value_gradient, down_gradient, up_gradient)


def solution(mesh):
    rows = P(("rep", "seq", "sub"), "head")
    sizes = (mesh.shape["seq"], mesh.shape["head"], mesh.shape["sub"])
    return jax.shard_map(
        functools.partial(on_device, sizes),
        mesh=mesh,
        in_specs=(rows, rows, rows, rows, P("head", "sub"), P("head", None), P()),
        out_specs=(rows, rows, rows, P(("rep", "head"), None), P("rep", "head")),
        check_vma=False,
    )
```

```python
import functools
import math

import jax
import jax.numpy as jnp
from jax import lax
from jax.experimental import pallas as pl
from jax.experimental.pallas import tpu as pltpu
from jax.sharding import PartitionSpec as P

HD = 128
GROUP = 2048
TILE = 256
HIDDEN = -1e30
SCALE = HD ** (-0.5)
LOG2_SCALE = SCALE * math.log2(math.e)


def dot_nt(left, right):
    return lax.dot_general(
        left, right, (((1,), (1,)), ((), ())), preferred_element_type=jnp.float32
    )


def dot_nn(left, right):
    return jnp.dot(left, right, preferred_element_type=jnp.float32)


def rows_of(ref, blocks, first, count):
    return ref[0:blocks, first : first + count, :].reshape(blocks * count, HD)


def scores_of(sub, keys_own, keys_other, queries, tok):
    def tail_hidden(scores, visible):
        head = scores.shape[0] - TILE
        tail = jnp.where(visible, scores[head:], HIDDEN)
        return tail if head == 0 else jnp.concatenate((scores[:head], tail), axis=0)

    key_at = lax.broadcasted_iota(jnp.int32, (TILE, TILE), 0)
    query_at = lax.broadcasted_iota(jnp.int32, (TILE, TILE), 1)
    own = tail_hidden(dot_nt(keys_own, queries), key_at <= query_at)
    other = tail_hidden(
        dot_nt(keys_other, queries), key_at // tok < query_at // tok + sub
    )
    return own, other


def attention_kernel(
    tok,
    sub_ref,
    own_ref,
    other_ref,
    query_ref,
    lora_ref,
    down_t_ref,
    dq_ref,
    pair_own_ref,
    pair_other_ref,
    mid_ref,
    down_grad_ref,
    dk_own,
    dv_own,
    dk_other,
    dv_other,
):
    blocks = own_ref.shape[0]
    step = TILE // tok
    sub = sub_ref[0]
    keys_own_t = rows_of(own_ref, blocks, 0, tok).T
    keys_other_t = rows_of(other_ref, blocks, 0, tok).T
    values_own_t = rows_of(own_ref, blocks, tok, tok).T
    values_other_t = rows_of(other_ref, blocks, tok, tok).T
    tiles = blocks // step
    down_total = None
    for tile in reversed(range(tiles)):
        upto = (tile + 1) * step
        width = upto * tok
        at = tile * TILE
        queries = query_ref[tile * step : upto, 0:tok, :].reshape(TILE, HD)
        douts = query_ref[tile * step : upto, tok : 2 * tok, :].reshape(TILE, HD)
        own, other = scores_of(
            sub, rows_of(own_ref, upto, 0, tok), rows_of(other_ref, upto, 0, tok), queries, tok
        )
        highest = jnp.maximum(
            jnp.max(own, axis=0, keepdims=True), jnp.max(other, axis=0, keepdims=True)
        )
        own = jnp.exp2((own - highest) * LOG2_SCALE)
        other = jnp.exp2((other - highest) * LOG2_SCALE)
        inverse = 1.0 / (
            jnp.sum(own, axis=0, keepdims=True) + jnp.sum(other, axis=0, keepdims=True)
        )
        own = own * inverse
        other = other * inverse
        own_lo = own.astype(jnp.bfloat16)
        other_lo = other.astype(jnp.bfloat16)
        attn = dot_nn(values_own_t[:, :width], own_lo) + dot_nn(
            values_other_t[:, :width], other_lo
        )
        attn = attn.astype(jnp.bfloat16)
        mid_ref[:, at : at + TILE] = dot_nn(down_t_ref[...], attn)
        down_term = dot_nt(lora_ref[:, at : at + TILE], attn)
        down_total = down_term if down_total is None else down_total + down_term
        dprob_own = dot_nt(rows_of(own_ref, upto, tok, tok), douts)
        dprob_other = dot_nt(rows_of(other_ref, upto, tok, tok), douts)
        delta = jnp.sum(own * dprob_own, axis=0, keepdims=True) + jnp.sum(
            other * dprob_other, axis=0, keepdims=True
        )
        ds_own = (own * (dprob_own - delta) * SCALE).astype(jnp.bfloat16)
        ds_other = (other * (dprob_other - delta) * SCALE).astype(jnp.bfloat16)
        dq = dot_nn(keys_own_t[:, :width], ds_own) + dot_nn(keys_other_t[:, :width], ds_other)
        dq_ref[tile * step : upto] = dq.T.astype(jnp.bfloat16).reshape(step, tok, HD)
        terms = (
            (dk_own, dot_nn(ds_own, queries)),
            (dk_other, dot_nn(ds_other, queries)),
            (dv_own, dot_nn(own_lo, douts)),
            (dv_other, dot_nn(other_lo, douts)),
        )
        for total, term in terms:
            if tile == tiles - 1:
                total[...] = term
            else:
                total[0:width] += term
    shape = (blocks, tok, HD)
    pair_own_ref[:, 0:tok, :] = dk_own[...].reshape(shape)
    pair_own_ref[:, tok : 2 * tok, :] = dv_own[...].reshape(shape)
    pair_other_ref[:, 0:tok, :] = dk_other[...].astype(jnp.bfloat16).reshape(shape)
    pair_other_ref[:, tok : 2 * tok, :] = dv_other[...].astype(jnp.bfloat16).reshape(shape)
    down_grad_ref[...] = 2.0 * down_total


def call_kernel(body, outs, scratch, flops, exps, *operands):
    in_bytes = sum(x.size * x.dtype.itemsize for x in operands)
    out_bytes = sum(x.size * x.dtype.itemsize for x in outs)
    specs = [pl.BlockSpec(memory_space=pltpu.SMEM)]
    specs += [pl.BlockSpec(memory_space=pltpu.VMEM)] * (len(operands) - 1)
    return pl.pallas_call(
        body,
        out_shape=outs,
        in_specs=specs,
        out_specs=[pl.BlockSpec(memory_space=pltpu.VMEM)] * len(outs),
        scratch_shapes=scratch,
        compiler_params=pltpu.CompilerParams(vmem_limit_bytes=48 * 1024 * 1024),
        cost_estimate=pl.CostEstimate(
            flops=flops, bytes_accessed=in_bytes + out_bytes, transcendentals=exps
        ),
    )(*operands)


def shape_of(shape, dtype):
    return jax.ShapeDtypeStruct(shape, dtype)


def all_summed(value, seqs, subs):
    steps = [("sub", 1, subs)] if subs > 1 else []
    bit = 1
    while bit < seqs:
        steps.append(("seq", bit, seqs))
        bit *= 2
    uppers = []
    for axis, bit, count in steps[:2]:
        pairs = [(i, i ^ bit) for i in range(count)]
        upper = (lax.axis_index(axis) // bit) % 2 == 1
        low, high = jnp.split(value, 2, axis=1)
        taken = lax.ppermute(jnp.where(upper, low, high), axis, pairs)
        value = jnp.where(upper, high, low) + taken
        uppers.append((axis, pairs, upper))
    for axis, bit, count in steps[2:]:
        value = value + lax.ppermute(value, axis, [(i, i ^ bit) for i in range(count)])
    for axis, pairs, upper in reversed(uppers):
        taken = lax.ppermute(value, axis, pairs)
        value = jnp.where(
            upper,
            jnp.concatenate((taken, value), axis=1),
            jnp.concatenate((value, taken), axis=1),
        )
    return value


def on_device(
    sizes,
    head_query_rows,
    head_key_rows,
    head_value_rows,
    output_gradient,
    output_matrix,
    adapter_down_weight,
    adapter_up_weight,
):
    seqs, heads, subs = sizes
    tok, feats = head_query_rows.shape
    cols = output_gradient.shape[1]
    low_rank = adapter_up_weight.shape[0]
    local_heads = feats // HD
    block_rows = tok * subs
    ranks = GROUP // block_rows
    copies = ranks // local_heads
    shift_blocks = GROUP // 2 // block_rows

    seq = lax.axis_index("seq")
    head = lax.axis_index("head")
    sub = lax.axis_index("sub")
    shift = jnp.where(head >= heads // 2, shift_blocks, 0)
    rank = (seq - shift + seqs) % ranks
    my_head = rank // copies

    groups = []
    for at_head in range(heads):
        moved = shift_blocks if at_head >= heads // 2 else 0
        for first in range(0, seqs, ranks):
            groups.append(
                [((first + moved + i) % seqs) * heads + at_head for i in range(ranks)]
            )

    def exchange(parts):
        return lax.all_to_all(
            parts, ("seq", "head"), 0, 0, axis_index_groups=groups, tiled=True
        )

    def by_head(rows):
        parts = rows.reshape(tok, local_heads, HD).transpose(1, 0, 2)
        return parts if copies == 1 else jnp.repeat(parts, copies, axis=0)

    def from_heads(parts):
        return parts[::copies].transpose(1, 0, 2).reshape(tok, feats)

    def swap(value):
        if subs == 1:
            return value
        return lax.ppermute(value, "sub", [(0, 1), (1, 0)])

    chunks = heads // subs
    pieces = []
    for k in range(heads):
        pairs = []
        for src_head in range(heads):
            for src_sub in range(subs):
                j = (src_head % chunks) * subs + src_sub
                dst = ((j + k) % heads) * subs + src_head // chunks
                pairs.append((src_head * subs + src_sub, dst))
        pieces.append(lax.ppermute(output_gradient, ("head", "sub"), pairs))

    own = exchange(jnp.concatenate([by_head(head_key_rows), by_head(head_value_rows)], axis=1))
    other = swap(own)

    up_half = lax.dynamic_slice_in_dim(adapter_up_weight, sub * chunks * cols, chunks * cols, 1)
    if chunks == 1:
        both = jnp.concatenate(pieces, axis=0)
        lora_all = dot_nt(both, up_half)
        grad_all = dot_nt(both, output_matrix)
        grad_all += 2.0 * dot_nt(lora_all.astype(jnp.bfloat16), adapter_down_weight)
        grads = [grad_all[k * tok : (k + 1) * tok] for k in range(heads)]
        loras = [lora_all[k * tok : (k + 1) * tok] for k in range(heads)]
    else:
        grads, loras = [], []
        for k in range(heads):
            at = (((head - k + heads) % heads) // subs) * cols
            lora = dot_nt(pieces[k], lax.dynamic_slice_in_dim(up_half, at, cols, 1))
            grad = dot_nt(pieces[k], lax.dynamic_slice_in_dim(output_matrix, at, cols, 1))
            grads.append(grad + 2.0 * dot_nt(lora.astype(jnp.bfloat16), adapter_down_weight))
            loras.append(lora)

    def terms_for(which, terms):
        total = None
        for k in range(heads):
            mine = ((head - k + heads) % heads) % subs == which
            term = jnp.where(mine, terms[k], 0.0)
            total = term if total is None else total + term
        return total

    packed = [jnp.concatenate((g, l), axis=1) for g, l in zip(grads, loras)]
    received = swap(terms_for(1 - sub, packed).astype(jnp.bfloat16))
    packed_own = terms_for(sub, packed) + received.astype(jnp.float32)
    attention_gradient = packed_own[:, :feats].astype(jnp.bfloat16)
    lora_up = packed_own[:, feats:]

    lora_rows = jnp.broadcast_to(lora_up.astype(jnp.bfloat16).T, (ranks, low_rank, tok))
    arrived = exchange(
        jnp.concatenate(
            [by_head(head_query_rows), by_head(attention_gradient), lora_rows], axis=1
        )
    )
    rows = ranks * tok
    lora_t = arrived[:, 2 * tok :].transpose(1, 0, 2).reshape(low_rank, rows)
    sub_arg = jnp.full((1,), sub, jnp.int32)
    down_head = lax.dynamic_slice_in_dim(adapter_down_weight, my_head * HD, HD, 0)
    pair_count = rows * (rows + TILE)
    dq, pair_own, pair_other, mid_t, down_part = call_kernel(
        functools.partial(attention_kernel, tok),
        [
            shape_of((ranks, tok, HD), jnp.bfloat16),
            shape_of((ranks, 2 * tok, HD), jnp.float32),
            shape_of((ranks, 2 * tok, HD), jnp.bfloat16),
            shape_of((low_rank, rows), jnp.float32),
            shape_of((low_rank, HD), jnp.float32),
        ],
        [pltpu.VMEM((rows, HD), jnp.float32)] * 4,
        12 * pair_count * HD,
        pair_count,
        sub_arg,
        own,
        other,
        arrived,
        lora_t,
        down_head.T,
    )
    pair = (pair_own + swap(pair_other).astype(jnp.float32)).astype(jnp.bfloat16)
    back = exchange(jnp.concatenate([dq, pair], axis=1))
    query_gradient = from_heads(back[:, :tok])
    key_gradient = from_heads(back[:, tok : 2 * tok])
    value_gradient = from_heads(back[:, 2 * tok :])

    first_copy = rank % copies == 0
    middle = mid_t if copies == 1 else jnp.where(first_copy, mid_t, 0.0)
    bit = ranks // 2
    while bit:
        pairs = [(g[i], g[i ^ bit]) for g in groups for i in range(ranks)]
        upper = (rank // bit) % 2 == 1
        low, high = jnp.split(middle, 2, axis=1)
        taken = lax.ppermute(jnp.where(upper, low, high), ("seq", "head"), pairs)
        middle = jnp.where(upper, high, low) + taken
        bit //= 2
    bit = 1
    while bit < heads:
        middle += lax.ppermute(middle, "head", [(i, i ^ bit) for i in range(heads)])
        bit *= 2

    up_part = 2.0 * dot_nn(middle.astype(jnp.bfloat16), output_gradient)
    own_slot = lax.broadcasted_iota(jnp.int32, (1, feats), 1) // HD == my_head
    own_slot &= first_copy
    down_placed = jnp.where(own_slot, jnp.tile(down_part, (1, local_heads)), 0.0)
    total = all_summed(jnp.concatenate((up_part, down_placed), axis=1), seqs, subs)
    up_gradient = total[:, :cols]
    down_gradient = total[:, cols:].T
    return (query_gradient, key_gradient, value_gradient, down_gradient, up_gradient)


def solution(mesh):
    rows = P(("rep", "seq", "sub"), "head")
    sizes = (mesh.shape["seq"], mesh.shape["head"], mesh.shape["sub"])
    return jax.shard_map(
        functools.partial(on_device, sizes),
        mesh=mesh,
        in_specs=(rows, rows, rows, rows, P("head", "sub"), P("head", None), P()),
        out_specs=(rows, rows, rows, P(("rep", "head"), None), P("rep", "head")),
        check_vma=False,
    )
```

```python
import functools
import math

import jax
import jax.numpy as jnp
from jax import lax
from jax.experimental import pallas as pl
from jax.experimental.pallas import tpu as pltpu
from jax.sharding import PartitionSpec as P

HD = 128
GROUP = 2048
TILE = 256
HIDDEN = -1e30
SCALE = HD ** (-0.5)
LOG2_SCALE = SCALE * math.log2(math.e)


def dot_nt(left, right):
    return lax.dot_general(
        left, right, (((1,), (1,)), ((), ())), preferred_element_type=jnp.float32
    )


def dot_nn(left, right):
    return jnp.dot(left, right, preferred_element_type=jnp.float32)


def rows_of(ref, blocks, first, count):
    return ref[0:blocks, first : first + count, :].reshape(blocks * count, HD)


def scores_of(sub, keys_own, keys_other, queries, tok):
    def tail_hidden(scores, visible):
        head = scores.shape[0] - TILE
        tail = jnp.where(visible, scores[head:], HIDDEN)
        return tail if head == 0 else jnp.concatenate((scores[:head], tail), axis=0)

    key_at = lax.broadcasted_iota(jnp.int32, (TILE, TILE), 0)
    query_at = lax.broadcasted_iota(jnp.int32, (TILE, TILE), 1)
    own = tail_hidden(dot_nt(keys_own, queries), key_at <= query_at)
    other = tail_hidden(
        dot_nt(keys_other, queries), key_at // tok < query_at // tok + sub
    )
    return own, other


def forward_kernel(tok, sub_ref, own_ref, other_ref, down_t_ref, attn_ref, mid_ref, stat_ref):
    blocks = own_ref.shape[0]
    step = TILE // tok
    sub = sub_ref[0]
    values_own_t = rows_of(own_ref, blocks, 2 * tok, tok).T
    values_other_t = rows_of(other_ref, blocks, tok, tok).T
    for tile in range(blocks // step):
        upto = (tile + 1) * step
        width = upto * tok
        at = tile * TILE
        queries = own_ref[tile * step : upto, 0:tok, :].reshape(TILE, HD)
        own, other = scores_of(
            sub, rows_of(own_ref, upto, tok, tok), rows_of(other_ref, upto, 0, tok), queries, tok
        )
        highest = jnp.maximum(
            jnp.max(own, axis=0, keepdims=True), jnp.max(other, axis=0, keepdims=True)
        )
        own = jnp.exp2((own - highest) * LOG2_SCALE)
        other = jnp.exp2((other - highest) * LOG2_SCALE)
        inverse = 1.0 / (
            jnp.sum(own, axis=0, keepdims=True) + jnp.sum(other, axis=0, keepdims=True)
        )
        attn = dot_nn(values_own_t[:, :width], own.astype(jnp.bfloat16)) + dot_nn(
            values_other_t[:, :width], other.astype(jnp.bfloat16)
        )
        attn = (attn * inverse).astype(jnp.bfloat16)
        attn_ref[:, at : at + TILE] = attn
        mid_ref[:, at : at + TILE] = dot_nn(down_t_ref[...], attn)
        stat_ref[0:1, at : at + TILE] = highest
        stat_ref[1:2, at : at + TILE] = inverse


def backward_kernel(
    tok,
    sub_ref,
    own_ref,
    other_ref,
    dout_ref,
    attn_ref,
    lora_ref,
    stat_ref,
    dq_ref,
    dk_own_ref,
    dv_own_ref,
    pair_other_ref,
    down_grad_ref,
    dk_own,
    dv_own,
    dk_other,
    dv_other,
):
    blocks = own_ref.shape[0]
    step = TILE // tok
    sub = sub_ref[0]
    keys_own_t = rows_of(own_ref, blocks, tok, tok).T
    keys_other_t = rows_of(other_ref, blocks, 0, tok).T
    tiles = blocks // step
    for tile in reversed(range(tiles)):
        upto = (tile + 1) * step
        width = upto * tok
        at = tile * TILE
        queries = own_ref[tile * step : upto, 0:tok, :].reshape(TILE, HD)
        douts = dout_ref[tile * step : upto, 0:tok, :].reshape(TILE, HD)
        highest = stat_ref[0:1, at : at + TILE]
        inverse = stat_ref[1:2, at : at + TILE]
        own, other = scores_of(
            sub, rows_of(own_ref, upto, tok, tok), rows_of(other_ref, upto, 0, tok), queries, tok
        )
        own = jnp.exp2((own - highest) * LOG2_SCALE) * inverse
        other = jnp.exp2((other - highest) * LOG2_SCALE) * inverse
        dprob_own = dot_nt(rows_of(own_ref, upto, 2 * tok, tok), douts)
        dprob_other = dot_nt(rows_of(other_ref, upto, tok, tok), douts)
        delta = jnp.sum(own * dprob_own, axis=0, keepdims=True) + jnp.sum(
            other * dprob_other, axis=0, keepdims=True
        )
        ds_own = (own * (dprob_own - delta) * SCALE).astype(jnp.bfloat16)
        ds_other = (other * (dprob_other - delta) * SCALE).astype(jnp.bfloat16)
        dq = dot_nn(keys_own_t[:, :width], ds_own) + dot_nn(keys_other_t[:, :width], ds_other)
        dq_ref[tile * step : upto] = dq.T.astype(jnp.bfloat16).reshape(step, tok, HD)
        terms = (
            (dk_own, dot_nn(ds_own, queries)),
            (dk_other, dot_nn(ds_other, queries)),
            (dv_own, dot_nn(own.astype(jnp.bfloat16), douts)),
            (dv_other, dot_nn(other.astype(jnp.bfloat16), douts)),
        )
        for total, term in terms:
            if tile == tiles - 1:
                total[...] = term
            else:
                total[0:width] += term
    shape = (blocks, tok, HD)
    dk_own_ref[...] = dk_own[...].reshape(shape)
    dv_own_ref[...] = dv_own[...].reshape(shape)
    pair_other_ref[:, 0:tok, :] = dk_other[...].astype(jnp.bfloat16).reshape(shape)
    pair_other_ref[:, tok : 2 * tok, :] = dv_other[...].astype(jnp.bfloat16).reshape(shape)
    low_rank = lora_ref.shape[0]
    down_grad_ref[...] = 2.0 * dot_nt(lora_ref[...], attn_ref[...])


def call_kernel(body, outs, scratch, flops, exps, *operands):
    in_bytes = sum(x.size * x.dtype.itemsize for x in operands)
    out_bytes = sum(x.size * x.dtype.itemsize for x in outs)
    specs = [pl.BlockSpec(memory_space=pltpu.SMEM)]
    specs += [pl.BlockSpec(memory_space=pltpu.VMEM)] * (len(operands) - 1)
    return pl.pallas_call(
        body,
        out_shape=outs,
        in_specs=specs,
        out_specs=[pl.BlockSpec(memory_space=pltpu.VMEM)] * len(outs),
        scratch_shapes=scratch,
        compiler_params=pltpu.CompilerParams(vmem_limit_bytes=48 * 1024 * 1024),
        cost_estimate=pl.CostEstimate(
            flops=flops, bytes_accessed=in_bytes + out_bytes, transcendentals=exps
        ),
    )(*operands)


def shape_of(shape, dtype):
    return jax.ShapeDtypeStruct(shape, dtype)


def all_summed(value, seqs, subs):
    steps = []
    bit = 1
    while bit < seqs:
        steps.append([(i, i ^ bit) for i in range(seqs)])
        bit *= 2
    if subs == 2:
        upper = lax.axis_index("sub") == 1
        across = [(0, 1), (1, 0)]
        low, high = jnp.split(value, 2, axis=1)
        taken = lax.ppermute(jnp.where(upper, low, high).astype(jnp.bfloat16), "sub", across)
        value = jnp.where(upper, high, low) + taken.astype(jnp.float32)
    for pairs in steps:
        taken = lax.ppermute(value.astype(jnp.bfloat16), "seq", pairs)
        value = value.astype(jnp.bfloat16).astype(jnp.float32) + taken.astype(jnp.float32)
    if subs == 2:
        taken = lax.ppermute(value, "sub", across)
        value = jnp.where(
            upper,
            jnp.concatenate((taken, value), axis=1),
            jnp.concatenate((value, taken), axis=1),
        )
    return value


def copy_kernel(moves, *refs):
    operands, outs, sems = refs[: moves[1]], refs[moves[1] : -1], refs[-1]
    copies = [
        pltpu.make_async_copy(operands[a].at[at], outs[b].at[to], sems.at[n])
        for n, (a, at, b, to) in enumerate(moves[0])
    ]
    for copy in copies:
        copy.start()
    for copy in copies:
        copy.wait()


def rearranged(moves, outs, *operands):
    size = sum(x.size * x.dtype.itemsize for x in operands)
    size += sum(x.size * x.dtype.itemsize for x in outs)
    return pl.pallas_call(
        functools.partial(copy_kernel, (moves, len(operands))),
        out_shape=outs,
        in_specs=[pl.BlockSpec(memory_space=pl.ANY)] * len(operands),
        out_specs=[pl.BlockSpec(memory_space=pl.ANY)] * len(outs),
        scratch_shapes=[pltpu.SemaphoreType.DMA((len(moves),))],
        cost_estimate=pl.CostEstimate(flops=0, bytes_accessed=size, transcendentals=0),
    )(*operands)


def dout_kernel(copies, tok, own_ref, taken_ref, message_ref):
    feats = own_ref.shape[1] - HD
    lora = (own_ref[:, feats:] + taken_ref[:, feats:].astype(jnp.float32)).T
    low_rank = message_ref.shape[1] - tok
    lora = lora[0:low_rank].astype(jnp.bfloat16)
    for rank in range(message_ref.shape[0]):
        at = (rank // copies) * HD
        part = own_ref[:, at : at + HD] + taken_ref[:, at : at + HD].astype(jnp.float32)
        message_ref[rank, 0:tok, :] = part.astype(jnp.bfloat16)
        message_ref[rank, tok : tok + low_rank, :] = lora


def on_device(
    sizes,
    head_query_rows,
    head_key_rows,
    head_value_rows,
    output_gradient,
    output_matrix,
    adapter_down_weight,
    adapter_up_weight,
):
    seqs, heads, subs = sizes
    tok, feats = head_query_rows.shape
    cols = output_gradient.shape[1]
    low_rank = adapter_up_weight.shape[0]
    local_heads = feats // HD
    block_rows = tok * subs
    ranks = GROUP // block_rows
    copies = ranks // local_heads
    shift_blocks = GROUP // 2 // block_rows

    seq = lax.axis_index("seq")
    head = lax.axis_index("head")
    sub = lax.axis_index("sub")
    shift = jnp.where(head >= heads // 2, shift_blocks, 0)
    rank = (seq - shift + seqs) % ranks
    my_head = rank // copies

    groups = []
    for at_head in range(heads):
        moved = shift_blocks if at_head >= heads // 2 else 0
        for first in range(0, seqs, ranks):
            groups.append(
                [((first + moved + i) % seqs) * heads + at_head for i in range(ranks)]
            )

    def exchange(parts):
        return lax.all_to_all(
            parts, ("seq", "head"), 0, 0, axis_index_groups=groups, tiled=True
        )

    def swap(value):
        if subs == 1:
            return value
        return lax.ppermute(value, "sub", [(0, 1), (1, 0)])

    head_cols = [pl.ds(i // copies * HD, HD) for i in range(ranks)]
    rows_at = [pl.ds(i * tok, tok) for i in range(3)]
    everything = pl.ds(0, tok)
    moves = [
        (n, (everything, head_cols[i]), 0, (i, rows_at[n]))
        for i in range(ranks)
        for n in range(3)
    ]
    (sent,) = rearranged(
        moves,
        [shape_of((ranks, 3 * tok, HD), head_query_rows.dtype)],
        head_query_rows,
        head_key_rows,
        head_value_rows,
    )
    sent, output_gradient = lax.optimization_barrier((sent, output_gradient))
    own = exchange(sent)
    other = swap(own[:, tok:])

    chunks = heads // subs
    pieces = []
    for k in range(heads):
        pairs = []
        for src_head in range(heads):
            for src_sub in range(subs):
                j = (src_head % chunks) * subs + src_sub
                dst = ((j + k) % heads) * subs + src_head // chunks
                pairs.append((src_head * subs + src_sub, dst))
        pieces.append(lax.ppermute(output_gradient, ("head", "sub"), pairs))

    up_half = lax.dynamic_slice_in_dim(adapter_up_weight, sub * chunks * cols, chunks * cols, 1)
    if chunks == 1:
        both = jnp.concatenate(pieces, axis=0)
        lora_all = dot_nt(both, up_half)
        grad_all = dot_nt(both, output_matrix)
        grad_all += 2.0 * dot_nt(lora_all.astype(jnp.bfloat16), adapter_down_weight)
        grads = [grad_all[k * tok : (k + 1) * tok] for k in range(heads)]
        loras = [lora_all[k * tok : (k + 1) * tok] for k in range(heads)]
    else:
        grads, loras = [], []
        for k in range(heads):
            at = (((head - k + heads) % heads) // subs) * cols
            lora = dot_nt(pieces[k], lax.dynamic_slice_in_dim(up_half, at, cols, 1))
            grad = dot_nt(pieces[k], lax.dynamic_slice_in_dim(output_matrix, at, cols, 1))
            grads.append(grad + 2.0 * dot_nt(lora.astype(jnp.bfloat16), adapter_down_weight))
            loras.append(lora)

    def terms_for(which, terms):
        total = None
        for k in range(heads):
            mine = ((head - k + heads) % heads) % subs == which
            term = jnp.where(mine, terms[k], 0.0)
            total = term if total is None else total + term
        return total

    spare = jnp.zeros((tok, HD - low_rank), jnp.float32)
    packed = [jnp.concatenate((g, l, spare), axis=1) for g, l in zip(grads, loras)]
    received = swap(terms_for(1 - sub, packed).astype(jnp.bfloat16))
    packed_own = terms_for(sub, packed)
    whole = pl.BlockSpec(memory_space=pltpu.VMEM)
    message = pl.pallas_call(
        functools.partial(dout_kernel, copies, tok),
        out_shape=shape_of((ranks, tok + low_rank, HD), jnp.bfloat16),
        in_specs=[whole, whole],
        out_specs=whole,
        cost_estimate=pl.CostEstimate(
            flops=packed_own.size, bytes_accessed=8 * packed_own.size, transcendentals=0
        ),
    )(packed_own, received)
    arrived = exchange(message)

    sub_arg = jnp.full((1,), sub, jnp.int32)
    down_head = lax.dynamic_slice_in_dim(adapter_down_weight, my_head * HD, HD, 0)
    rows = ranks * tok
    pair_count = rows * (rows + TILE)
    attn_t, mid_t, stats = call_kernel(
        functools.partial(forward_kernel, tok),
        [
            shape_of((HD, rows), jnp.bfloat16),
            shape_of((low_rank, rows), jnp.float32),
            shape_of((8, rows), jnp.float32),
        ],
        [],
        4 * pair_count * HD,
        pair_count,
        sub_arg,
        own,
        other,
        down_head.T,
    )

    first_copy = rank % copies == 0
    middle = mid_t if copies == 1 else jnp.where(first_copy, mid_t, 0.0)
    bit = ranks // 2
    while bit:
        pairs = [(g[i], g[i ^ bit]) for g in groups for i in range(ranks)]
        upper = (rank // bit) % 2 == 1
        low, high = jnp.split(middle, 2, axis=1)
        taken = lax.ppermute(jnp.where(upper, low, high), ("seq", "head"), pairs)
        middle = jnp.where(upper, high, low) + taken
        bit //= 2
    bit = 1
    while bit < heads:
        middle += lax.ppermute(middle, "head", [(i, i ^ bit) for i in range(heads)])
        bit *= 2
    up_part = 2.0 * dot_nn(middle.astype(jnp.bfloat16), output_gradient)

    lora_t = arrived[:, tok:].transpose(1, 0, 2).reshape(low_rank, rows)
    dq, dk_own, dv_own, pair_other, down_part = call_kernel(
        functools.partial(backward_kernel, tok),
        [
            shape_of((ranks, tok, HD), jnp.bfloat16),
            shape_of((ranks, tok, HD), jnp.float32),
            shape_of((ranks, tok, HD), jnp.float32),
            shape_of((ranks, 2 * tok, HD), jnp.bfloat16),
            shape_of((low_rank, HD), jnp.float32),
        ],
        [pltpu.VMEM((rows, HD), jnp.float32)] * 4,
        10 * pair_count * HD,
        pair_count,
        sub_arg,
        own,
        other,
        arrived,
        attn_t,
        lora_t,
        stats,
    )
    pair_received = swap(pair_other).astype(jnp.float32)
    dk = (dk_own + pair_received[:, :tok]).astype(jnp.bfloat16)
    dv = (dv_own + pair_received[:, tok:]).astype(jnp.bfloat16)
    back = exchange(jnp.concatenate([dq, dk, dv], axis=1))
    out_moves = [
        (0, (i * copies, rows_at[n]), n, (everything, pl.ds(i * HD, HD)))
        for i in range(local_heads)
        for n in range(3)
    ]
    query_gradient, key_gradient, value_gradient = rearranged(
        out_moves, [shape_of((tok, feats), back.dtype)] * 3, back
    )

    own_slot = lax.broadcasted_iota(jnp.int32, (1, feats), 1) // HD == my_head
    own_slot &= first_copy
    down_placed = jnp.where(own_slot, jnp.tile(down_part, (1, local_heads)), 0.0)
    total = all_summed(jnp.concatenate((up_part, down_placed), axis=1), seqs, subs)
    up_gradient = total[:, :cols]
    down_gradient = total[:, cols:].T
    return (query_gradient, key_gradient, value_gradient, down_gradient, up_gradient)


def solution(mesh):
    rows = P(("rep", "seq", "sub"), "head")
    sizes = (mesh.shape["seq"], mesh.shape["head"], mesh.shape["sub"])
    return jax.shard_map(
        functools.partial(on_device, sizes),
        mesh=mesh,
        in_specs=(rows, rows, rows, rows, P("head", "sub"), P("head", None), P()),
        out_specs=(rows, rows, rows, P(("rep", "head"), None), P("rep", "head")),
        check_vma=False,
    )
```

```python
import functools
import math

import jax
import jax.numpy as jnp
from jax import lax
from jax.experimental import pallas as pl
from jax.experimental.pallas import tpu as pltpu
from jax.sharding import PartitionSpec as P

HD = 128
GROUP = 2048
TILE = 256
HIDDEN = -1e30
SCALE = HD ** (-0.5)
LOG2_SCALE = SCALE * math.log2(math.e)


def dot_nt(left, right):
    return lax.dot_general(
        left, right, (((1,), (1,)), ((), ())), preferred_element_type=jnp.float32
    )


def dot_nn(left, right):
    return jnp.dot(left, right, preferred_element_type=jnp.float32)


def rows_of(ref, blocks, first, count):
    return ref[0:blocks, first : first + count, :].reshape(blocks * count, HD)


def scores_of(sub, keys_own, keys_other, queries, tok):
    def tail_hidden(scores, visible):
        head = scores.shape[0] - TILE
        tail = jnp.where(visible, scores[head:], HIDDEN)
        return tail if head == 0 else jnp.concatenate((scores[:head], tail), axis=0)

    key_at = lax.broadcasted_iota(jnp.int32, (TILE, TILE), 0)
    query_at = lax.broadcasted_iota(jnp.int32, (TILE, TILE), 1)
    own = tail_hidden(dot_nt(keys_own, queries), key_at <= query_at)
    other = tail_hidden(
        dot_nt(keys_other, queries), key_at // tok < query_at // tok + sub
    )
    return own, other


def forward_kernel(tok, sub_ref, own_ref, other_ref, down_t_ref, attn_ref, mid_ref, stat_ref):
    blocks = own_ref.shape[0]
    step = TILE // tok
    sub = sub_ref[0]
    values_own_t = rows_of(own_ref, blocks, 2 * tok, tok).T
    values_other_t = rows_of(other_ref, blocks, tok, tok).T
    for tile in range(blocks // step):
        upto = (tile + 1) * step
        width = upto * tok
        at = tile * TILE
        queries = own_ref[tile * step : upto, 0:tok, :].reshape(TILE, HD)
        own, other = scores_of(
            sub, rows_of(own_ref, upto, tok, tok), rows_of(other_ref, upto, 0, tok), queries, tok
        )
        highest = jnp.maximum(
            jnp.max(own, axis=0, keepdims=True), jnp.max(other, axis=0, keepdims=True)
        )
        own = jnp.exp2((own - highest) * LOG2_SCALE)
        other = jnp.exp2((other - highest) * LOG2_SCALE)
        inverse = 1.0 / (
            jnp.sum(own, axis=0, keepdims=True) + jnp.sum(other, axis=0, keepdims=True)
        )
        attn = dot_nn(values_own_t[:, :width], own.astype(jnp.bfloat16)) + dot_nn(
            values_other_t[:, :width], other.astype(jnp.bfloat16)
        )
        attn = (attn * inverse).astype(jnp.bfloat16)
        attn_ref[:, at : at + TILE] = attn
        mid_ref[:, at : at + TILE] = dot_nn(down_t_ref[...], attn)
        stat_ref[0:1, at : at + TILE] = highest
        stat_ref[1:2, at : at + TILE] = inverse


def backward_kernel(
    tok,
    sub_ref,
    own_ref,
    other_ref,
    dout_ref,
    attn_ref,
    lora_ref,
    stat_ref,
    dq_ref,
    dk_own_ref,
    dv_own_ref,
    pair_other_ref,
    down_grad_ref,
    dk_own,
    dv_own,
    dk_other,
    dv_other,
):
    blocks = own_ref.shape[0]
    step = TILE // tok
    sub = sub_ref[0]
    keys_own_t = rows_of(own_ref, blocks, tok, tok).T
    keys_other_t = rows_of(other_ref, blocks, 0, tok).T
    tiles = blocks // step
    for tile in reversed(range(tiles)):
        upto = (tile + 1) * step
        width = upto * tok
        at = tile * TILE
        queries = own_ref[tile * step : upto, 0:tok, :].reshape(TILE, HD)
        douts = dout_ref[tile * step : upto, 0:tok, :].reshape(TILE, HD)
        highest = stat_ref[0:1, at : at + TILE]
        inverse = stat_ref[1:2, at : at + TILE]
        own, other = scores_of(
            sub, rows_of(own_ref, upto, tok, tok), rows_of(other_ref, upto, 0, tok), queries, tok
        )
        own = jnp.exp2((own - highest) * LOG2_SCALE) * inverse
        other = jnp.exp2((other - highest) * LOG2_SCALE) * inverse
        dprob_own = dot_nt(rows_of(own_ref, upto, 2 * tok, tok), douts)
        dprob_other = dot_nt(rows_of(other_ref, upto, tok, tok), douts)
        delta = jnp.sum(own * dprob_own, axis=0, keepdims=True) + jnp.sum(
            other * dprob_other, axis=0, keepdims=True
        )
        ds_own = (own * (dprob_own - delta) * SCALE).astype(jnp.bfloat16)
        ds_other = (other * (dprob_other - delta) * SCALE).astype(jnp.bfloat16)
        dq = dot_nn(keys_own_t[:, :width], ds_own) + dot_nn(keys_other_t[:, :width], ds_other)
        dq_ref[tile * step : upto] = dq.T.astype(jnp.bfloat16).reshape(step, tok, HD)
        terms = (
            (dk_own, dot_nn(ds_own, queries)),
            (dk_other, dot_nn(ds_other, queries)),
            (dv_own, dot_nn(own.astype(jnp.bfloat16), douts)),
            (dv_other, dot_nn(other.astype(jnp.bfloat16), douts)),
        )
        for total, term in terms:
            if tile == tiles - 1:
                total[...] = term
            else:
                total[0:width] += term
    shape = (blocks, tok, HD)
    dk_own_ref[...] = dk_own[...].reshape(shape)
    dv_own_ref[...] = dv_own[...].reshape(shape)
    pair_other_ref[:, 0:tok, :] = dk_other[...].astype(jnp.bfloat16).reshape(shape)
    pair_other_ref[:, tok : 2 * tok, :] = dv_other[...].astype(jnp.bfloat16).reshape(shape)
    low_rank = lora_ref.shape[0]
    down_grad_ref[...] = 2.0 * dot_nt(lora_ref[...], attn_ref[...])


def call_kernel(body, outs, scratch, flops, exps, *operands):
    in_bytes = sum(x.size * x.dtype.itemsize for x in operands)
    out_bytes = sum(x.size * x.dtype.itemsize for x in outs)
    specs = [pl.BlockSpec(memory_space=pltpu.SMEM)]
    specs += [pl.BlockSpec(memory_space=pltpu.VMEM)] * (len(operands) - 1)
    return pl.pallas_call(
        body,
        out_shape=outs,
        in_specs=specs,
        out_specs=[pl.BlockSpec(memory_space=pltpu.VMEM)] * len(outs),
        scratch_shapes=scratch,
        compiler_params=pltpu.CompilerParams(vmem_limit_bytes=48 * 1024 * 1024),
        cost_estimate=pl.CostEstimate(
            flops=flops, bytes_accessed=in_bytes + out_bytes, transcendentals=exps
        ),
    )(*operands)


def shape_of(shape, dtype):
    return jax.ShapeDtypeStruct(shape, dtype)


def xor_order(pieces, index):
    bit = 1
    while bit < len(pieces):
        odd = (index // bit) % 2 == 1
        pieces = [jnp.where(odd, pieces[k ^ bit], pieces[k]) for k in range(len(pieces))]
        bit *= 2
    return pieces


def message_kernel(copies, *refs):
    tok = refs[0].shape[0]
    message_ref = refs[-1]
    for rank in range(message_ref.shape[0]):
        at = (rank // copies) * HD
        for n, ref in enumerate(refs[:-1]):
            message_ref[rank, n * tok : (n + 1) * tok, :] = ref[:, at : at + HD]


def unpack_kernel(copies, back_ref, *out_refs):
    for n, ref in enumerate(out_refs):
        tok = ref.shape[0]
        for at_head in range(ref.shape[1] // HD):
            part = back_ref[at_head * copies, n * tok : (n + 1) * tok, :]
            ref[:, at_head * HD : (at_head + 1) * HD] = part


def in_vmem(body, outs, *operands):
    whole = pl.BlockSpec(memory_space=pltpu.VMEM)
    size = sum(x.size * x.dtype.itemsize for x in operands)
    size += sum(x.size * x.dtype.itemsize for x in outs)
    return pl.pallas_call(
        body,
        out_shape=outs,
        in_specs=[whole] * len(operands),
        out_specs=[whole] * len(outs),
        compiler_params=pltpu.CompilerParams(vmem_limit_bytes=16 * 1024 * 1024),
        cost_estimate=pl.CostEstimate(flops=0, bytes_accessed=size, transcendentals=0),
    )(*operands)


def dout_kernel(copies, tok, own_ref, taken_ref, message_ref):
    feats = own_ref.shape[1] - HD
    lora = (own_ref[:, feats:] + taken_ref[:, feats:].astype(jnp.float32)).T
    low_rank = message_ref.shape[1] - tok
    lora = lora[0:low_rank].astype(jnp.bfloat16)
    for rank in range(message_ref.shape[0]):
        at = (rank // copies) * HD
        part = own_ref[:, at : at + HD] + taken_ref[:, at : at + HD].astype(jnp.float32)
        message_ref[rank, 0:tok, :] = part.astype(jnp.bfloat16)
        message_ref[rank, tok : tok + low_rank, :] = lora


def on_device(
    sizes,
    head_query_rows,
    head_key_rows,
    head_value_rows,
    output_gradient,
    output_matrix,
    adapter_down_weight,
    adapter_up_weight,
):
    seqs, heads, subs = sizes
    tok, feats = head_query_rows.shape
    cols = output_gradient.shape[1]
    low_rank = adapter_up_weight.shape[0]
    local_heads = feats // HD
    block_rows = tok * subs
    ranks = GROUP // block_rows
    copies = ranks // local_heads
    shift_blocks = GROUP // 2 // block_rows

    seq = lax.axis_index("seq")
    head = lax.axis_index("head")
    sub = lax.axis_index("sub")
    shift = jnp.where(head >= heads // 2, shift_blocks, 0)
    rank = (seq - shift + seqs) % ranks
    my_head = rank // copies

    groups = []
    for at_head in range(heads):
        moved = shift_blocks if at_head >= heads // 2 else 0
        for first in range(0, seqs, ranks):
            groups.append(
                [((first + moved + i) % seqs) * heads + at_head for i in range(ranks)]
            )

    def exchange(parts):
        return lax.all_to_all(
            parts, ("seq", "head"), 0, 0, axis_index_groups=groups, tiled=True
        )

    def swap(value):
        if subs == 1:
            return value
        return lax.ppermute(value, "sub", [(0, 1), (1, 0)])

    (sent,) = in_vmem(
        functools.partial(message_kernel, copies),
        [shape_of((ranks, 3 * tok, HD), head_query_rows.dtype)],
        head_query_rows,
        head_key_rows,
        head_value_rows,
    )
    sent, output_gradient = lax.optimization_barrier((sent, output_gradient))
    own = exchange(sent)

    chunks = heads // subs
    pieces = []
    for k in range(heads):
        pairs = []
        for src_head in range(heads):
            for src_sub in range(subs):
                j = (src_head % chunks) * subs + src_sub
                dst = ((j + k) % heads) * subs + src_head // chunks
                pairs.append((src_head * subs + src_sub, dst))
        pieces.append(lax.ppermute(output_gradient, ("head", "sub"), pairs))

    up_half = lax.dynamic_slice_in_dim(adapter_up_weight, sub * chunks * cols, chunks * cols, 1)
    if chunks == 1:
        both = jnp.concatenate(pieces, axis=0)
        lora_all = dot_nt(both, up_half)
        grad_all = dot_nt(both, output_matrix)
        grad_all += 2.0 * dot_nt(lora_all.astype(jnp.bfloat16), adapter_down_weight)
        grads = [grad_all[k * tok : (k + 1) * tok] for k in range(heads)]
        loras = [lora_all[k * tok : (k + 1) * tok] for k in range(heads)]
    else:
        grads, loras = [], []
        for k in range(heads):
            at = (((head - k + heads) % heads) // subs) * cols
            lora = dot_nt(pieces[k], lax.dynamic_slice_in_dim(up_half, at, cols, 1))
            grad = dot_nt(pieces[k], lax.dynamic_slice_in_dim(output_matrix, at, cols, 1))
            grads.append(grad + 2.0 * dot_nt(lora.astype(jnp.bfloat16), adapter_down_weight))
            loras.append(lora)

    def terms_for(which, terms):
        total = None
        for k in range(heads):
            mine = ((head - k + heads) % heads) % subs == which
            term = jnp.where(mine, terms[k], 0.0)
            total = term if total is None else total + term
        return total

    spare = jnp.zeros((tok, HD - low_rank), jnp.float32)
    packed = [jnp.concatenate((g, l, spare), axis=1) for g, l in zip(grads, loras)]
    received = swap(terms_for(1 - sub, packed).astype(jnp.bfloat16))
    packed_own = terms_for(sub, packed)
    (message,) = in_vmem(
        functools.partial(dout_kernel, copies, tok),
        [shape_of((ranks, tok + low_rank, HD), jnp.bfloat16)],
        packed_own,
        received,
    )
    own, message = lax.optimization_barrier((own, message))
    other = swap(own[:, tok:])
    arrived = exchange(message)

    sub_arg = jnp.full((1,), sub, jnp.int32)
    down_head = lax.dynamic_slice_in_dim(adapter_down_weight, my_head * HD, HD, 0)
    rows = ranks * tok
    pair_count = rows * (rows + TILE)
    attn_t, mid_t, stats = call_kernel(
        functools.partial(forward_kernel, tok),
        [
            shape_of((HD, rows), jnp.bfloat16),
            shape_of((low_rank, rows), jnp.float32),
            shape_of((8, rows), jnp.float32),
        ],
        [],
        4 * pair_count * HD,
        pair_count,
        sub_arg,
        own,
        other,
        down_head.T,
    )

    first_copy = rank % copies == 0
    if copies > 1:
        mid_t = jnp.where(first_copy, mid_t, 0.0)
    middle_terms = xor_order(jnp.split(mid_t.astype(jnp.bfloat16), ranks, axis=1), rank)
    middle = None
    for k in range(ranks):
        for e in range(heads):
            pairs = []
            for g in groups:
                for i in range(ranks):
                    seq_to, head_from = g[i ^ k] // heads, g[i] % heads
                    pairs.append((g[i], seq_to * heads + (head_from + e) % heads))
            taken = middle_terms[k]
            if k or e:
                taken = lax.ppermute(taken, ("seq", "head"), pairs)
            taken = taken.astype(jnp.float32)
            middle = taken if middle is None else middle + taken

    peers = seqs * subs
    width = cols // peers
    place = seq * subs + sub
    up_part = 2.0 * dot_nn(middle.astype(jnp.bfloat16), output_gradient)
    up_terms = xor_order(jnp.split(up_part.astype(jnp.bfloat16), peers, axis=1), place)
    up_piece = up_terms[0].astype(jnp.float32)
    for k in range(1, peers):
        pairs = [(i, i ^ k) for i in range(peers)]
        up_piece += lax.ppermute(up_terms[k], ("seq", "sub"), pairs).astype(jnp.float32)

    lora_t = arrived[:, tok:].transpose(1, 0, 2).reshape(low_rank, rows)
    dq, dk_own, dv_own, pair_other, down_part = call_kernel(
        functools.partial(backward_kernel, tok),
        [
            shape_of((ranks, tok, HD), jnp.bfloat16),
            shape_of((ranks, tok, HD), jnp.float32),
            shape_of((ranks, tok, HD), jnp.float32),
            shape_of((ranks, 2 * tok, HD), jnp.bfloat16),
            shape_of((low_rank, HD), jnp.float32),
        ],
        [pltpu.VMEM((rows, HD), jnp.float32)] * 4,
        10 * pair_count * HD,
        pair_count,
        sub_arg,
        own,
        other,
        arrived,
        attn_t,
        lora_t,
        stats,
    )
    pair_received = swap(pair_other).astype(jnp.float32)
    dk = (dk_own + pair_received[:, :tok]).astype(jnp.bfloat16)
    dv = (dv_own + pair_received[:, tok:]).astype(jnp.bfloat16)
    back = exchange(jnp.concatenate([dq, dk, dv], axis=1))
    query_gradient, key_gradient, value_gradient = in_vmem(
        functools.partial(unpack_kernel, copies),
        [shape_of((tok, feats), back.dtype)] * 3,
        back,
    )

    mine = jnp.concatenate((down_part, up_piece), axis=1).astype(jnp.bfloat16)
    everyone = [mine]
    for k in range(1, peers):
        pairs = [(i, i ^ k) for i in range(peers)]
        everyone.append(lax.ppermute(mine, ("seq", "sub"), pairs))
    everyone = xor_order(everyone, place)
    up_gradient = jnp.concatenate([x[:, HD:] for x in everyone], axis=1).astype(jnp.float32)
    down_terms = []
    for i in range(seqs):
        at_seq = [x[:, :HD].astype(jnp.float32) for x in everyone[i * subs : (i + 1) * subs]]
        down_terms.append(functools.reduce(jnp.add, at_seq))
    down_heads = []
    for i in range(0, ranks, copies):
        same = [
            jnp.where(
                head >= heads // 2, down_terms[(first + shift_blocks) % seqs], down_terms[first]
            )
            for first in range(i, seqs, ranks)
        ]
        down_heads.append(functools.reduce(jnp.add, same))
    down_gradient = jnp.concatenate(down_heads, axis=1).T
    return (query_gradient, key_gradient, value_gradient, down_gradient, up_gradient)


def solution(mesh):
    rows = P(("rep", "seq", "sub"), "head")
    sizes = (mesh.shape["seq"], mesh.shape["head"], mesh.shape["sub"])
    return jax.shard_map(
        functools.partial(on_device, sizes),
        mesh=mesh,
        in_specs=(rows, rows, rows, rows, P("head", "sub"), P("head", None), P()),
        out_specs=(rows, rows, rows, P(("rep", "head"), None), P("rep", "head")),
        check_vma=False,
    )
```

```python
import functools
import math

import jax
import jax.numpy as jnp
from jax import lax
from jax.experimental import pallas as pl
from jax.experimental.pallas import tpu as pltpu
from jax.sharding import PartitionSpec as P

HD = 128
GROUP = 2048
TILE = 256
HIDDEN = -1e30
SCALE = HD ** (-0.5)
LOG2_SCALE = SCALE * math.log2(math.e)


def dot_nt(left, right):
    return lax.dot_general(
        left, right, (((1,), (1,)), ((), ())), preferred_element_type=jnp.float32
    )


def dot_nn(left, right):
    return jnp.dot(left, right, preferred_element_type=jnp.float32)


def rows_of(ref, blocks, first, count):
    return ref[0:blocks, first : first + count, :].reshape(blocks * count, HD)


def scores_of(sub, keys_own, keys_other, queries, tok):
    def tail_hidden(scores, visible):
        head = scores.shape[0] - TILE
        tail = jnp.where(visible, scores[head:], HIDDEN)
        return tail if head == 0 else jnp.concatenate((scores[:head], tail), axis=0)

    key_at = lax.broadcasted_iota(jnp.int32, (TILE, TILE), 0)
    query_at = lax.broadcasted_iota(jnp.int32, (TILE, TILE), 1)
    own = tail_hidden(dot_nt(keys_own, queries), key_at <= query_at)
    other = tail_hidden(
        dot_nt(keys_other, queries), key_at // tok < query_at // tok + sub
    )
    return own, other


def forward_kernel(tok, sub_ref, own_ref, other_ref, down_t_ref, attn_ref, mid_ref, stat_ref):
    blocks = own_ref.shape[0]
    step = TILE // tok
    sub = sub_ref[0]
    values_own_t = rows_of(own_ref, blocks, 2 * tok, tok).T
    values_other_t = rows_of(other_ref, blocks, tok, tok).T
    for tile in range(blocks // step):
        upto = (tile + 1) * step
        width = upto * tok
        at = tile * TILE
        queries = own_ref[tile * step : upto, 0:tok, :].reshape(TILE, HD)
        own, other = scores_of(
            sub, rows_of(own_ref, upto, tok, tok), rows_of(other_ref, upto, 0, tok), queries, tok
        )
        highest = jnp.maximum(
            jnp.max(own, axis=0, keepdims=True), jnp.max(other, axis=0, keepdims=True)
        )
        own = jnp.exp2((own - highest) * LOG2_SCALE)
        other = jnp.exp2((other - highest) * LOG2_SCALE)
        inverse = 1.0 / (
            jnp.sum(own, axis=0, keepdims=True) + jnp.sum(other, axis=0, keepdims=True)
        )
        attn = dot_nn(values_own_t[:, :width], own.astype(jnp.bfloat16)) + dot_nn(
            values_other_t[:, :width], other.astype(jnp.bfloat16)
        )
        attn = (attn * inverse).astype(jnp.bfloat16)
        attn_ref[:, at : at + TILE] = attn
        mid_ref[:, at : at + TILE] = dot_nn(down_t_ref[...], attn)
        stat_ref[0:1, at : at + TILE] = highest
        stat_ref[1:2, at : at + TILE] = inverse


def backward_kernel(
    tok,
    sub_ref,
    own_ref,
    other_ref,
    dout_ref,
    attn_ref,
    lora_ref,
    stat_ref,
    dq_ref,
    dk_own_ref,
    dv_own_ref,
    pair_other_ref,
    down_grad_ref,
    dk_own,
    dv_own,
    dk_other,
    dv_other,
):
    blocks = own_ref.shape[0]
    step = TILE // tok
    sub = sub_ref[0]
    keys_own_t = rows_of(own_ref, blocks, tok, tok).T
    keys_other_t = rows_of(other_ref, blocks, 0, tok).T
    tiles = blocks // step
    for tile in reversed(range(tiles)):
        upto = (tile + 1) * step
        width = upto * tok
        at = tile * TILE
        queries = own_ref[tile * step : upto, 0:tok, :].reshape(TILE, HD)
        douts = dout_ref[tile * step : upto, 0:tok, :].reshape(TILE, HD)
        highest = stat_ref[0:1, at : at + TILE]
        inverse = stat_ref[1:2, at : at + TILE]
        own, other = scores_of(
            sub, rows_of(own_ref, upto, tok, tok), rows_of(other_ref, upto, 0, tok), queries, tok
        )
        own = jnp.exp2((own - highest) * LOG2_SCALE) * inverse
        other = jnp.exp2((other - highest) * LOG2_SCALE) * inverse
        dprob_own = dot_nt(rows_of(own_ref, upto, 2 * tok, tok), douts)
        dprob_other = dot_nt(rows_of(other_ref, upto, tok, tok), douts)
        delta = jnp.sum(own * dprob_own, axis=0, keepdims=True) + jnp.sum(
            other * dprob_other, axis=0, keepdims=True
        )
        ds_own = (own * (dprob_own - delta) * SCALE).astype(jnp.bfloat16)
        ds_other = (other * (dprob_other - delta) * SCALE).astype(jnp.bfloat16)
        dq = dot_nn(keys_own_t[:, :width], ds_own) + dot_nn(keys_other_t[:, :width], ds_other)
        dq_ref[tile * step : upto] = dq.T.astype(jnp.bfloat16).reshape(step, tok, HD)
        terms = (
            (dk_own, dot_nn(ds_own, queries)),
            (dk_other, dot_nn(ds_other, queries)),
            (dv_own, dot_nn(own.astype(jnp.bfloat16), douts)),
            (dv_other, dot_nn(other.astype(jnp.bfloat16), douts)),
        )
        for total, term in terms:
            if tile == tiles - 1:
                total[...] = term
            else:
                total[0:width] += term
    shape = (blocks, tok, HD)
    dk_own_ref[...] = dk_own[...].reshape(shape)
    dv_own_ref[...] = dv_own[...].reshape(shape)
    pair_other_ref[:, 0:tok, :] = dk_other[...].astype(jnp.bfloat16).reshape(shape)
    pair_other_ref[:, tok : 2 * tok, :] = dv_other[...].astype(jnp.bfloat16).reshape(shape)
    low_rank = lora_ref.shape[0]
    down_grad_ref[...] = 2.0 * dot_nt(lora_ref[...], attn_ref[...])


def call_kernel(body, outs, scratch, flops, exps, *operands):
    in_bytes = sum(x.size * x.dtype.itemsize for x in operands)
    out_bytes = sum(x.size * x.dtype.itemsize for x in outs)
    specs = [pl.BlockSpec(memory_space=pltpu.SMEM)]
    specs += [pl.BlockSpec(memory_space=pltpu.VMEM)] * (len(operands) - 1)
    return pl.pallas_call(
        body,
        out_shape=outs,
        in_specs=specs,
        out_specs=[pl.BlockSpec(memory_space=pltpu.VMEM)] * len(outs),
        scratch_shapes=scratch,
        compiler_params=pltpu.CompilerParams(vmem_limit_bytes=48 * 1024 * 1024),
        cost_estimate=pl.CostEstimate(
            flops=flops, bytes_accessed=in_bytes + out_bytes, transcendentals=exps
        ),
    )(*operands)


def shape_of(shape, dtype):
    return jax.ShapeDtypeStruct(shape, dtype)


def message_kernel(copies, *refs):
    operands, message_ref, sems = refs[:-2], refs[-2], refs[-1]
    tok = operands[0].shape[0]
    blocks = []
    for rank in range(message_ref.shape[0]):
        cols = pl.ds((rank // copies) * HD, HD)
        for n, ref in enumerate(operands):
            to = message_ref.at[rank, pl.ds(n * tok, tok), :]
            blocks.append(pltpu.make_async_copy(ref.at[:, cols], to, sems.at[len(blocks)]))
    for block in blocks:
        block.start()
    for block in blocks:
        block.wait()


def message_of(copies, ranks, *operands):
    tok = operands[0].shape[0]
    shape = (ranks, len(operands) * tok, HD)
    return pl.pallas_call(
        functools.partial(message_kernel, copies),
        out_shape=shape_of(shape, operands[0].dtype),
        in_specs=[pl.BlockSpec(memory_space=pltpu.HBM)] * len(operands),
        out_specs=pl.BlockSpec(memory_space=pltpu.VMEM),
        scratch_shapes=[pltpu.SemaphoreType.DMA((ranks * len(operands),))],
        cost_estimate=pl.CostEstimate(
            flops=0, bytes_accessed=4 * math.prod(shape), transcendentals=0
        ),
    )(*operands)


def unpack_kernel(copies, back_ref, *out_refs):
    for n, ref in enumerate(out_refs):
        tok = ref.shape[0]
        for at_head in range(ref.shape[1] // HD):
            part = back_ref[at_head * copies, n * tok : (n + 1) * tok, :]
            ref[:, at_head * HD : (at_head + 1) * HD] = part


def in_vmem(body, outs, *operands):
    whole = pl.BlockSpec(memory_space=pltpu.VMEM)
    size = sum(x.size * x.dtype.itemsize for x in operands)
    size += sum(x.size * x.dtype.itemsize for x in outs)
    return pl.pallas_call(
        body,
        out_shape=outs,
        in_specs=[whole] * len(operands),
        out_specs=[whole] * len(outs),
        compiler_params=pltpu.CompilerParams(vmem_limit_bytes=16 * 1024 * 1024),
        cost_estimate=pl.CostEstimate(flops=0, bytes_accessed=size, transcendentals=0),
    )(*operands)


def dout_kernel(copies, tok, own_ref, taken_ref, message_ref):
    feats = own_ref.shape[1] - HD
    lora = (own_ref[:, feats:] + taken_ref[:, feats:].astype(jnp.float32)).T
    low_rank = message_ref.shape[1] - tok
    lora = lora[0:low_rank].astype(jnp.bfloat16)
    for rank in range(message_ref.shape[0]):
        at = (rank // copies) * HD
        part = own_ref[:, at : at + HD] + taken_ref[:, at : at + HD].astype(jnp.float32)
        message_ref[rank, 0:tok, :] = part.astype(jnp.bfloat16)
        message_ref[rank, tok : tok + low_rank, :] = lora


def on_device(
    sizes,
    head_query_rows,
    head_key_rows,
    head_value_rows,
    output_gradient,
    output_matrix,
    adapter_down_weight,
    adapter_up_weight,
):
    seqs, heads, subs = sizes
    tok, feats = head_query_rows.shape
    cols = output_gradient.shape[1]
    low_rank = adapter_up_weight.shape[0]
    local_heads = feats // HD
    block_rows = tok * subs
    ranks = GROUP // block_rows
    copies = ranks // local_heads
    shift_blocks = GROUP // 2 // block_rows

    seq = lax.axis_index("seq")
    head = lax.axis_index("head")
    sub = lax.axis_index("sub")
    shift = jnp.where(head >= heads // 2, shift_blocks, 0)
    rank = (seq - shift + seqs) % ranks
    my_head = rank // copies

    groups = []
    for at_head in range(heads):
        moved = shift_blocks if at_head >= heads // 2 else 0
        for first in range(0, seqs, ranks):
            groups.append(
                [((first + moved + i) % seqs) * heads + at_head for i in range(ranks)]
            )

    def exchange(parts):
        return lax.all_to_all(
            parts, ("seq", "head"), 0, 0, axis_index_groups=groups, tiled=True
        )

    def swap(value):
        if subs == 1:
            return value
        return lax.ppermute(value, "sub", [(0, 1), (1, 0)])

    sent = message_of(copies, ranks, head_query_rows, head_key_rows, head_value_rows)
    sent, output_gradient = lax.optimization_barrier((sent, output_gradient))
    own = exchange(sent)

    chunks = heads // subs
    pieces = []
    for k in range(heads):
        pairs = []
        for src_head in range(heads):
            for src_sub in range(subs):
                j = (src_head % chunks) * subs + src_sub
                dst = ((j + k) % heads) * subs + src_head // chunks
                pairs.append((src_head * subs + src_sub, dst))
        pieces.append(lax.ppermute(output_gradient, ("head", "sub"), pairs))

    up_half = lax.dynamic_slice_in_dim(adapter_up_weight, sub * chunks * cols, chunks * cols, 1)
    if chunks == 1:
        both = jnp.concatenate(pieces, axis=0)
        lora_all = dot_nt(both, up_half)
        grad_all = dot_nt(both, output_matrix)
        grad_all += 2.0 * dot_nt(lora_all.astype(jnp.bfloat16), adapter_down_weight)
        grads = [grad_all[k * tok : (k + 1) * tok] for k in range(heads)]
        loras = [lora_all[k * tok : (k + 1) * tok] for k in range(heads)]
    else:
        grads, loras = [], []
        for k in range(heads):
            at = (((head - k + heads) % heads) // subs) * cols
            lora = dot_nt(pieces[k], lax.dynamic_slice_in_dim(up_half, at, cols, 1))
            grad = dot_nt(pieces[k], lax.dynamic_slice_in_dim(output_matrix, at, cols, 1))
            grads.append(grad + 2.0 * dot_nt(lora.astype(jnp.bfloat16), adapter_down_weight))
            loras.append(lora)

    def terms_for(which, terms):
        total = None
        for k in range(heads):
            mine = ((head - k + heads) % heads) % subs == which
            term = jnp.where(mine, terms[k], 0.0)
            total = term if total is None else total + term
        return total

    spare = jnp.zeros((tok, HD - low_rank), jnp.float32)
    packed = [jnp.concatenate((g, l, spare), axis=1) for g, l in zip(grads, loras)]
    received = swap(terms_for(1 - sub, packed).astype(jnp.bfloat16))
    packed_own = terms_for(sub, packed)
    (message,) = in_vmem(
        functools.partial(dout_kernel, copies, tok),
        [shape_of((ranks, tok + low_rank, HD), jnp.bfloat16)],
        packed_own,
        received,
    )
    own, message = lax.optimization_barrier((own, message))
    other = swap(own[:, tok:])
    arrived = exchange(message)

    sub_arg = jnp.full((1,), sub, jnp.int32)
    down_head = lax.dynamic_slice_in_dim(adapter_down_weight, my_head * HD, HD, 0)
    rows = ranks * tok
    pair_count = rows * (rows + TILE)
    attn_t, mid_t, stats = call_kernel(
        functools.partial(forward_kernel, tok),
        [
            shape_of((HD, rows), jnp.bfloat16),
            shape_of((low_rank, rows), jnp.float32),
            shape_of((8, rows), jnp.float32),
        ],
        [],
        4 * pair_count * HD,
        pair_count,
        sub_arg,
        own,
        other,
        down_head.T,
    )

    first_copy = rank % copies == 0
    if copies > 1:
        mid_t = jnp.where(first_copy, mid_t, 0.0)
    middle_terms = lax.all_gather(mid_t.astype(jnp.bfloat16), ("seq", "head"))
    middle_terms = middle_terms.reshape(seqs, heads, low_rank, rows)
    middle = jnp.zeros((low_rank, tok), jnp.float32)
    for at_head in range(heads):
        moved = shift_blocks if at_head >= heads // 2 else 0
        at = (seq - moved + seqs) % seqs
        terms = jnp.roll(middle_terms[:, at_head], -moved, axis=0)
        start = (at // ranks * ranks, 0, at % ranks * tok)
        terms = lax.dynamic_slice(terms, start, (ranks, low_rank, tok))
        middle += jnp.sum(terms.astype(jnp.float32), axis=0)
    up_part = 2.0 * dot_nn(middle.astype(jnp.bfloat16), output_gradient)

    lora_t = arrived[:, tok:].transpose(1, 0, 2).reshape(low_rank, rows)
    dq, dk_own, dv_own, pair_other, down_part = call_kernel(
        functools.partial(backward_kernel, tok),
        [
            shape_of((ranks, tok, HD), jnp.bfloat16),
            shape_of((ranks, tok, HD), jnp.float32),
            shape_of((ranks, tok, HD), jnp.float32),
            shape_of((ranks, 2 * tok, HD), jnp.bfloat16),
            shape_of((low_rank, HD), jnp.float32),
        ],
        [pltpu.VMEM((rows, HD), jnp.float32)] * 4,
        10 * pair_count * HD,
        pair_count,
        sub_arg,
        own,
        other,
        arrived,
        attn_t,
        lora_t,
        stats,
    )
    pair_received = swap(pair_other).astype(jnp.float32)
    dk = (dk_own + pair_received[:, :tok]).astype(jnp.bfloat16)
    dv = (dv_own + pair_received[:, tok:]).astype(jnp.bfloat16)
    back = exchange(jnp.concatenate([dq, dk, dv], axis=1))
    query_gradient, key_gradient, value_gradient = in_vmem(
        functools.partial(unpack_kernel, copies),
        [shape_of((tok, feats), back.dtype)] * 3,
        back,
    )

    mine = jnp.concatenate((up_part, down_part), axis=1).astype(jnp.bfloat16)
    everyone = lax.all_gather(mine, ("seq", "sub"))
    up_gradient = jnp.sum(everyone[:, :, :cols].astype(jnp.float32), axis=0)
    down_terms = everyone[:, :, cols:].astype(jnp.float32).reshape(seqs, subs, low_rank, HD)
    down_terms = jnp.sum(down_terms, axis=1)
    down_terms = jnp.where(
        head >= heads // 2, jnp.roll(down_terms, -shift_blocks, axis=0), down_terms
    )
    down_terms = jnp.sum(down_terms.reshape(seqs // ranks, ranks, low_rank, HD), axis=0)
    down_gradient = down_terms[::copies].transpose(0, 2, 1).reshape(feats, low_rank)
    return (query_gradient, key_gradient, value_gradient, down_gradient, up_gradient)


def solution(mesh):
    rows = P(("rep", "seq", "sub"), "head")
    sizes = (mesh.shape["seq"], mesh.shape["head"], mesh.shape["sub"])
    return jax.shard_map(
        functools.partial(on_device, sizes),
        mesh=mesh,
        in_specs=(rows, rows, rows, rows, P("head", "sub"), P("head", None), P()),
        out_specs=(rows, rows, rows, P(("rep", "head"), None), P("rep", "head")),
        check_vma=False,
    )
```

```python
import functools
import math

import jax
import jax.numpy as jnp
from jax import lax
from jax.experimental import pallas as pl
from jax.experimental.pallas import tpu as pltpu
from jax.sharding import PartitionSpec as P

HD = 128
GROUP = 2048
TILE = 256
HIDDEN = -1e30
SCALE = HD ** (-0.5)
LOG2_SCALE = SCALE * math.log2(math.e)


def dot_nt(left, right):
    return lax.dot_general(
        left, right, (((1,), (1,)), ((), ())), preferred_element_type=jnp.float32
    )


def dot_nn(left, right):
    return jnp.dot(left, right, preferred_element_type=jnp.float32)


def rows_of(ref, blocks, first, count):
    return ref[0:blocks, first : first + count, :].reshape(blocks * count, HD)


def scores_of(sub, keys_own, keys_other, queries, tok):
    def tail_hidden(scores, visible):
        head = scores.shape[0] - TILE
        tail = jnp.where(visible, scores[head:], HIDDEN)
        return tail if head == 0 else jnp.concatenate((scores[:head], tail), axis=0)

    key_at = lax.broadcasted_iota(jnp.int32, (TILE, TILE), 0)
    query_at = lax.broadcasted_iota(jnp.int32, (TILE, TILE), 1)
    own = tail_hidden(dot_nt(keys_own, queries), key_at <= query_at)
    other = tail_hidden(
        dot_nt(keys_other, queries), key_at // tok < query_at // tok + sub
    )
    return own, other


def forward_kernel(tok, sub_ref, own_ref, other_ref, down_t_ref, attn_ref, mid_ref, stat_ref):
    blocks = own_ref.shape[0]
    step = TILE // tok
    sub = sub_ref[0]
    values_own_t = rows_of(own_ref, blocks, 2 * tok, tok).T
    values_other_t = rows_of(other_ref, blocks, tok, tok).T
    for tile in range(blocks // step):
        upto = (tile + 1) * step
        width = upto * tok
        at = tile * TILE
        queries = own_ref[tile * step : upto, 0:tok, :].reshape(TILE, HD)
        own, other = scores_of(
            sub, rows_of(own_ref, upto, tok, tok), rows_of(other_ref, upto, 0, tok), queries, tok
        )
        highest = jnp.maximum(
            jnp.max(own, axis=0, keepdims=True), jnp.max(other, axis=0, keepdims=True)
        )
        own = jnp.exp2((own - highest) * LOG2_SCALE)
        other = jnp.exp2((other - highest) * LOG2_SCALE)
        inverse = 1.0 / (
            jnp.sum(own, axis=0, keepdims=True) + jnp.sum(other, axis=0, keepdims=True)
        )
        attn = dot_nn(values_own_t[:, :width], own.astype(jnp.bfloat16)) + dot_nn(
            values_other_t[:, :width], other.astype(jnp.bfloat16)
        )
        attn = (attn * inverse).astype(jnp.bfloat16)
        attn_ref[:, at : at + TILE] = attn
        mid_ref[:, at : at + TILE] = dot_nn(down_t_ref[...], attn)
        stat_ref[0:1, at : at + TILE] = highest
        stat_ref[1:2, at : at + TILE] = inverse


def backward_kernel(
    tok,
    sub_ref,
    own_ref,
    other_ref,
    dout_ref,
    attn_ref,
    lora_ref,
    stat_ref,
    dq_ref,
    dk_own_ref,
    dv_own_ref,
    pair_other_ref,
    down_grad_ref,
    dk_own,
    dv_own,
    dk_other,
    dv_other,
):
    blocks = own_ref.shape[0]
    step = TILE // tok
    sub = sub_ref[0]
    keys_own_t = rows_of(own_ref, blocks, tok, tok).T
    keys_other_t = rows_of(other_ref, blocks, 0, tok).T
    tiles = blocks // step
    for tile in reversed(range(tiles)):
        upto = (tile + 1) * step
        width = upto * tok
        at = tile * TILE
        queries = own_ref[tile * step : upto, 0:tok, :].reshape(TILE, HD)
        douts = dout_ref[tile * step : upto, 0:tok, :].reshape(TILE, HD)
        highest = stat_ref[0:1, at : at + TILE]
        inverse = stat_ref[1:2, at : at + TILE]
        own, other = scores_of(
            sub, rows_of(own_ref, upto, tok, tok), rows_of(other_ref, upto, 0, tok), queries, tok
        )
        own = jnp.exp2((own - highest) * LOG2_SCALE) * inverse
        other = jnp.exp2((other - highest) * LOG2_SCALE) * inverse
        dprob_own = dot_nt(rows_of(own_ref, upto, 2 * tok, tok), douts)
        dprob_other = dot_nt(rows_of(other_ref, upto, tok, tok), douts)
        delta = jnp.sum(own * dprob_own, axis=0, keepdims=True) + jnp.sum(
            other * dprob_other, axis=0, keepdims=True
        )
        ds_own = (own * (dprob_own - delta) * SCALE).astype(jnp.bfloat16)
        ds_other = (other * (dprob_other - delta) * SCALE).astype(jnp.bfloat16)
        dq = dot_nn(keys_own_t[:, :width], ds_own) + dot_nn(keys_other_t[:, :width], ds_other)
        dq_ref[tile * step : upto] = dq.T.astype(jnp.bfloat16).reshape(step, tok, HD)
        terms = (
            (dk_own, dot_nn(ds_own, queries)),
            (dk_other, dot_nn(ds_other, queries)),
            (dv_own, dot_nn(own.astype(jnp.bfloat16), douts)),
            (dv_other, dot_nn(other.astype(jnp.bfloat16), douts)),
        )
        for total, term in terms:
            if tile == tiles - 1:
                total[...] = term
            else:
                total[0:width] += term
    shape = (blocks, tok, HD)
    dk_own_ref[...] = dk_own[...].reshape(shape)
    dv_own_ref[...] = dv_own[...].reshape(shape)
    pair_other_ref[:, 0:tok, :] = dk_other[...].astype(jnp.bfloat16).reshape(shape)
    pair_other_ref[:, tok : 2 * tok, :] = dv_other[...].astype(jnp.bfloat16).reshape(shape)
    low_rank = lora_ref.shape[0]
    down_grad_ref[...] = 2.0 * dot_nt(lora_ref[...], attn_ref[...])


def call_kernel(body, outs, scratch, flops, exps, *operands):
    in_bytes = sum(x.size * x.dtype.itemsize for x in operands)
    out_bytes = sum(x.size * x.dtype.itemsize for x in outs)
    specs = [pl.BlockSpec(memory_space=pltpu.SMEM)]
    specs += [pl.BlockSpec(memory_space=pltpu.VMEM)] * (len(operands) - 1)
    return pl.pallas_call(
        body,
        out_shape=outs,
        in_specs=specs,
        out_specs=[pl.BlockSpec(memory_space=pltpu.VMEM)] * len(outs),
        scratch_shapes=scratch,
        compiler_params=pltpu.CompilerParams(vmem_limit_bytes=48 * 1024 * 1024),
        cost_estimate=pl.CostEstimate(
            flops=flops, bytes_accessed=in_bytes + out_bytes, transcendentals=exps
        ),
    )(*operands)


def shape_of(shape, dtype):
    return jax.ShapeDtypeStruct(shape, dtype)


def all_summed(value, seqs, subs):
    steps = []
    bit = 1
    while bit < seqs:
        steps.append([(i, i ^ bit) for i in range(seqs)])
        bit *= 2
    if subs == 2:
        upper = lax.axis_index("sub") == 1
        across = [(0, 1), (1, 0)]
        low, high = jnp.split(value, 2, axis=1)
        taken = lax.ppermute(jnp.where(upper, low, high).astype(jnp.bfloat16), "sub", across)
        value = jnp.where(upper, high, low) + taken.astype(jnp.float32)
    for pairs in steps:
        taken = lax.ppermute(value.astype(jnp.bfloat16), "seq", pairs)
        value = value.astype(jnp.bfloat16).astype(jnp.float32) + taken.astype(jnp.float32)
    if subs == 2:
        taken = lax.ppermute(value, "sub", across)
        value = jnp.where(
            upper,
            jnp.concatenate((taken, value), axis=1),
            jnp.concatenate((value, taken), axis=1),
        )
    return value


def message_kernel(copies, *refs):
    operands, message_ref, sems = refs[:-2], refs[-2], refs[-1]
    tok = operands[0].shape[0]
    blocks = []
    for rank in range(message_ref.shape[0]):
        cols = pl.ds((rank // copies) * HD, HD)
        for n, ref in enumerate(operands):
            to = message_ref.at[rank, pl.ds(n * tok, tok), :]
            blocks.append(pltpu.make_async_copy(ref.at[:, cols], to, sems.at[len(blocks)]))
    for block in blocks:
        block.start()
    for block in blocks:
        block.wait()


def message_of(copies, ranks, *operands):
    tok = operands[0].shape[0]
    shape = (ranks, len(operands) * tok, HD)
    return pl.pallas_call(
        functools.partial(message_kernel, copies),
        out_shape=shape_of(shape, operands[0].dtype),
        in_specs=[pl.BlockSpec(memory_space=pltpu.HBM)] * len(operands),
        out_specs=pl.BlockSpec(memory_space=pltpu.VMEM),
        scratch_shapes=[pltpu.SemaphoreType.DMA((ranks * len(operands),))],
        cost_estimate=pl.CostEstimate(
            flops=0, bytes_accessed=4 * math.prod(shape), transcendentals=0
        ),
    )(*operands)


def unpack_kernel(copies, back_ref, *out_refs):
    for n, ref in enumerate(out_refs):
        tok = ref.shape[0]
        for at_head in range(ref.shape[1] // HD):
            part = back_ref[at_head * copies, n * tok : (n + 1) * tok, :]
            ref[:, at_head * HD : (at_head + 1) * HD] = part


def in_vmem(body, outs, *operands):
    whole = pl.BlockSpec(memory_space=pltpu.VMEM)
    size = sum(x.size * x.dtype.itemsize for x in operands)
    size += sum(x.size * x.dtype.itemsize for x in outs)
    return pl.pallas_call(
        body,
        out_shape=outs,
        in_specs=[whole] * len(operands),
        out_specs=[whole] * len(outs),
        compiler_params=pltpu.CompilerParams(vmem_limit_bytes=16 * 1024 * 1024),
        cost_estimate=pl.CostEstimate(flops=0, bytes_accessed=size, transcendentals=0),
    )(*operands)


def dout_kernel(copies, tok, own_ref, taken_ref, message_ref):
    feats = own_ref.shape[1] - HD
    lora = (own_ref[:, feats:] + taken_ref[:, feats:].astype(jnp.float32)).T
    low_rank = message_ref.shape[1] - tok
    lora = lora[0:low_rank].astype(jnp.bfloat16)
    for rank in range(message_ref.shape[0]):
        at = (rank // copies) * HD
        part = own_ref[:, at : at + HD] + taken_ref[:, at : at + HD].astype(jnp.float32)
        message_ref[rank, 0:tok, :] = part.astype(jnp.bfloat16)
        message_ref[rank, tok : tok + low_rank, :] = lora


def on_device(
    sizes,
    head_query_rows,
    head_key_rows,
    head_value_rows,
    output_gradient,
    output_matrix,
    adapter_down_weight,
    adapter_up_weight,
):
    seqs, heads, subs = sizes
    tok, feats = head_query_rows.shape
    cols = output_gradient.shape[1]
    low_rank = adapter_up_weight.shape[0]
    local_heads = feats // HD
    block_rows = tok * subs
    ranks = GROUP // block_rows
    copies = ranks // local_heads
    shift_blocks = GROUP // 2 // block_rows

    seq = lax.axis_index("seq")
    head = lax.axis_index("head")
    sub = lax.axis_index("sub")
    shift = jnp.where(head >= heads // 2, shift_blocks, 0)
    rank = (seq - shift + seqs) % ranks
    my_head = rank // copies

    groups = []
    for at_head in range(heads):
        moved = shift_blocks if at_head >= heads // 2 else 0
        for first in range(0, seqs, ranks):
            groups.append(
                [((first + moved + i) % seqs) * heads + at_head for i in range(ranks)]
            )

    def exchange(parts):
        return lax.all_to_all(
            parts, ("seq", "head"), 0, 0, axis_index_groups=groups, tiled=True
        )

    def middle_of(blocks):
        if seqs > ranks:
            spread = jnp.zeros((seqs // ranks,) + blocks.shape, blocks.dtype)
            at = (seq - shift + seqs) % seqs // ranks
            blocks = lax.dynamic_update_slice(spread, blocks[None], (at, 0, 0, 0))
        blocks = blocks.reshape((seqs,) + blocks.shape[-2:])
        blocks = jnp.where(
            head >= heads // 2, jnp.roll(blocks, shift_blocks, axis=0), blocks
        )
        sent = jnp.repeat(blocks, heads, axis=0)
        terms = lax.all_to_all(sent, ("seq", "head"), 0, 0, tiled=True)
        return jnp.sum(terms.astype(jnp.float32), axis=0)

    def swap(value):
        if subs == 1:
            return value
        return lax.ppermute(value, "sub", [(0, 1), (1, 0)])

    sent = message_of(copies, ranks, head_query_rows, head_key_rows, head_value_rows)
    sent, output_gradient = lax.optimization_barrier((sent, output_gradient))
    own = exchange(sent)

    chunks = heads // subs
    pieces = []
    for k in range(heads):
        pairs = []
        for src_head in range(heads):
            for src_sub in range(subs):
                j = (src_head % chunks) * subs + src_sub
                dst = ((j + k) % heads) * subs + src_head // chunks
                pairs.append((src_head * subs + src_sub, dst))
        pieces.append(lax.ppermute(output_gradient, ("head", "sub"), pairs))

    up_half = lax.dynamic_slice_in_dim(adapter_up_weight, sub * chunks * cols, chunks * cols, 1)
    if chunks == 1:
        both = jnp.concatenate(pieces, axis=0)
        lora_all = dot_nt(both, up_half)
        grad_all = dot_nt(both, output_matrix)
        grad_all += 2.0 * dot_nt(lora_all.astype(jnp.bfloat16), adapter_down_weight)
        grads = [grad_all[k * tok : (k + 1) * tok] for k in range(heads)]
        loras = [lora_all[k * tok : (k + 1) * tok] for k in range(heads)]
    else:
        grads, loras = [], []
        for k in range(heads):
            at = (((head - k + heads) % heads) // subs) * cols
            lora = dot_nt(pieces[k], lax.dynamic_slice_in_dim(up_half, at, cols, 1))
            grad = dot_nt(pieces[k], lax.dynamic_slice_in_dim(output_matrix, at, cols, 1))
            grads.append(grad + 2.0 * dot_nt(lora.astype(jnp.bfloat16), adapter_down_weight))
            loras.append(lora)

    def terms_for(which, terms):
        total = None
        for k in range(heads):
            mine = ((head - k + heads) % heads) % subs == which
            term = jnp.where(mine, terms[k], 0.0)
            total = term if total is None else total + term
        return total

    spare = jnp.zeros((tok, HD - low_rank), jnp.float32)
    packed = [jnp.concatenate((g, l, spare), axis=1) for g, l in zip(grads, loras)]
    received = swap(terms_for(1 - sub, packed).astype(jnp.bfloat16))
    packed_own = terms_for(sub, packed)
    (message,) = in_vmem(
        functools.partial(dout_kernel, copies, tok),
        [shape_of((ranks, tok + low_rank, HD), jnp.bfloat16)],
        packed_own,
        received,
    )
    own, message = lax.optimization_barrier((own, message))
    other = swap(own[:, tok:])
    arrived = exchange(message)

    sub_arg = jnp.full((1,), sub, jnp.int32)
    down_head = lax.dynamic_slice_in_dim(adapter_down_weight, my_head * HD, HD, 0)
    rows = ranks * tok
    pair_count = rows * (rows + TILE)
    attn_t, mid_t, stats = call_kernel(
        functools.partial(forward_kernel, tok),
        [
            shape_of((HD, rows), jnp.bfloat16),
            shape_of((low_rank, rows), jnp.float32),
            shape_of((8, rows), jnp.float32),
        ],
        [],
        4 * pair_count * HD,
        pair_count,
        sub_arg,
        own,
        other,
        down_head.T,
    )

    first_copy = rank % copies == 0
    if copies > 1:
        mid_t = jnp.where(first_copy, mid_t, 0.0)
    mid_blocks = mid_t.astype(jnp.bfloat16).reshape(low_rank, ranks, tok).transpose(1, 0, 2)
    middle = middle_of(mid_blocks)
    up_part = 2.0 * dot_nn(middle.astype(jnp.bfloat16), output_gradient)

    lora_t = arrived[:, tok:].transpose(1, 0, 2).reshape(low_rank, rows)
    dq, dk_own, dv_own, pair_other, down_part = call_kernel(
        functools.partial(backward_kernel, tok),
        [
            shape_of((ranks, tok, HD), jnp.bfloat16),
            shape_of((ranks, tok, HD), jnp.float32),
            shape_of((ranks, tok, HD), jnp.float32),
            shape_of((ranks, 2 * tok, HD), jnp.bfloat16),
            shape_of((low_rank, HD), jnp.float32),
        ],
        [pltpu.VMEM((rows, HD), jnp.float32)] * 4,
        10 * pair_count * HD,
        pair_count,
        sub_arg,
        own,
        other,
        arrived,
        attn_t,
        lora_t,
        stats,
    )
    pair_received = swap(pair_other).astype(jnp.float32)
    dk = (dk_own + pair_received[:, :tok]).astype(jnp.bfloat16)
    dv = (dv_own + pair_received[:, tok:]).astype(jnp.bfloat16)
    own_slot = lax.broadcasted_iota(jnp.int32, (1, feats), 1) // HD == my_head
    own_slot &= first_copy
    down_placed = jnp.where(own_slot, jnp.tile(down_part, (1, local_heads)), 0.0)
    lora_grads = jnp.concatenate((up_part, down_placed), axis=1)
    back_message = jnp.concatenate([dq, dk, dv], axis=1)
    back_message, lora_grads = lax.optimization_barrier((back_message, lora_grads))
    back = exchange(back_message)
    query_gradient, key_gradient, value_gradient = in_vmem(
        functools.partial(unpack_kernel, copies),
        [shape_of((tok, feats), back.dtype)] * 3,
        back,
    )

    total = all_summed(lora_grads, seqs, subs)
    up_gradient = total[:, :cols]
    down_gradient = total[:, cols:].T
    return (query_gradient, key_gradient, value_gradient, down_gradient, up_gradient)


def solution(mesh):
    rows = P(("rep", "seq", "sub"), "head")
    sizes = (mesh.shape["seq"], mesh.shape["head"], mesh.shape["sub"])
    return jax.shard_map(
        functools.partial(on_device, sizes),
        mesh=mesh,
        in_specs=(rows, rows, rows, rows, P("head", "sub"), P("head", None), P()),
        out_specs=(rows, rows, rows, P(("rep", "head"), None), P("rep", "head")),
        check_vma=False,
    )
```

```python
import functools
import math

import jax
import jax.numpy as jnp
from jax import lax
from jax.experimental import pallas as pl
from jax.experimental.pallas import tpu as pltpu
from jax.sharding import PartitionSpec as P

HD = 128
GROUP = 2048
TILE = 256
HIDDEN = -1e30
SCALE = HD ** (-0.5)
LOG2_SCALE = SCALE * math.log2(math.e)


def dot_nt(left, right):
    return lax.dot_general(
        left, right, (((1,), (1,)), ((), ())), preferred_element_type=jnp.float32
    )


def dot_nn(left, right):
    return jnp.dot(left, right, preferred_element_type=jnp.float32)


def rows_of(ref, blocks, first, count):
    return ref[0:blocks, first : first + count, :].reshape(blocks * count, HD)


def scores_of(sub, keys_own, keys_other, queries, tok):
    def tail_hidden(scores, visible):
        head = scores.shape[0] - TILE
        tail = jnp.where(visible, scores[head:], HIDDEN)
        return tail if head == 0 else jnp.concatenate((scores[:head], tail), axis=0)

    key_at = lax.broadcasted_iota(jnp.int32, (TILE, TILE), 0)
    query_at = lax.broadcasted_iota(jnp.int32, (TILE, TILE), 1)
    own = tail_hidden(dot_nt(keys_own, queries), key_at <= query_at)
    other = tail_hidden(
        dot_nt(keys_other, queries), key_at // tok < query_at // tok + sub
    )
    return own, other


def forward_kernel(tok, sub_ref, own_ref, other_ref, down_t_ref, attn_ref, mid_ref, stat_ref):
    blocks = own_ref.shape[0]
    step = TILE // tok
    sub = sub_ref[0]
    values_own_t = rows_of(own_ref, blocks, 2 * tok, tok).T
    values_other_t = rows_of(other_ref, blocks, tok, tok).T
    for tile in range(blocks // step):
        upto = (tile + 1) * step
        width = upto * tok
        at = tile * TILE
        queries = own_ref[tile * step : upto, 0:tok, :].reshape(TILE, HD)
        own, other = scores_of(
            sub, rows_of(own_ref, upto, tok, tok), rows_of(other_ref, upto, 0, tok), queries, tok
        )
        highest = jnp.maximum(
            jnp.max(own, axis=0, keepdims=True), jnp.max(other, axis=0, keepdims=True)
        )
        own = jnp.exp2((own - highest) * LOG2_SCALE)
        other = jnp.exp2((other - highest) * LOG2_SCALE)
        inverse = 1.0 / (
            jnp.sum(own, axis=0, keepdims=True) + jnp.sum(other, axis=0, keepdims=True)
        )
        attn = dot_nn(values_own_t[:, :width], own.astype(jnp.bfloat16)) + dot_nn(
            values_other_t[:, :width], other.astype(jnp.bfloat16)
        )
        attn = (attn * inverse).astype(jnp.bfloat16)
        attn_ref[:, at : at + TILE] = attn
        mid_ref[:, at : at + TILE] = dot_nn(down_t_ref[...], attn)
        stat_ref[0:1, at : at + TILE] = highest
        stat_ref[1:2, at : at + TILE] = inverse


def backward_kernel(
    tok,
    sub_ref,
    own_ref,
    other_ref,
    dout_ref,
    attn_ref,
    lora_ref,
    stat_ref,
    dq_ref,
    dk_own_ref,
    dv_own_ref,
    pair_other_ref,
    down_grad_ref,
    dk_own,
    dv_own,
    dk_other,
    dv_other,
):
    blocks = own_ref.shape[0]
    step = TILE // tok
    sub = sub_ref[0]
    keys_own_t = rows_of(own_ref, blocks, tok, tok).T
    keys_other_t = rows_of(other_ref, blocks, 0, tok).T
    tiles = blocks // step
    for tile in reversed(range(tiles)):
        upto = (tile + 1) * step
        width = upto * tok
        at = tile * TILE
        queries = own_ref[tile * step : upto, 0:tok, :].reshape(TILE, HD)
        douts = dout_ref[tile * step : upto, 0:tok, :].reshape(TILE, HD)
        highest = stat_ref[0:1, at : at + TILE]
        inverse = stat_ref[1:2, at : at + TILE]
        own, other = scores_of(
            sub, rows_of(own_ref, upto, tok, tok), rows_of(other_ref, upto, 0, tok), queries, tok
        )
        own = jnp.exp2((own - highest) * LOG2_SCALE) * inverse
        other = jnp.exp2((other - highest) * LOG2_SCALE) * inverse
        dprob_own = dot_nt(rows_of(own_ref, upto, 2 * tok, tok), douts)
        dprob_other = dot_nt(rows_of(other_ref, upto, tok, tok), douts)
        delta = jnp.sum(own * dprob_own, axis=0, keepdims=True) + jnp.sum(
            other * dprob_other, axis=0, keepdims=True
        )
        ds_own = (own * (dprob_own - delta) * SCALE).astype(jnp.bfloat16)
        ds_other = (other * (dprob_other - delta) * SCALE).astype(jnp.bfloat16)
        dq = dot_nn(keys_own_t[:, :width], ds_own) + dot_nn(keys_other_t[:, :width], ds_other)
        dq_ref[tile * step : upto] = dq.T.astype(jnp.bfloat16).reshape(step, tok, HD)
        terms = (
            (dk_own, dot_nn(ds_own, queries)),
            (dk_other, dot_nn(ds_other, queries)),
            (dv_own, dot_nn(own.astype(jnp.bfloat16), douts)),
            (dv_other, dot_nn(other.astype(jnp.bfloat16), douts)),
        )
        for total, term in terms:
            if tile == tiles - 1:
                total[...] = term
            else:
                total[0:width] += term
    shape = (blocks, tok, HD)
    dk_own_ref[...] = dk_own[...].reshape(shape)
    dv_own_ref[...] = dv_own[...].reshape(shape)
    pair_other_ref[:, 0:tok, :] = dk_other[...].astype(jnp.bfloat16).reshape(shape)
    pair_other_ref[:, tok : 2 * tok, :] = dv_other[...].astype(jnp.bfloat16).reshape(shape)
    low_rank = lora_ref.shape[0]
    down_grad_ref[...] = 2.0 * dot_nt(lora_ref[...], attn_ref[...])


def call_kernel(body, outs, scratch, flops, exps, *operands):
    in_bytes = sum(x.size * x.dtype.itemsize for x in operands)
    out_bytes = sum(x.size * x.dtype.itemsize for x in outs)
    specs = [pl.BlockSpec(memory_space=pltpu.SMEM)]
    specs += [pl.BlockSpec(memory_space=pltpu.VMEM)] * (len(operands) - 1)
    return pl.pallas_call(
        body,
        out_shape=outs,
        in_specs=specs,
        out_specs=[pl.BlockSpec(memory_space=pltpu.VMEM)] * len(outs),
        scratch_shapes=scratch,
        compiler_params=pltpu.CompilerParams(vmem_limit_bytes=48 * 1024 * 1024),
        cost_estimate=pl.CostEstimate(
            flops=flops, bytes_accessed=in_bytes + out_bytes, transcendentals=exps
        ),
    )(*operands)


def shape_of(shape, dtype):
    return jax.ShapeDtypeStruct(shape, dtype)


def all_summed(value, seqs, subs):
    steps = []
    bit = 1
    while bit < seqs:
        steps.append([(i, i ^ bit) for i in range(seqs)])
        bit *= 2
    if subs == 2:
        upper = lax.axis_index("sub") == 1
        across = [(0, 1), (1, 0)]
        low, high = jnp.split(value, 2, axis=1)
        taken = lax.ppermute(jnp.where(upper, low, high).astype(jnp.bfloat16), "sub", across)
        value = jnp.where(upper, high, low) + taken.astype(jnp.float32)
    for pairs in steps:
        taken = lax.ppermute(value.astype(jnp.bfloat16), "seq", pairs)
        value = value.astype(jnp.bfloat16).astype(jnp.float32) + taken.astype(jnp.float32)
    if subs == 2:
        taken = lax.ppermute(value, "sub", across)
        value = jnp.where(
            upper,
            jnp.concatenate((taken, value), axis=1),
            jnp.concatenate((value, taken), axis=1),
        )
    return value


def message_kernel(copies, *refs):
    operands, message_ref, sems = refs[:-2], refs[-2], refs[-1]
    tok = operands[0].shape[0]
    blocks = []
    for rank in range(message_ref.shape[0]):
        cols = pl.ds((rank // copies) * HD, HD)
        for n, ref in enumerate(operands):
            to = message_ref.at[rank, pl.ds(n * tok, tok), :]
            blocks.append(pltpu.make_async_copy(ref.at[:, cols], to, sems.at[len(blocks)]))
    for block in blocks:
        block.start()
    for block in blocks:
        block.wait()


def message_of(copies, ranks, *operands):
    tok = operands[0].shape[0]
    shape = (ranks, len(operands) * tok, HD)
    return pl.pallas_call(
        functools.partial(message_kernel, copies),
        out_shape=shape_of(shape, operands[0].dtype),
        in_specs=[pl.BlockSpec(memory_space=pltpu.HBM)] * len(operands),
        out_specs=pl.BlockSpec(memory_space=pltpu.VMEM),
        scratch_shapes=[pltpu.SemaphoreType.DMA((ranks * len(operands),))],
        cost_estimate=pl.CostEstimate(
            flops=0, bytes_accessed=4 * math.prod(shape), transcendentals=0
        ),
    )(*operands)


def unpack_kernel(copies, back_ref, *out_refs):
    for n, ref in enumerate(out_refs):
        tok = ref.shape[0]
        for at_head in range(ref.shape[1] // HD):
            part = back_ref[at_head * copies, n * tok : (n + 1) * tok, :]
            ref[:, at_head * HD : (at_head + 1) * HD] = part


def in_vmem(body, outs, *operands):
    whole = pl.BlockSpec(memory_space=pltpu.VMEM)
    size = sum(x.size * x.dtype.itemsize for x in operands)
    size += sum(x.size * x.dtype.itemsize for x in outs)
    return pl.pallas_call(
        body,
        out_shape=outs,
        in_specs=[whole] * len(operands),
        out_specs=[whole] * len(outs),
        compiler_params=pltpu.CompilerParams(vmem_limit_bytes=16 * 1024 * 1024),
        cost_estimate=pl.CostEstimate(flops=0, bytes_accessed=size, transcendentals=0),
    )(*operands)


def dout_kernel(copies, tok, own_ref, taken_ref, mid_ref, message_ref):
    feats = own_ref.shape[1] - HD
    low_rank = mid_ref.shape[0]
    lora = (own_ref[:, feats:] + taken_ref[:, feats:].astype(jnp.float32)).T
    lora = lora[0:low_rank].astype(jnp.bfloat16)
    for rank in range(message_ref.shape[0]):
        at = (rank // copies) * HD
        part = own_ref[:, at : at + HD] + taken_ref[:, at : at + HD].astype(jnp.float32)
        message_ref[rank, 0:tok, :] = part.astype(jnp.bfloat16)
        message_ref[rank, tok : tok + low_rank, :] = lora
        mid = mid_ref[:, rank * tok : (rank + 1) * tok].astype(jnp.bfloat16)
        message_ref[rank, tok + low_rank : tok + 2 * low_rank, :] = mid


def on_device(
    sizes,
    head_query_rows,
    head_key_rows,
    head_value_rows,
    output_gradient,
    output_matrix,
    adapter_down_weight,
    adapter_up_weight,
):
    seqs, heads, subs = sizes
    tok, feats = head_query_rows.shape
    cols = output_gradient.shape[1]
    low_rank = adapter_up_weight.shape[0]
    local_heads = feats // HD
    block_rows = tok * subs
    ranks = GROUP // block_rows
    copies = ranks // local_heads
    shift_blocks = GROUP // 2 // block_rows

    seq = lax.axis_index("seq")
    head = lax.axis_index("head")
    sub = lax.axis_index("sub")
    shift = jnp.where(head >= heads // 2, shift_blocks, 0)
    rank = (seq - shift + seqs) % ranks
    my_head = rank // copies

    groups = []
    for at_head in range(heads):
        moved = shift_blocks if at_head >= heads // 2 else 0
        for first in range(0, seqs, ranks):
            groups.append(
                [((first + moved + i) % seqs) * heads + at_head for i in range(ranks)]
            )

    def exchange(parts):
        return lax.all_to_all(
            parts, ("seq", "head"), 0, 0, axis_index_groups=groups, tiled=True
        )

    def swap(value):
        if subs == 1:
            return value
        return lax.ppermute(value, "sub", [(0, 1), (1, 0)])

    sent = message_of(copies, ranks, head_query_rows, head_key_rows, head_value_rows)
    sent, output_gradient = lax.optimization_barrier((sent, output_gradient))
    own = exchange(sent)

    chunks = heads // subs
    pieces = []
    for k in range(heads):
        pairs = []
        for src_head in range(heads):
            for src_sub in range(subs):
                j = (src_head % chunks) * subs + src_sub
                dst = ((j + k) % heads) * subs + src_head // chunks
                pairs.append((src_head * subs + src_sub, dst))
        pieces.append(lax.ppermute(output_gradient, ("head", "sub"), pairs))

    up_half = lax.dynamic_slice_in_dim(adapter_up_weight, sub * chunks * cols, chunks * cols, 1)
    if chunks == 1:
        both = jnp.concatenate(pieces, axis=0)
        lora_all = dot_nt(both, up_half)
        grad_all = dot_nt(both, output_matrix)
        grad_all += 2.0 * dot_nt(lora_all.astype(jnp.bfloat16), adapter_down_weight)
        grads = [grad_all[k * tok : (k + 1) * tok] for k in range(heads)]
        loras = [lora_all[k * tok : (k + 1) * tok] for k in range(heads)]
    else:
        grads, loras = [], []
        for k in range(heads):
            at = (((head - k + heads) % heads) // subs) * cols
            lora = dot_nt(pieces[k], lax.dynamic_slice_in_dim(up_half, at, cols, 1))
            grad = dot_nt(pieces[k], lax.dynamic_slice_in_dim(output_matrix, at, cols, 1))
            grads.append(grad + 2.0 * dot_nt(lora.astype(jnp.bfloat16), adapter_down_weight))
            loras.append(lora)

    def terms_for(which, terms):
        total = None
        for k in range(heads):
            mine = ((head - k + heads) % heads) % subs == which
            term = jnp.where(mine, terms[k], 0.0)
            total = term if total is None else total + term
        return total

    spare = jnp.zeros((tok, HD - low_rank), jnp.float32)
    packed = [jnp.concatenate((g, l, spare), axis=1) for g, l in zip(grads, loras)]
    received = swap(terms_for(1 - sub, packed).astype(jnp.bfloat16))
    packed_own = terms_for(sub, packed)
    other = swap(own[:, tok:])

    sub_arg = jnp.full((1,), sub, jnp.int32)
    down_head = lax.dynamic_slice_in_dim(adapter_down_weight, my_head * HD, HD, 0)
    rows = ranks * tok
    pair_count = rows * (rows + TILE)
    attn_t, mid_t, stats = call_kernel(
        functools.partial(forward_kernel, tok),
        [
            shape_of((HD, rows), jnp.bfloat16),
            shape_of((low_rank, rows), jnp.float32),
            shape_of((8, rows), jnp.float32),
        ],
        [],
        4 * pair_count * HD,
        pair_count,
        sub_arg,
        own,
        other,
        down_head.T,
    )

    first_copy = rank % copies == 0
    if copies > 1:
        mid_t = jnp.where(first_copy, mid_t, 0.0)
    (message,) = in_vmem(
        functools.partial(dout_kernel, copies, tok),
        [shape_of((ranks, tok + 2 * low_rank, HD), jnp.bfloat16)],
        packed_own,
        received,
        mid_t,
    )
    arrived = exchange(message)
    middle = jnp.sum(arrived[:, tok + low_rank :].astype(jnp.float32), axis=0)
    bit = 1
    while bit < heads:
        middle += lax.ppermute(middle, "head", [(i, i ^ bit) for i in range(heads)])
        bit *= 2
    up_part = 2.0 * dot_nn(middle.astype(jnp.bfloat16), output_gradient)

    lora_t = arrived[:, tok : tok + low_rank].transpose(1, 0, 2).reshape(low_rank, rows)
    dq, dk_own, dv_own, pair_other, down_part = call_kernel(
        functools.partial(backward_kernel, tok),
        [
            shape_of((ranks, tok, HD), jnp.bfloat16),
            shape_of((ranks, tok, HD), jnp.float32),
            shape_of((ranks, tok, HD), jnp.float32),
            shape_of((ranks, 2 * tok, HD), jnp.bfloat16),
            shape_of((low_rank, HD), jnp.float32),
        ],
        [pltpu.VMEM((rows, HD), jnp.float32)] * 4,
        10 * pair_count * HD,
        pair_count,
        sub_arg,
        own,
        other,
        arrived,
        attn_t,
        lora_t,
        stats,
    )
    pair_received = swap(pair_other).astype(jnp.float32)
    dk = (dk_own + pair_received[:, :tok]).astype(jnp.bfloat16)
    dv = (dv_own + pair_received[:, tok:]).astype(jnp.bfloat16)
    own_slot = lax.broadcasted_iota(jnp.int32, (1, feats), 1) // HD == my_head
    own_slot &= first_copy
    down_placed = jnp.where(own_slot, jnp.tile(down_part, (1, local_heads)), 0.0)
    lora_grads = jnp.concatenate((up_part, down_placed), axis=1)
    back_message = jnp.concatenate([dq, dk, dv], axis=1)
    back = exchange(back_message)
    query_gradient, key_gradient, value_gradient = in_vmem(
        functools.partial(unpack_kernel, copies),
        [shape_of((tok, feats), back.dtype)] * 3,
        back,
    )

    _, lora_grads = lax.optimization_barrier((back_message, lora_grads))
    total = all_summed(lora_grads, seqs, subs)
    up_gradient = total[:, :cols]
    down_gradient = total[:, cols:].T
    return (query_gradient, key_gradient, value_gradient, down_gradient, up_gradient)


def solution(mesh):
    rows = P(("rep", "seq", "sub"), "head")
    sizes = (mesh.shape["seq"], mesh.shape["head"], mesh.shape["sub"])
    return jax.shard_map(
        functools.partial(on_device, sizes),
        mesh=mesh,
        in_specs=(rows, rows, rows, rows, P("head", "sub"), P("head", None), P()),
        out_specs=(rows, rows, rows, P(("rep", "head"), None), P("rep", "head")),
        check_vma=False,
    )
```

```python
import functools
import math

import jax
import jax.numpy as jnp
from jax import lax
from jax.experimental import pallas as pl
from jax.experimental.pallas import tpu as pltpu
from jax.sharding import PartitionSpec as P

HD = 128
GROUP = 2048
TILE = 256
HIDDEN = -1e30
SCALE = HD ** (-0.5)
LOG2_SCALE = SCALE * math.log2(math.e)


def dot_nt(left, right):
    return lax.dot_general(
        left, right, (((1,), (1,)), ((), ())), preferred_element_type=jnp.float32
    )


def dot_nn(left, right):
    return jnp.dot(left, right, preferred_element_type=jnp.float32)


def rows_of(ref, blocks, first, count):
    return ref[0:blocks, first : first + count, :].reshape(blocks * count, HD)


def scores_of(sub, keys_own, keys_other, queries, tok):
    def tail_hidden(scores, visible):
        head = scores.shape[0] - TILE
        tail = jnp.where(visible, scores[head:], HIDDEN)
        return tail if head == 0 else jnp.concatenate((scores[:head], tail), axis=0)

    key_at = lax.broadcasted_iota(jnp.int32, (TILE, TILE), 0)
    query_at = lax.broadcasted_iota(jnp.int32, (TILE, TILE), 1)
    own = tail_hidden(dot_nt(keys_own, queries), key_at <= query_at)
    other = tail_hidden(
        dot_nt(keys_other, queries), key_at // tok < query_at // tok + sub
    )
    return own, other


def forward_kernel(tok, sub_ref, own_ref, other_ref, down_t_ref, attn_ref, mid_ref, stat_ref):
    blocks = own_ref.shape[0]
    step = TILE // tok
    sub = sub_ref[0]
    values_own_t = rows_of(own_ref, blocks, 2 * tok, tok).T
    values_other_t = rows_of(other_ref, blocks, tok, tok).T
    for tile in range(blocks // step):
        upto = (tile + 1) * step
        width = upto * tok
        at = tile * TILE
        queries = own_ref[tile * step : upto, 0:tok, :].reshape(TILE, HD)
        own, other = scores_of(
            sub, rows_of(own_ref, upto, tok, tok), rows_of(other_ref, upto, 0, tok), queries, tok
        )
        highest = jnp.maximum(
            jnp.max(own, axis=0, keepdims=True), jnp.max(other, axis=0, keepdims=True)
        )
        own = jnp.exp2((own - highest) * LOG2_SCALE)
        other = jnp.exp2((other - highest) * LOG2_SCALE)
        inverse = 1.0 / (
            jnp.sum(own, axis=0, keepdims=True) + jnp.sum(other, axis=0, keepdims=True)
        )
        attn = dot_nn(values_own_t[:, :width], own.astype(jnp.bfloat16)) + dot_nn(
            values_other_t[:, :width], other.astype(jnp.bfloat16)
        )
        attn = (attn * inverse).astype(jnp.bfloat16)
        attn_ref[:, at : at + TILE] = attn
        mid_ref[:, at : at + TILE] = dot_nn(down_t_ref[...], attn)
        stat_ref[0:1, at : at + TILE] = highest
        stat_ref[1:2, at : at + TILE] = inverse


def backward_kernel(
    tok,
    sub_ref,
    own_ref,
    other_ref,
    dout_ref,
    attn_ref,
    lora_ref,
    stat_ref,
    dq_ref,
    dk_own_ref,
    dv_own_ref,
    pair_other_ref,
    down_grad_ref,
    dk_own,
    dv_own,
    dk_other,
    dv_other,
):
    blocks = own_ref.shape[0]
    step = TILE // tok
    sub = sub_ref[0]
    keys_own_t = rows_of(own_ref, blocks, tok, tok).T
    keys_other_t = rows_of(other_ref, blocks, 0, tok).T
    tiles = blocks // step
    for tile in reversed(range(tiles)):
        upto = (tile + 1) * step
        width = upto * tok
        at = tile * TILE
        queries = own_ref[tile * step : upto, 0:tok, :].reshape(TILE, HD)
        douts = dout_ref[tile * step : upto, 0:tok, :].reshape(TILE, HD)
        highest = stat_ref[0:1, at : at + TILE]
        inverse = stat_ref[1:2, at : at + TILE]
        own, other = scores_of(
            sub, rows_of(own_ref, upto, tok, tok), rows_of(other_ref, upto, 0, tok), queries, tok
        )
        own = jnp.exp2((own - highest) * LOG2_SCALE) * inverse
        other = jnp.exp2((other - highest) * LOG2_SCALE) * inverse
        dprob_own = dot_nt(rows_of(own_ref, upto, 2 * tok, tok), douts)
        dprob_other = dot_nt(rows_of(other_ref, upto, tok, tok), douts)
        delta = jnp.sum(own * dprob_own, axis=0, keepdims=True) + jnp.sum(
            other * dprob_other, axis=0, keepdims=True
        )
        ds_own = (own * (dprob_own - delta) * SCALE).astype(jnp.bfloat16)
        ds_other = (other * (dprob_other - delta) * SCALE).astype(jnp.bfloat16)
        dq = dot_nn(keys_own_t[:, :width], ds_own) + dot_nn(keys_other_t[:, :width], ds_other)
        dq_ref[tile * step : upto] = dq.T.astype(jnp.bfloat16).reshape(step, tok, HD)
        terms = (
            (dk_own, dot_nn(ds_own, queries)),
            (dk_other, dot_nn(ds_other, queries)),
            (dv_own, dot_nn(own.astype(jnp.bfloat16), douts)),
            (dv_other, dot_nn(other.astype(jnp.bfloat16), douts)),
        )
        for total, term in terms:
            if tile == tiles - 1:
                total[...] = term
            else:
                total[0:width] += term
    shape = (blocks, tok, HD)
    dk_own_ref[...] = dk_own[...].reshape(shape)
    dv_own_ref[...] = dv_own[...].reshape(shape)
    pair_other_ref[:, 0:tok, :] = dk_other[...].astype(jnp.bfloat16).reshape(shape)
    pair_other_ref[:, tok : 2 * tok, :] = dv_other[...].astype(jnp.bfloat16).reshape(shape)
    low_rank = lora_ref.shape[0]
    down_grad_ref[...] = 2.0 * dot_nt(lora_ref[...], attn_ref[...])


def call_kernel(body, outs, scratch, flops, exps, *operands):
    in_bytes = sum(x.size * x.dtype.itemsize for x in operands)
    out_bytes = sum(x.size * x.dtype.itemsize for x in outs)
    specs = [pl.BlockSpec(memory_space=pltpu.SMEM)]
    specs += [pl.BlockSpec(memory_space=pltpu.VMEM)] * (len(operands) - 1)
    return pl.pallas_call(
        body,
        out_shape=outs,
        in_specs=specs,
        out_specs=[pl.BlockSpec(memory_space=pltpu.VMEM)] * len(outs),
        scratch_shapes=scratch,
        compiler_params=pltpu.CompilerParams(vmem_limit_bytes=48 * 1024 * 1024),
        cost_estimate=pl.CostEstimate(
            flops=flops, bytes_accessed=in_bytes + out_bytes, transcendentals=exps
        ),
    )(*operands)


def shape_of(shape, dtype):
    return jax.ShapeDtypeStruct(shape, dtype)


def butterfly_sum(value, axis, bits, count):
    for bit in bits:
        pairs = [(i, i ^ bit) for i in range(count)]
        value = value.astype(jnp.bfloat16)
        taken = lax.ppermute(value, axis, pairs)
        value = value.astype(jnp.float32) + taken.astype(jnp.float32)
    return value


def powers_below(count):
    return [1 << n for n in range(count.bit_length() - 1)]


def message_kernel(copies, *refs):
    operands, message_ref, sems = refs[:-2], refs[-2], refs[-1]
    tok = operands[0].shape[0]
    blocks = []
    for rank in range(message_ref.shape[0]):
        cols = pl.ds((rank // copies) * HD, HD)
        for n, ref in enumerate(operands):
            to = message_ref.at[rank, pl.ds(n * tok, tok), :]
            blocks.append(pltpu.make_async_copy(ref.at[:, cols], to, sems.at[len(blocks)]))
    for block in blocks:
        block.start()
    for block in blocks:
        block.wait()


def message_of(copies, ranks, *operands):
    tok = operands[0].shape[0]
    shape = (ranks, len(operands) * tok, HD)
    return pl.pallas_call(
        functools.partial(message_kernel, copies),
        out_shape=shape_of(shape, operands[0].dtype),
        in_specs=[pl.BlockSpec(memory_space=pltpu.HBM)] * len(operands),
        out_specs=pl.BlockSpec(memory_space=pltpu.VMEM),
        scratch_shapes=[pltpu.SemaphoreType.DMA((ranks * len(operands),))],
        cost_estimate=pl.CostEstimate(
            flops=0, bytes_accessed=4 * math.prod(shape), transcendentals=0
        ),
    )(*operands)


def unpack_kernel(copies, back_ref, *out_refs):
    for n, ref in enumerate(out_refs):
        tok = ref.shape[0]
        for at_head in range(ref.shape[1] // HD):
            part = back_ref[at_head * copies, n * tok : (n + 1) * tok, :]
            ref[:, at_head * HD : (at_head + 1) * HD] = part


def in_vmem(body, outs, *operands):
    whole = pl.BlockSpec(memory_space=pltpu.VMEM)
    size = sum(x.size * x.dtype.itemsize for x in operands)
    size += sum(x.size * x.dtype.itemsize for x in outs)
    return pl.pallas_call(
        body,
        out_shape=outs,
        in_specs=[whole] * len(operands),
        out_specs=[whole] * len(outs),
        compiler_params=pltpu.CompilerParams(vmem_limit_bytes=16 * 1024 * 1024),
        cost_estimate=pl.CostEstimate(flops=0, bytes_accessed=size, transcendentals=0),
    )(*operands)


def dout_kernel(copies, tok, own_ref, taken_ref, mid_ref, message_ref):
    feats = own_ref.shape[1] - HD
    low_rank = mid_ref.shape[0]
    lora = (own_ref[:, feats:] + taken_ref[:, feats:].astype(jnp.float32)).T
    lora = lora[0:low_rank].astype(jnp.bfloat16)
    for rank in range(message_ref.shape[0]):
        at = (rank // copies) * HD
        part = own_ref[:, at : at + HD] + taken_ref[:, at : at + HD].astype(jnp.float32)
        message_ref[rank, 0:tok, :] = part.astype(jnp.bfloat16)
        message_ref[rank, tok : tok + low_rank, :] = lora
        mid = mid_ref[:, rank * tok : (rank + 1) * tok].astype(jnp.bfloat16)
        message_ref[rank, tok + low_rank : tok + 2 * low_rank, :] = mid


def on_device(
    sizes,
    head_query_rows,
    head_key_rows,
    head_value_rows,
    output_gradient,
    output_matrix,
    adapter_down_weight,
    adapter_up_weight,
):
    seqs, heads, subs = sizes
    tok, feats = head_query_rows.shape
    cols = output_gradient.shape[1]
    low_rank = adapter_up_weight.shape[0]
    local_heads = feats // HD
    block_rows = tok * subs
    ranks = GROUP // block_rows
    copies = ranks // local_heads
    shift_blocks = GROUP // 2 // block_rows

    seq = lax.axis_index("seq")
    head = lax.axis_index("head")
    sub = lax.axis_index("sub")
    shift = jnp.where(head >= heads // 2, shift_blocks, 0)
    rank = (seq - shift + seqs) % ranks
    my_head = rank // copies

    groups = []
    for at_head in range(heads):
        moved = shift_blocks if at_head >= heads // 2 else 0
        for first in range(0, seqs, ranks):
            groups.append(
                [((first + moved + i) % seqs) * heads + at_head for i in range(ranks)]
            )

    def exchange(parts):
        return lax.all_to_all(
            parts, ("seq", "head"), 0, 0, axis_index_groups=groups, tiled=True
        )

    def swap(value):
        if subs == 1:
            return value
        return lax.ppermute(value, "sub", [(0, 1), (1, 0)])

    sent = message_of(copies, ranks, head_query_rows, head_key_rows, head_value_rows)
    sent, output_gradient = lax.optimization_barrier((sent, output_gradient))
    own = exchange(sent)

    chunks = heads // subs
    pieces = []
    for k in range(heads):
        pairs = []
        for src_head in range(heads):
            for src_sub in range(subs):
                j = (src_head % chunks) * subs + src_sub
                dst = ((j + k) % heads) * subs + src_head // chunks
                pairs.append((src_head * subs + src_sub, dst))
        pieces.append(lax.ppermute(output_gradient, ("head", "sub"), pairs))

    up_half = lax.dynamic_slice_in_dim(adapter_up_weight, sub * chunks * cols, chunks * cols, 1)
    if chunks == 1:
        both = jnp.concatenate(pieces, axis=0)
        lora_all = dot_nt(both, up_half)
        grad_all = dot_nt(both, output_matrix)
        grad_all += 2.0 * dot_nt(lora_all.astype(jnp.bfloat16), adapter_down_weight)
        grads = [grad_all[k * tok : (k + 1) * tok] for k in range(heads)]
        loras = [lora_all[k * tok : (k + 1) * tok] for k in range(heads)]
    else:
        grads, loras = [], []
        for k in range(heads):
            at = (((head - k + heads) % heads) // subs) * cols
            lora = dot_nt(pieces[k], lax.dynamic_slice_in_dim(up_half, at, cols, 1))
            grad = dot_nt(pieces[k], lax.dynamic_slice_in_dim(output_matrix, at, cols, 1))
            grads.append(grad + 2.0 * dot_nt(lora.astype(jnp.bfloat16), adapter_down_weight))
            loras.append(lora)

    def terms_for(which, terms):
        total = None
        for k in range(heads):
            mine = ((head - k + heads) % heads) % subs == which
            term = jnp.where(mine, terms[k], 0.0)
            total = term if total is None else total + term
        return total

    spare = jnp.zeros((tok, HD - low_rank), jnp.float32)
    packed = [jnp.concatenate((g, l, spare), axis=1) for g, l in zip(grads, loras)]
    received = swap(terms_for(1 - sub, packed).astype(jnp.bfloat16))
    packed_own = terms_for(sub, packed)
    other = swap(own[:, tok:])

    sub_arg = jnp.full((1,), sub, jnp.int32)
    down_head = lax.dynamic_slice_in_dim(adapter_down_weight, my_head * HD, HD, 0)
    rows = ranks * tok
    pair_count = rows * (rows + TILE)
    attn_t, mid_t, stats = call_kernel(
        functools.partial(forward_kernel, tok),
        [
            shape_of((HD, rows), jnp.bfloat16),
            shape_of((low_rank, rows), jnp.float32),
            shape_of((8, rows), jnp.float32),
        ],
        [],
        4 * pair_count * HD,
        pair_count,
        sub_arg,
        own,
        other,
        down_head.T,
    )

    first_copy = rank % copies == 0
    if copies > 1:
        mid_t = jnp.where(first_copy, mid_t, 0.0)
    (message,) = in_vmem(
        functools.partial(dout_kernel, copies, tok),
        [shape_of((ranks, tok + 2 * low_rank, HD), jnp.bfloat16)],
        packed_own,
        received,
        mid_t,
    )
    arrived = exchange(message)
    middle = jnp.sum(arrived[:, tok + low_rank :].astype(jnp.float32), axis=0)
    bit = 1
    while bit < heads:
        middle += lax.ppermute(middle, "head", [(i, i ^ bit) for i in range(heads)])
        bit *= 2
    up_part = 2.0 * dot_nn(middle.astype(jnp.bfloat16), output_gradient)

    lora_t = arrived[:, tok : tok + low_rank].transpose(1, 0, 2).reshape(low_rank, rows)
    dq, dk_own, dv_own, pair_other, down_part = call_kernel(
        functools.partial(backward_kernel, tok),
        [
            shape_of((ranks, tok, HD), jnp.bfloat16),
            shape_of((ranks, tok, HD), jnp.float32),
            shape_of((ranks, tok, HD), jnp.float32),
            shape_of((ranks, 2 * tok, HD), jnp.bfloat16),
            shape_of((low_rank, HD), jnp.float32),
        ],
        [pltpu.VMEM((rows, HD), jnp.float32)] * 4,
        10 * pair_count * HD,
        pair_count,
        sub_arg,
        own,
        other,
        arrived,
        attn_t,
        lora_t,
        stats,
    )
    pair_received = swap(pair_other).astype(jnp.float32)
    down_rows = jnp.where(first_copy, down_part + swap(down_part), 0.0)
    dk = (dk_own + pair_received[:, :tok]).astype(jnp.bfloat16)
    dv = (dv_own + pair_received[:, tok:]).astype(jnp.bfloat16)
    down_rows = jnp.broadcast_to(down_rows.astype(jnp.bfloat16), (ranks, low_rank, HD))
    back_message = jnp.concatenate([dq, dk, dv, down_rows], axis=1)
    back = exchange(back_message)
    query_gradient, key_gradient, value_gradient = in_vmem(
        functools.partial(unpack_kernel, copies),
        [shape_of((tok, feats), back.dtype)] * 3,
        back,
    )
    down_terms = back[::copies, 3 * tok :].astype(jnp.float32)
    if seqs > ranks:
        bits = [bit for bit in powers_below(seqs) if bit >= ranks]
        down_terms = butterfly_sum(down_terms, "seq", bits, seqs)
    down_gradient = down_terms.transpose(0, 2, 1).reshape(feats, low_rank)

    up_sum = butterfly_sum(up_part, "seq", powers_below(seqs), seqs)
    _, up_sum = lax.optimization_barrier((back, up_sum))
    up_gradient = butterfly_sum(up_sum, "sub", powers_below(subs), subs)
    return (query_gradient, key_gradient, value_gradient, down_gradient, up_gradient)


def solution(mesh):
    rows = P(("rep", "seq", "sub"), "head")
    sizes = (mesh.shape["seq"], mesh.shape["head"], mesh.shape["sub"])
    return jax.shard_map(
        functools.partial(on_device, sizes),
        mesh=mesh,
        in_specs=(rows, rows, rows, rows, P("head", "sub"), P("head", None), P()),
        out_specs=(rows, rows, rows, P(("rep", "head"), None), P("rep", "head")),
        check_vma=False,
    )
```

```python
import functools
import math

import jax
import jax.numpy as jnp
from jax import lax
from jax.experimental import pallas as pl
from jax.experimental.pallas import tpu as pltpu
from jax.sharding import PartitionSpec as P

HD = 128
GROUP = 2048
TILE = 256
HIDDEN = -1e30
SCALE = HD ** (-0.5)
LOG2_SCALE = SCALE * math.log2(math.e)


def dot_nt(left, right):
    return lax.dot_general(
        left, right, (((1,), (1,)), ((), ())), preferred_element_type=jnp.float32
    )


def dot_nn(left, right):
    return jnp.dot(left, right, preferred_element_type=jnp.float32)


def rows_of(ref, blocks, first, count):
    return ref[0:blocks, first : first + count, :].reshape(blocks * count, HD)


def scores_of(sub, keys_own, keys_other, queries, tok):
    def tail_hidden(scores, visible):
        head = scores.shape[0] - TILE
        tail = jnp.where(visible, scores[head:], HIDDEN)
        return tail if head == 0 else jnp.concatenate((scores[:head], tail), axis=0)

    key_at = lax.broadcasted_iota(jnp.int32, (TILE, TILE), 0)
    query_at = lax.broadcasted_iota(jnp.int32, (TILE, TILE), 1)
    own = tail_hidden(dot_nt(keys_own, queries), key_at <= query_at)
    other = tail_hidden(
        dot_nt(keys_other, queries), key_at // tok < query_at // tok + sub
    )
    return own, other


def attention_kernel(
    tok,
    sub_ref,
    own_ref,
    other_ref,
    query_ref,
    down_t_ref,
    first_ref,
    pair_own_ref,
    pair_other_ref,
    down_grad_ref,
    dk_own,
    dv_own,
    dk_other,
    dv_other,
):
    blocks = own_ref.shape[0]
    step = TILE // tok
    sub = sub_ref[0]
    low_rank = down_t_ref.shape[0]
    keys_own_t = rows_of(own_ref, blocks, 0, tok).T
    keys_other_t = rows_of(other_ref, blocks, 0, tok).T
    values_own_t = rows_of(own_ref, blocks, tok, tok).T
    values_other_t = rows_of(other_ref, blocks, tok, tok).T
    tiles = blocks // step
    down_total = None
    for tile in reversed(range(tiles)):
        upto = (tile + 1) * step
        width = upto * tok
        queries = query_ref[tile * step : upto, 0:tok, :].reshape(TILE, HD)
        douts = query_ref[tile * step : upto, tok : 2 * tok, :].reshape(TILE, HD)
        own, other = scores_of(
            sub, rows_of(own_ref, upto, 0, tok), rows_of(other_ref, upto, 0, tok), queries, tok
        )
        highest = jnp.maximum(
            jnp.max(own, axis=0, keepdims=True), jnp.max(other, axis=0, keepdims=True)
        )
        own = jnp.exp2((own - highest) * LOG2_SCALE)
        other = jnp.exp2((other - highest) * LOG2_SCALE)
        inverse = 1.0 / (
            jnp.sum(own, axis=0, keepdims=True) + jnp.sum(other, axis=0, keepdims=True)
        )
        own = own * inverse
        other = other * inverse
        own_lo = own.astype(jnp.bfloat16)
        other_lo = other.astype(jnp.bfloat16)
        attn = dot_nn(values_own_t[:, :width], own_lo) + dot_nn(
            values_other_t[:, :width], other_lo
        )
        attn = attn.astype(jnp.bfloat16)
        mid = dot_nn(down_t_ref[...], attn).astype(jnp.bfloat16)
        for i in range(step):
            block = tile * step + i
            first_ref[block, tok : tok + low_rank, :] = mid[:, i * tok : (i + 1) * tok]
            lora = query_ref[block, 2 * tok : 2 * tok + low_rank, :]
            down_term = dot_nt(lora, attn[:, i * tok : (i + 1) * tok])
            down_total = down_term if down_total is None else down_total + down_term
        dprob_own = dot_nt(rows_of(own_ref, upto, tok, tok), douts)
        dprob_other = dot_nt(rows_of(other_ref, upto, tok, tok), douts)
        delta = jnp.sum(own * dprob_own, axis=0, keepdims=True) + jnp.sum(
            other * dprob_other, axis=0, keepdims=True
        )
        ds_own = (own * (dprob_own - delta) * SCALE).astype(jnp.bfloat16)
        ds_other = (other * (dprob_other - delta) * SCALE).astype(jnp.bfloat16)
        dq = dot_nn(keys_own_t[:, :width], ds_own) + dot_nn(keys_other_t[:, :width], ds_other)
        first_ref[tile * step : upto, 0:tok, :] = dq.T.astype(jnp.bfloat16).reshape(step, tok, HD)
        terms = (
            (dk_own, dot_nn(ds_own, queries)),
            (dk_other, dot_nn(ds_other, queries)),
            (dv_own, dot_nn(own_lo, douts)),
            (dv_other, dot_nn(other_lo, douts)),
        )
        for total, term in terms:
            if tile == tiles - 1:
                total[...] = term
            else:
                total[0:width] += term
    shape = (blocks, tok, HD)
    pair_own_ref[:, 0:tok, :] = dk_own[...].reshape(shape)
    pair_own_ref[:, tok : 2 * tok, :] = dv_own[...].reshape(shape)
    pair_other_ref[:, 0:tok, :] = dk_other[...].astype(jnp.bfloat16).reshape(shape)
    pair_other_ref[:, tok : 2 * tok, :] = dv_other[...].astype(jnp.bfloat16).reshape(shape)
    down_grad_ref[...] = 2.0 * down_total


def call_kernel(body, outs, scratch, flops, exps, *operands):
    in_bytes = sum(x.size * x.dtype.itemsize for x in operands)
    out_bytes = sum(x.size * x.dtype.itemsize for x in outs)
    specs = [pl.BlockSpec(memory_space=pltpu.SMEM)]
    specs += [pl.BlockSpec(memory_space=pltpu.VMEM)] * (len(operands) - 1)
    return pl.pallas_call(
        body,
        out_shape=outs,
        in_specs=specs,
        out_specs=[pl.BlockSpec(memory_space=pltpu.VMEM)] * len(outs),
        scratch_shapes=scratch,
        compiler_params=pltpu.CompilerParams(vmem_limit_bytes=48 * 1024 * 1024),
        cost_estimate=pl.CostEstimate(
            flops=flops, bytes_accessed=in_bytes + out_bytes, transcendentals=exps
        ),
    )(*operands)


def shape_of(shape, dtype):
    return jax.ShapeDtypeStruct(shape, dtype)


def butterfly_sum(value, axis, bits, count):
    def taken(value, mask):
        return lax.ppermute(value, axis, [(i, i ^ mask) for i in range(count)])

    while bits:
        now, bits = bits[:2], bits[2:]
        value = value.astype(jnp.bfloat16)
        near = value.astype(jnp.float32) + taken(value, now[0]).astype(jnp.float32)
        if len(now) == 2:
            far = taken(value, now[1]).astype(jnp.float32)
            far += taken(value, now[0] | now[1]).astype(jnp.float32)
            near += far
        value = near
    return value


def powers_below(count):
    return [1 << n for n in range(count.bit_length() - 1)]


def message_kernel(copies, *refs):
    operands, message_ref, sems = refs[:-2], refs[-2], refs[-1]
    tok = operands[0].shape[0]
    blocks = []
    for rank in range(message_ref.shape[0]):
        cols = pl.ds((rank // copies) * HD, HD)
        for n, ref in enumerate(operands):
            to = message_ref.at[rank, pl.ds(n * tok, tok), :]
            blocks.append(pltpu.make_async_copy(ref.at[:, cols], to, sems.at[len(blocks)]))
    for block in blocks:
        block.start()
    for block in blocks:
        block.wait()


def message_of(copies, ranks, *operands):
    tok = operands[0].shape[0]
    shape = (ranks, len(operands) * tok, HD)
    return pl.pallas_call(
        functools.partial(message_kernel, copies),
        out_shape=shape_of(shape, operands[0].dtype),
        in_specs=[pl.BlockSpec(memory_space=pltpu.HBM)] * len(operands),
        out_specs=pl.BlockSpec(memory_space=pltpu.VMEM),
        scratch_shapes=[pltpu.SemaphoreType.DMA((ranks * len(operands),))],
        cost_estimate=pl.CostEstimate(
            flops=0, bytes_accessed=4 * math.prod(shape), transcendentals=0
        ),
    )(*operands)


def unpack_kernel(copies, back_ref, *out_refs):
    for n, ref in enumerate(out_refs):
        tok = ref.shape[0]
        for at_head in range(ref.shape[1] // HD):
            part = back_ref[at_head * copies, n * tok : (n + 1) * tok, :]
            ref[:, at_head * HD : (at_head + 1) * HD] = part


def in_vmem(body, outs, *operands):
    whole = pl.BlockSpec(memory_space=pltpu.VMEM)
    size = sum(x.size * x.dtype.itemsize for x in operands)
    size += sum(x.size * x.dtype.itemsize for x in outs)
    return pl.pallas_call(
        body,
        out_shape=outs,
        in_specs=[whole] * len(operands),
        out_specs=[whole] * len(outs),
        compiler_params=pltpu.CompilerParams(vmem_limit_bytes=16 * 1024 * 1024),
        cost_estimate=pl.CostEstimate(flops=0, bytes_accessed=size, transcendentals=0),
    )(*operands)


def second_kernel(copies, tok, low_rank, query_ref, own_ref, taken_ref, message_ref):
    feats = own_ref.shape[1] - HD
    lora = (own_ref[:, feats:] + taken_ref[:, feats:].astype(jnp.float32)).T
    lora = lora[0:low_rank].astype(jnp.bfloat16)
    for rank in range(message_ref.shape[0]):
        at = (rank // copies) * HD
        part = own_ref[:, at : at + HD] + taken_ref[:, at : at + HD].astype(jnp.float32)
        message_ref[rank, 0:tok, :] = query_ref[:, at : at + HD]
        message_ref[rank, tok : 2 * tok, :] = part.astype(jnp.bfloat16)
        message_ref[rank, 2 * tok : 2 * tok + low_rank, :] = lora


def on_device(
    sizes,
    head_query_rows,
    head_key_rows,
    head_value_rows,
    output_gradient,
    output_matrix,
    adapter_down_weight,
    adapter_up_weight,
):
    seqs, heads, subs = sizes
    tok, feats = head_query_rows.shape
    cols = output_gradient.shape[1]
    low_rank = adapter_up_weight.shape[0]
    local_heads = feats // HD
    block_rows = tok * subs
    ranks = GROUP // block_rows
    copies = ranks // local_heads
    shift_blocks = GROUP // 2 // block_rows

    seq = lax.axis_index("seq")
    head = lax.axis_index("head")
    sub = lax.axis_index("sub")
    shift = jnp.where(head >= heads // 2, shift_blocks, 0)
    rank = (seq - shift + seqs) % ranks
    my_head = rank // copies

    groups = []
    for at_head in range(heads):
        moved = shift_blocks if at_head >= heads // 2 else 0
        for first in range(0, seqs, ranks):
            groups.append(
                [((first + moved + i) % seqs) * heads + at_head for i in range(ranks)]
            )

    def exchange(parts):
        return lax.all_to_all(
            parts, ("seq", "head"), 0, 0, axis_index_groups=groups, tiled=True
        )

    def swap(value):
        if subs == 1:
            return value
        return lax.ppermute(value, "sub", [(0, 1), (1, 0)])

    sent = message_of(copies, ranks, head_key_rows, head_value_rows)
    sent, output_gradient = lax.optimization_barrier((sent, output_gradient))
    own = exchange(sent)

    chunks = heads // subs
    pieces = []
    for k in range(heads):
        pairs = []
        for src_head in range(heads):
            for src_sub in range(subs):
                j = (src_head % chunks) * subs + src_sub
                dst = ((j + k) % heads) * subs + src_head // chunks
                pairs.append((src_head * subs + src_sub, dst))
        pieces.append(lax.ppermute(output_gradient, ("head", "sub"), pairs))

    up_half = lax.dynamic_slice_in_dim(adapter_up_weight, sub * chunks * cols, chunks * cols, 1)
    if chunks == 1:
        both = jnp.concatenate(pieces, axis=0)
        lora_all = dot_nt(both, up_half)
        grad_all = dot_nt(both, output_matrix)
        grad_all += 2.0 * dot_nt(lora_all.astype(jnp.bfloat16), adapter_down_weight)
        grads = [grad_all[k * tok : (k + 1) * tok] for k in range(heads)]
        loras = [lora_all[k * tok : (k + 1) * tok] for k in range(heads)]
    else:
        grads, loras = [], []
        for k in range(heads):
            at = (((head - k + heads) % heads) // subs) * cols
            lora = dot_nt(pieces[k], lax.dynamic_slice_in_dim(up_half, at, cols, 1))
            grad = dot_nt(pieces[k], lax.dynamic_slice_in_dim(output_matrix, at, cols, 1))
            grads.append(grad + 2.0 * dot_nt(lora.astype(jnp.bfloat16), adapter_down_weight))
            loras.append(lora)

    def terms_for(which, terms):
        total = None
        for k in range(heads):
            mine = ((head - k + heads) % heads) % subs == which
            term = jnp.where(mine, terms[k], 0.0)
            total = term if total is None else total + term
        return total

    spare = jnp.zeros((tok, HD - low_rank), jnp.float32)
    packed = [jnp.concatenate((g, l, spare), axis=1) for g, l in zip(grads, loras)]
    received = swap(terms_for(1 - sub, packed).astype(jnp.bfloat16))
    packed_own = terms_for(sub, packed)

    (message,) = in_vmem(
        functools.partial(second_kernel, copies, tok, low_rank),
        [shape_of((ranks, 2 * tok + low_rank, HD), jnp.bfloat16)],
        head_query_rows,
        packed_own,
        received,
    )
    own, message = lax.optimization_barrier((own, message))
    arrived = exchange(message)
    other = swap(own)

    sub_arg = jnp.full((1,), sub, jnp.int32)
    down_head = lax.dynamic_slice_in_dim(adapter_down_weight, my_head * HD, HD, 0)
    rows = ranks * tok
    pair_count = rows * (rows + TILE)
    first_back, pair_own, pair_other, down_part = call_kernel(
        functools.partial(attention_kernel, tok),
        [
            shape_of((ranks, tok + low_rank, HD), jnp.bfloat16),
            shape_of((ranks, 2 * tok, HD), jnp.float32),
            shape_of((ranks, 2 * tok, HD), jnp.bfloat16),
            shape_of((low_rank, HD), jnp.float32),
        ],
        [pltpu.VMEM((rows, HD), jnp.float32)] * 4,
        12 * pair_count * HD,
        pair_count,
        sub_arg,
        own,
        other,
        arrived,
        down_head.T,
    )

    first = exchange(first_back)
    (query_gradient,) = in_vmem(
        functools.partial(unpack_kernel, copies), [shape_of((tok, feats), first.dtype)], first
    )

    pair_sum = (pair_own + swap(pair_other).astype(jnp.float32)).astype(jnp.bfloat16)
    down_rows = (down_part + swap(down_part)).astype(jnp.bfloat16)
    down_rows = jnp.broadcast_to(down_rows, (ranks, low_rank, HD))
    back = exchange(jnp.concatenate([pair_sum, down_rows], axis=1))
    key_gradient, value_gradient = in_vmem(
        functools.partial(unpack_kernel, copies),
        [shape_of((tok, feats), back.dtype)] * 2,
        back,
    )
    down_terms = back[::copies, 2 * tok :].astype(jnp.float32)
    if seqs > ranks:
        bits = [bit for bit in powers_below(seqs) if bit >= ranks]
        down_terms = butterfly_sum(down_terms, "seq", bits, seqs)
    down_gradient = down_terms.transpose(0, 2, 1).reshape(feats, low_rank)

    middle = jnp.sum(first[::copies, tok:].astype(jnp.float32), axis=0)
    middle = butterfly_sum(middle, "head", powers_below(heads), heads)
    up_part = 2.0 * dot_nn(middle.astype(jnp.bfloat16), output_gradient)
    up_sum = butterfly_sum(up_part, "seq", powers_below(seqs), seqs)
    _, up_sum = lax.optimization_barrier((back, up_sum))
    up_gradient = butterfly_sum(up_sum, "sub", powers_below(subs), subs)
    return (query_gradient, key_gradient, value_gradient, down_gradient, up_gradient)


def solution(mesh):
    rows = P(("rep", "seq", "sub"), "head")
    sizes = (mesh.shape["seq"], mesh.shape["head"], mesh.shape["sub"])
    return jax.shard_map(
        functools.partial(on_device, sizes),
        mesh=mesh,
        in_specs=(rows, rows, rows, rows, P("head", "sub"), P("head", None), P()),
        out_specs=(rows, rows, rows, P(("rep", "head"), None), P("rep", "head")),
        check_vma=False,
    )
```

```python
import functools
import math

import jax
import jax.numpy as jnp
from jax import lax
from jax.experimental import pallas as pl
from jax.experimental.pallas import tpu as pltpu
from jax.sharding import PartitionSpec as P

HD = 128
GROUP = 2048
TILE = 256
HIDDEN = -1e30
SCALE = HD ** (-0.5)
LOG2_SCALE = SCALE * math.log2(math.e)


def dot_nt(left, right):
    return lax.dot_general(
        left, right, (((1,), (1,)), ((), ())), preferred_element_type=jnp.float32
    )


def dot_nn(left, right):
    return jnp.dot(left, right, preferred_element_type=jnp.float32)


def rows_of(ref, blocks, first, count):
    return ref[0:blocks, first : first + count, :].reshape(blocks * count, HD)


def scores_of(sub, keys_own, keys_other, queries, tok):
    def tail_hidden(scores, visible):
        head = scores.shape[0] - TILE
        tail = jnp.where(visible, scores[head:], HIDDEN)
        return tail if head == 0 else jnp.concatenate((scores[:head], tail), axis=0)

    key_at = lax.broadcasted_iota(jnp.int32, (TILE, TILE), 0)
    query_at = lax.broadcasted_iota(jnp.int32, (TILE, TILE), 1)
    own = tail_hidden(dot_nt(keys_own, queries), key_at <= query_at)
    other = tail_hidden(
        dot_nt(keys_other, queries), key_at // tok < query_at // tok + sub
    )
    return own, other


def forward_kernel(tok, sub_ref, own_ref, other_ref, down_t_ref, attn_ref, mid_ref, stat_ref):
    blocks = own_ref.shape[0]
    step = TILE // tok
    sub = sub_ref[0]
    values_own_t = rows_of(own_ref, blocks, 2 * tok, tok).T
    values_other_t = rows_of(other_ref, blocks, tok, tok).T
    for tile in range(blocks // step):
        upto = (tile + 1) * step
        width = upto * tok
        at = tile * TILE
        queries = own_ref[tile * step : upto, 0:tok, :].reshape(TILE, HD)
        own, other = scores_of(
            sub, rows_of(own_ref, upto, tok, tok), rows_of(other_ref, upto, 0, tok), queries, tok
        )
        highest = jnp.maximum(
            jnp.max(own, axis=0, keepdims=True), jnp.max(other, axis=0, keepdims=True)
        )
        own = jnp.exp2((own - highest) * LOG2_SCALE)
        other = jnp.exp2((other - highest) * LOG2_SCALE)
        inverse = 1.0 / (
            jnp.sum(own, axis=0, keepdims=True) + jnp.sum(other, axis=0, keepdims=True)
        )
        attn = dot_nn(values_own_t[:, :width], own.astype(jnp.bfloat16)) + dot_nn(
            values_other_t[:, :width], other.astype(jnp.bfloat16)
        )
        attn = (attn * inverse).astype(jnp.bfloat16)
        attn_ref[:, at : at + TILE] = attn
        mid_ref[:, at : at + TILE] = dot_nn(down_t_ref[...], attn)
        stat_ref[0:1, at : at + TILE] = highest
        stat_ref[1:2, at : at + TILE] = inverse


def backward_kernel(
    tok,
    sub_ref,
    own_ref,
    other_ref,
    dout_ref,
    attn_ref,
    lora_ref,
    stat_ref,
    dq_ref,
    dk_own_ref,
    dv_own_ref,
    pair_other_ref,
    down_grad_ref,
    dk_own,
    dv_own,
    dk_other,
    dv_other,
):
    blocks = own_ref.shape[0]
    step = TILE // tok
    sub = sub_ref[0]
    keys_own_t = rows_of(own_ref, blocks, tok, tok).T
    keys_other_t = rows_of(other_ref, blocks, 0, tok).T
    tiles = blocks // step
    for tile in reversed(range(tiles)):
        upto = (tile + 1) * step
        width = upto * tok
        at = tile * TILE
        queries = own_ref[tile * step : upto, 0:tok, :].reshape(TILE, HD)
        douts = dout_ref[tile * step : upto, 0:tok, :].reshape(TILE, HD)
        highest = stat_ref[0:1, at : at + TILE]
        inverse = stat_ref[1:2, at : at + TILE]
        own, other = scores_of(
            sub, rows_of(own_ref, upto, tok, tok), rows_of(other_ref, upto, 0, tok), queries, tok
        )
        own = jnp.exp2((own - highest) * LOG2_SCALE) * inverse
        other = jnp.exp2((other - highest) * LOG2_SCALE) * inverse
        dprob_own = dot_nt(rows_of(own_ref, upto, 2 * tok, tok), douts)
        dprob_other = dot_nt(rows_of(other_ref, upto, tok, tok), douts)
        delta = jnp.sum(own * dprob_own, axis=0, keepdims=True) + jnp.sum(
            other * dprob_other, axis=0, keepdims=True
        )
        ds_own = (own * (dprob_own - delta) * SCALE).astype(jnp.bfloat16)
        ds_other = (other * (dprob_other - delta) * SCALE).astype(jnp.bfloat16)
        dq = dot_nn(keys_own_t[:, :width], ds_own) + dot_nn(keys_other_t[:, :width], ds_other)
        dq_ref[tile * step : upto] = dq.T.astype(jnp.bfloat16).reshape(step, tok, HD)
        terms = (
            (dk_own, dot_nn(ds_own, queries)),
            (dk_other, dot_nn(ds_other, queries)),
            (dv_own, dot_nn(own.astype(jnp.bfloat16), douts)),
            (dv_other, dot_nn(other.astype(jnp.bfloat16), douts)),
        )
        for total, term in terms:
            if tile == tiles - 1:
                total[...] = term
            else:
                total[0:width] += term
    shape = (blocks, tok, HD)
    dk_own_ref[...] = dk_own[...].reshape(shape)
    dv_own_ref[...] = dv_own[...].reshape(shape)
    pair_other_ref[:, 0:tok, :] = dk_other[...].astype(jnp.bfloat16).reshape(shape)
    pair_other_ref[:, tok : 2 * tok, :] = dv_other[...].astype(jnp.bfloat16).reshape(shape)
    low_rank = lora_ref.shape[0]
    down_grad_ref[...] = 2.0 * dot_nt(lora_ref[...], attn_ref[...])


def call_kernel(body, outs, scratch, flops, exps, *operands, declared=None):
    in_bytes = sum(x.size * x.dtype.itemsize for x in operands)
    out_bytes = sum(x.size * x.dtype.itemsize for x in outs)
    specs = [pl.BlockSpec(memory_space=pltpu.SMEM)]
    specs += [pl.BlockSpec(memory_space=pltpu.VMEM)] * (len(operands) - 1)
    return pl.pallas_call(
        body,
        out_shape=outs,
        in_specs=specs,
        out_specs=[pl.BlockSpec(memory_space=pltpu.VMEM)] * len(outs),
        scratch_shapes=scratch,
        compiler_params=pltpu.CompilerParams(vmem_limit_bytes=48 * 1024 * 1024),
        cost_estimate=pl.CostEstimate(
            flops=flops,
            bytes_accessed=declared or in_bytes + out_bytes,
            transcendentals=exps,
        ),
    )(*operands)


def shape_of(shape, dtype):
    return jax.ShapeDtypeStruct(shape, dtype)


def butterfly_sum(value, axis, bits, count):
    for bit in bits:
        pairs = [(i, i ^ bit) for i in range(count)]
        value = value.astype(jnp.bfloat16)
        taken = lax.ppermute(value, axis, pairs)
        value = value.astype(jnp.float32) + taken.astype(jnp.float32)
    return value


def powers_below(count):
    return [1 << n for n in range(count.bit_length() - 1)]


def message_kernel(copies, *refs):
    operands, message_ref, sems = refs[:-2], refs[-2], refs[-1]
    tok = operands[0].shape[0]
    blocks = []
    for rank in range(message_ref.shape[0]):
        cols = pl.ds((rank // copies) * HD, HD)
        for n, ref in enumerate(operands):
            to = message_ref.at[rank, pl.ds(n * tok, tok), :]
            blocks.append(pltpu.make_async_copy(ref.at[:, cols], to, sems.at[len(blocks)]))
    for block in blocks:
        block.start()
    for block in blocks:
        block.wait()


def message_of(copies, ranks, *operands):
    tok = operands[0].shape[0]
    shape = (ranks, len(operands) * tok, HD)
    return pl.pallas_call(
        functools.partial(message_kernel, copies),
        out_shape=shape_of(shape, operands[0].dtype),
        in_specs=[pl.BlockSpec(memory_space=pltpu.HBM)] * len(operands),
        out_specs=pl.BlockSpec(memory_space=pltpu.VMEM),
        scratch_shapes=[pltpu.SemaphoreType.DMA((ranks * len(operands),))],
        cost_estimate=pl.CostEstimate(
            flops=0, bytes_accessed=4 * math.prod(shape), transcendentals=0
        ),
    )(*operands)


def unpack_kernel(copies, back_ref, *out_refs):
    for n, ref in enumerate(out_refs):
        tok = ref.shape[0]
        for at_head in range(ref.shape[1] // HD):
            part = back_ref[at_head * copies, n * tok : (n + 1) * tok, :]
            ref[:, at_head * HD : (at_head + 1) * HD] = part


def in_vmem(body, outs, *operands):
    whole = pl.BlockSpec(memory_space=pltpu.VMEM)
    size = sum(x.size * x.dtype.itemsize for x in operands)
    size += sum(x.size * x.dtype.itemsize for x in outs)
    return pl.pallas_call(
        body,
        out_shape=outs,
        in_specs=[whole] * len(operands),
        out_specs=[whole] * len(outs),
        compiler_params=pltpu.CompilerParams(vmem_limit_bytes=16 * 1024 * 1024),
        cost_estimate=pl.CostEstimate(flops=0, bytes_accessed=size, transcendentals=0),
    )(*operands)


def cotangent_kernel(chunks, plan_ref, *refs):
    pieces, (matrix_ref, up_ref, down_ref, own_ref, sent_ref) = refs[:-5], refs[-5:]
    tok, cols = pieces[0].shape
    feats, low_rank = down_ref.shape
    count = len(pieces)
    if chunks == 1:
        stacks = [(jnp.concatenate([p[...] for p in pieces], axis=0), pl.ds(0, cols))]
    else:
        stacks = [
            (p[...], pl.ds(pl.multiple_of(plan_ref[count + k], HD), cols))
            for k, p in enumerate(pieces)
        ]
    mine = [plan_ref[k] == 1 for k in range(count)]

    def split(terms):
        parts = [t[i : i + tok] for t in terms for i in range(0, t.shape[0], tok)]
        own = [jnp.where(m, p, 0.0) for m, p in zip(mine, parts)]
        sent = [jnp.where(m, 0.0, p) for m, p in zip(mine, parts)]
        return functools.reduce(jnp.add, own), functools.reduce(jnp.add, sent)

    loras = [dot_nt(rows, up_ref[:, at]) for rows, at in stacks]
    spare = jnp.zeros((tok, HD - low_rank), jnp.float32)
    own, sent = split(loras)
    own_ref[:, feats:] = jnp.concatenate((own, spare), axis=1)
    sent_ref[:, feats:] = jnp.concatenate((sent, spare), axis=1).astype(jnp.bfloat16)
    for first in range(0, feats, TILE):
        here = pl.ds(first, TILE)
        terms = [
            dot_nt(rows, matrix_ref[here, at])
            + 2.0 * dot_nt(lora.astype(jnp.bfloat16), down_ref[here, :])
            for (rows, at), lora in zip(stacks, loras)
        ]
        own, sent = split(terms)
        own_ref[:, here] = own
        sent_ref[:, here] = sent.astype(jnp.bfloat16)


def dout_kernel(copies, tok, own_ref, taken_ref, mid_ref, message_ref):
    feats = own_ref.shape[1] - HD
    low_rank = mid_ref.shape[0]
    lora = (own_ref[:, feats:] + taken_ref[:, feats:].astype(jnp.float32)).T
    lora = lora[0:low_rank].astype(jnp.bfloat16)
    for rank in range(message_ref.shape[0]):
        at = (rank // copies) * HD
        part = own_ref[:, at : at + HD] + taken_ref[:, at : at + HD].astype(jnp.float32)
        message_ref[rank, 0:tok, :] = part.astype(jnp.bfloat16)
        message_ref[rank, tok : tok + low_rank, :] = lora
        mid = mid_ref[:, rank * tok : (rank + 1) * tok].astype(jnp.bfloat16)
        message_ref[rank, tok + low_rank : tok + 2 * low_rank, :] = mid


def on_device(
    sizes,
    head_query_rows,
    head_key_rows,
    head_value_rows,
    output_gradient,
    output_matrix,
    adapter_down_weight,
    adapter_up_weight,
):
    seqs, heads, subs = sizes
    tok, feats = head_query_rows.shape
    cols = output_gradient.shape[1]
    low_rank = adapter_up_weight.shape[0]
    local_heads = feats // HD
    block_rows = tok * subs
    ranks = GROUP // block_rows
    copies = ranks // local_heads
    shift_blocks = GROUP // 2 // block_rows

    seq = lax.axis_index("seq")
    head = lax.axis_index("head")
    sub = lax.axis_index("sub")
    shift = jnp.where(head >= heads // 2, shift_blocks, 0)
    rank = (seq - shift + seqs) % ranks
    my_head = rank // copies

    groups = []
    for at_head in range(heads):
        moved = shift_blocks if at_head >= heads // 2 else 0
        for first in range(0, seqs, ranks):
            groups.append(
                [((first + moved + i) % seqs) * heads + at_head for i in range(ranks)]
            )

    def exchange(parts):
        return lax.all_to_all(
            parts, ("seq", "head"), 0, 0, axis_index_groups=groups, tiled=True
        )

    def swap(value):
        if subs == 1:
            return value
        return lax.ppermute(value, "sub", [(0, 1), (1, 0)])

    sent = message_of(copies, ranks, head_query_rows, head_key_rows, head_value_rows)
    sent, output_gradient = lax.optimization_barrier((sent, output_gradient))
    own = exchange(sent)

    chunks = heads // subs
    pieces = []
    for k in range(heads):
        pairs = []
        for src_head in range(heads):
            for src_sub in range(subs):
                j = (src_head % chunks) * subs + src_sub
                dst = ((j + k) % heads) * subs + src_head // chunks
                pairs.append((src_head * subs + src_sub, dst))
        pieces.append(lax.ppermute(output_gradient, ("head", "sub"), pairs))

    up_half = lax.dynamic_slice_in_dim(adapter_up_weight, sub * chunks * cols, chunks * cols, 1)
    sources = [(head - k + heads) % heads for k in range(heads)]
    plan = [(j % subs == sub).astype(jnp.int32) for j in sources]
    plan += [(j // subs * cols).astype(jnp.int32) for j in sources]
    packed_own, packed_sent = call_kernel(
        functools.partial(cotangent_kernel, chunks),
        [
            shape_of((tok, feats + HD), jnp.float32),
            shape_of((tok, feats + HD), jnp.bfloat16),
        ],
        [],
        0,
        0,
        jnp.stack(plan),
        *pieces,
        output_matrix,
        up_half,
        adapter_down_weight,
        declared=1024,
    )
    received = swap(packed_sent)
    other = swap(own[:, tok:])

    sub_arg = jnp.full((1,), sub, jnp.int32)
    down_head = lax.dynamic_slice_in_dim(adapter_down_weight, my_head * HD, HD, 0)
    rows = ranks * tok
    pair_count = rows * (rows + TILE)
    attn_t, mid_t, stats = call_kernel(
        functools.partial(forward_kernel, tok),
        [
            shape_of((HD, rows), jnp.bfloat16),
            shape_of((low_rank, rows), jnp.float32),
            shape_of((8, rows), jnp.float32),
        ],
        [],
        4 * pair_count * HD,
        pair_count,
        sub_arg,
        own,
        other,
        down_head.T,
    )

    first_copy = rank % copies == 0
    if copies > 1:
        mid_t = jnp.where(first_copy, mid_t, 0.0)
    (message,) = in_vmem(
        functools.partial(dout_kernel, copies, tok),
        [shape_of((ranks, tok + 2 * low_rank, HD), jnp.bfloat16)],
        packed_own,
        received,
        mid_t,
    )
    arrived = exchange(message)
    middle = jnp.sum(arrived[:, tok + low_rank :].astype(jnp.float32), axis=0)
    bit = 1
    while bit < heads:
        middle += lax.ppermute(middle, "head", [(i, i ^ bit) for i in range(heads)])
        bit *= 2
    up_part = 2.0 * dot_nn(middle.astype(jnp.bfloat16), output_gradient)

    lora_t = arrived[:, tok : tok + low_rank].transpose(1, 0, 2).reshape(low_rank, rows)
    dq, dk_own, dv_own, pair_other, down_part = call_kernel(
        functools.partial(backward_kernel, tok),
        [
            shape_of((ranks, tok, HD), jnp.bfloat16),
            shape_of((ranks, tok, HD), jnp.float32),
            shape_of((ranks, tok, HD), jnp.float32),
            shape_of((ranks, 2 * tok, HD), jnp.bfloat16),
            shape_of((low_rank, HD), jnp.float32),
        ],
        [pltpu.VMEM((rows, HD), jnp.float32)] * 4,
        10 * pair_count * HD,
        pair_count,
        sub_arg,
        own,
        other,
        arrived,
        attn_t,
        lora_t,
        stats,
    )
    pair_received = swap(pair_other).astype(jnp.float32)
    down_rows = jnp.where(first_copy, down_part + swap(down_part), 0.0)
    dk = (dk_own + pair_received[:, :tok]).astype(jnp.bfloat16)
    dv = (dv_own + pair_received[:, tok:]).astype(jnp.bfloat16)
    down_rows = jnp.broadcast_to(down_rows.astype(jnp.bfloat16), (ranks, low_rank, HD))
    back_message = jnp.concatenate([dq, dk, dv, down_rows], axis=1)
    back = exchange(back_message)
    query_gradient, key_gradient, value_gradient = in_vmem(
        functools.partial(unpack_kernel, copies),
        [shape_of((tok, feats), back.dtype)] * 3,
        back,
    )
    down_terms = back[::copies, 3 * tok :].astype(jnp.float32)
    if seqs > ranks:
        bits = [bit for bit in powers_below(seqs) if bit >= ranks]
        down_terms = butterfly_sum(down_terms, "seq", bits, seqs)
    down_gradient = down_terms.transpose(0, 2, 1).reshape(feats, low_rank)

    up_sum = butterfly_sum(up_part, "seq", powers_below(seqs), seqs)
    _, up_sum = lax.optimization_barrier((back, up_sum))
    up_gradient = butterfly_sum(up_sum, "sub", powers_below(subs), subs)
    return (query_gradient, key_gradient, value_gradient, down_gradient, up_gradient)


def solution(mesh):
    rows = P(("rep", "seq", "sub"), "head")
    sizes = (mesh.shape["seq"], mesh.shape["head"], mesh.shape["sub"])
    return jax.shard_map(
        functools.partial(on_device, sizes),
        mesh=mesh,
        in_specs=(rows, rows, rows, rows, P("head", "sub"), P("head", None), P()),
        out_specs=(rows, rows, rows, P(("rep", "head"), None), P("rep", "head")),
        check_vma=False,
    )
```

```python
import functools
import math

import jax
import jax.numpy as jnp
from jax import lax
from jax.experimental import pallas as pl
from jax.experimental.pallas import tpu as pltpu
from jax.sharding import PartitionSpec as P

HD = 128
GROUP = 2048
TILE = 256
HIDDEN = -1e30
SCALE = HD ** (-0.5)
LOG2_SCALE = SCALE * math.log2(math.e)


def dot_nt(left, right):
    return lax.dot_general(
        left, right, (((1,), (1,)), ((), ())), preferred_element_type=jnp.float32
    )


def dot_nn(left, right):
    return jnp.dot(left, right, preferred_element_type=jnp.float32)


def chunk_of(ref, tile, slot_of, first, count):
    step = TILE // count
    blocks = [ref[slot_of(tile * step + i), first : first + count, :] for i in range(step)]
    return jnp.concatenate(blocks, axis=0)


def masks_of(sub, tok):
    key_at = lax.broadcasted_iota(jnp.int32, (TILE, TILE), 0)
    query_at = lax.broadcasted_iota(jnp.int32, (TILE, TILE), 1)
    return key_at <= query_at, key_at // tok < query_at // tok + sub


def folded(value, reduce):
    return reduce(value.reshape(TILE // 8, 8, TILE), axis=0)


def slots(scalar_ref, blocks):
    return lambda block: (block + scalar_ref[1]) % blocks


def forward_kernel(
    tok, scalar_ref, own_ref, other_ref, down_t_ref, attn_ref, mid_ref, stat_ref, values_t
):
    blocks = own_ref.shape[0]
    step = TILE // tok
    slot_of = slots(scalar_ref, blocks)
    masks = masks_of(scalar_ref[0], tok)
    refs = ((own_ref, tok), (other_ref, 0))
    for tile in range(blocks // step):
        at = tile * TILE
        queries = chunk_of(own_ref, tile, slot_of, 0, tok)
        for side, (ref, first) in enumerate(refs):
            values = chunk_of(ref, tile, slot_of, first + tok, tok)
            values_t[side, :, at : at + TILE] = values.T
        chunks = []
        highest = None
        for part in range(tile + 1):
            for side, (ref, first) in enumerate(refs):
                scores = dot_nt(chunk_of(ref, part, slot_of, first, tok), queries)
                if part == tile:
                    scores = jnp.where(masks[side], scores, HIDDEN)
                chunks.append((part, side, scores))
                top = folded(scores, jnp.max)
                highest = top if highest is None else jnp.maximum(highest, top)
        highest = jnp.max(highest, axis=0, keepdims=True)
        total = jnp.zeros((8, TILE), jnp.float32)
        attn = jnp.zeros((HD, TILE), jnp.float32)
        for part, side, scores in chunks:
            powers = jnp.exp2((scores - highest) * LOG2_SCALE)
            total += folded(powers, jnp.sum)
            values = values_t[side, :, part * TILE : (part + 1) * TILE]
            attn += dot_nn(values, powers.astype(jnp.bfloat16))
        inverse = 1.0 / jnp.sum(total, axis=0, keepdims=True)
        attn = (attn * inverse).astype(jnp.bfloat16)
        attn_ref[:, at : at + TILE] = attn
        mid = dot_nn(down_t_ref[...], attn)
        for i in range(step):
            slot = slot_of(tile * step + i)
            mid_ref[slot] = mid[:, i * tok : (i + 1) * tok].astype(jnp.bfloat16)
        stat_ref[0:1, at : at + TILE] = highest
        stat_ref[1:2, at : at + TILE] = inverse


def backward_kernel(
    tok,
    scalar_ref,
    own_ref,
    other_ref,
    dout_ref,
    attn_ref,
    stat_ref,
    dq_ref,
    dk_own_ref,
    dv_own_ref,
    pair_other_ref,
    down_grad_ref,
    keys_t,
    dk,
    dv,
):
    blocks = own_ref.shape[0]
    step = TILE // tok
    low_rank = down_grad_ref.shape[0]
    slot_of = slots(scalar_ref, blocks)
    masks = masks_of(scalar_ref[0], tok)
    refs = ((own_ref, tok), (other_ref, 0))
    tiles = blocks // step
    for tile in range(tiles):
        for side, (ref, first) in enumerate(refs):
            keys = chunk_of(ref, tile, slot_of, first, tok)
            keys_t[side, :, tile * TILE : (tile + 1) * TILE] = keys.T
    down_total = jnp.zeros((low_rank, HD), jnp.float32)
    for tile in reversed(range(tiles)):
        at = tile * TILE
        queries = chunk_of(own_ref, tile, slot_of, 0, tok)
        douts = chunk_of(dout_ref, tile, slot_of, 0, tok)
        highest = stat_ref[0:1, at : at + TILE]
        inverse = stat_ref[1:2, at : at + TILE]
        delta = jnp.zeros((8, TILE), jnp.float32)
        chunks = []
        for part in range(tile + 1):
            here = pl.ds(part * TILE, TILE)
            for side, (ref, first) in enumerate(refs):
                scores = dot_nt(chunk_of(ref, part, slot_of, first, tok), queries)
                if part == tile:
                    scores = jnp.where(masks[side], scores, HIDDEN)
                prob = jnp.exp2((scores - highest) * LOG2_SCALE) * inverse
                dprob = dot_nt(chunk_of(ref, part, slot_of, first + tok, tok), douts)
                delta += folded(prob * dprob, jnp.sum)
                dv_term = dot_nn(prob.astype(jnp.bfloat16), douts)
                if tile == tiles - 1:
                    dv[side, here, :] = dv_term
                else:
                    dv[side, here, :] += dv_term
                chunks.append((part, side, prob, dprob))
        delta = jnp.sum(delta, axis=0, keepdims=True)
        dq = jnp.zeros((HD, TILE), jnp.float32)
        for part, side, prob, dprob in chunks:
            here = pl.ds(part * TILE, TILE)
            dscore = (prob * (dprob - delta)).astype(jnp.bfloat16)
            dq += dot_nn(keys_t[side, :, here], dscore)
            dk_term = dot_nn(dscore, queries)
            if tile == tiles - 1:
                dk[side, here, :] = dk_term
            else:
                dk[side, here, :] += dk_term
        dq = (dq * SCALE).T.astype(jnp.bfloat16)
        for i in range(step):
            slot = slot_of(tile * step + i)
            dq_ref[slot] = dq[i * tok : (i + 1) * tok]
            lora = dout_ref[slot, tok : tok + low_rank, :]
            attn = attn_ref[:, at + i * tok : at + (i + 1) * tok]
            down_total += dot_nt(lora, attn)
    for block in range(blocks):
        here = pl.ds(block * tok, tok)
        slot = slot_of(block)
        dk_own_ref[slot] = dk[0, here, :] * SCALE
        dv_own_ref[slot] = dv[0, here, :]
        pair_other_ref[slot, 0:tok, :] = (dk[1, here, :] * SCALE).astype(jnp.bfloat16)
        pair_other_ref[slot, tok : 2 * tok, :] = dv[1, here, :].astype(jnp.bfloat16)
    down_grad_ref[...] = 2.0 * down_total


def call_kernel(body, outs, scratch, flops, exps, *operands, declared=None, limit=48):
    in_bytes = sum(x.size * x.dtype.itemsize for x in operands)
    out_bytes = sum(x.size * x.dtype.itemsize for x in outs)
    specs = [pl.BlockSpec(memory_space=pltpu.SMEM)]
    specs += [pl.BlockSpec(memory_space=pltpu.VMEM)] * (len(operands) - 1)
    return pl.pallas_call(
        body,
        out_shape=outs,
        in_specs=specs,
        out_specs=[pl.BlockSpec(memory_space=pltpu.VMEM)] * len(outs),
        scratch_shapes=scratch,
        compiler_params=pltpu.CompilerParams(vmem_limit_bytes=limit * 1024 * 1024),
        cost_estimate=pl.CostEstimate(
            flops=flops,
            bytes_accessed=declared or in_bytes + out_bytes,
            transcendentals=exps,
        ),
    )(*operands)


def shape_of(shape, dtype):
    return jax.ShapeDtypeStruct(shape, dtype)


def butterfly_sum(value, axis, bits, count):
    for bit in bits:
        pairs = [(i, i ^ bit) for i in range(count)]
        value = value.astype(jnp.bfloat16)
        taken = lax.ppermute(value, axis, pairs)
        value = value.astype(jnp.float32) + taken.astype(jnp.float32)
    return value


def powers_below(count):
    return [1 << n for n in range(count.bit_length() - 1)]


def message_kernel(copies, *refs):
    operands, message_ref, sems = refs[:-2], refs[-2], refs[-1]
    tok = operands[0].shape[0]
    blocks = []
    for rank in range(message_ref.shape[0]):
        cols = pl.ds((rank // copies) * HD, HD)
        for n, ref in enumerate(operands):
            to = message_ref.at[rank, pl.ds(n * tok, tok), :]
            blocks.append(pltpu.make_async_copy(ref.at[:, cols], to, sems.at[len(blocks)]))
    for block in blocks:
        block.start()
    for block in blocks:
        block.wait()


def message_of(copies, ranks, *operands):
    tok = operands[0].shape[0]
    shape = (ranks, len(operands) * tok, HD)
    return pl.pallas_call(
        functools.partial(message_kernel, copies),
        out_shape=shape_of(shape, operands[0].dtype),
        in_specs=[pl.BlockSpec(memory_space=pltpu.HBM)] * len(operands),
        out_specs=pl.BlockSpec(memory_space=pltpu.VMEM),
        scratch_shapes=[pltpu.SemaphoreType.DMA((ranks * len(operands),))],
        cost_estimate=pl.CostEstimate(
            flops=0, bytes_accessed=4 * math.prod(shape), transcendentals=0
        ),
    )(*operands)


def unpack_kernel(copies, back_ref, *refs):
    out_refs, down_ref = refs[:3], refs[3] if len(refs) > 3 else None
    tok = out_refs[0].shape[0]
    for at_head in range(out_refs[0].shape[1] // HD):
        cols = slice(at_head * HD, (at_head + 1) * HD)
        for n, ref in enumerate(out_refs):
            ref[:, cols] = back_ref[at_head * copies, n * tok : (n + 1) * tok, :]
        if down_ref is not None:
            down_ref[cols, :] = back_ref[at_head * copies, 3 * tok :, :].astype(jnp.float32).T


def in_vmem(body, outs, *operands):
    whole = pl.BlockSpec(memory_space=pltpu.VMEM)
    size = sum(x.size * x.dtype.itemsize for x in operands)
    size += sum(x.size * x.dtype.itemsize for x in outs)
    return pl.pallas_call(
        body,
        out_shape=outs,
        in_specs=[whole] * len(operands),
        out_specs=[whole] * len(outs),
        compiler_params=pltpu.CompilerParams(vmem_limit_bytes=16 * 1024 * 1024),
        cost_estimate=pl.CostEstimate(flops=0, bytes_accessed=size, transcendentals=0),
    )(*operands)


def cotangent_kernel(chunks, plan_ref, *refs):
    pieces, (matrix_ref, up_ref, down_ref, own_ref, sent_ref) = refs[:-5], refs[-5:]
    tok, cols = pieces[0].shape
    feats, low_rank = down_ref.shape
    count = len(pieces)
    if chunks == 1:
        stacks = [(jnp.concatenate([p[...] for p in pieces], axis=0), pl.ds(0, cols))]
    else:
        stacks = [
            (p[...], pl.ds(pl.multiple_of(plan_ref[count + k], HD), cols))
            for k, p in enumerate(pieces)
        ]
    mine = [plan_ref[k] == 1 for k in range(count)]

    def split(terms):
        parts = [t[i : i + tok] for t in terms for i in range(0, t.shape[0], tok)]
        own = [jnp.where(m, p, 0.0) for m, p in zip(mine, parts)]
        sent = [jnp.where(m, 0.0, p) for m, p in zip(mine, parts)]
        return functools.reduce(jnp.add, own), functools.reduce(jnp.add, sent)

    loras = [dot_nt(rows, up_ref[:, at]) for rows, at in stacks]
    spare = jnp.zeros((tok, HD - low_rank), jnp.float32)
    own, sent = split(loras)
    own_ref[:, feats:] = jnp.concatenate((own, spare), axis=1)
    sent_ref[:, feats:] = jnp.concatenate((sent, spare), axis=1).astype(jnp.bfloat16)
    for first in range(0, feats, TILE):
        here = pl.ds(first, TILE)
        terms = [
            dot_nt(rows, matrix_ref[here, at])
            + 2.0 * dot_nt(lora.astype(jnp.bfloat16), down_ref[here, :])
            for (rows, at), lora in zip(stacks, loras)
        ]
        own, sent = split(terms)
        own_ref[:, here] = own
        sent_ref[:, here] = sent.astype(jnp.bfloat16)


def dout_kernel(copies, tok, own_ref, taken_ref, mid_ref, message_ref):
    feats = own_ref.shape[1] - HD
    low_rank = mid_ref.shape[1]
    lora = (own_ref[:, feats:] + taken_ref[:, feats:].astype(jnp.float32)).T
    lora = lora[0:low_rank].astype(jnp.bfloat16)
    for rank in range(message_ref.shape[0]):
        at = (rank // copies) * HD
        part = own_ref[:, at : at + HD] + taken_ref[:, at : at + HD].astype(jnp.float32)
        message_ref[rank, 0:tok, :] = part.astype(jnp.bfloat16)
        message_ref[rank, tok : tok + low_rank, :] = lora
        message_ref[rank, tok + low_rank : tok + 2 * low_rank, :] = mid_ref[rank]


def on_device(
    sizes,
    head_query_rows,
    head_key_rows,
    head_value_rows,
    output_gradient,
    output_matrix,
    adapter_down_weight,
    adapter_up_weight,
):
    seqs, heads, subs = sizes
    tok, feats = head_query_rows.shape
    cols = output_gradient.shape[1]
    low_rank = adapter_up_weight.shape[0]
    local_heads = feats // HD
    block_rows = tok * subs
    ranks = GROUP // block_rows
    copies = ranks // local_heads
    shift_blocks = GROUP // 2 // block_rows

    seq = lax.axis_index("seq")
    head = lax.axis_index("head")
    sub = lax.axis_index("sub")
    shifted = head >= heads // 2
    rank = (seq + shift_blocks) % ranks
    my_head = rank // copies

    groups = []
    for at_head in range(heads):
        for first in range(0, seqs, ranks):
            members = [first + shift_blocks + i for i in range(ranks)]
            if at_head < heads // 2:
                members = [first + (m - first) % ranks for m in members]
            members = [m % seqs for m in members]
            groups.append([m * heads + at_head for m in members])
    turned = jnp.where(shifted, 0, shift_blocks)
    scalars = jnp.stack((sub, turned)).astype(jnp.int32)

    def exchange(parts):
        return lax.all_to_all(
            parts, ("seq", "head"), 0, 0, axis_index_groups=groups, tiled=True
        )

    def swap(value):
        if subs == 1:
            return value
        return lax.ppermute(value, "sub", [(0, 1), (1, 0)])

    sent = message_of(copies, ranks, head_query_rows, head_key_rows, head_value_rows)
    sent, output_gradient = lax.optimization_barrier((sent, output_gradient))
    own = exchange(sent)

    chunks = heads // subs
    pieces = []
    for k in range(heads):
        pairs = []
        for src_head in range(heads):
            for src_sub in range(subs):
                j = (src_head % chunks) * subs + src_sub
                dst = ((j + k) % heads) * subs + src_head // chunks
                pairs.append((src_head * subs + src_sub, dst))
        pieces.append(lax.ppermute(output_gradient, ("head", "sub"), pairs))

    up_half = lax.dynamic_slice_in_dim(adapter_up_weight, sub * chunks * cols, chunks * cols, 1)
    sources = [(head - k + heads) % heads for k in range(heads)]
    plan = [(j % subs == sub).astype(jnp.int32) for j in sources]
    plan += [(j // subs * cols).astype(jnp.int32) for j in sources]
    packed_own, packed_sent = call_kernel(
        functools.partial(cotangent_kernel, chunks),
        [
            shape_of((tok, feats + HD), jnp.float32),
            shape_of((tok, feats + HD), jnp.bfloat16),
        ],
        [],
        0,
        0,
        jnp.stack(plan),
        *pieces,
        output_matrix,
        up_half,
        adapter_down_weight,
        declared=1024,
        limit=16,
    )
    received = swap(packed_sent)
    own, _ = lax.optimization_barrier((own, packed_sent))
    other = swap(own[:, tok:])

    down_head = lax.dynamic_slice_in_dim(adapter_down_weight, my_head * HD, HD, 0)
    rows = ranks * tok
    pair_count = rows * (rows + TILE)
    attn_t, middle_rows, stats = call_kernel(
        functools.partial(forward_kernel, tok),
        [
            shape_of((HD, rows), jnp.bfloat16),
            shape_of((ranks, low_rank, tok), jnp.bfloat16),
            shape_of((8, rows), jnp.float32),
        ],
        [pltpu.VMEM((2, HD, rows), jnp.bfloat16)],
        4 * pair_count * HD,
        pair_count,
        scalars,
        own,
        other,
        down_head.T,
    )

    first_copy = rank % copies == 0
    if copies > 1:
        middle_rows = jnp.where(first_copy, middle_rows, 0.0)
    (message,) = in_vmem(
        functools.partial(dout_kernel, copies, tok),
        [shape_of((ranks, tok + 2 * low_rank, HD), jnp.bfloat16)],
        packed_own,
        received,
        middle_rows,
    )
    arrived = exchange(message)
    middle = jnp.sum(arrived[:, tok + low_rank :].astype(jnp.float32), axis=0)
    bit = 1
    while bit < heads:
        middle += lax.ppermute(middle, "head", [(i, i ^ bit) for i in range(heads)])
        bit *= 2
    up_part = 2.0 * dot_nn(middle.astype(jnp.bfloat16), output_gradient)

    dq, dk_own, dv_own, pair_other, down_part = call_kernel(
        functools.partial(backward_kernel, tok),
        [
            shape_of((ranks, tok, HD), jnp.bfloat16),
            shape_of((ranks, tok, HD), jnp.float32),
            shape_of((ranks, tok, HD), jnp.float32),
            shape_of((ranks, 2 * tok, HD), jnp.bfloat16),
            shape_of((low_rank, HD), jnp.float32),
        ],
        [pltpu.VMEM((2, HD, rows), jnp.bfloat16)]
        + [pltpu.VMEM((2, rows, HD), jnp.float32)] * 2,
        10 * pair_count * HD,
        pair_count,
        scalars,
        own,
        other,
        arrived,
        attn_t,
        stats,
    )
    pair_received = swap(pair_other).astype(jnp.float32)
    down_rows = jnp.where(first_copy, down_part + swap(down_part), 0.0)
    dk = (dk_own + pair_received[:, :tok]).astype(jnp.bfloat16)
    dv = (dv_own + pair_received[:, tok:]).astype(jnp.bfloat16)
    down_rows = jnp.broadcast_to(down_rows.astype(jnp.bfloat16), (ranks, low_rank, HD))
    back_message = jnp.concatenate([dq, dk, dv, down_rows], axis=1)
    back = exchange(back_message)
    outs = [shape_of((tok, feats), back.dtype)] * 3
    if seqs == ranks:
        outs.append(shape_of((feats, low_rank), jnp.float32))
    outs = list(in_vmem(functools.partial(unpack_kernel, copies), outs, back))
    if seqs > ranks:
        bits = [bit for bit in powers_below(seqs) if bit >= ranks]
        down_terms = back[::copies, 3 * tok :].astype(jnp.float32)
        down_terms = butterfly_sum(down_terms, "seq", bits, seqs)
        outs.append(down_terms.transpose(0, 2, 1).reshape(feats, low_rank))
    query_gradient, key_gradient, value_gradient, down_gradient = outs

    up_sum = butterfly_sum(up_part, "seq", powers_below(seqs), seqs)
    _, up_sum = lax.optimization_barrier((back, up_sum))
    up_gradient = butterfly_sum(up_sum, "sub", powers_below(subs), subs)
    return (query_gradient, key_gradient, value_gradient, down_gradient, up_gradient)


def solution(mesh):
    rows = P(("rep", "seq", "sub"), "head")
    sizes = (mesh.shape["seq"], mesh.shape["head"], mesh.shape["sub"])
    return jax.shard_map(
        functools.partial(on_device, sizes),
        mesh=mesh,
        in_specs=(rows, rows, rows, rows, P("head", "sub"), P("head", None), P()),
        out_specs=(rows, rows, rows, P(("rep", "head"), None), P("rep", "head")),
        check_vma=False,
    )
```

```python
import functools
import math

import jax
import jax.numpy as jnp
from jax import lax
from jax.experimental import pallas as pl
from jax.experimental.pallas import tpu as pltpu
from jax.sharding import PartitionSpec as P

HD = 128
GROUP = 2048
TILE = 256
HIDDEN = -1e30
SCALE = HD ** (-0.5)
LOG2_SCALE = SCALE * math.log2(math.e)


def dot_nt(left, right):
    return lax.dot_general(
        left, right, (((1,), (1,)), ((), ())), preferred_element_type=jnp.float32
    )


def dot_nn(left, right):
    return jnp.dot(left, right, preferred_element_type=jnp.float32)


def rows_of(ref, blocks, slot_of, first, count):
    parts = [ref[slot_of(block), first : first + count, :] for block in blocks]
    return jnp.concatenate(parts, axis=0)


def slots(scalar_ref, blocks):
    return lambda block: (block + scalar_ref[1]) % blocks


def scores_of(sub, keys_own, keys_other, queries, tok):
    def tail_hidden(scores, visible):
        head = scores.shape[0] - TILE
        tail = jnp.where(visible, scores[head:], HIDDEN)
        return tail if head == 0 else jnp.concatenate((scores[:head], tail), axis=0)

    key_at = lax.broadcasted_iota(jnp.int32, (TILE, TILE), 0)
    query_at = lax.broadcasted_iota(jnp.int32, (TILE, TILE), 1)
    own = tail_hidden(dot_nt(keys_own, queries), key_at <= query_at)
    other = tail_hidden(
        dot_nt(keys_other, queries), key_at // tok < query_at // tok + sub
    )
    return own, other


def forward_kernel(
    tok, scalar_ref, own_ref, other_ref, down_t_ref, attn_ref, mid_ref, stat_ref
):
    blocks = own_ref.shape[0]
    step = TILE // tok
    sub = scalar_ref[0]
    slot_of = slots(scalar_ref, blocks)
    keys_own = rows_of(own_ref, range(blocks), slot_of, tok, tok)
    keys_other = rows_of(other_ref, range(blocks), slot_of, 0, tok)
    values_own_t = rows_of(own_ref, range(blocks), slot_of, 2 * tok, tok).T
    values_other_t = rows_of(other_ref, range(blocks), slot_of, tok, tok).T
    for tile in range(blocks // step):
        here = range(tile * step, (tile + 1) * step)
        width = (tile + 1) * TILE
        at = tile * TILE
        queries = rows_of(own_ref, here, slot_of, 0, tok)
        own, other = scores_of(sub, keys_own[:width], keys_other[:width], queries, tok)
        highest = jnp.maximum(
            jnp.max(own, axis=0, keepdims=True), jnp.max(other, axis=0, keepdims=True)
        )
        own = jnp.exp2((own - highest) * LOG2_SCALE)
        other = jnp.exp2((other - highest) * LOG2_SCALE)
        inverse = 1.0 / (
            jnp.sum(own, axis=0, keepdims=True) + jnp.sum(other, axis=0, keepdims=True)
        )
        attn = dot_nn(values_own_t[:, :width], own.astype(jnp.bfloat16)) + dot_nn(
            values_other_t[:, :width], other.astype(jnp.bfloat16)
        )
        attn = (attn * inverse).astype(jnp.bfloat16)
        attn_ref[:, at : at + TILE] = attn
        mid = dot_nn(down_t_ref[...], attn)
        for i, block in enumerate(here):
            mid_ref[slot_of(block)] = mid[:, i * tok : (i + 1) * tok].astype(jnp.bfloat16)
        stat_ref[0:1, at : at + TILE] = highest
        stat_ref[1:2, at : at + TILE] = inverse


def backward_kernel(
    tok,
    scalar_ref,
    own_ref,
    other_ref,
    dout_ref,
    attn_ref,
    stat_ref,
    dq_ref,
    dk_own_ref,
    dv_own_ref,
    pair_other_ref,
    down_grad_ref,
    dk_own,
    dv_own,
    dk_other,
    dv_other,
):
    blocks = own_ref.shape[0]
    step = TILE // tok
    sub = scalar_ref[0]
    low_rank = down_grad_ref.shape[0]
    slot_of = slots(scalar_ref, blocks)
    keys_own = rows_of(own_ref, range(blocks), slot_of, tok, tok)
    keys_other = rows_of(other_ref, range(blocks), slot_of, 0, tok)
    values_own = rows_of(own_ref, range(blocks), slot_of, 2 * tok, tok)
    values_other = rows_of(other_ref, range(blocks), slot_of, tok, tok)
    keys_own_t = keys_own.T
    keys_other_t = keys_other.T
    tiles = blocks // step
    down_total = jnp.zeros((low_rank, HD), jnp.float32)
    for tile in reversed(range(tiles)):
        here = range(tile * step, (tile + 1) * step)
        width = (tile + 1) * TILE
        at = tile * TILE
        queries = rows_of(own_ref, here, slot_of, 0, tok)
        douts = rows_of(dout_ref, here, slot_of, 0, tok)
        highest = stat_ref[0:1, at : at + TILE]
        inverse = stat_ref[1:2, at : at + TILE]
        own, other = scores_of(sub, keys_own[:width], keys_other[:width], queries, tok)
        own = jnp.exp2((own - highest) * LOG2_SCALE) * inverse
        other = jnp.exp2((other - highest) * LOG2_SCALE) * inverse
        dprob_own = dot_nt(values_own[:width], douts)
        dprob_other = dot_nt(values_other[:width], douts)
        delta = jnp.sum(own * dprob_own, axis=0, keepdims=True) + jnp.sum(
            other * dprob_other, axis=0, keepdims=True
        )
        ds_own = (own * (dprob_own - delta)).astype(jnp.bfloat16)
        ds_other = (other * (dprob_other - delta)).astype(jnp.bfloat16)
        dq = dot_nn(keys_own_t[:, :width], ds_own) + dot_nn(keys_other_t[:, :width], ds_other)
        dq = (dq * SCALE).T.astype(jnp.bfloat16)
        terms = (
            (dk_own, dot_nn(ds_own, queries)),
            (dk_other, dot_nn(ds_other, queries)),
            (dv_own, dot_nn(own.astype(jnp.bfloat16), douts)),
            (dv_other, dot_nn(other.astype(jnp.bfloat16), douts)),
        )
        for total, term in terms:
            if tile == tiles - 1:
                total[...] = term
            else:
                total[0:width] += term
        for i, block in enumerate(here):
            slot = slot_of(block)
            dq_ref[slot] = dq[i * tok : (i + 1) * tok]
            lora = dout_ref[slot, tok : tok + low_rank, :]
            attn = attn_ref[:, at + i * tok : at + (i + 1) * tok]
            down_total += dot_nt(lora, attn)
    for block in range(blocks):
        rows = pl.ds(block * tok, tok)
        slot = slot_of(block)
        dk_own_ref[slot] = dk_own[rows, :] * SCALE
        dv_own_ref[slot] = dv_own[rows, :]
        pair_other_ref[slot, 0:tok, :] = (dk_other[rows, :] * SCALE).astype(jnp.bfloat16)
        pair_other_ref[slot, tok : 2 * tok, :] = dv_other[rows, :].astype(jnp.bfloat16)
    down_grad_ref[...] = 2.0 * down_total


def call_kernel(body, outs, scratch, flops, exps, *operands, declared=None, limit=48, in_hbm=()):
    in_bytes = sum(x.size * x.dtype.itemsize for x in operands)
    out_bytes = sum(x.size * x.dtype.itemsize for x in outs)
    specs = [pl.BlockSpec(memory_space=pltpu.SMEM)]
    for n in range(len(operands) - 1):
        space = pltpu.HBM if n in in_hbm else pltpu.VMEM
        specs.append(pl.BlockSpec(memory_space=space))
    return pl.pallas_call(
        body,
        out_shape=outs,
        in_specs=specs,
        out_specs=[pl.BlockSpec(memory_space=pltpu.VMEM)] * len(outs),
        scratch_shapes=scratch,
        compiler_params=pltpu.CompilerParams(vmem_limit_bytes=limit * 1024 * 1024),
        cost_estimate=pl.CostEstimate(
            flops=flops,
            bytes_accessed=declared or in_bytes + out_bytes,
            transcendentals=exps,
        ),
    )(*operands)


def shape_of(shape, dtype):
    return jax.ShapeDtypeStruct(shape, dtype)


def butterfly_sum(value, axis, bits, count):
    for bit in bits:
        pairs = [(i, i ^ bit) for i in range(count)]
        value = value.astype(jnp.bfloat16)
        taken = lax.ppermute(value, axis, pairs)
        value = value.astype(jnp.float32) + taken.astype(jnp.float32)
    return value


def powers_below(count):
    return [1 << n for n in range(count.bit_length() - 1)]


def message_kernel(copies, *refs):
    count = (len(refs) - 3) // 2
    operands, message_ref = refs[:count], refs[count]
    held, in_sems, out_sems = refs[count + 1 : -2], refs[-2], refs[-1]
    tok = operands[0].shape[0]
    arriving = [
        pltpu.make_async_copy(ref, to, in_sems.at[n])
        for n, (ref, to) in enumerate(zip(operands, held))
    ]
    for copy in arriving:
        copy.start()
    leaving = []
    for n, (copy, ref) in enumerate(zip(arriving, held)):
        copy.wait()
        for rank in range(message_ref.shape[0]):
            cols = pl.ds((rank // copies) * HD, HD)
            to = message_ref.at[rank, pl.ds(n * tok, tok), :]
            leaving.append(pltpu.make_async_copy(ref.at[:, cols], to, out_sems.at[len(leaving)]))
            leaving[-1].start()
    for copy in leaving:
        copy.wait()


def message_of(copies, ranks, *operands):
    tok = operands[0].shape[0]
    count = len(operands)
    shape = (ranks, count * tok, HD)
    return pl.pallas_call(
        functools.partial(message_kernel, copies),
        out_shape=shape_of(shape, operands[0].dtype),
        in_specs=[pl.BlockSpec(memory_space=pltpu.HBM)] * count,
        out_specs=pl.BlockSpec(memory_space=pltpu.HBM),
        scratch_shapes=[pltpu.VMEM(x.shape, x.dtype) for x in operands]
        + [pltpu.SemaphoreType.DMA((count,)), pltpu.SemaphoreType.DMA((ranks * count,))],
        cost_estimate=pl.CostEstimate(
            flops=0, bytes_accessed=4 * math.prod(shape), transcendentals=0
        ),
    )(*operands)


def unpack_kernel(copies, back_ref, *refs):
    out_refs, down_ref = refs[:3], refs[3] if len(refs) > 3 else None
    tok = out_refs[0].shape[0]
    for at_head in range(out_refs[0].shape[1] // HD):
        cols = slice(at_head * HD, (at_head + 1) * HD)
        for n, ref in enumerate(out_refs):
            ref[:, cols] = back_ref[at_head * copies, n * tok : (n + 1) * tok, :]
        if down_ref is not None:
            down_ref[:, cols] = back_ref[at_head * copies, 3 * tok :, :].astype(jnp.float32)


def in_vmem(body, outs, *operands):
    whole = pl.BlockSpec(memory_space=pltpu.VMEM)
    size = sum(x.size * x.dtype.itemsize for x in operands)
    size += sum(x.size * x.dtype.itemsize for x in outs)
    return pl.pallas_call(
        body,
        out_shape=outs,
        in_specs=[whole] * len(operands),
        out_specs=[whole] * len(outs),
        compiler_params=pltpu.CompilerParams(vmem_limit_bytes=16 * 1024 * 1024),
        cost_estimate=pl.CostEstimate(flops=0, bytes_accessed=size, transcendentals=0),
    )(*operands)


def cotangent_kernel(chunks, plan_ref, *refs):
    pieces, (matrix_hbm, up_ref, down_ref, own_ref, sent_ref, matrix_ref, sems) = refs[:-7], refs[-7:]
    tok, cols = pieces[0].shape
    feats, low_rank = down_ref.shape
    arriving = [
        pltpu.make_async_copy(
            matrix_hbm.at[pl.ds(first, TILE), :],
            matrix_ref.at[pl.ds(first, TILE), :],
            sems.at[first // TILE],
        )
        for first in range(0, feats, TILE)
    ]
    for copy in arriving:
        copy.start()
    count = len(pieces)
    if chunks == 1:
        stacks = [(jnp.concatenate([p[...] for p in pieces], axis=0), pl.ds(0, cols))]
    else:
        stacks = [
            (p[...], pl.ds(pl.multiple_of(plan_ref[count + k], HD), cols))
            for k, p in enumerate(pieces)
        ]
    mine = [plan_ref[k] == 1 for k in range(count)]

    def split(terms):
        parts = [t[i : i + tok] for t in terms for i in range(0, t.shape[0], tok)]
        own = [jnp.where(m, p, 0.0) for m, p in zip(mine, parts)]
        sent = [jnp.where(m, 0.0, p) for m, p in zip(mine, parts)]
        return functools.reduce(jnp.add, own), functools.reduce(jnp.add, sent)

    loras = [dot_nt(rows, up_ref[:, at]) for rows, at in stacks]
    spare = jnp.zeros((tok, HD - low_rank), jnp.float32)
    own, sent = split(loras)
    own_ref[:, feats:] = jnp.concatenate((own, spare), axis=1)
    sent_ref[:, feats:] = jnp.concatenate((sent, spare), axis=1).astype(jnp.bfloat16)
    for first in range(0, feats, TILE):
        here = pl.ds(first, TILE)
        arriving[first // TILE].wait()
        terms = [
            dot_nt(rows, matrix_ref[here, at])
            + 2.0 * dot_nt(lora.astype(jnp.bfloat16), down_ref[here, :])
            for (rows, at), lora in zip(stacks, loras)
        ]
        own, sent = split(terms)
        own_ref[:, here] = own
        sent_ref[:, here] = sent.astype(jnp.bfloat16)


def dout_kernel(copies, tok, own_ref, taken_ref, mid_ref, message_ref):
    feats = own_ref.shape[1] - HD
    low_rank = mid_ref.shape[1]
    lora = (own_ref[:, feats:] + taken_ref[:, feats:].astype(jnp.float32)).T
    lora = lora[0:low_rank].astype(jnp.bfloat16)
    for rank in range(message_ref.shape[0]):
        at = (rank // copies) * HD
        part = own_ref[:, at : at + HD] + taken_ref[:, at : at + HD].astype(jnp.float32)
        message_ref[rank, 0:tok, :] = part.astype(jnp.bfloat16)
        message_ref[rank, tok : tok + low_rank, :] = lora
        message_ref[rank, tok + low_rank : tok + 2 * low_rank, :] = mid_ref[rank]


def on_device(
    sizes,
    head_query_rows,
    head_key_rows,
    head_value_rows,
    output_gradient,
    output_matrix,
    adapter_down_weight,
    adapter_up_weight,
):
    seqs, heads, subs = sizes
    tok, feats = head_query_rows.shape
    cols = output_gradient.shape[1]
    low_rank = adapter_up_weight.shape[0]
    local_heads = feats // HD
    block_rows = tok * subs
    ranks = GROUP // block_rows
    copies = ranks // local_heads
    shift_blocks = GROUP // 2 // block_rows

    seq = lax.axis_index("seq")
    head = lax.axis_index("head")
    sub = lax.axis_index("sub")
    shifted = head >= heads // 2
    rank = (seq + shift_blocks) % ranks
    my_head = rank // copies

    groups = []
    for at_head in range(heads):
        for first in range(0, seqs, ranks):
            members = [first + shift_blocks + i for i in range(ranks)]
            if at_head < heads // 2:
                members = [first + (m - first) % ranks for m in members]
            members = [m % seqs for m in members]
            groups.append([m * heads + at_head for m in members])
    turned = jnp.where(shifted, 0, shift_blocks)
    scalars = jnp.stack((sub, turned)).astype(jnp.int32)

    def exchange(parts):
        return lax.all_to_all(
            parts, ("seq", "head"), 0, 0, axis_index_groups=groups, tiled=True
        )

    def swap(value):
        if subs == 1:
            return value
        return lax.ppermute(value, "sub", [(0, 1), (1, 0)])

    sent = message_of(copies, ranks, head_query_rows, head_key_rows, head_value_rows)
    sent, output_gradient = lax.optimization_barrier((sent, output_gradient))
    own = exchange(sent)

    chunks = heads // subs
    pieces = []
    for k in range(heads):
        pairs = []
        for src_head in range(heads):
            for src_sub in range(subs):
                j = (src_head % chunks) * subs + src_sub
                dst = ((j + k) % heads) * subs + src_head // chunks
                pairs.append((src_head * subs + src_sub, dst))
        pieces.append(lax.ppermute(output_gradient, ("head", "sub"), pairs))

    up_half = lax.dynamic_slice_in_dim(adapter_up_weight, sub * chunks * cols, chunks * cols, 1)
    sources = [(head - k + heads) % heads for k in range(heads)]
    plan = [(j % subs == sub).astype(jnp.int32) for j in sources]
    plan += [(j // subs * cols).astype(jnp.int32) for j in sources]
    packed_own, packed_sent = call_kernel(
        functools.partial(cotangent_kernel, chunks),
        [
            shape_of((tok, feats + HD), jnp.float32),
            shape_of((tok, feats + HD), jnp.bfloat16),
        ],
        [
            pltpu.VMEM(output_matrix.shape, output_matrix.dtype),
            pltpu.SemaphoreType.DMA((feats // TILE,)),
        ],
        0,
        0,
        jnp.stack(plan),
        *pieces,
        output_matrix,
        up_half,
        adapter_down_weight,
        declared=1024,
        limit=16,
        in_hbm=(heads,),
    )
    received = swap(packed_sent)
    own, _ = lax.optimization_barrier((own, packed_sent))
    other = swap(own[:, tok:])

    down_head = lax.dynamic_slice_in_dim(adapter_down_weight, my_head * HD, HD, 0)
    rows = ranks * tok
    pair_count = rows * (rows + TILE)
    attn_t, middle_rows, stats = call_kernel(
        functools.partial(forward_kernel, tok),
        [
            shape_of((HD, rows), jnp.bfloat16),
            shape_of((ranks, low_rank, tok), jnp.bfloat16),
            shape_of((8, rows), jnp.float32),
        ],
        [],
        4 * pair_count * HD,
        pair_count,
        scalars,
        own,
        other,
        down_head.T,
        limit=16,
    )

    first_copy = rank % copies == 0
    if copies > 1:
        middle_rows = jnp.where(first_copy, middle_rows, 0.0)
    (message,) = in_vmem(
        functools.partial(dout_kernel, copies, tok),
        [shape_of((ranks, tok + 2 * low_rank, HD), jnp.bfloat16)],
        packed_own,
        received,
        middle_rows,
    )
    arrived = exchange(message)
    middle = jnp.sum(arrived[:, tok + low_rank :].astype(jnp.float32), axis=0)
    bit = 1
    while bit < heads:
        middle += lax.ppermute(middle, "head", [(i, i ^ bit) for i in range(heads)])
        bit *= 2
    up_part = 2.0 * dot_nn(middle.astype(jnp.bfloat16), output_gradient)

    dq, dk_own, dv_own, pair_other, down_part = call_kernel(
        functools.partial(backward_kernel, tok),
        [
            shape_of((ranks, tok, HD), jnp.bfloat16),
            shape_of((ranks, tok, HD), jnp.float32),
            shape_of((ranks, tok, HD), jnp.float32),
            shape_of((ranks, 2 * tok, HD), jnp.bfloat16),
            shape_of((low_rank, HD), jnp.float32),
        ],
        [pltpu.VMEM((rows, HD), jnp.float32)] * 4,
        10 * pair_count * HD,
        pair_count,
        scalars,
        own,
        other,
        arrived,
        attn_t,
        stats,
        limit=28,
    )
    pair_received = swap(pair_other).astype(jnp.float32)
    down_rows = jnp.where(first_copy, down_part + swap(down_part), 0.0)
    dk = (dk_own + pair_received[:, :tok]).astype(jnp.bfloat16)
    dv = (dv_own + pair_received[:, tok:]).astype(jnp.bfloat16)
    down_rows = jnp.broadcast_to(down_rows.astype(jnp.bfloat16), (ranks, low_rank, HD))
    back_message = jnp.concatenate([dq, dk, dv, down_rows], axis=1)
    back = exchange(back_message)
    outs = [shape_of((tok, feats), back.dtype)] * 3
    if seqs == ranks:
        outs.append(shape_of((low_rank, feats), jnp.float32))
    outs = list(in_vmem(functools.partial(unpack_kernel, copies), outs, back))
    if seqs > ranks:
        bits = [bit for bit in powers_below(seqs) if bit >= ranks]
        down_terms = back[::copies, 3 * tok :].astype(jnp.float32)
        down_terms = butterfly_sum(down_terms, "seq", bits, seqs)
        outs.append(down_terms.transpose(1, 0, 2).reshape(low_rank, feats))
    query_gradient, key_gradient, value_gradient, down_gradient = outs

    up_sum = butterfly_sum(up_part, "seq", powers_below(seqs), seqs)
    _, up_sum = lax.optimization_barrier((back, up_sum))
    up_gradient = butterfly_sum(up_sum, "sub", powers_below(subs), subs)
    return (query_gradient, key_gradient, value_gradient, down_gradient.T, up_gradient)


def solution(mesh):
    rows = P(("rep", "seq", "sub"), "head")
    sizes = (mesh.shape["seq"], mesh.shape["head"], mesh.shape["sub"])
    return jax.shard_map(
        functools.partial(on_device, sizes),
        mesh=mesh,
        in_specs=(rows, rows, rows, rows, P("head", "sub"), P("head", None), P()),
        out_specs=(rows, rows, rows, P(("rep", "head"), None), P("rep", "head")),
        check_vma=False,
    )
```

```python
import functools
import math

import jax
import jax.numpy as jnp
from jax import lax
from jax.experimental import pallas as pl
from jax.experimental.pallas import tpu as pltpu
from jax.sharding import PartitionSpec as P

HD = 128
GROUP = 2048
TILE = 256
HIDDEN = -1e30
SCALE = HD ** (-0.5)
LOG2_SCALE = SCALE * math.log2(math.e)


def dot_nt(left, right):
    return lax.dot_general(
        left, right, (((1,), (1,)), ((), ())), preferred_element_type=jnp.float32
    )


def dot_nn(left, right):
    return jnp.dot(left, right, preferred_element_type=jnp.float32)


def rows_of(ref, blocks, slot_of, first, count):
    parts = [ref[slot_of(block), first : first + count, :] for block in blocks]
    return jnp.concatenate(parts, axis=0)


def slots(scalar_ref, blocks):
    return lambda block: (block + scalar_ref[1]) % blocks


def scores_of(sub, keys_own, keys_other, queries, tok):
    def tail_hidden(scores, visible):
        head = scores.shape[0] - TILE
        tail = jnp.where(visible, scores[head:], HIDDEN)
        return tail if head == 0 else jnp.concatenate((scores[:head], tail), axis=0)

    key_at = lax.broadcasted_iota(jnp.int32, (TILE, TILE), 0)
    query_at = lax.broadcasted_iota(jnp.int32, (TILE, TILE), 1)
    own = tail_hidden(dot_nt(keys_own, queries), key_at <= query_at)
    other = tail_hidden(
        dot_nt(keys_other, queries), key_at // tok < query_at // tok + sub
    )
    return own, other


def forward_kernel(
    tok, scalar_ref, own_ref, other_ref, down_t_ref, attn_ref, mid_ref, stat_ref
):
    blocks = own_ref.shape[0]
    step = TILE // tok
    sub = scalar_ref[0]
    slot_of = slots(scalar_ref, blocks)
    values_own_t = rows_of(own_ref, range(blocks), slot_of, 2 * tok, tok).T
    values_other_t = rows_of(other_ref, range(blocks), slot_of, tok, tok).T
    for tile in range(blocks // step):
        here = range(tile * step, (tile + 1) * step)
        width = (tile + 1) * TILE
        at = tile * TILE
        upto = range((tile + 1) * step)
        queries = rows_of(own_ref, here, slot_of, 0, tok)
        keys_own = rows_of(own_ref, upto, slot_of, tok, tok)
        keys_other = rows_of(other_ref, upto, slot_of, 0, tok)
        own, other = scores_of(sub, keys_own, keys_other, queries, tok)
        highest = jnp.maximum(
            jnp.max(own, axis=0, keepdims=True), jnp.max(other, axis=0, keepdims=True)
        )
        own = jnp.exp2((own - highest) * LOG2_SCALE)
        other = jnp.exp2((other - highest) * LOG2_SCALE)
        inverse = 1.0 / (
            jnp.sum(own, axis=0, keepdims=True) + jnp.sum(other, axis=0, keepdims=True)
        )
        attn = dot_nn(values_own_t[:, :width], own.astype(jnp.bfloat16)) + dot_nn(
            values_other_t[:, :width], other.astype(jnp.bfloat16)
        )
        attn = (attn * inverse).astype(jnp.bfloat16)
        attn_ref[:, at : at + TILE] = attn
        mid = dot_nn(down_t_ref[...], attn)
        for i, block in enumerate(here):
            mid_ref[slot_of(block)] = mid[:, i * tok : (i + 1) * tok].astype(jnp.bfloat16)
        stat_ref[0:1, at : at + TILE] = highest
        stat_ref[1:2, at : at + TILE] = inverse


def backward_kernel(
    tok,
    scalar_ref,
    own_ref,
    other_ref,
    dout_ref,
    attn_ref,
    stat_ref,
    dq_ref,
    dk_own_ref,
    dv_own_ref,
    pair_other_ref,
    down_grad_ref,
    dk_own,
    dv_own,
    dk_other,
    dv_other,
):
    blocks = own_ref.shape[0]
    step = TILE // tok
    sub = scalar_ref[0]
    low_rank = down_grad_ref.shape[0]
    slot_of = slots(scalar_ref, blocks)
    keys_own_t = rows_of(own_ref, range(blocks), slot_of, tok, tok).T
    keys_other_t = rows_of(other_ref, range(blocks), slot_of, 0, tok).T
    tiles = blocks // step
    down_total = jnp.zeros((low_rank, HD), jnp.float32)
    for tile in reversed(range(tiles)):
        here = range(tile * step, (tile + 1) * step)
        width = (tile + 1) * TILE
        at = tile * TILE
        queries = rows_of(own_ref, here, slot_of, 0, tok)
        douts = rows_of(dout_ref, here, slot_of, 0, tok)
        highest = stat_ref[0:1, at : at + TILE]
        inverse = stat_ref[1:2, at : at + TILE]
        upto = range((tile + 1) * step)
        keys_own = rows_of(own_ref, upto, slot_of, tok, tok)
        keys_other = rows_of(other_ref, upto, slot_of, 0, tok)
        own, other = scores_of(sub, keys_own, keys_other, queries, tok)
        own = jnp.exp2((own - highest) * LOG2_SCALE) * inverse
        other = jnp.exp2((other - highest) * LOG2_SCALE) * inverse
        dprob_own = dot_nt(rows_of(own_ref, upto, slot_of, 2 * tok, tok), douts)
        dprob_other = dot_nt(rows_of(other_ref, upto, slot_of, tok, tok), douts)
        delta = jnp.sum(own * dprob_own, axis=0, keepdims=True) + jnp.sum(
            other * dprob_other, axis=0, keepdims=True
        )
        ds_own = (own * (dprob_own - delta)).astype(jnp.bfloat16)
        ds_other = (other * (dprob_other - delta)).astype(jnp.bfloat16)
        dq = dot_nn(keys_own_t[:, :width], ds_own) + dot_nn(keys_other_t[:, :width], ds_other)
        dq = (dq * SCALE).T.astype(jnp.bfloat16)
        terms = (
            (dk_own, dot_nn(ds_own, queries)),
            (dk_other, dot_nn(ds_other, queries)),
            (dv_own, dot_nn(own.astype(jnp.bfloat16), douts)),
            (dv_other, dot_nn(other.astype(jnp.bfloat16), douts)),
        )
        for total, term in terms:
            if tile == tiles - 1:
                total[...] = term
            else:
                total[0:width] += term
        for i, block in enumerate(here):
            slot = slot_of(block)
            dq_ref[slot] = dq[i * tok : (i + 1) * tok]
            lora = dout_ref[slot, tok : tok + low_rank, :]
            attn = attn_ref[:, at + i * tok : at + (i + 1) * tok]
            down_total += dot_nt(lora, attn)
    for block in range(blocks):
        rows = pl.ds(block * tok, tok)
        slot = slot_of(block)
        dk_own_ref[slot] = dk_own[rows, :] * SCALE
        dv_own_ref[slot] = dv_own[rows, :]
        pair_other_ref[slot, 0:tok, :] = (dk_other[rows, :] * SCALE).astype(jnp.bfloat16)
        pair_other_ref[slot, tok : 2 * tok, :] = dv_other[rows, :].astype(jnp.bfloat16)
    down_grad_ref[...] = 2.0 * down_total


def call_kernel(body, outs, scratch, flops, exps, *operands, declared=None, limit=48, in_hbm=()):
    in_bytes = sum(x.size * x.dtype.itemsize for x in operands)
    out_bytes = sum(x.size * x.dtype.itemsize for x in outs)
    specs = [pl.BlockSpec(memory_space=pltpu.SMEM)]
    for n in range(len(operands) - 1):
        space = pltpu.HBM if n in in_hbm else pltpu.VMEM
        specs.append(pl.BlockSpec(memory_space=space))
    return pl.pallas_call(
        body,
        out_shape=outs,
        in_specs=specs,
        out_specs=[pl.BlockSpec(memory_space=pltpu.VMEM)] * len(outs),
        scratch_shapes=scratch,
        compiler_params=pltpu.CompilerParams(vmem_limit_bytes=limit * 1024 * 1024),
        cost_estimate=pl.CostEstimate(
            flops=flops,
            bytes_accessed=declared or in_bytes + out_bytes,
            transcendentals=exps,
        ),
    )(*operands)


def shape_of(shape, dtype):
    return jax.ShapeDtypeStruct(shape, dtype)


def butterfly_sum(value, axis, bits, count):
    for bit in bits:
        pairs = [(i, i ^ bit) for i in range(count)]
        value = value.astype(jnp.bfloat16)
        taken = lax.ppermute(value, axis, pairs)
        value = value.astype(jnp.float32) + taken.astype(jnp.float32)
    return value


def powers_below(count):
    return [1 << n for n in range(count.bit_length() - 1)]


def message_kernel(copies, *refs):
    count = (len(refs) - 3) // 2
    operands, message_ref = refs[:count], refs[count]
    held, in_sems, out_sems = refs[count + 1 : -2], refs[-2], refs[-1]
    tok = operands[0].shape[0]
    arriving = [
        pltpu.make_async_copy(ref, to, in_sems.at[n])
        for n, (ref, to) in enumerate(zip(operands, held))
    ]
    for copy in arriving:
        copy.start()
    leaving = []
    for n, (copy, ref) in enumerate(zip(arriving, held)):
        copy.wait()
        for rank in range(message_ref.shape[0]):
            cols = pl.ds((rank // copies) * HD, HD)
            to = message_ref.at[rank, pl.ds(n * tok, tok), :]
            leaving.append(pltpu.make_async_copy(ref.at[:, cols], to, out_sems.at[len(leaving)]))
            leaving[-1].start()
    for copy in leaving:
        copy.wait()


def message_of(copies, ranks, *operands):
    tok = operands[0].shape[0]
    count = len(operands)
    shape = (ranks, count * tok, HD)
    return pl.pallas_call(
        functools.partial(message_kernel, copies),
        out_shape=shape_of(shape, operands[0].dtype),
        in_specs=[pl.BlockSpec(memory_space=pltpu.HBM)] * count,
        out_specs=pl.BlockSpec(memory_space=pltpu.HBM),
        scratch_shapes=[pltpu.VMEM(x.shape, x.dtype) for x in operands]
        + [pltpu.SemaphoreType.DMA((count,)), pltpu.SemaphoreType.DMA((ranks * count,))],
        compiler_params=pltpu.CompilerParams(vmem_limit_bytes=4 * 1024 * 1024),
        cost_estimate=pl.CostEstimate(
            flops=0, bytes_accessed=4 * math.prod(shape), transcendentals=0
        ),
    )(*operands)


def unpack_kernel(copies, back_ref, *refs):
    out_refs, down_ref = refs[:3], refs[3] if len(refs) > 3 else None
    tok = out_refs[0].shape[0]
    for at_head in range(out_refs[0].shape[1] // HD):
        cols = slice(at_head * HD, (at_head + 1) * HD)
        for n, ref in enumerate(out_refs):
            ref[:, cols] = back_ref[at_head * copies, n * tok : (n + 1) * tok, :]
        if down_ref is not None:
            down_ref[:, cols] = back_ref[at_head * copies, 3 * tok :, :].astype(jnp.float32)


def in_vmem(body, outs, *operands):
    whole = pl.BlockSpec(memory_space=pltpu.VMEM)
    size = sum(x.size * x.dtype.itemsize for x in operands)
    size += sum(x.size * x.dtype.itemsize for x in outs)
    return pl.pallas_call(
        body,
        out_shape=outs,
        in_specs=[whole] * len(operands),
        out_specs=[whole] * len(outs),
        compiler_params=pltpu.CompilerParams(vmem_limit_bytes=16 * 1024 * 1024),
        cost_estimate=pl.CostEstimate(flops=0, bytes_accessed=size, transcendentals=0),
    )(*operands)


def cotangent_kernel(chunks, plan_ref, *refs):
    pieces, (matrix_hbm, up_ref, down_ref, own_ref, sent_ref, matrix_ref, sems) = refs[:-7], refs[-7:]
    tok, cols = pieces[0].shape
    feats, low_rank = down_ref.shape
    arriving = [
        pltpu.make_async_copy(
            matrix_hbm.at[pl.ds(first, TILE), :],
            matrix_ref.at[pl.ds(first, TILE), :],
            sems.at[first // TILE],
        )
        for first in range(0, feats, TILE)
    ]
    for copy in arriving:
        copy.start()
    count = len(pieces)
    if chunks == 1:
        stacks = [(jnp.concatenate([p[...] for p in pieces], axis=0), pl.ds(0, cols))]
    else:
        stacks = [
            (p[...], pl.ds(pl.multiple_of(plan_ref[count + k], HD), cols))
            for k, p in enumerate(pieces)
        ]
    mine = [plan_ref[k] == 1 for k in range(count)]

    def split(terms):
        parts = [t[i : i + tok] for t in terms for i in range(0, t.shape[0], tok)]
        own = [jnp.where(m, p, 0.0) for m, p in zip(mine, parts)]
        sent = [jnp.where(m, 0.0, p) for m, p in zip(mine, parts)]
        return functools.reduce(jnp.add, own), functools.reduce(jnp.add, sent)

    loras = [dot_nt(rows, up_ref[:, at]) for rows, at in stacks]
    spare = jnp.zeros((tok, HD - low_rank), jnp.float32)
    own, sent = split(loras)
    own_ref[:, feats:] = jnp.concatenate((own, spare), axis=1)
    sent_ref[:, feats:] = jnp.concatenate((sent, spare), axis=1).astype(jnp.bfloat16)
    for first in range(0, feats, TILE):
        here = pl.ds(first, TILE)
        arriving[first // TILE].wait()
        terms = [
            dot_nt(rows, matrix_ref[here, at])
            + 2.0 * dot_nt(lora.astype(jnp.bfloat16), down_ref[here, :])
            for (rows, at), lora in zip(stacks, loras)
        ]
        own, sent = split(terms)
        own_ref[:, here] = own
        sent_ref[:, here] = sent.astype(jnp.bfloat16)


def dout_kernel(copies, tok, own_ref, taken_ref, mid_ref, message_ref):
    feats = own_ref.shape[1] - HD
    low_rank = mid_ref.shape[1]
    lora = (own_ref[:, feats:] + taken_ref[:, feats:].astype(jnp.float32)).T
    lora = lora[0:low_rank].astype(jnp.bfloat16)
    for rank in range(message_ref.shape[0]):
        at = (rank // copies) * HD
        part = own_ref[:, at : at + HD] + taken_ref[:, at : at + HD].astype(jnp.float32)
        message_ref[rank, 0:tok, :] = part.astype(jnp.bfloat16)
        message_ref[rank, tok : tok + low_rank, :] = lora
        message_ref[rank, tok + low_rank : tok + 2 * low_rank, :] = mid_ref[rank]


def on_device(
    sizes,
    head_query_rows,
    head_key_rows,
    head_value_rows,
    output_gradient,
    output_matrix,
    adapter_down_weight,
    adapter_up_weight,
):
    seqs, heads, subs = sizes
    tok, feats = head_query_rows.shape
    cols = output_gradient.shape[1]
    low_rank = adapter_up_weight.shape[0]
    local_heads = feats // HD
    block_rows = tok * subs
    ranks = GROUP // block_rows
    copies = ranks // local_heads
    shift_blocks = GROUP // 2 // block_rows

    seq = lax.axis_index("seq")
    head = lax.axis_index("head")
    sub = lax.axis_index("sub")
    shifted = head >= heads // 2
    rank = (seq + shift_blocks) % ranks
    my_head = rank // copies

    groups = []
    for at_head in range(heads):
        for first in range(0, seqs, ranks):
            members = [first + shift_blocks + i for i in range(ranks)]
            if at_head < heads // 2:
                members = [first + (m - first) % ranks for m in members]
            members = [m % seqs for m in members]
            groups.append([m * heads + at_head for m in members])
    turned = jnp.where(shifted, 0, shift_blocks)
    scalars = jnp.stack((sub, turned)).astype(jnp.int32)

    def exchange(parts):
        return lax.all_to_all(
            parts, ("seq", "head"), 0, 0, axis_index_groups=groups, tiled=True
        )

    def swap(value):
        if subs == 1:
            return value
        return lax.ppermute(value, "sub", [(0, 1), (1, 0)])

    sent = message_of(copies, ranks, head_query_rows, head_key_rows, head_value_rows)
    sent, output_gradient = lax.optimization_barrier((sent, output_gradient))
    own = exchange(sent)

    chunks = heads // subs
    pieces = []
    for k in range(heads):
        pairs = []
        for src_head in range(heads):
            for src_sub in range(subs):
                j = (src_head % chunks) * subs + src_sub
                dst = ((j + k) % heads) * subs + src_head // chunks
                pairs.append((src_head * subs + src_sub, dst))
        pieces.append(lax.ppermute(output_gradient, ("head", "sub"), pairs))

    up_half = lax.dynamic_slice_in_dim(adapter_up_weight, sub * chunks * cols, chunks * cols, 1)
    sources = [(head - k + heads) % heads for k in range(heads)]
    plan = [(j % subs == sub).astype(jnp.int32) for j in sources]
    plan += [(j // subs * cols).astype(jnp.int32) for j in sources]
    packed_own, packed_sent = call_kernel(
        functools.partial(cotangent_kernel, chunks),
        [
            shape_of((tok, feats + HD), jnp.float32),
            shape_of((tok, feats + HD), jnp.bfloat16),
        ],
        [
            pltpu.VMEM(output_matrix.shape, output_matrix.dtype),
            pltpu.SemaphoreType.DMA((feats // TILE,)),
        ],
        0,
        0,
        jnp.stack(plan),
        *pieces,
        output_matrix,
        up_half,
        adapter_down_weight,
        declared=1024,
        limit=57,
        in_hbm=(heads,),
    )
    received = swap(packed_sent)
    own, _ = lax.optimization_barrier((own, packed_sent))
    other = swap(own[:, tok:])

    down_head = lax.dynamic_slice_in_dim(adapter_down_weight, my_head * HD, HD, 0)
    rows = ranks * tok
    pair_count = rows * (rows + TILE)
    attn_t, middle_rows, stats = call_kernel(
        functools.partial(forward_kernel, tok),
        [
            shape_of((HD, rows), jnp.bfloat16),
            shape_of((ranks, low_rank, tok), jnp.bfloat16),
            shape_of((8, rows), jnp.float32),
        ],
        [],
        4 * pair_count * HD,
        pair_count,
        scalars,
        own,
        other,
        down_head.T,
        limit=16,
    )

    first_copy = rank % copies == 0
    if copies > 1:
        middle_rows = jnp.where(first_copy, middle_rows, 0.0)
    (message,) = in_vmem(
        functools.partial(dout_kernel, copies, tok),
        [shape_of((ranks, tok + 2 * low_rank, HD), jnp.bfloat16)],
        packed_own,
        received,
        middle_rows,
    )
    arrived = exchange(message)
    middle = jnp.sum(arrived[:, tok + low_rank :].astype(jnp.float32), axis=0)
    bit = 1
    while bit < heads:
        middle += lax.ppermute(middle, "head", [(i, i ^ bit) for i in range(heads)])
        bit *= 2
    up_part = 2.0 * dot_nn(middle.astype(jnp.bfloat16), output_gradient)

    dq, dk_own, dv_own, pair_other, down_part = call_kernel(
        functools.partial(backward_kernel, tok),
        [
            shape_of((ranks, tok, HD), jnp.bfloat16),
            shape_of((ranks, tok, HD), jnp.float32),
            shape_of((ranks, tok, HD), jnp.float32),
            shape_of((ranks, 2 * tok, HD), jnp.bfloat16),
            shape_of((low_rank, HD), jnp.float32),
        ],
        [pltpu.VMEM((rows, HD), jnp.float32)] * 4,
        10 * pair_count * HD,
        pair_count,
        scalars,
        own,
        other,
        arrived,
        attn_t,
        stats,
        limit=28,
    )
    pair_received = swap(pair_other).astype(jnp.float32)
    down_rows = jnp.where(first_copy, down_part + swap(down_part), 0.0)
    dk = (dk_own + pair_received[:, :tok]).astype(jnp.bfloat16)
    dv = (dv_own + pair_received[:, tok:]).astype(jnp.bfloat16)
    down_rows = jnp.broadcast_to(down_rows.astype(jnp.bfloat16), (ranks, low_rank, HD))
    back_message = jnp.concatenate([dq, dk, dv, down_rows], axis=1)
    back = exchange(back_message)
    outs = [shape_of((tok, feats), back.dtype)] * 3
    if seqs == ranks:
        outs.append(shape_of((low_rank, feats), jnp.float32))
    outs = list(in_vmem(functools.partial(unpack_kernel, copies), outs, back))
    if seqs > ranks:
        bits = [bit for bit in powers_below(seqs) if bit >= ranks]
        down_terms = back[::copies, 3 * tok :].astype(jnp.float32)
        down_terms = butterfly_sum(down_terms, "seq", bits, seqs)
        outs.append(down_terms.transpose(1, 0, 2).reshape(low_rank, feats))
    query_gradient, key_gradient, value_gradient, down_gradient = outs

    up_sum = butterfly_sum(up_part, "seq", powers_below(seqs), seqs)
    _, up_sum = lax.optimization_barrier((back, up_sum))
    up_gradient = butterfly_sum(up_sum, "sub", powers_below(subs), subs)
    return (query_gradient, key_gradient, value_gradient, down_gradient.T, up_gradient)


def solution(mesh):
    rows = P(("rep", "seq", "sub"), "head")
    sizes = (mesh.shape["seq"], mesh.shape["head"], mesh.shape["sub"])
    return jax.shard_map(
        functools.partial(on_device, sizes),
        mesh=mesh,
        in_specs=(rows, rows, rows, rows, P("head", "sub"), P("head", None), P()),
        out_specs=(rows, rows, rows, P(("rep", "head"), None), P("rep", "head")),
        check_vma=False,
    )
```

```python
import functools
import math

import jax
import jax.numpy as jnp
from jax import lax
from jax.experimental import pallas as pl
from jax.experimental.pallas import tpu as pltpu
from jax.sharding import PartitionSpec as P

HD = 128
GROUP = 2048
TILE = 256
HIDDEN = -1e30
SCALE = HD ** (-0.5)
LOG2_SCALE = SCALE * math.log2(math.e)


def dot_nt(left, right):
    return lax.dot_general(
        left, right, (((1,), (1,)), ((), ())), preferred_element_type=jnp.float32
    )


def dot_nn(left, right):
    return jnp.dot(left, right, preferred_element_type=jnp.float32)


def rows_of(ref, blocks, slot_of, first, count):
    parts = [ref[slot_of(block), first : first + count, :] for block in blocks]
    return jnp.concatenate(parts, axis=0)


def in_either_order(body, scalar_ref, blocks):
    for turn in (0, blocks // 2):
        pl.when(scalar_ref[1] == turn)(
            functools.partial(body, lambda block, turn=turn: (block + turn) % blocks)
        )


def scores_of(sub, keys_own, keys_other, queries, tok):
    def tail_hidden(scores, visible):
        head = scores.shape[0] - TILE
        tail = jnp.where(visible, scores[head:], HIDDEN)
        return tail if head == 0 else jnp.concatenate((scores[:head], tail), axis=0)

    key_at = lax.broadcasted_iota(jnp.int32, (TILE, TILE), 0)
    query_at = lax.broadcasted_iota(jnp.int32, (TILE, TILE), 1)
    own = tail_hidden(dot_nt(keys_own, queries), key_at <= query_at)
    other = tail_hidden(
        dot_nt(keys_other, queries), key_at // tok < query_at // tok + sub
    )
    return own, other


def forward_kernel(tok, scalar_ref, own_ref, *refs):
    body = functools.partial(forward_body, tok, scalar_ref, own_ref, *refs)
    in_either_order(body, scalar_ref, own_ref.shape[0])


def forward_body(
    tok, scalar_ref, own_ref, other_ref, down_t_ref, attn_ref, mid_ref, stat_ref, slot_of
):
    blocks = own_ref.shape[0]
    step = TILE // tok
    sub = scalar_ref[0]
    values_own_t = rows_of(own_ref, range(blocks), slot_of, 2 * tok, tok).T
    values_other_t = rows_of(other_ref, range(blocks), slot_of, tok, tok).T
    for tile in range(blocks // step):
        here = range(tile * step, (tile + 1) * step)
        width = (tile + 1) * TILE
        at = tile * TILE
        upto = range((tile + 1) * step)
        queries = rows_of(own_ref, here, slot_of, 0, tok)
        keys_own = rows_of(own_ref, upto, slot_of, tok, tok)
        keys_other = rows_of(other_ref, upto, slot_of, 0, tok)
        own, other = scores_of(sub, keys_own, keys_other, queries, tok)
        highest = jnp.maximum(
            jnp.max(own, axis=0, keepdims=True), jnp.max(other, axis=0, keepdims=True)
        )
        own = jnp.exp2((own - highest) * LOG2_SCALE)
        other = jnp.exp2((other - highest) * LOG2_SCALE)
        inverse = 1.0 / (
            jnp.sum(own, axis=0, keepdims=True) + jnp.sum(other, axis=0, keepdims=True)
        )
        attn = dot_nn(values_own_t[:, :width], own.astype(jnp.bfloat16)) + dot_nn(
            values_other_t[:, :width], other.astype(jnp.bfloat16)
        )
        attn = (attn * inverse).astype(jnp.bfloat16)
        attn_ref[:, at : at + TILE] = attn
        mid = dot_nn(down_t_ref[...], attn)
        for i, block in enumerate(here):
            mid_ref[slot_of(block)] = mid[:, i * tok : (i + 1) * tok].astype(jnp.bfloat16)
        stat_ref[0:1, at : at + TILE] = highest
        stat_ref[1:2, at : at + TILE] = inverse


def backward_kernel(tok, scalar_ref, own_ref, *refs):
    body = functools.partial(backward_body, tok, scalar_ref, own_ref, *refs)
    in_either_order(body, scalar_ref, own_ref.shape[0])


def backward_body(
    tok,
    scalar_ref,
    own_ref,
    other_ref,
    dout_ref,
    attn_ref,
    stat_ref,
    dq_ref,
    dk_own_ref,
    dv_own_ref,
    pair_other_ref,
    down_grad_ref,
    dk_own,
    dv_own,
    dk_other,
    dv_other,
    slot_of,
):
    blocks = own_ref.shape[0]
    step = TILE // tok
    sub = scalar_ref[0]
    low_rank = down_grad_ref.shape[0]
    keys_own_t = rows_of(own_ref, range(blocks), slot_of, tok, tok).T
    keys_other_t = rows_of(other_ref, range(blocks), slot_of, 0, tok).T
    tiles = blocks // step
    down_total = jnp.zeros((low_rank, HD), jnp.float32)
    for tile in reversed(range(tiles)):
        here = range(tile * step, (tile + 1) * step)
        width = (tile + 1) * TILE
        at = tile * TILE
        queries = rows_of(own_ref, here, slot_of, 0, tok)
        douts_t = jnp.concatenate([dout_ref[slot_of(b), 0:HD, :] for b in here], axis=1)
        highest = stat_ref[0:1, at : at + TILE]
        inverse = stat_ref[1:2, at : at + TILE]
        upto = range((tile + 1) * step)
        keys_own = rows_of(own_ref, upto, slot_of, tok, tok)
        keys_other = rows_of(other_ref, upto, slot_of, 0, tok)
        own, other = scores_of(sub, keys_own, keys_other, queries, tok)
        own = jnp.exp2((own - highest) * LOG2_SCALE) * inverse
        other = jnp.exp2((other - highest) * LOG2_SCALE) * inverse
        dprob_own = dot_nn(rows_of(own_ref, upto, slot_of, 2 * tok, tok), douts_t)
        dprob_other = dot_nn(rows_of(other_ref, upto, slot_of, tok, tok), douts_t)
        delta = jnp.sum(own * dprob_own, axis=0, keepdims=True) + jnp.sum(
            other * dprob_other, axis=0, keepdims=True
        )
        ds_own = (own * (dprob_own - delta)).astype(jnp.bfloat16)
        ds_other = (other * (dprob_other - delta)).astype(jnp.bfloat16)
        dq = dot_nn(keys_own_t[:, :width], ds_own) + dot_nn(keys_other_t[:, :width], ds_other)
        dq = (dq * SCALE).T.astype(jnp.bfloat16)
        terms = (
            (dk_own, dot_nn(ds_own, queries)),
            (dk_other, dot_nn(ds_other, queries)),
            (dv_own, dot_nt(own.astype(jnp.bfloat16), douts_t)),
            (dv_other, dot_nt(other.astype(jnp.bfloat16), douts_t)),
        )
        for total, term in terms:
            if tile == tiles - 1:
                total[...] = term
            else:
                total[0:width] += term
        for i, block in enumerate(here):
            slot = slot_of(block)
            dq_ref[slot] = dq[i * tok : (i + 1) * tok]
            lora = dout_ref[slot, HD : HD + low_rank, :]
            attn = attn_ref[:, at + i * tok : at + (i + 1) * tok]
            down_total += dot_nt(lora, attn)
    for block in range(blocks):
        rows = pl.ds(block * tok, tok)
        slot = slot_of(block)
        dk_own_ref[slot] = dk_own[rows, :] * SCALE
        dv_own_ref[slot] = dv_own[rows, :]
        pair_other_ref[slot, 0:tok, :] = (dk_other[rows, :] * SCALE).astype(jnp.bfloat16)
        pair_other_ref[slot, tok : 2 * tok, :] = dv_other[rows, :].astype(jnp.bfloat16)
    down_grad_ref[...] = 2.0 * down_total


def call_kernel(body, outs, scratch, flops, exps, *operands, declared=None, limit=48):
    in_bytes = sum(x.size * x.dtype.itemsize for x in operands)
    out_bytes = sum(x.size * x.dtype.itemsize for x in outs)
    specs = [pl.BlockSpec(memory_space=pltpu.SMEM)]
    specs += [pl.BlockSpec(memory_space=pltpu.VMEM)] * (len(operands) - 1)
    return pl.pallas_call(
        body,
        out_shape=outs,
        in_specs=specs,
        out_specs=[pl.BlockSpec(memory_space=pltpu.VMEM)] * len(outs),
        scratch_shapes=scratch,
        compiler_params=pltpu.CompilerParams(vmem_limit_bytes=limit * 1024 * 1024),
        cost_estimate=pl.CostEstimate(
            flops=flops,
            bytes_accessed=declared or in_bytes + out_bytes,
            transcendentals=exps,
        ),
    )(*operands)


def shape_of(shape, dtype):
    return jax.ShapeDtypeStruct(shape, dtype)


def butterfly_sum(value, axis, bits, count):
    for bit in bits:
        pairs = [(i, i ^ bit) for i in range(count)]
        value = value.astype(jnp.bfloat16)
        taken = lax.ppermute(value, axis, pairs)
        value = value.astype(jnp.float32) + taken.astype(jnp.float32)
    return value


def powers_below(count):
    return [1 << n for n in range(count.bit_length() - 1)]


def message_kernel(copies, *refs):
    count = (len(refs) - 3) // 2
    operands, message_ref = refs[:count], refs[count]
    held, in_sems, out_sems = refs[count + 1 : -2], refs[-2], refs[-1]
    tok = operands[0].shape[0]
    arriving = [
        pltpu.make_async_copy(ref, to, in_sems.at[n])
        for n, (ref, to) in enumerate(zip(operands, held))
    ]
    for copy in arriving:
        copy.start()
    leaving = []
    for n, (copy, ref) in enumerate(zip(arriving, held)):
        copy.wait()
        for rank in range(message_ref.shape[0]):
            cols = pl.ds((rank // copies) * HD, HD)
            to = message_ref.at[rank, pl.ds(n * tok, tok), :]
            leaving.append(pltpu.make_async_copy(ref.at[:, cols], to, out_sems.at[len(leaving)]))
            leaving[-1].start()
    for copy in leaving:
        copy.wait()


def message_of(copies, ranks, *operands):
    tok = operands[0].shape[0]
    count = len(operands)
    shape = (ranks, count * tok, HD)
    return pl.pallas_call(
        functools.partial(message_kernel, copies),
        out_shape=shape_of(shape, operands[0].dtype),
        in_specs=[pl.BlockSpec(memory_space=pltpu.HBM)] * count,
        out_specs=pl.BlockSpec(memory_space=pltpu.HBM),
        scratch_shapes=[pltpu.VMEM(x.shape, x.dtype) for x in operands]
        + [pltpu.SemaphoreType.DMA((count,)), pltpu.SemaphoreType.DMA((ranks * count,))],
        cost_estimate=pl.CostEstimate(
            flops=0, bytes_accessed=4 * math.prod(shape), transcendentals=0
        ),
    )(*operands)


def unpack_kernel(copies, back_ref, *refs):
    out_refs, down_ref = refs[:3], refs[3] if len(refs) > 3 else None
    tok = out_refs[0].shape[0]
    for at_head in range(out_refs[0].shape[1] // HD):
        cols = slice(at_head * HD, (at_head + 1) * HD)
        for n, ref in enumerate(out_refs):
            ref[:, cols] = back_ref[at_head * copies, n * tok : (n + 1) * tok, :]
        if down_ref is not None:
            down_ref[:, cols] = back_ref[at_head * copies, 3 * tok :, :].astype(jnp.float32)


def in_vmem(body, outs, *operands):
    whole = pl.BlockSpec(memory_space=pltpu.VMEM)
    size = sum(x.size * x.dtype.itemsize for x in operands)
    size += sum(x.size * x.dtype.itemsize for x in outs)
    return pl.pallas_call(
        body,
        out_shape=outs,
        in_specs=[whole] * len(operands),
        out_specs=[whole] * len(outs),
        compiler_params=pltpu.CompilerParams(vmem_limit_bytes=16 * 1024 * 1024),
        cost_estimate=pl.CostEstimate(flops=0, bytes_accessed=size, transcendentals=0),
    )(*operands)


def staged_kernel(from_ref, to_ref, sems):
    count = sems.shape[0]
    size = from_ref.shape[0] // count
    copies = [
        pltpu.make_async_copy(
            from_ref.at[pl.ds(n * size, size), :], to_ref.at[pl.ds(n * size, size), :], sems.at[n]
        )
        for n in range(count)
    ]
    for copy in copies:
        copy.start()
    for copy in copies:
        copy.wait()


def staged(value, limit):
    return pl.pallas_call(
        staged_kernel,
        out_shape=shape_of(value.shape, value.dtype),
        in_specs=[pl.BlockSpec(memory_space=pltpu.HBM)],
        out_specs=pl.BlockSpec(memory_space=pltpu.VMEM),
        scratch_shapes=[pltpu.SemaphoreType.DMA((4,))],
        compiler_params=pltpu.CompilerParams(vmem_limit_bytes=limit * 1024 * 1024),
        cost_estimate=pl.CostEstimate(
            flops=0, bytes_accessed=2 * value.size * value.dtype.itemsize, transcendentals=0
        ),
    )(value)


def cotangent_kernel(chunks, plan_ref, *refs):
    pieces, (matrix_ref, up_ref, down_ref, own_ref, sent_ref) = refs[:-5], refs[-5:]
    tok, cols = pieces[0].shape
    feats, low_rank = down_ref.shape
    count = len(pieces)
    if chunks == 1:
        stacks = [(jnp.concatenate([p[...] for p in pieces], axis=0), pl.ds(0, cols))]
    else:
        stacks = [
            (p[...], pl.ds(pl.multiple_of(plan_ref[count + k], HD), cols))
            for k, p in enumerate(pieces)
        ]
    mine = [plan_ref[k] == 1 for k in range(count)]

    def store(here, terms):
        parts = [t[:, i : i + tok] for t in terms for i in range(0, t.shape[1], tok)]
        own = [jnp.where(m, p, 0.0) for m, p in zip(mine, parts)]
        sent = [jnp.where(m, 0.0, p) for m, p in zip(mine, parts)]
        own_ref[here, :] = functools.reduce(jnp.add, own)
        sent_ref[here, :] = functools.reduce(jnp.add, sent).astype(jnp.bfloat16)

    loras = [dot_nt(up_ref[:, at], rows) for rows, at in stacks]
    store(pl.ds(feats, low_rank), loras)
    for first in range(0, feats, TILE):
        here = pl.ds(first, TILE)
        terms = [
            dot_nt(matrix_ref[here, at], rows)
            + 2.0 * dot_nn(down_ref[here, :], lora.astype(jnp.bfloat16))
            for (rows, at), lora in zip(stacks, loras)
        ]
        store(here, terms)


def dout_kernel(copies, own_ref, taken_ref, mid_ref, message_ref):
    low_rank = mid_ref.shape[1]
    feats = own_ref.shape[0] - low_rank
    lora = own_ref[feats:, :] + taken_ref[feats:, :].astype(jnp.float32)
    for rank in range(message_ref.shape[0]):
        at = pl.ds((rank // copies) * HD, HD)
        part = own_ref[at, :] + taken_ref[at, :].astype(jnp.float32)
        message_ref[rank, 0:HD, :] = part.astype(jnp.bfloat16)
        message_ref[rank, HD : HD + low_rank, :] = lora.astype(jnp.bfloat16)
        message_ref[rank, HD + low_rank : HD + 2 * low_rank, :] = mid_ref[rank]


def on_device(
    sizes,
    head_query_rows,
    head_key_rows,
    head_value_rows,
    output_gradient,
    output_matrix,
    adapter_down_weight,
    adapter_up_weight,
):
    seqs, heads, subs = sizes
    tok, feats = head_query_rows.shape
    cols = output_gradient.shape[1]
    low_rank = adapter_up_weight.shape[0]
    local_heads = feats // HD
    block_rows = tok * subs
    ranks = GROUP // block_rows
    copies = ranks // local_heads
    shift_blocks = GROUP // 2 // block_rows

    seq = lax.axis_index("seq")
    head = lax.axis_index("head")
    sub = lax.axis_index("sub")
    shifted = head >= heads // 2
    rank = (seq + shift_blocks) % ranks
    my_head = rank // copies

    groups = []
    for at_head in range(heads):
        for first in range(0, seqs, ranks):
            members = [first + shift_blocks + i for i in range(ranks)]
            if at_head < heads // 2:
                members = [first + (m - first) % ranks for m in members]
            members = [m % seqs for m in members]
            groups.append([m * heads + at_head for m in members])
    turned = jnp.where(shifted, 0, shift_blocks)
    scalars = jnp.stack((sub, turned)).astype(jnp.int32)

    def exchange(parts):
        return lax.all_to_all(
            parts, ("seq", "head"), 0, 0, axis_index_groups=groups, tiled=True
        )

    def swap(value):
        if subs == 1:
            return value
        return lax.ppermute(value, "sub", [(0, 1), (1, 0)])

    sent = message_of(copies, ranks, head_query_rows, head_key_rows, head_value_rows)
    sent, output_gradient, output_matrix = lax.optimization_barrier(
        (sent, output_gradient, output_matrix)
    )
    own = exchange(sent)

    chunks = heads // subs
    pieces = []
    for k in range(heads):
        pairs = []
        for src_head in range(heads):
            for src_sub in range(subs):
                j = (src_head % chunks) * subs + src_sub
                dst = ((j + k) % heads) * subs + src_head // chunks
                pairs.append((src_head * subs + src_sub, dst))
        pieces.append(lax.ppermute(output_gradient, ("head", "sub"), pairs))

    up_half = lax.dynamic_slice_in_dim(adapter_up_weight, sub * chunks * cols, chunks * cols, 1)
    sources = [(head - k + heads) % heads for k in range(heads)]
    plan = [(j % subs == sub).astype(jnp.int32) for j in sources]
    plan += [(j // subs * cols).astype(jnp.int32) for j in sources]
    packed_own, packed_sent = call_kernel(
        functools.partial(cotangent_kernel, chunks),
        [
            shape_of((feats + low_rank, tok), jnp.float32),
            shape_of((feats + low_rank, tok), jnp.bfloat16),
        ],
        [],
        0,
        0,
        jnp.stack(plan),
        *pieces,
        staged(output_matrix, 55),
        up_half,
        adapter_down_weight,
        declared=1024,
        limit=16,
    )
    received = swap(packed_sent)
    own, _ = lax.optimization_barrier((own, packed_sent))
    other = swap(own[:, tok:])

    down_head = lax.dynamic_slice_in_dim(adapter_down_weight, my_head * HD, HD, 0)
    rows = ranks * tok
    pair_count = rows * (rows + TILE)
    attn_t, middle_rows, stats = call_kernel(
        functools.partial(forward_kernel, tok),
        [
            shape_of((HD, rows), jnp.bfloat16),
            shape_of((ranks, low_rank, tok), jnp.bfloat16),
            shape_of((8, rows), jnp.float32),
        ],
        [],
        4 * pair_count * HD,
        pair_count,
        scalars,
        own,
        other,
        down_head.T,
        limit=16,
    )

    first_copy = rank % copies == 0
    if copies > 1:
        middle_rows = jnp.where(first_copy, middle_rows, 0.0)
    (message,) = in_vmem(
        functools.partial(dout_kernel, copies),
        [shape_of((ranks, HD + 2 * low_rank, tok), jnp.bfloat16)],
        packed_own,
        received,
        middle_rows,
    )
    arrived = exchange(message)
    middle = jnp.sum(arrived[:, HD + low_rank :].astype(jnp.float32), axis=0)
    bit = 1
    while bit < heads:
        middle += lax.ppermute(middle, "head", [(i, i ^ bit) for i in range(heads)])
        bit *= 2
    up_part = 2.0 * dot_nn(middle.astype(jnp.bfloat16), output_gradient)

    dq, dk_own, dv_own, pair_other, down_part = call_kernel(
        functools.partial(backward_kernel, tok),
        [
            shape_of((ranks, tok, HD), jnp.bfloat16),
            shape_of((ranks, tok, HD), jnp.float32),
            shape_of((ranks, tok, HD), jnp.float32),
            shape_of((ranks, 2 * tok, HD), jnp.bfloat16),
            shape_of((low_rank, HD), jnp.float32),
        ],
        [pltpu.VMEM((rows, HD), jnp.float32)] * 4,
        10 * pair_count * HD,
        pair_count,
        scalars,
        own,
        other,
        arrived,
        attn_t,
        stats,
        limit=28,
    )
    pair_received = swap(pair_other).astype(jnp.float32)
    down_rows = jnp.where(first_copy, down_part + swap(down_part), 0.0)
    dk = (dk_own + pair_received[:, :tok]).astype(jnp.bfloat16)
    dv = (dv_own + pair_received[:, tok:]).astype(jnp.bfloat16)
    down_rows = jnp.broadcast_to(down_rows.astype(jnp.bfloat16), (ranks, low_rank, HD))
    back_message = jnp.concatenate([dq, dk, dv, down_rows], axis=1)
    back = exchange(back_message)
    outs = [shape_of((tok, feats), back.dtype)] * 3
    if seqs == ranks:
        outs.append(shape_of((low_rank, feats), jnp.float32))
    outs = list(in_vmem(functools.partial(unpack_kernel, copies), outs, back))
    if seqs > ranks:
        bits = [bit for bit in powers_below(seqs) if bit >= ranks]
        down_terms = back[::copies, 3 * tok :].astype(jnp.float32)
        down_terms = butterfly_sum(down_terms, "seq", bits, seqs)
        outs.append(down_terms.transpose(1, 0, 2).reshape(low_rank, feats))
    query_gradient, key_gradient, value_gradient, down_gradient = outs

    up_sum = butterfly_sum(up_part, "seq", powers_below(seqs), seqs)
    _, up_sum = lax.optimization_barrier((back, up_sum))
    up_gradient = butterfly_sum(up_sum, "sub", powers_below(subs), subs)
    return (query_gradient, key_gradient, value_gradient, down_gradient.T, up_gradient)


def solution(mesh):
    rows = P(("rep", "seq", "sub"), "head")
    sizes = (mesh.shape["seq"], mesh.shape["head"], mesh.shape["sub"])
    return jax.shard_map(
        functools.partial(on_device, sizes),
        mesh=mesh,
        in_specs=(rows, rows, rows, rows, P("head", "sub"), P("head", None), P()),
        out_specs=(rows, rows, rows, P(("rep", "head"), None), P("rep", "head")),
        check_vma=False,
    )
```

```python
import functools
import math

import jax
import jax.numpy as jnp
from jax import lax
from jax.experimental import pallas as pl
from jax.experimental.pallas import tpu as pltpu
from jax.sharding import PartitionSpec as P

HD = 128
GROUP = 2048
TILE = 256
HIDDEN = -1e30
SCALE = HD ** (-0.5)
LOG2_SCALE = SCALE * math.log2(math.e)


def dot_nt(left, right):
    return lax.dot_general(
        left, right, (((1,), (1,)), ((), ())), preferred_element_type=jnp.float32
    )


def dot_nn(left, right):
    return jnp.dot(left, right, preferred_element_type=jnp.float32)


def rows_of(ref, run, first, count):
    start, blocks = run
    return ref[start : start + blocks, first : first + count, :].reshape(blocks * count, HD)


def in_either_order(body, scalar_ref, blocks):
    for turn in (0, blocks // 2):
        pl.when(scalar_ref[1] == turn)(functools.partial(body, turn))


def runs_of(turn, blocks, upto):
    whole = min(upto, blocks - turn)
    return [(turn, whole)] + ([(0, upto - whole)] if upto > whole else [])


def scores_of(queries, sides, runs, masks, tok):
    scores = []
    for (ref, first), visible in zip(sides, masks):
        for n, run in enumerate(runs):
            part = dot_nt(rows_of(ref, run, first, tok), queries)
            if n == len(runs) - 1:
                head = part.shape[0] - TILE
                tail = jnp.where(visible, part[head:], HIDDEN)
                part = tail if head == 0 else jnp.concatenate((part[:head], tail), axis=0)
            scores.append(part)
    return scores


def masks_of(sub, tok):
    key_at = lax.broadcasted_iota(jnp.int32, (TILE, TILE), 0)
    query_at = lax.broadcasted_iota(jnp.int32, (TILE, TILE), 1)
    return key_at <= query_at, key_at // tok < query_at // tok + sub


def summed(terms):
    return functools.reduce(jnp.add, terms)


def forward_kernel(tok, scalar_ref, own_ref, *refs):
    body = functools.partial(forward_body, tok, scalar_ref, own_ref, *refs)
    in_either_order(body, scalar_ref, own_ref.shape[0])


def forward_body(
    tok, scalar_ref, own_ref, other_ref, down_t_ref, attn_ref, mid_ref, stat_ref, turn
):
    blocks = own_ref.shape[0]
    step = TILE // tok
    masks = masks_of(scalar_ref[0], tok)
    sides = ((own_ref, tok), (other_ref, 0))
    everything = (0, blocks)
    values_t = [rows_of(ref, everything, first + tok, tok).T for ref, first in sides]
    for tile in range(blocks // step):
        at = tile * TILE
        start = (tile * step + turn) % blocks
        runs = runs_of(turn, blocks, (tile + 1) * step)
        queries = rows_of(own_ref, (start, step), 0, tok)
        scores = scores_of(queries, sides, runs, masks, tok)
        tops = [jnp.max(part, axis=0, keepdims=True) for part in scores]
        highest = functools.reduce(jnp.maximum, tops)
        powers = [jnp.exp2((part - highest) * LOG2_SCALE) for part in scores]
        inverse = 1.0 / summed([jnp.sum(part, axis=0, keepdims=True) for part in powers])
        places = [(n, run) for n in range(2) for run in runs]
        attn = summed(
            [
                dot_nn(
                    values_t[n][:, first * tok : (first + count) * tok],
                    part.astype(jnp.bfloat16),
                )
                for (n, (first, count)), part in zip(places, powers)
            ]
        )
        attn = (attn * inverse).astype(jnp.bfloat16)
        attn_ref[:, at : at + TILE] = attn
        mid = dot_nn(down_t_ref[...], attn)
        for i in range(step):
            mid_ref[start + i] = mid[:, i * tok : (i + 1) * tok].astype(jnp.bfloat16)
        stat_ref[0:1, at : at + TILE] = highest
        stat_ref[1:2, at : at + TILE] = inverse


def backward_kernel(tok, scalar_ref, own_ref, *refs):
    body = functools.partial(backward_body, tok, scalar_ref, own_ref, *refs)
    in_either_order(body, scalar_ref, own_ref.shape[0])


def backward_body(
    tok,
    scalar_ref,
    own_ref,
    other_ref,
    dout_ref,
    attn_ref,
    stat_ref,
    dq_ref,
    dk_own_ref,
    dv_own_ref,
    pair_other_ref,
    down_grad_ref,
    dk_own,
    dv_own,
    dk_other,
    dv_other,
    turn,
):
    blocks = own_ref.shape[0]
    step = TILE // tok
    low_rank = down_grad_ref.shape[0]
    masks = masks_of(scalar_ref[0], tok)
    sides = ((own_ref, tok), (other_ref, 0))
    everything = (0, blocks)
    keys_t = [rows_of(ref, everything, first, tok).T for ref, first in sides]
    dk, dv = (dk_own, dk_other), (dv_own, dv_other)
    tiles = blocks // step
    down_total = jnp.zeros((low_rank, HD), jnp.float32)
    for tile in reversed(range(tiles)):
        at = tile * TILE
        start = (tile * step + turn) % blocks
        runs = runs_of(turn, blocks, (tile + 1) * step)
        queries = rows_of(own_ref, (start, step), 0, tok)
        douts_t = jnp.concatenate([dout_ref[start + i, 0:HD, :] for i in range(step)], axis=1)
        highest = stat_ref[0:1, at : at + TILE]
        inverse = stat_ref[1:2, at : at + TILE]
        scores = scores_of(queries, sides, runs, masks, tok)
        places = [(n, run) for n in range(2) for run in runs]
        probs = [jnp.exp2((part - highest) * LOG2_SCALE) * inverse for part in scores]
        dprobs = [
            dot_nn(rows_of(sides[n][0], run, sides[n][1] + tok, tok), douts_t)
            for n, run in places
        ]
        delta = summed(
            [jnp.sum(p * d, axis=0, keepdims=True) for p, d in zip(probs, dprobs)]
        )
        dscores = [(p * (d - delta)).astype(jnp.bfloat16) for p, d in zip(probs, dprobs)]
        dq = summed(
            [
                dot_nn(keys_t[n][:, first * tok : (first + count) * tok], part)
                for (n, (first, count)), part in zip(places, dscores)
            ]
        )
        dq = (dq * SCALE).T.astype(jnp.bfloat16)
        for (n, (first, count)), prob, dscore in zip(places, probs, dscores):
            rows = pl.ds(first * tok, count * tok)
            dk_term = dot_nn(dscore, queries)
            dv_term = dot_nt(prob.astype(jnp.bfloat16), douts_t)
            if tile == tiles - 1:
                dk[n][rows, :] = dk_term
                dv[n][rows, :] = dv_term
            else:
                dk[n][rows, :] += dk_term
                dv[n][rows, :] += dv_term
        for i in range(step):
            slot = start + i
            dq_ref[slot] = dq[i * tok : (i + 1) * tok]
            lora = dout_ref[slot, HD : HD + low_rank, :]
            attn = attn_ref[:, at + i * tok : at + (i + 1) * tok]
            down_total += dot_nt(lora, attn)
    shape = (blocks, tok, HD)
    dk_own_ref[...] = (dk_own[...] * SCALE).reshape(shape)
    dv_own_ref[...] = dv_own[...].reshape(shape)
    pair_other_ref[:, 0:tok, :] = (dk_other[...] * SCALE).astype(jnp.bfloat16).reshape(shape)
    pair_other_ref[:, tok : 2 * tok, :] = dv_other[...].astype(jnp.bfloat16).reshape(shape)
    down_grad_ref[...] = 2.0 * down_total


def call_kernel(body, outs, scratch, flops, exps, *operands, limit=48):
    in_bytes = sum(x.size * x.dtype.itemsize for x in operands)
    out_bytes = sum(x.size * x.dtype.itemsize for x in outs)
    specs = [pl.BlockSpec(memory_space=pltpu.SMEM)]
    specs += [pl.BlockSpec(memory_space=pltpu.VMEM)] * (len(operands) - 1)
    return pl.pallas_call(
        body,
        out_shape=outs,
        in_specs=specs,
        out_specs=[pl.BlockSpec(memory_space=pltpu.VMEM)] * len(outs),
        scratch_shapes=scratch,
        compiler_params=pltpu.CompilerParams(vmem_limit_bytes=limit * 1024 * 1024),
        cost_estimate=pl.CostEstimate(
            flops=flops,
            bytes_accessed=in_bytes + out_bytes,
            transcendentals=exps,
        ),
    )(*operands)


def shape_of(shape, dtype):
    return jax.ShapeDtypeStruct(shape, dtype)


def butterfly_sum(value, axis, bits, count):
    for bit in bits:
        pairs = [(i, i ^ bit) for i in range(count)]
        value = value.astype(jnp.bfloat16)
        taken = lax.ppermute(value, axis, pairs)
        value = value.astype(jnp.float32) + taken.astype(jnp.float32)
    return value


def powers_below(count):
    return [1 << n for n in range(count.bit_length() - 1)]


def message_kernel(copies, *refs):
    count = (len(refs) - 3) // 2
    operands, message_ref = refs[:count], refs[count]
    held, in_sems, out_sems = refs[count + 1 : -2], refs[-2], refs[-1]
    tok = operands[0].shape[0]
    arriving = [
        pltpu.make_async_copy(ref, to, in_sems.at[n])
        for n, (ref, to) in enumerate(zip(operands, held))
    ]
    for copy in arriving:
        copy.start()
    leaving = []
    for n, (copy, ref) in enumerate(zip(arriving, held)):
        copy.wait()
        for rank in range(message_ref.shape[0]):
            cols = pl.ds((rank // copies) * HD, HD)
            to = message_ref.at[rank, pl.ds(n * tok, tok), :]
            leaving.append(pltpu.make_async_copy(ref.at[:, cols], to, out_sems.at[len(leaving)]))
            leaving[-1].start()
    for copy in leaving:
        copy.wait()


def message_of(copies, ranks, *operands):
    tok = operands[0].shape[0]
    count = len(operands)
    shape = (ranks, count * tok, HD)
    return pl.pallas_call(
        functools.partial(message_kernel, copies),
        out_shape=shape_of(shape, operands[0].dtype),
        in_specs=[pl.BlockSpec(memory_space=pltpu.HBM)] * count,
        out_specs=pl.BlockSpec(memory_space=pltpu.HBM),
        scratch_shapes=[pltpu.VMEM(x.shape, x.dtype) for x in operands]
        + [pltpu.SemaphoreType.DMA((count,)), pltpu.SemaphoreType.DMA((ranks * count,))],
        cost_estimate=pl.CostEstimate(
            flops=0, bytes_accessed=4 * math.prod(shape), transcendentals=0
        ),
    )(*operands)


def unpack_kernel(copies, back_ref, *refs):
    out_refs, down_ref = refs[:3], refs[3] if len(refs) > 3 else None
    tok = out_refs[0].shape[0]
    for at_head in range(out_refs[0].shape[1] // HD):
        cols = slice(at_head * HD, (at_head + 1) * HD)
        for n, ref in enumerate(out_refs):
            ref[:, cols] = back_ref[at_head * copies, n * tok : (n + 1) * tok, :]
        if down_ref is not None:
            down_ref[:, cols] = back_ref[at_head * copies, 3 * tok :, :].astype(jnp.float32)


def in_vmem(body, outs, *operands):
    whole = pl.BlockSpec(memory_space=pltpu.VMEM)
    size = sum(x.size * x.dtype.itemsize for x in operands)
    size += sum(x.size * x.dtype.itemsize for x in outs)
    return pl.pallas_call(
        body,
        out_shape=outs,
        in_specs=[whole] * len(operands),
        out_specs=[whole] * len(outs),
        compiler_params=pltpu.CompilerParams(vmem_limit_bytes=16 * 1024 * 1024),
        cost_estimate=pl.CostEstimate(flops=0, bytes_accessed=size, transcendentals=0),
    )(*operands)


def dout_kernel(copies, own_ref, taken_ref, mid_ref, message_ref):
    low_rank = mid_ref.shape[1]
    feats = own_ref.shape[0] - low_rank
    lora = own_ref[feats:, :] + taken_ref[feats:, :].astype(jnp.float32)
    for rank in range(message_ref.shape[0]):
        at = pl.ds((rank // copies) * HD, HD)
        part = own_ref[at, :] + taken_ref[at, :].astype(jnp.float32)
        message_ref[rank, 0:HD, :] = part.astype(jnp.bfloat16)
        message_ref[rank, HD : HD + low_rank, :] = lora.astype(jnp.bfloat16)
        message_ref[rank, HD + low_rank : HD + 2 * low_rank, :] = mid_ref[rank]


def on_device(
    sizes,
    head_query_rows,
    head_key_rows,
    head_value_rows,
    output_gradient,
    output_matrix,
    adapter_down_weight,
    adapter_up_weight,
):
    seqs, heads, subs = sizes
    tok, feats = head_query_rows.shape
    cols = output_gradient.shape[1]
    low_rank = adapter_up_weight.shape[0]
    local_heads = feats // HD
    block_rows = tok * subs
    ranks = GROUP // block_rows
    copies = ranks // local_heads
    shift_blocks = GROUP // 2 // block_rows

    seq = lax.axis_index("seq")
    head = lax.axis_index("head")
    sub = lax.axis_index("sub")
    shifted = head >= heads // 2
    rank = (seq + shift_blocks) % ranks
    my_head = rank // copies

    groups = []
    for at_head in range(heads):
        for first in range(0, seqs, ranks):
            members = [first + shift_blocks + i for i in range(ranks)]
            if at_head < heads // 2:
                members = [first + (m - first) % ranks for m in members]
            members = [m % seqs for m in members]
            groups.append([m * heads + at_head for m in members])
    turned = jnp.where(shifted, 0, shift_blocks)
    scalars = jnp.stack((sub, turned)).astype(jnp.int32)

    def exchange(parts):
        return lax.all_to_all(
            parts, ("seq", "head"), 0, 0, axis_index_groups=groups, tiled=True
        )

    def swap(value):
        if subs == 1:
            return value
        return lax.ppermute(value, "sub", [(0, 1), (1, 0)])

    sent = message_of(copies, ranks, head_query_rows, head_key_rows, head_value_rows)
    sent, output_gradient = lax.optimization_barrier((sent, output_gradient))
    own = exchange(sent)

    chunks = heads // subs
    pieces = []
    for k in range(heads):
        pairs = []
        for src_head in range(heads):
            for src_sub in range(subs):
                j = (src_head % chunks) * subs + src_sub
                dst = ((j + k) % heads) * subs + src_head // chunks
                pairs.append((src_head * subs + src_sub, dst))
        pieces.append(lax.ppermute(output_gradient, ("head", "sub"), pairs))

    up_half = lax.dynamic_slice_in_dim(adapter_up_weight, sub * chunks * cols, chunks * cols, 1)
    sources = [(head - k + heads) % heads for k in range(heads)]
    _, pieces = lax.optimization_barrier((own, pieces))

    def terms_of(rows, at):
        matrix, up = output_matrix, up_half
        if chunks > 1:
            matrix = lax.dynamic_slice_in_dim(matrix, at, cols, 1)
            up = lax.dynamic_slice_in_dim(up, at, cols, 1)
        lora = dot_nt(up, rows)
        grad = dot_nt(matrix, rows)
        grad += 2.0 * dot_nn(adapter_down_weight, lora.astype(jnp.bfloat16))
        return jnp.concatenate((grad, lora), axis=0)

    if chunks == 1:
        terms = jnp.split(terms_of(jnp.concatenate(pieces, axis=0), 0), heads, axis=1)
    else:
        terms = [terms_of(p, j // subs * cols) for p, j in zip(pieces, sources)]
    mine = [j % subs == sub for j in sources]
    packed_own = summed([jnp.where(m, t, 0.0) for m, t in zip(mine, terms)])
    packed_sent = summed([jnp.where(m, 0.0, t) for m, t in zip(mine, terms)])
    received = swap(packed_sent.astype(jnp.bfloat16))
    other = swap(own[:, tok:])

    down_head = lax.dynamic_slice_in_dim(adapter_down_weight, my_head * HD, HD, 0)
    rows = ranks * tok
    pair_count = rows * (rows + TILE)
    attn_t, middle_rows, stats = call_kernel(
        functools.partial(forward_kernel, tok),
        [
            shape_of((HD, rows), jnp.bfloat16),
            shape_of((ranks, low_rank, tok), jnp.bfloat16),
            shape_of((8, rows), jnp.float32),
        ],
        [],
        4 * pair_count * HD,
        pair_count,
        scalars,
        own,
        other,
        down_head.T,
        limit=16,
    )

    first_copy = rank % copies == 0
    if copies > 1:
        middle_rows = jnp.where(first_copy, middle_rows, 0.0)
    (message,) = in_vmem(
        functools.partial(dout_kernel, copies),
        [shape_of((ranks, HD + 2 * low_rank, tok), jnp.bfloat16)],
        packed_own,
        received,
        middle_rows,
    )
    arrived = exchange(message)
    middle = jnp.sum(arrived[:, HD + low_rank :].astype(jnp.float32), axis=0)
    bit = 1
    while bit < heads:
        middle += lax.ppermute(middle, "head", [(i, i ^ bit) for i in range(heads)])
        bit *= 2
    up_part = 2.0 * dot_nn(middle.astype(jnp.bfloat16), output_gradient)

    dq, dk_own, dv_own, pair_other, down_part = call_kernel(
        functools.partial(backward_kernel, tok),
        [
            shape_of((ranks, tok, HD), jnp.bfloat16),
            shape_of((ranks, tok, HD), jnp.float32),
            shape_of((ranks, tok, HD), jnp.float32),
            shape_of((ranks, 2 * tok, HD), jnp.bfloat16),
            shape_of((low_rank, HD), jnp.float32),
        ],
        [pltpu.VMEM((rows, HD), jnp.float32)] * 4,
        10 * pair_count * HD,
        pair_count,
        scalars,
        own,
        other,
        arrived,
        attn_t,
        stats,
        limit=28,
    )
    pair_received = swap(pair_other).astype(jnp.float32)
    down_rows = jnp.where(first_copy, down_part + swap(down_part), 0.0)
    dk = (dk_own + pair_received[:, :tok]).astype(jnp.bfloat16)
    dv = (dv_own + pair_received[:, tok:]).astype(jnp.bfloat16)
    down_rows = jnp.broadcast_to(down_rows.astype(jnp.bfloat16), (ranks, low_rank, HD))
    back_message = jnp.concatenate([dq, dk, dv, down_rows], axis=1)
    back = exchange(back_message)
    outs = [shape_of((tok, feats), back.dtype)] * 3
    if seqs == ranks:
        outs.append(shape_of((low_rank, feats), jnp.float32))
    outs = list(in_vmem(functools.partial(unpack_kernel, copies), outs, back))
    if seqs > ranks:
        bits = [bit for bit in powers_below(seqs) if bit >= ranks]
        down_terms = back[::copies, 3 * tok :].astype(jnp.float32)
        down_terms = butterfly_sum(down_terms, "seq", bits, seqs)
        outs.append(down_terms.transpose(1, 0, 2).reshape(low_rank, feats))
    query_gradient, key_gradient, value_gradient, down_gradient = outs

    up_sum = butterfly_sum(up_part, "seq", powers_below(seqs), seqs)
    _, up_sum = lax.optimization_barrier((back, up_sum))
    up_gradient = butterfly_sum(up_sum, "sub", powers_below(subs), subs)
    return (query_gradient, key_gradient, value_gradient, down_gradient.T, up_gradient)


def solution(mesh):
    rows = P(("rep", "seq", "sub"), "head")
    sizes = (mesh.shape["seq"], mesh.shape["head"], mesh.shape["sub"])
    return jax.shard_map(
        functools.partial(on_device, sizes),
        mesh=mesh,
        in_specs=(rows, rows, rows, rows, P("head", "sub"), P("head", None), P()),
        out_specs=(rows, rows, rows, P(("rep", "head"), None), P("rep", "head")),
        check_vma=False,
    )
```

```python
import functools
import math

import jax
import jax.numpy as jnp
from jax import lax
from jax.experimental import pallas as pl
from jax.experimental.pallas import tpu as pltpu
from jax.sharding import PartitionSpec as P

HD = 128
GROUP = 2048
TILE = 256
HIDDEN = -1e30
SCALE = HD ** (-0.5)
LOG2_SCALE = SCALE * math.log2(math.e)


def dot_nt(left, right):
    return lax.dot_general(
        left, right, (((1,), (1,)), ((), ())), preferred_element_type=jnp.float32
    )


def dot_nn(left, right):
    return jnp.dot(left, right, preferred_element_type=jnp.float32)


def rows_of(ref, blocks, first, count):
    return ref[0:blocks, first : first + count, :].reshape(blocks * count, HD)


def scores_of(sub, keys_own, keys_other, queries, tok):
    def tail_hidden(scores, visible):
        head = scores.shape[0] - TILE
        tail = jnp.where(visible, scores[head:], HIDDEN)
        return tail if head == 0 else jnp.concatenate((scores[:head], tail), axis=0)

    key_at = lax.broadcasted_iota(jnp.int32, (TILE, TILE), 0)
    query_at = lax.broadcasted_iota(jnp.int32, (TILE, TILE), 1)
    own = tail_hidden(dot_nt(keys_own, queries), key_at <= query_at)
    other = tail_hidden(
        dot_nt(keys_other, queries), key_at // tok < query_at // tok + sub
    )
    return own, other


def summed(terms):
    return functools.reduce(jnp.add, terms)


def forward_kernel(
    tok, scalar_ref, own_ref, other_ref, down_t_ref, attn_ref, mid_ref, stat_ref
):
    blocks = own_ref.shape[0]
    step = TILE // tok
    sub = scalar_ref[0]
    values_own_t = rows_of(own_ref, blocks, 2 * tok, tok).T
    values_other_t = rows_of(other_ref, blocks, tok, tok).T
    for tile in range(blocks // step):
        upto = (tile + 1) * step
        width = upto * tok
        at = tile * TILE
        queries = own_ref[tile * step : upto, 0:tok, :].reshape(TILE, HD)
        own, other = scores_of(
            sub, rows_of(own_ref, upto, tok, tok), rows_of(other_ref, upto, 0, tok), queries, tok
        )
        highest = jnp.maximum(
            jnp.max(own, axis=0, keepdims=True), jnp.max(other, axis=0, keepdims=True)
        )
        own = jnp.exp2((own - highest) * LOG2_SCALE)
        other = jnp.exp2((other - highest) * LOG2_SCALE)
        inverse = 1.0 / (
            jnp.sum(own, axis=0, keepdims=True) + jnp.sum(other, axis=0, keepdims=True)
        )
        attn = dot_nn(values_own_t[:, :width], own.astype(jnp.bfloat16)) + dot_nn(
            values_other_t[:, :width], other.astype(jnp.bfloat16)
        )
        attn = (attn * inverse).astype(jnp.bfloat16)
        attn_ref[:, at : at + TILE] = attn
        mid_ref[:, at : at + TILE] = dot_nn(down_t_ref[...], attn)
        stat_ref[0:1, at : at + TILE] = highest
        stat_ref[1:2, at : at + TILE] = inverse


def backward_kernel(
    tok,
    scalar_ref,
    own_ref,
    other_ref,
    dout_ref,
    attn_ref,
    stat_ref,
    dq_ref,
    dk_own_ref,
    dv_own_ref,
    pair_other_ref,
    down_grad_ref,
    dk_own,
    dv_own,
    dk_other,
    dv_other,
):
    blocks = own_ref.shape[0]
    step = TILE // tok
    sub = scalar_ref[0]
    low_rank = down_grad_ref.shape[0]
    keys_own_t = rows_of(own_ref, blocks, tok, tok).T
    keys_other_t = rows_of(other_ref, blocks, 0, tok).T
    tiles = blocks // step
    down_total = jnp.zeros((low_rank, HD), jnp.float32)
    for tile in reversed(range(tiles)):
        upto = (tile + 1) * step
        width = upto * tok
        at = tile * TILE
        queries = own_ref[tile * step : upto, 0:tok, :].reshape(TILE, HD)
        douts_t = jnp.concatenate(
            [dout_ref[block, 0:HD, :] for block in range(tile * step, upto)], axis=1
        )
        highest = stat_ref[0:1, at : at + TILE]
        inverse = stat_ref[1:2, at : at + TILE]
        own, other = scores_of(
            sub, rows_of(own_ref, upto, tok, tok), rows_of(other_ref, upto, 0, tok), queries, tok
        )
        own = jnp.exp2((own - highest) * LOG2_SCALE) * inverse
        other = jnp.exp2((other - highest) * LOG2_SCALE) * inverse
        dprob_own = dot_nn(rows_of(own_ref, upto, 2 * tok, tok), douts_t)
        dprob_other = dot_nn(rows_of(other_ref, upto, tok, tok), douts_t)
        delta = jnp.sum(own * dprob_own, axis=0, keepdims=True) + jnp.sum(
            other * dprob_other, axis=0, keepdims=True
        )
        ds_own = (own * (dprob_own - delta)).astype(jnp.bfloat16)
        ds_other = (other * (dprob_other - delta)).astype(jnp.bfloat16)
        dq = dot_nn(keys_own_t[:, :width], ds_own) + dot_nn(keys_other_t[:, :width], ds_other)
        dq = (dq * SCALE).T.astype(jnp.bfloat16)
        dq_ref[tile * step : upto] = dq.reshape(step, tok, HD)
        terms = (
            (dk_own, dot_nn(ds_own, queries)),
            (dk_other, dot_nn(ds_other, queries)),
            (dv_own, dot_nt(own.astype(jnp.bfloat16), douts_t)),
            (dv_other, dot_nt(other.astype(jnp.bfloat16), douts_t)),
        )
        for total, term in terms:
            if tile == tiles - 1:
                total[...] = term
            else:
                total[0:width] += term
        for i in range(step):
            lora = dout_ref[tile * step + i, HD : HD + low_rank, :]
            attn = attn_ref[:, at + i * tok : at + (i + 1) * tok]
            down_total += dot_nt(lora, attn)
    shape = (blocks, tok, HD)
    dk_own_ref[...] = (dk_own[...] * SCALE).reshape(shape)
    dv_own_ref[...] = dv_own[...].reshape(shape)
    pair_other_ref[:, 0:tok, :] = (dk_other[...] * SCALE).astype(jnp.bfloat16).reshape(shape)
    pair_other_ref[:, tok : 2 * tok, :] = dv_other[...].astype(jnp.bfloat16).reshape(shape)
    down_grad_ref[...] = 2.0 * down_total


def call_kernel(body, outs, scratch, flops, exps, *operands, limit=48):
    in_bytes = sum(x.size * x.dtype.itemsize for x in operands)
    out_bytes = sum(x.size * x.dtype.itemsize for x in outs)
    specs = [pl.BlockSpec(memory_space=pltpu.SMEM)]
    specs += [pl.BlockSpec(memory_space=pltpu.VMEM)] * (len(operands) - 1)
    return pl.pallas_call(
        body,
        out_shape=outs,
        in_specs=specs,
        out_specs=[pl.BlockSpec(memory_space=pltpu.VMEM)] * len(outs),
        scratch_shapes=scratch,
        compiler_params=pltpu.CompilerParams(vmem_limit_bytes=limit * 1024 * 1024),
        cost_estimate=pl.CostEstimate(
            flops=flops,
            bytes_accessed=in_bytes + out_bytes,
            transcendentals=exps,
        ),
    )(*operands)


def shape_of(shape, dtype):
    return jax.ShapeDtypeStruct(shape, dtype)


def butterfly_sum(value, axis, bits, count):
    def taken(value, mask):
        return lax.ppermute(value, axis, [(i, i ^ mask) for i in range(count)])

    while bits:
        now, bits = bits[:2], bits[2:]
        value = value.astype(jnp.bfloat16)
        near = value.astype(jnp.float32) + taken(value, now[0]).astype(jnp.float32)
        if len(now) == 2:
            far = taken(value, now[1]).astype(jnp.float32)
            far += taken(value, now[0] | now[1]).astype(jnp.float32)
            near += far
        value = near
    return value


def powers_below(count):
    return [1 << n for n in range(count.bit_length() - 1)]


def message_kernel(copies, *refs):
    count = (len(refs) - 3) // 2
    operands, message_ref = refs[:count], refs[count]
    held, in_sems, out_sems = refs[count + 1 : -2], refs[-2], refs[-1]
    tok = operands[0].shape[0]
    arriving = [
        pltpu.make_async_copy(ref, to, in_sems.at[n])
        for n, (ref, to) in enumerate(zip(operands, held))
    ]
    for copy in arriving:
        copy.start()
    leaving = []
    for n, (copy, ref) in enumerate(zip(arriving, held)):
        copy.wait()
        for rank in range(message_ref.shape[0]):
            cols = pl.ds((rank // copies) * HD, HD)
            to = message_ref.at[rank, pl.ds(n * tok, tok), :]
            leaving.append(pltpu.make_async_copy(ref.at[:, cols], to, out_sems.at[len(leaving)]))
            leaving[-1].start()
    for copy in leaving:
        copy.wait()


def message_of(copies, ranks, *operands):
    tok = operands[0].shape[0]
    count = len(operands)
    shape = (ranks, count * tok, HD)
    return pl.pallas_call(
        functools.partial(message_kernel, copies),
        out_shape=shape_of(shape, operands[0].dtype),
        in_specs=[pl.BlockSpec(memory_space=pltpu.HBM)] * count,
        out_specs=pl.BlockSpec(memory_space=pltpu.HBM),
        scratch_shapes=[pltpu.VMEM(x.shape, x.dtype) for x in operands]
        + [pltpu.SemaphoreType.DMA((count,)), pltpu.SemaphoreType.DMA((ranks * count,))],
        cost_estimate=pl.CostEstimate(
            flops=0, bytes_accessed=4 * math.prod(shape), transcendentals=0
        ),
    )(*operands)


def unpack_kernel(copies, back_ref, *refs):
    out_refs, down_ref = refs[:3], refs[3] if len(refs) > 3 else None
    tok = out_refs[0].shape[0]
    for at_head in range(out_refs[0].shape[1] // HD):
        cols = slice(at_head * HD, (at_head + 1) * HD)
        for n, ref in enumerate(out_refs):
            ref[:, cols] = back_ref[at_head * copies, n * tok : (n + 1) * tok, :]
        if down_ref is not None:
            down_ref[:, cols] = back_ref[at_head * copies, 3 * tok :, :].astype(jnp.float32)


def in_vmem(body, outs, *operands):
    whole = pl.BlockSpec(memory_space=pltpu.VMEM)
    size = sum(x.size * x.dtype.itemsize for x in operands)
    size += sum(x.size * x.dtype.itemsize for x in outs)
    return pl.pallas_call(
        body,
        out_shape=outs,
        in_specs=[whole] * len(operands),
        out_specs=[whole] * len(outs),
        compiler_params=pltpu.CompilerParams(vmem_limit_bytes=16 * 1024 * 1024),
        cost_estimate=pl.CostEstimate(flops=0, bytes_accessed=size, transcendentals=0),
    )(*operands)


def dout_kernel(copies, own_ref, taken_ref, mid_ref, message_ref):
    low_rank = mid_ref.shape[1]
    feats = own_ref.shape[0] - low_rank
    lora = own_ref[feats:, :] + taken_ref[feats:, :].astype(jnp.float32)
    for rank in range(message_ref.shape[0]):
        at = pl.ds((rank // copies) * HD, HD)
        part = own_ref[at, :] + taken_ref[at, :].astype(jnp.float32)
        message_ref[rank, 0:HD, :] = part.astype(jnp.bfloat16)
        message_ref[rank, HD : HD + low_rank, :] = lora.astype(jnp.bfloat16)
        message_ref[rank, HD + low_rank : HD + 2 * low_rank, :] = mid_ref[rank]


def on_device(
    sizes,
    head_query_rows,
    head_key_rows,
    head_value_rows,
    output_gradient,
    output_matrix,
    adapter_down_weight,
    adapter_up_weight,
):
    seqs, heads, subs = sizes
    tok, feats = head_query_rows.shape
    cols = output_gradient.shape[1]
    low_rank = adapter_up_weight.shape[0]
    local_heads = feats // HD
    block_rows = tok * subs
    ranks = GROUP // block_rows
    copies = ranks // local_heads
    shift_blocks = GROUP // 2 // block_rows

    seq = lax.axis_index("seq")
    head = lax.axis_index("head")
    sub = lax.axis_index("sub")
    shifted = head >= heads // 2
    rank = (seq + shift_blocks) % ranks
    my_head = rank // copies

    groups = []
    for at_head in range(heads):
        for first in range(0, seqs, ranks):
            members = [first + shift_blocks + i for i in range(ranks)]
            if at_head < heads // 2:
                members = [first + (m - first) % ranks for m in members]
            members = [m % seqs for m in members]
            groups.append([m * heads + at_head for m in members])
    scalars = jnp.full((1,), sub, jnp.int32)

    def in_order(blocks):
        half = ranks // 2
        turned = jnp.concatenate((blocks[half:], blocks[:half]), axis=0)
        return jnp.where(shifted, blocks, turned)


    def exchange(parts):
        return lax.all_to_all(
            parts, ("seq", "head"), 0, 0, axis_index_groups=groups, tiled=True
        )

    def swap(value):
        if subs == 1:
            return value
        return lax.ppermute(value, "sub", [(0, 1), (1, 0)])

    sent = message_of(copies, ranks, head_query_rows, head_key_rows, head_value_rows)
    sent, output_gradient = lax.optimization_barrier((sent, output_gradient))
    own = exchange(sent)

    chunks = heads // subs
    pieces = []
    for k in range(heads):
        pairs = []
        for src_head in range(heads):
            for src_sub in range(subs):
                j = (src_head % chunks) * subs + src_sub
                dst = ((j + k) % heads) * subs + src_head // chunks
                pairs.append((src_head * subs + src_sub, dst))
        pieces.append(lax.ppermute(output_gradient, ("head", "sub"), pairs))

    up_half = lax.dynamic_slice_in_dim(adapter_up_weight, sub * chunks * cols, chunks * cols, 1)
    sources = [(head - k + heads) % heads for k in range(heads)]

    def terms_of(rows, at):
        matrix, up = output_matrix, up_half
        if chunks > 1:
            matrix = lax.dynamic_slice_in_dim(matrix, at, cols, 1)
            up = lax.dynamic_slice_in_dim(up, at, cols, 1)
        lora = dot_nt(up, rows)
        lora_term = 2.0 * dot_nn(adapter_down_weight, lora.astype(jnp.bfloat16))
        _, rows = lax.optimization_barrier((own, rows))
        grad = dot_nt(matrix, rows) + lora_term
        return jnp.concatenate((grad, lora), axis=0)

    if chunks == 1:
        terms = jnp.split(terms_of(jnp.concatenate(pieces, axis=0), 0), heads, axis=1)
    else:
        terms = [terms_of(p, j // subs * cols) for p, j in zip(pieces, sources)]
    mine = [j % subs == sub for j in sources]
    packed_own = summed([jnp.where(m, t, 0.0) for m, t in zip(mine, terms)])
    packed_sent = summed([jnp.where(m, 0.0, t) for m, t in zip(mine, terms)])
    received = swap(packed_sent.astype(jnp.bfloat16))
    own = in_order(own)
    other = swap(own[:, tok:])

    down_head = lax.dynamic_slice_in_dim(adapter_down_weight, my_head * HD, HD, 0)
    rows = ranks * tok
    pair_count = rows * (rows + TILE)
    attn_t, middle_rows, stats = call_kernel(
        functools.partial(forward_kernel, tok),
        [
            shape_of((HD, rows), jnp.bfloat16),
            shape_of((low_rank, rows), jnp.float32),
            shape_of((8, rows), jnp.float32),
        ],
        [],
        4 * pair_count * HD,
        pair_count,
        scalars,
        own,
        other,
        down_head.T,
        limit=16,
    )

    first_copy = rank % copies == 0
    middle_rows = middle_rows.astype(jnp.bfloat16).reshape(low_rank, ranks, tok)
    middle_rows = in_order(middle_rows.transpose(1, 0, 2))
    if copies > 1:
        middle_rows = jnp.where(first_copy, middle_rows, 0.0)
    (message,) = in_vmem(
        functools.partial(dout_kernel, copies),
        [shape_of((ranks, HD + 2 * low_rank, tok), jnp.bfloat16)],
        packed_own,
        received,
        middle_rows,
    )
    arrived = exchange(message)
    middle = jnp.sum(arrived[:, HD + low_rank :].astype(jnp.float32), axis=0)
    bit = 1
    while bit < heads:
        middle += lax.ppermute(middle, "head", [(i, i ^ bit) for i in range(heads)])
        bit *= 2
    up_part = 2.0 * dot_nn(middle.astype(jnp.bfloat16), output_gradient)

    dq, dk_own, dv_own, pair_other, down_part = call_kernel(
        functools.partial(backward_kernel, tok),
        [
            shape_of((ranks, tok, HD), jnp.bfloat16),
            shape_of((ranks, tok, HD), jnp.float32),
            shape_of((ranks, tok, HD), jnp.float32),
            shape_of((ranks, 2 * tok, HD), jnp.bfloat16),
            shape_of((low_rank, HD), jnp.float32),
        ],
        [pltpu.VMEM((rows, HD), jnp.float32)] * 4,
        10 * pair_count * HD,
        pair_count,
        scalars,
        own,
        other,
        in_order(arrived[:, : HD + low_rank]),
        attn_t,
        stats,
        limit=28,
    )
    pair_received = swap(pair_other).astype(jnp.float32)
    down_rows = jnp.where(first_copy, down_part + swap(down_part), 0.0)
    dk = (dk_own + pair_received[:, :tok]).astype(jnp.bfloat16)
    dv = (dv_own + pair_received[:, tok:]).astype(jnp.bfloat16)
    down_rows = jnp.broadcast_to(down_rows.astype(jnp.bfloat16), (ranks, low_rank, HD))
    back_message = jnp.concatenate([*map(in_order, (dq, dk, dv)), down_rows], axis=1)
    back = exchange(back_message)
    outs = [shape_of((tok, feats), back.dtype)] * 3
    if seqs == ranks:
        outs.append(shape_of((low_rank, feats), jnp.float32))
    outs = list(in_vmem(functools.partial(unpack_kernel, copies), outs, back))
    if seqs > ranks:
        bits = [bit for bit in powers_below(seqs) if bit >= ranks]
        down_terms = back[::copies, 3 * tok :].astype(jnp.float32)
        down_terms = butterfly_sum(down_terms, "seq", bits, seqs)
        outs.append(down_terms.transpose(1, 0, 2).reshape(low_rank, feats))
    query_gradient, key_gradient, value_gradient, down_gradient = outs

    up_sum = butterfly_sum(up_part, "seq", powers_below(seqs), seqs)
    _, up_sum = lax.optimization_barrier((back, up_sum))
    up_gradient = butterfly_sum(up_sum, "sub", powers_below(subs), subs)
    return (query_gradient, key_gradient, value_gradient, down_gradient.T, up_gradient)


def solution(mesh):
    rows = P(("rep", "seq", "sub"), "head")
    sizes = (mesh.shape["seq"], mesh.shape["head"], mesh.shape["sub"])
    return jax.shard_map(
        functools.partial(on_device, sizes),
        mesh=mesh,
        in_specs=(rows, rows, rows, rows, P("head", "sub"), P("head", None), P()),
        out_specs=(rows, rows, rows, P(("rep", "head"), None), P("rep", "head")),
        check_vma=False,
    )
```

```python
import functools
import math

import jax
import jax.numpy as jnp
from jax import lax
from jax.experimental import pallas as pl
from jax.experimental.pallas import tpu as pltpu
from jax.sharding import PartitionSpec as P

HD = 128
GROUP = 2048
TILE = 256
HIDDEN = -1e30
SCALE = HD ** (-0.5)
LOG2_SCALE = SCALE * math.log2(math.e)


def dot_nt(left, right):
    return lax.dot_general(
        left, right, (((1,), (1,)), ((), ())), preferred_element_type=jnp.float32
    )


def dot_nn(left, right):
    return jnp.dot(left, right, preferred_element_type=jnp.float32)


def rows_of(ref, blocks, first, count):
    return ref[0:blocks, first : first + count, :].reshape(blocks * count, HD)


def scores_of(sub, keys_own, keys_other, queries, tok):
    def tail_hidden(scores, visible):
        head = scores.shape[0] - TILE
        tail = jnp.where(visible, scores[head:], HIDDEN)
        return tail if head == 0 else jnp.concatenate((scores[:head], tail), axis=0)

    key_at = lax.broadcasted_iota(jnp.int32, (TILE, TILE), 0)
    query_at = lax.broadcasted_iota(jnp.int32, (TILE, TILE), 1)
    own = tail_hidden(dot_nt(keys_own, queries), key_at <= query_at)
    other = tail_hidden(
        dot_nt(keys_other, queries), key_at // tok < query_at // tok + sub
    )
    return own, other


def summed(terms):
    return functools.reduce(jnp.add, terms)


def forward_kernel(
    tok, scalar_ref, own_ref, other_ref, down_t_ref, attn_ref, mid_ref, stat_ref
):
    blocks = own_ref.shape[0]
    step = TILE // tok
    sub = scalar_ref[0]
    values_own_t = rows_of(own_ref, blocks, 2 * tok, tok).T
    values_other_t = rows_of(other_ref, blocks, tok, tok).T
    for tile in range(blocks // step):
        upto = (tile + 1) * step
        width = upto * tok
        at = tile * TILE
        queries = own_ref[tile * step : upto, 0:tok, :].reshape(TILE, HD)
        own, other = scores_of(
            sub, rows_of(own_ref, upto, tok, tok), rows_of(other_ref, upto, 0, tok), queries, tok
        )
        highest = jnp.maximum(
            jnp.max(own, axis=0, keepdims=True), jnp.max(other, axis=0, keepdims=True)
        )
        own = jnp.exp2((own - highest) * LOG2_SCALE)
        other = jnp.exp2((other - highest) * LOG2_SCALE)
        inverse = 1.0 / (
            jnp.sum(own, axis=0, keepdims=True) + jnp.sum(other, axis=0, keepdims=True)
        )
        attn = dot_nn(values_own_t[:, :width], own.astype(jnp.bfloat16)) + dot_nn(
            values_other_t[:, :width], other.astype(jnp.bfloat16)
        )
        attn = (attn * inverse).astype(jnp.bfloat16)
        attn_ref[:, at : at + TILE] = attn
        mid_ref[:, at : at + TILE] = dot_nn(down_t_ref[...], attn)
        stat_ref[0:1, at : at + TILE] = highest
        stat_ref[1:2, at : at + TILE] = inverse


def backward_kernel(
    tok,
    scalar_ref,
    own_ref,
    other_ref,
    dout_ref,
    attn_ref,
    stat_ref,
    dq_ref,
    dk_own_ref,
    dv_own_ref,
    pair_other_ref,
    down_grad_ref,
    dk_own,
    dv_own,
    dk_other,
    dv_other,
):
    blocks = own_ref.shape[0]
    step = TILE // tok
    sub = scalar_ref[0]
    low_rank = down_grad_ref.shape[0]
    keys_own_t = rows_of(own_ref, blocks, tok, tok).T
    keys_other_t = rows_of(other_ref, blocks, 0, tok).T
    tiles = blocks // step
    down_total = jnp.zeros((low_rank, HD), jnp.float32)
    for tile in reversed(range(tiles)):
        upto = (tile + 1) * step
        width = upto * tok
        at = tile * TILE
        queries = own_ref[tile * step : upto, 0:tok, :].reshape(TILE, HD)
        douts_t = jnp.concatenate(
            [dout_ref[block, 0:HD, :] for block in range(tile * step, upto)], axis=1
        )
        highest = stat_ref[0:1, at : at + TILE]
        inverse = stat_ref[1:2, at : at + TILE]
        own, other = scores_of(
            sub, rows_of(own_ref, upto, tok, tok), rows_of(other_ref, upto, 0, tok), queries, tok
        )
        own = jnp.exp2((own - highest) * LOG2_SCALE) * inverse
        other = jnp.exp2((other - highest) * LOG2_SCALE) * inverse
        dprob_own = dot_nn(rows_of(own_ref, upto, 2 * tok, tok), douts_t)
        dprob_other = dot_nn(rows_of(other_ref, upto, tok, tok), douts_t)
        delta = jnp.sum(own * dprob_own, axis=0, keepdims=True) + jnp.sum(
            other * dprob_other, axis=0, keepdims=True
        )
        ds_own = (own * (dprob_own - delta)).astype(jnp.bfloat16)
        ds_other = (other * (dprob_other - delta)).astype(jnp.bfloat16)
        dq = dot_nn(keys_own_t[:, :width], ds_own) + dot_nn(keys_other_t[:, :width], ds_other)
        dq = (dq * SCALE).T.astype(jnp.bfloat16)
        dq_ref[tile * step : upto] = dq.reshape(step, tok, HD)
        terms = (
            (dk_own, dot_nn(ds_own, queries)),
            (dk_other, dot_nn(ds_other, queries)),
            (dv_own, dot_nt(own.astype(jnp.bfloat16), douts_t)),
            (dv_other, dot_nt(other.astype(jnp.bfloat16), douts_t)),
        )
        for total, term in terms:
            if tile == tiles - 1:
                total[...] = term
            else:
                total[0:width] += term
        for i in range(step):
            lora = dout_ref[tile * step + i, HD : HD + low_rank, :]
            attn = attn_ref[:, at + i * tok : at + (i + 1) * tok]
            down_total += dot_nt(lora, attn)
    shape = (blocks, tok, HD)
    dk_own_ref[...] = (dk_own[...] * SCALE).reshape(shape)
    dv_own_ref[...] = dv_own[...].reshape(shape)
    pair_other_ref[:, 0:tok, :] = (dk_other[...] * SCALE).astype(jnp.bfloat16).reshape(shape)
    pair_other_ref[:, tok : 2 * tok, :] = dv_other[...].astype(jnp.bfloat16).reshape(shape)
    down_grad_ref[...] = 2.0 * down_total


def call_kernel(body, outs, scratch, flops, exps, *operands, limit=48):
    in_bytes = sum(x.size * x.dtype.itemsize for x in operands)
    out_bytes = sum(x.size * x.dtype.itemsize for x in outs)
    specs = [pl.BlockSpec(memory_space=pltpu.SMEM)]
    specs += [pl.BlockSpec(memory_space=pltpu.VMEM)] * (len(operands) - 1)
    return pl.pallas_call(
        body,
        out_shape=outs,
        in_specs=specs,
        out_specs=[pl.BlockSpec(memory_space=pltpu.VMEM)] * len(outs),
        scratch_shapes=scratch,
        compiler_params=pltpu.CompilerParams(vmem_limit_bytes=limit * 1024 * 1024),
        cost_estimate=pl.CostEstimate(
            flops=flops,
            bytes_accessed=in_bytes + out_bytes,
            transcendentals=exps,
        ),
    )(*operands)


def shape_of(shape, dtype):
    return jax.ShapeDtypeStruct(shape, dtype)


def butterfly_sum(value, axis, bits, count):
    for bit in bits:
        pairs = [(i, i ^ bit) for i in range(count)]
        value = value.astype(jnp.bfloat16)
        taken = lax.ppermute(value, axis, pairs)
        value = value.astype(jnp.float32) + taken.astype(jnp.float32)
    return value


def powers_below(count):
    return [1 << n for n in range(count.bit_length() - 1)]


def message_kernel(copies, *refs):
    count = (len(refs) - 3) // 2
    operands, message_ref = refs[:count], refs[count]
    held, in_sems, out_sems = refs[count + 1 : -2], refs[-2], refs[-1]
    tok = operands[0].shape[0]
    arriving = [
        pltpu.make_async_copy(ref, to, in_sems.at[n])
        for n, (ref, to) in enumerate(zip(operands, held))
    ]
    for copy in arriving:
        copy.start()
    leaving = []
    for n, (copy, ref) in enumerate(zip(arriving, held)):
        copy.wait()
        for rank in range(message_ref.shape[0]):
            cols = pl.ds((rank // copies) * HD, HD)
            to = message_ref.at[rank, pl.ds(n * tok, tok), :]
            leaving.append(pltpu.make_async_copy(ref.at[:, cols], to, out_sems.at[len(leaving)]))
            leaving[-1].start()
    for copy in leaving:
        copy.wait()


def message_of(copies, ranks, *operands):
    tok = operands[0].shape[0]
    count = len(operands)
    shape = (ranks, count * tok, HD)
    return pl.pallas_call(
        functools.partial(message_kernel, copies),
        out_shape=shape_of(shape, operands[0].dtype),
        in_specs=[pl.BlockSpec(memory_space=pltpu.HBM)] * count,
        out_specs=pl.BlockSpec(memory_space=pltpu.HBM),
        scratch_shapes=[pltpu.VMEM(x.shape, x.dtype) for x in operands]
        + [pltpu.SemaphoreType.DMA((count,)), pltpu.SemaphoreType.DMA((ranks * count,))],
        cost_estimate=pl.CostEstimate(
            flops=0, bytes_accessed=4 * math.prod(shape), transcendentals=0
        ),
    )(*operands)


def unpack_kernel(copies, back_ref, *refs):
    out_refs, down_ref = refs[:3], refs[3] if len(refs) > 3 else None
    tok = out_refs[0].shape[0]
    for at_head in range(out_refs[0].shape[1] // HD):
        cols = slice(at_head * HD, (at_head + 1) * HD)
        for n, ref in enumerate(out_refs):
            ref[:, cols] = back_ref[at_head * copies, n * tok : (n + 1) * tok, :]
        if down_ref is not None:
            down_ref[:, cols] = back_ref[at_head * copies, 3 * tok :, :].astype(jnp.float32)


def in_vmem(body, outs, *operands):
    whole = pl.BlockSpec(memory_space=pltpu.VMEM)
    size = sum(x.size * x.dtype.itemsize for x in operands)
    size += sum(x.size * x.dtype.itemsize for x in outs)
    return pl.pallas_call(
        body,
        out_shape=outs,
        in_specs=[whole] * len(operands),
        out_specs=[whole] * len(outs),
        compiler_params=pltpu.CompilerParams(vmem_limit_bytes=16 * 1024 * 1024),
        cost_estimate=pl.CostEstimate(flops=0, bytes_accessed=size, transcendentals=0),
    )(*operands)


def dout_kernel(copies, own_ref, taken_ref, mid_ref, message_ref):
    low_rank = mid_ref.shape[1]
    feats = own_ref.shape[0] - low_rank
    lora = own_ref[feats:, :] + taken_ref[feats:, :].astype(jnp.float32)
    for rank in range(message_ref.shape[0]):
        at = pl.ds((rank // copies) * HD, HD)
        part = own_ref[at, :] + taken_ref[at, :].astype(jnp.float32)
        message_ref[rank, 0:HD, :] = part.astype(jnp.bfloat16)
        message_ref[rank, HD : HD + low_rank, :] = lora.astype(jnp.bfloat16)
        message_ref[rank, HD + low_rank : HD + 2 * low_rank, :] = mid_ref[rank]


def on_device(
    sizes,
    head_query_rows,
    head_key_rows,
    head_value_rows,
    output_gradient,
    output_matrix,
    adapter_down_weight,
    adapter_up_weight,
):
    seqs, heads, subs = sizes
    tok, feats = head_query_rows.shape
    cols = output_gradient.shape[1]
    low_rank = adapter_up_weight.shape[0]
    local_heads = feats // HD
    block_rows = tok * subs
    ranks = GROUP // block_rows
    copies = ranks // local_heads
    shift_blocks = GROUP // 2 // block_rows

    seq = lax.axis_index("seq")
    head = lax.axis_index("head")
    sub = lax.axis_index("sub")
    shifted = head >= heads // 2
    rank = (seq + shift_blocks) % ranks
    my_head = rank // copies

    groups = []
    for at_head in range(heads):
        for first in range(0, seqs, ranks):
            members = [first + shift_blocks + i for i in range(ranks)]
            if at_head < heads // 2:
                members = [first + (m - first) % ranks for m in members]
            members = [m % seqs for m in members]
            groups.append([m * heads + at_head for m in members])
    scalars = jnp.full((1,), sub, jnp.int32)

    def in_order(blocks):
        half = ranks // 2
        turned = jnp.concatenate((blocks[half:], blocks[:half]), axis=0)
        return jnp.where(shifted, blocks, turned)


    def exchange(parts):
        return lax.all_to_all(
            parts, ("seq", "head"), 0, 0, axis_index_groups=groups, tiled=True
        )

    def swap(value):
        if subs == 1:
            return value
        return lax.ppermute(value, "sub", [(0, 1), (1, 0)])

    sent = message_of(copies, ranks, head_query_rows, head_key_rows, head_value_rows)
    sent, output_gradient = lax.optimization_barrier((sent, output_gradient))
    own = exchange(sent)

    chunks = heads // subs
    pieces = []
    for k in range(heads):
        pairs = []
        for src_head in range(heads):
            for src_sub in range(subs):
                j = (src_head % chunks) * subs + src_sub
                dst = ((j + k) % heads) * subs + src_head // chunks
                pairs.append((src_head * subs + src_sub, dst))
        pieces.append(lax.ppermute(output_gradient, ("head", "sub"), pairs))

    up_half = lax.dynamic_slice_in_dim(adapter_up_weight, sub * chunks * cols, chunks * cols, 1)
    sources = [(head - k + heads) % heads for k in range(heads)]
    _, pieces = lax.optimization_barrier((own, pieces))

    def terms_of(rows, at):
        matrix, up = output_matrix, up_half
        if chunks > 1:
            matrix = lax.dynamic_slice_in_dim(matrix, at, cols, 1)
            up = lax.dynamic_slice_in_dim(up, at, cols, 1)
        lora = dot_nt(up, rows)
        grad = dot_nt(matrix, rows)
        grad += 2.0 * dot_nn(adapter_down_weight, lora.astype(jnp.bfloat16))
        return jnp.concatenate((grad, lora), axis=0)

    if chunks == 1:
        terms = jnp.split(terms_of(jnp.concatenate(pieces, axis=0), 0), heads, axis=1)
    else:
        terms = [terms_of(p, j // subs * cols) for p, j in zip(pieces, sources)]
    mine = [j % subs == sub for j in sources]
    packed_own = summed([jnp.where(m, t, 0.0) for m, t in zip(mine, terms)])
    packed_sent = summed([jnp.where(m, 0.0, t) for m, t in zip(mine, terms)])
    received = swap(packed_sent.astype(jnp.bfloat16))
    own = in_order(own)
    other = swap(own[:, tok:])

    down_head = lax.dynamic_slice_in_dim(adapter_down_weight, my_head * HD, HD, 0)
    rows = ranks * tok
    pair_count = rows * (rows + TILE)
    attn_t, middle_rows, stats = call_kernel(
        functools.partial(forward_kernel, tok),
        [
            shape_of((HD, rows), jnp.bfloat16),
            shape_of((low_rank, rows), jnp.float32),
            shape_of((8, rows), jnp.float32),
        ],
        [],
        4 * pair_count * HD,
        pair_count,
        scalars,
        own,
        other,
        down_head.T,
        limit=16,
    )

    first_copy = rank % copies == 0
    middle_rows = middle_rows.astype(jnp.bfloat16).reshape(low_rank, ranks, tok)
    middle_rows = in_order(middle_rows.transpose(1, 0, 2))
    if copies > 1:
        middle_rows = jnp.where(first_copy, middle_rows, 0.0)
    (message,) = in_vmem(
        functools.partial(dout_kernel, copies),
        [shape_of((ranks, HD + 2 * low_rank, tok), jnp.bfloat16)],
        packed_own,
        received,
        middle_rows,
    )
    arrived = exchange(message)
    middle = jnp.sum(arrived[:, HD + low_rank :].astype(jnp.float32), axis=0)
    bit = 1
    while bit < heads:
        middle += lax.ppermute(middle, "head", [(i, i ^ bit) for i in range(heads)])
        bit *= 2
    up_part = 2.0 * dot_nn(middle.astype(jnp.bfloat16), output_gradient)

    dq, dk_own, dv_own, pair_other, down_part = call_kernel(
        functools.partial(backward_kernel, tok),
        [
            shape_of((ranks, tok, HD), jnp.bfloat16),
            shape_of((ranks, tok, HD), jnp.float32),
            shape_of((ranks, tok, HD), jnp.float32),
            shape_of((ranks, 2 * tok, HD), jnp.bfloat16),
            shape_of((low_rank, HD), jnp.float32),
        ],
        [pltpu.VMEM((rows, HD), jnp.float32)] * 4,
        10 * pair_count * HD,
        pair_count,
        scalars,
        own,
        other,
        in_order(arrived[:, : HD + low_rank]),
        attn_t,
        stats,
        limit=28,
    )
    pair_other, _ = lax.optimization_barrier((pair_other, middle))
    pair_received = swap(pair_other).astype(jnp.float32)
    down_rows = jnp.where(first_copy, down_part + swap(down_part), 0.0)
    dk = (dk_own + pair_received[:, :tok]).astype(jnp.bfloat16)
    dv = (dv_own + pair_received[:, tok:]).astype(jnp.bfloat16)
    down_rows = jnp.broadcast_to(down_rows.astype(jnp.bfloat16), (ranks, low_rank, HD))
    back_message = jnp.concatenate([*map(in_order, (dq, dk, dv)), down_rows], axis=1)
    back = exchange(back_message)
    outs = [shape_of((tok, feats), back.dtype)] * 3
    if seqs == ranks:
        outs.append(shape_of((low_rank, feats), jnp.float32))
    outs = list(in_vmem(functools.partial(unpack_kernel, copies), outs, back))
    if seqs > ranks:
        bits = [bit for bit in powers_below(seqs) if bit >= ranks]
        down_terms = back[::copies, 3 * tok :].astype(jnp.float32)
        down_terms = butterfly_sum(down_terms, "seq", bits, seqs)
        outs.append(down_terms.transpose(1, 0, 2).reshape(low_rank, feats))
    query_gradient, key_gradient, value_gradient, down_gradient = outs

    up_sum = butterfly_sum(up_part, "seq", powers_below(seqs), seqs)
    _, up_sum = lax.optimization_barrier((back, up_sum))
    up_gradient = butterfly_sum(up_sum, "sub", powers_below(subs), subs)
    return (query_gradient, key_gradient, value_gradient, down_gradient.T, up_gradient)


def solution(mesh):
    rows = P(("rep", "seq", "sub"), "head")
    sizes = (mesh.shape["seq"], mesh.shape["head"], mesh.shape["sub"])
    return jax.shard_map(
        functools.partial(on_device, sizes),
        mesh=mesh,
        in_specs=(rows, rows, rows, rows, P("head", "sub"), P("head", None), P()),
        out_specs=(rows, rows, rows, P(("rep", "head"), None), P("rep", "head")),
        check_vma=False,
    )
```

```python
import functools
import math

import jax
import jax.numpy as jnp
from jax import lax
from jax.experimental import pallas as pl
from jax.experimental.pallas import tpu as pltpu
from jax.sharding import PartitionSpec as P

HD = 128
GROUP = 2048
TILE = 256
HIDDEN = -1e30
SCALE = HD ** (-0.5)
LOG2_SCALE = SCALE * math.log2(math.e)


def dot_nt(left, right):
    return lax.dot_general(
        left, right, (((1,), (1,)), ((), ())), preferred_element_type=jnp.float32
    )


def dot_nn(left, right):
    return jnp.dot(left, right, preferred_element_type=jnp.float32)


def rows_of(ref, blocks, first, count):
    return ref[0:blocks, first : first + count, :].reshape(blocks * count, HD)


def scores_of(keys, queries, visible):
    scores = dot_nt(keys, queries)
    head = scores.shape[0] - TILE
    tail = jnp.where(visible, scores[head:], HIDDEN)
    return tail if head == 0 else jnp.concatenate((scores[:head], tail), axis=0)


def own_visible():
    key_at = lax.broadcasted_iota(jnp.int32, (TILE, TILE), 0)
    return key_at <= lax.broadcasted_iota(jnp.int32, (TILE, TILE), 1)


def other_visible(sub, tok):
    key_at = lax.broadcasted_iota(jnp.int32, (TILE, TILE), 0)
    query_at = lax.broadcasted_iota(jnp.int32, (TILE, TILE), 1)
    return key_at // tok < query_at // tok + sub


def summed(terms):
    return functools.reduce(jnp.add, terms)


def forward_own_kernel(tok, scalar_ref, own_ref, total_ref, stat_ref):
    blocks = own_ref.shape[0]
    step = TILE // tok
    values_t = rows_of(own_ref, blocks, 2 * tok, tok).T
    for tile in range(blocks // step):
        upto = (tile + 1) * step
        at = tile * TILE
        queries = own_ref[tile * step : upto, 0:tok, :].reshape(TILE, HD)
        scores = scores_of(rows_of(own_ref, upto, tok, tok), queries, own_visible())
        highest = jnp.max(scores, axis=0, keepdims=True)
        powers = jnp.exp2((scores - highest) * LOG2_SCALE)
        total_ref[:, at : at + TILE] = dot_nn(
            values_t[:, : upto * tok], powers.astype(jnp.bfloat16)
        )
        stat_ref[0:1, at : at + TILE] = highest
        stat_ref[1:2, at : at + TILE] = jnp.sum(powers, axis=0, keepdims=True)


def forward_kernel(
    tok,
    scalar_ref,
    own_ref,
    other_ref,
    total_ref,
    own_stat_ref,
    down_t_ref,
    attn_ref,
    mid_ref,
    stat_ref,
):
    blocks = own_ref.shape[0]
    step = TILE // tok
    sub = scalar_ref[0]
    values_t = rows_of(other_ref, blocks, tok, tok).T
    for tile in range(blocks // step):
        upto = (tile + 1) * step
        at = tile * TILE
        here = pl.ds(at, TILE)
        queries = own_ref[tile * step : upto, 0:tok, :].reshape(TILE, HD)
        scores = scores_of(
            rows_of(other_ref, upto, 0, tok), queries, other_visible(sub, tok)
        )
        own_highest = own_stat_ref[0:1, here]
        highest = jnp.maximum(own_highest, jnp.max(scores, axis=0, keepdims=True))
        powers = jnp.exp2((scores - highest) * LOG2_SCALE)
        share = jnp.exp2((own_highest - highest) * LOG2_SCALE)
        inverse = 1.0 / (
            own_stat_ref[1:2, here] * share + jnp.sum(powers, axis=0, keepdims=True)
        )
        attn = dot_nn(values_t[:, : upto * tok], powers.astype(jnp.bfloat16))
        attn = ((attn + total_ref[:, here] * share) * inverse).astype(jnp.bfloat16)
        attn_ref[:, here] = attn
        mid_ref[:, here] = dot_nn(down_t_ref[...], attn)
        stat_ref[0:1, here] = highest
        stat_ref[1:2, here] = inverse


def backward_kernel(
    tok,
    scalar_ref,
    own_ref,
    other_ref,
    dout_ref,
    attn_ref,
    stat_ref,
    dq_ref,
    dk_own_ref,
    dv_own_ref,
    pair_other_ref,
    down_grad_ref,
    dk_own,
    dv_own,
    dk_other,
    dv_other,
):
    blocks = own_ref.shape[0]
    step = TILE // tok
    sub = scalar_ref[0]
    low_rank = down_grad_ref.shape[0]
    keys_own_t = rows_of(own_ref, blocks, tok, tok).T
    keys_other_t = rows_of(other_ref, blocks, 0, tok).T
    tiles = blocks // step
    down_total = jnp.zeros((low_rank, HD), jnp.float32)
    for tile in reversed(range(tiles)):
        upto = (tile + 1) * step
        width = upto * tok
        at = tile * TILE
        queries = own_ref[tile * step : upto, 0:tok, :].reshape(TILE, HD)
        douts_t = jnp.concatenate(
            [dout_ref[block, 0:HD, :] for block in range(tile * step, upto)], axis=1
        )
        highest = stat_ref[0:1, at : at + TILE]
        inverse = stat_ref[1:2, at : at + TILE]
        own = scores_of(rows_of(own_ref, upto, tok, tok), queries, own_visible())
        other = scores_of(
            rows_of(other_ref, upto, 0, tok), queries, other_visible(sub, tok)
        )
        own = jnp.exp2((own - highest) * LOG2_SCALE) * inverse
        other = jnp.exp2((other - highest) * LOG2_SCALE) * inverse
        dprob_own = dot_nn(rows_of(own_ref, upto, 2 * tok, tok), douts_t)
        dprob_other = dot_nn(rows_of(other_ref, upto, tok, tok), douts_t)
        delta = jnp.sum(own * dprob_own, axis=0, keepdims=True) + jnp.sum(
            other * dprob_other, axis=0, keepdims=True
        )
        ds_own = (own * (dprob_own - delta)).astype(jnp.bfloat16)
        ds_other = (other * (dprob_other - delta)).astype(jnp.bfloat16)
        dq = dot_nn(keys_own_t[:, :width], ds_own) + dot_nn(keys_other_t[:, :width], ds_other)
        dq = (dq * SCALE).T.astype(jnp.bfloat16)
        dq_ref[tile * step : upto] = dq.reshape(step, tok, HD)
        terms = (
            (dk_own, dot_nn(ds_own, queries)),
            (dk_other, dot_nn(ds_other, queries)),
            (dv_own, dot_nt(own.astype(jnp.bfloat16), douts_t)),
            (dv_other, dot_nt(other.astype(jnp.bfloat16), douts_t)),
        )
        for total, term in terms:
            if tile == tiles - 1:
                total[...] = term
            else:
                total[0:width] += term
        for i in range(step):
            lora = dout_ref[tile * step + i, HD : HD + low_rank, :]
            attn = attn_ref[:, at + i * tok : at + (i + 1) * tok]
            down_total += dot_nt(lora, attn)
    shape = (blocks, tok, HD)
    dk_own_ref[...] = (dk_own[...] * SCALE).reshape(shape)
    dv_own_ref[...] = dv_own[...].reshape(shape)
    pair_other_ref[:, 0:tok, :] = (dk_other[...] * SCALE).astype(jnp.bfloat16).reshape(shape)
    pair_other_ref[:, tok : 2 * tok, :] = dv_other[...].astype(jnp.bfloat16).reshape(shape)
    down_grad_ref[...] = 2.0 * down_total


def call_kernel(body, outs, scratch, flops, exps, *operands, declared=None, limit=48):
    in_bytes = sum(x.size * x.dtype.itemsize for x in operands)
    out_bytes = sum(x.size * x.dtype.itemsize for x in outs)
    specs = [pl.BlockSpec(memory_space=pltpu.SMEM)]
    specs += [pl.BlockSpec(memory_space=pltpu.VMEM)] * (len(operands) - 1)
    return pl.pallas_call(
        body,
        out_shape=outs,
        in_specs=specs,
        out_specs=[pl.BlockSpec(memory_space=pltpu.VMEM)] * len(outs),
        scratch_shapes=scratch,
        compiler_params=pltpu.CompilerParams(vmem_limit_bytes=limit * 1024 * 1024),
        cost_estimate=pl.CostEstimate(
            flops=flops,
            bytes_accessed=declared or in_bytes + out_bytes,
            transcendentals=exps,
        ),
    )(*operands)


def shape_of(shape, dtype):
    return jax.ShapeDtypeStruct(shape, dtype)


def butterfly_sum(value, axis, bits, count):
    for bit in bits:
        pairs = [(i, i ^ bit) for i in range(count)]
        value = value.astype(jnp.bfloat16)
        taken = lax.ppermute(value, axis, pairs)
        value = value.astype(jnp.float32) + taken.astype(jnp.float32)
    return value


def powers_below(count):
    return [1 << n for n in range(count.bit_length() - 1)]


def message_kernel(copies, *refs):
    count = (len(refs) - 3) // 2
    operands, message_ref = refs[:count], refs[count]
    held, in_sems, out_sems = refs[count + 1 : -2], refs[-2], refs[-1]
    tok = operands[0].shape[0]
    arriving = [
        pltpu.make_async_copy(ref, to, in_sems.at[n])
        for n, (ref, to) in enumerate(zip(operands, held))
    ]
    for copy in arriving:
        copy.start()
    leaving = []
    for n, (copy, ref) in enumerate(zip(arriving, held)):
        copy.wait()
        for rank in range(message_ref.shape[0]):
            cols = pl.ds((rank // copies) * HD, HD)
            to = message_ref.at[rank, pl.ds(n * tok, tok), :]
            leaving.append(pltpu.make_async_copy(ref.at[:, cols], to, out_sems.at[len(leaving)]))
            leaving[-1].start()
    for copy in leaving:
        copy.wait()


def message_of(copies, ranks, *operands):
    tok = operands[0].shape[0]
    count = len(operands)
    shape = (ranks, count * tok, HD)
    return pl.pallas_call(
        functools.partial(message_kernel, copies),
        out_shape=shape_of(shape, operands[0].dtype),
        in_specs=[pl.BlockSpec(memory_space=pltpu.HBM)] * count,
        out_specs=pl.BlockSpec(memory_space=pltpu.HBM),
        scratch_shapes=[pltpu.VMEM(x.shape, x.dtype) for x in operands]
        + [pltpu.SemaphoreType.DMA((count,)), pltpu.SemaphoreType.DMA((ranks * count,))],
        cost_estimate=pl.CostEstimate(
            flops=0, bytes_accessed=4 * math.prod(shape), transcendentals=0
        ),
    )(*operands)


def unpack_kernel(copies, back_ref, *refs):
    out_refs, down_ref = refs[:3], refs[3] if len(refs) > 3 else None
    tok = out_refs[0].shape[0]
    for at_head in range(out_refs[0].shape[1] // HD):
        cols = slice(at_head * HD, (at_head + 1) * HD)
        for n, ref in enumerate(out_refs):
            ref[:, cols] = back_ref[at_head * copies, n * tok : (n + 1) * tok, :]
        if down_ref is not None:
            down_ref[:, cols] = back_ref[at_head * copies, 3 * tok :, :].astype(jnp.float32)


def in_vmem(body, outs, *operands):
    whole = pl.BlockSpec(memory_space=pltpu.VMEM)
    size = sum(x.size * x.dtype.itemsize for x in operands)
    size += sum(x.size * x.dtype.itemsize for x in outs)
    return pl.pallas_call(
        body,
        out_shape=outs,
        in_specs=[whole] * len(operands),
        out_specs=[whole] * len(outs),
        compiler_params=pltpu.CompilerParams(vmem_limit_bytes=16 * 1024 * 1024),
        cost_estimate=pl.CostEstimate(flops=0, bytes_accessed=size, transcendentals=0),
    )(*operands)


def cotangent_kernel(chunks, plan_ref, *refs):
    pieces, (matrix_ref, up_ref, own_ref, sent_ref) = refs[:-4], refs[-4:]
    tok, cols = pieces[0].shape
    feats, low_rank = matrix_ref.shape[0], up_ref.shape[0]
    count = len(pieces)
    if chunks == 1:
        stacks = [(jnp.concatenate([p[...] for p in pieces], axis=0), pl.ds(0, cols))]
    else:
        stacks = [
            (p[...], pl.ds(pl.multiple_of(plan_ref[count + k], HD), cols))
            for k, p in enumerate(pieces)
        ]
    mine = [plan_ref[k] == 1 for k in range(count)]
    for ref, here in ((matrix_ref, pl.ds(0, feats)), (up_ref, pl.ds(feats, low_rank))):
        terms = [dot_nt(ref[:, at], rows) for rows, at in stacks]
        parts = [t[:, i : i + tok] for t in terms for i in range(0, t.shape[1], tok)]
        own_ref[here, :] = summed([jnp.where(m, p, 0.0) for m, p in zip(mine, parts)])
        sent = summed([jnp.where(m, 0.0, p) for m, p in zip(mine, parts)])
        sent_ref[here, :] = sent.astype(jnp.bfloat16)


def dout_kernel(copies, own_ref, taken_ref, mid_ref, message_ref):
    low_rank = mid_ref.shape[1]
    feats = own_ref.shape[0] - low_rank
    lora = own_ref[feats:, :] + taken_ref[feats:, :].astype(jnp.float32)
    for rank in range(message_ref.shape[0]):
        at = pl.ds((rank // copies) * HD, HD)
        part = own_ref[at, :] + taken_ref[at, :].astype(jnp.float32)
        message_ref[rank, 0:HD, :] = part.astype(jnp.bfloat16)
        message_ref[rank, HD : HD + low_rank, :] = lora.astype(jnp.bfloat16)
        message_ref[rank, HD + low_rank : HD + 2 * low_rank, :] = mid_ref[rank]


def on_device(
    sizes,
    head_query_rows,
    head_key_rows,
    head_value_rows,
    output_gradient,
    output_matrix,
    adapter_down_weight,
    adapter_up_weight,
):
    seqs, heads, subs = sizes
    tok, feats = head_query_rows.shape
    cols = output_gradient.shape[1]
    low_rank = adapter_up_weight.shape[0]
    local_heads = feats // HD
    block_rows = tok * subs
    ranks = GROUP // block_rows
    copies = ranks // local_heads
    shift_blocks = GROUP // 2 // block_rows

    seq = lax.axis_index("seq")
    head = lax.axis_index("head")
    sub = lax.axis_index("sub")
    shifted = head >= heads // 2
    rank = (seq + shift_blocks) % ranks
    my_head = rank // copies

    groups = []
    for at_head in range(heads):
        for first in range(0, seqs, ranks):
            members = [first + shift_blocks + i for i in range(ranks)]
            if at_head < heads // 2:
                members = [first + (m - first) % ranks for m in members]
            members = [m % seqs for m in members]
            groups.append([m * heads + at_head for m in members])
    scalars = jnp.full((1,), sub, jnp.int32)

    def in_order(blocks):
        half = ranks // 2
        turned = jnp.concatenate((blocks[half:], blocks[:half]), axis=0)
        return jnp.where(shifted, blocks, turned)


    def exchange(parts):
        return lax.all_to_all(
            parts, ("seq", "head"), 0, 0, axis_index_groups=groups, tiled=True
        )

    def swap(value):
        if subs == 1:
            return value
        return lax.ppermute(value, "sub", [(0, 1), (1, 0)])

    sent = message_of(copies, ranks, head_query_rows, head_key_rows, head_value_rows)
    sent, output_gradient, output_matrix = lax.optimization_barrier(
        (sent, output_gradient, output_matrix)
    )
    own = exchange(sent)

    chunks = heads // subs
    pieces = []
    for k in range(heads):
        pairs = []
        for src_head in range(heads):
            for src_sub in range(subs):
                j = (src_head % chunks) * subs + src_sub
                dst = ((j + k) % heads) * subs + src_head // chunks
                pairs.append((src_head * subs + src_sub, dst))
        pieces.append(lax.ppermute(output_gradient, ("head", "sub"), pairs))

    up_half = lax.dynamic_slice_in_dim(adapter_up_weight, sub * chunks * cols, chunks * cols, 1)
    folded = dot_nn(adapter_down_weight, up_half)
    folded = (output_matrix.astype(jnp.float32) + 2.0 * folded).astype(jnp.bfloat16)
    sources = [(head - k + heads) % heads for k in range(heads)]
    plan = [(j % subs == sub).astype(jnp.int32) for j in sources]
    plan += [(j // subs * cols).astype(jnp.int32) for j in sources]
    packed_own, packed_sent = call_kernel(
        functools.partial(cotangent_kernel, chunks),
        [
            shape_of((feats + low_rank, tok), jnp.float32),
            shape_of((feats + low_rank, tok), jnp.bfloat16),
        ],
        [],
        0,
        0,
        jnp.stack(plan),
        *pieces,
        folded,
        up_half,
        declared=1024,
        limit=16,
    )
    received = swap(packed_sent)
    own, _ = lax.optimization_barrier((own, packed_sent))
    own = in_order(own)
    other = swap(own[:, tok:])

    down_head = lax.dynamic_slice_in_dim(adapter_down_weight, my_head * HD, HD, 0)
    rows = ranks * tok
    pair_count = rows * (rows + TILE)
    own_total, own_stats = call_kernel(
        functools.partial(forward_own_kernel, tok),
        [shape_of((HD, rows), jnp.float32), shape_of((8, rows), jnp.float32)],
        [],
        2 * pair_count * HD,
        pair_count // 2,
        scalars,
        own,
        limit=16,
    )
    attn_t, middle_rows, stats = call_kernel(
        functools.partial(forward_kernel, tok),
        [
            shape_of((HD, rows), jnp.bfloat16),
            shape_of((low_rank, rows), jnp.float32),
            shape_of((8, rows), jnp.float32),
        ],
        [],
        2 * pair_count * HD,
        pair_count // 2,
        scalars,
        own,
        other,
        own_total,
        own_stats,
        down_head.T,
        limit=16,
    )

    first_copy = rank % copies == 0
    middle_rows = middle_rows.astype(jnp.bfloat16).reshape(low_rank, ranks, tok)
    middle_rows = in_order(middle_rows.transpose(1, 0, 2))
    if copies > 1:
        middle_rows = jnp.where(first_copy, middle_rows, 0.0)
    (message,) = in_vmem(
        functools.partial(dout_kernel, copies),
        [shape_of((ranks, HD + 2 * low_rank, tok), jnp.bfloat16)],
        packed_own,
        received,
        middle_rows,
    )
    arrived = exchange(message)
    middle = jnp.sum(arrived[:, HD + low_rank :].astype(jnp.float32), axis=0)
    bit = 1
    while bit < heads:
        middle += lax.ppermute(middle, "head", [(i, i ^ bit) for i in range(heads)])
        bit *= 2
    up_part = 2.0 * dot_nn(middle.astype(jnp.bfloat16), output_gradient)

    dq, dk_own, dv_own, pair_other, down_part = call_kernel(
        functools.partial(backward_kernel, tok),
        [
            shape_of((ranks, tok, HD), jnp.bfloat16),
            shape_of((ranks, tok, HD), jnp.float32),
            shape_of((ranks, tok, HD), jnp.float32),
            shape_of((ranks, 2 * tok, HD), jnp.bfloat16),
            shape_of((low_rank, HD), jnp.float32),
        ],
        [pltpu.VMEM((rows, HD), jnp.float32)] * 4,
        10 * pair_count * HD,
        pair_count,
        scalars,
        own,
        other,
        in_order(arrived[:, : HD + low_rank]),
        attn_t,
        stats,
        limit=28,
    )
    pair_other, _ = lax.optimization_barrier((pair_other, middle))
    pair_received = swap(pair_other).astype(jnp.float32)
    down_rows = jnp.where(first_copy, down_part + swap(down_part), 0.0)
    dk = (dk_own + pair_received[:, :tok]).astype(jnp.bfloat16)
    dv = (dv_own + pair_received[:, tok:]).astype(jnp.bfloat16)
    down_rows = jnp.broadcast_to(down_rows.astype(jnp.bfloat16), (ranks, low_rank, HD))
    back_message = jnp.concatenate([*map(in_order, (dq, dk, dv)), down_rows], axis=1)
    back = exchange(back_message)
    outs = [shape_of((tok, feats), back.dtype)] * 3
    if seqs == ranks:
        outs.append(shape_of((low_rank, feats), jnp.float32))
    outs = list(in_vmem(functools.partial(unpack_kernel, copies), outs, back))
    if seqs > ranks:
        bits = [bit for bit in powers_below(seqs) if bit >= ranks]
        down_terms = back[::copies, 3 * tok :].astype(jnp.float32)
        down_terms = butterfly_sum(down_terms, "seq", bits, seqs)
        outs.append(down_terms.transpose(1, 0, 2).reshape(low_rank, feats))
    query_gradient, key_gradient, value_gradient, down_gradient = outs

    bits = powers_below(seqs)
    up_sum = butterfly_sum(up_part, "seq", bits[:1] + bits[:0:-1], seqs)
    _, up_sum = lax.optimization_barrier((back, up_sum))
    up_gradient = butterfly_sum(up_sum, "sub", powers_below(subs), subs)
    return (query_gradient, key_gradient, value_gradient, down_gradient.T, up_gradient)


def solution(mesh):
    rows = P(("rep", "seq", "sub"), "head")
    sizes = (mesh.shape["seq"], mesh.shape["head"], mesh.shape["sub"])
    return jax.shard_map(
        functools.partial(on_device, sizes),
        mesh=mesh,
        in_specs=(rows, rows, rows, rows, P("head", "sub"), P("head", None), P()),
        out_specs=(rows, rows, rows, P(("rep", "head"), None), P("rep", "head")),
        check_vma=False,
    )
```

```python
import functools
import math

import jax
import jax.numpy as jnp
from jax import lax
from jax.experimental import pallas as pl
from jax.experimental.pallas import tpu as pltpu
from jax.sharding import PartitionSpec as P

HD = 128
GROUP = 2048
TILE = 256
HIDDEN = -1e30
SCALE = HD ** (-0.5)
LOG2_SCALE = SCALE * math.log2(math.e)


def dot_nt(left, right):
    return lax.dot_general(
        left, right, (((1,), (1,)), ((), ())), preferred_element_type=jnp.float32
    )


def dot_nn(left, right):
    return jnp.dot(left, right, preferred_element_type=jnp.float32)


def rows_of(ref, blocks, first, count):
    return ref[0:blocks, first : first + count, :].reshape(blocks * count, HD)


def scores_of(keys, queries, visible):
    scores = dot_nt(keys, queries)
    head = scores.shape[0] - TILE
    tail = jnp.where(visible, scores[head:], HIDDEN)
    return tail if head == 0 else jnp.concatenate((scores[:head], tail), axis=0)


def tile_index(dimension):
    shape = (TILE, 1) if dimension == 0 else (1, TILE)
    return lax.broadcasted_iota(jnp.int32, shape, dimension)


def own_visible():
    return tile_index(0) <= tile_index(1)


def other_visible(sub, tok):
    return tile_index(0) // tok < tile_index(1) // tok + sub


def summed(terms):
    return functools.reduce(jnp.add, terms)


def forward_own_kernel(tok, scalar_ref, own_ref, total_ref, stat_ref):
    blocks = own_ref.shape[0]
    step = TILE // tok
    values_t = rows_of(own_ref, blocks, 2 * tok, tok).T
    for tile in range(blocks // step):
        upto = (tile + 1) * step
        at = tile * TILE
        queries = own_ref[tile * step : upto, 0:tok, :].reshape(TILE, HD)
        scores = scores_of(rows_of(own_ref, upto, tok, tok), queries, own_visible())
        highest = jnp.max(scores, axis=0, keepdims=True)
        powers = jnp.exp2((scores - highest) * LOG2_SCALE)
        total_ref[:, at : at + TILE] = dot_nn(
            values_t[:, : upto * tok], powers.astype(jnp.bfloat16)
        )
        stat_ref[0:1, at : at + TILE] = highest
        stat_ref[1:2, at : at + TILE] = jnp.sum(powers, axis=0, keepdims=True)


def forward_kernel(
    tok,
    scalar_ref,
    own_ref,
    other_ref,
    total_ref,
    own_stat_ref,
    down_t_ref,
    attn_ref,
    mid_ref,
    stat_ref,
):
    blocks = own_ref.shape[0]
    step = TILE // tok
    sub = scalar_ref[0]
    values_t = rows_of(other_ref, blocks, tok, tok).T
    for tile in range(blocks // step):
        upto = (tile + 1) * step
        at = tile * TILE
        here = pl.ds(at, TILE)
        queries = own_ref[tile * step : upto, 0:tok, :].reshape(TILE, HD)
        scores = scores_of(
            rows_of(other_ref, upto, 0, tok), queries, other_visible(sub, tok)
        )
        own_highest = own_stat_ref[0:1, here]
        highest = jnp.maximum(own_highest, jnp.max(scores, axis=0, keepdims=True))
        powers = jnp.exp2((scores - highest) * LOG2_SCALE)
        share = jnp.exp2((own_highest - highest) * LOG2_SCALE)
        inverse = 1.0 / (
            own_stat_ref[1:2, here] * share + jnp.sum(powers, axis=0, keepdims=True)
        )
        attn = dot_nn(values_t[:, : upto * tok], powers.astype(jnp.bfloat16))
        attn = ((attn + total_ref[:, here] * share) * inverse).astype(jnp.bfloat16)
        attn_ref[:, here] = attn
        mid_ref[:, here] = dot_nn(down_t_ref[...], attn)
        stat_ref[0:1, here] = highest
        stat_ref[1:2, here] = inverse


def backward_kernel(
    tok,
    scalar_ref,
    own_ref,
    other_ref,
    dout_ref,
    attn_ref,
    stat_ref,
    dq_ref,
    dk_own_ref,
    dv_own_ref,
    pair_other_ref,
    down_grad_ref,
    dk_own,
    dv_own,
    dk_other,
    dv_other,
):
    blocks = own_ref.shape[0]
    step = TILE // tok
    sub = scalar_ref[0]
    low_rank = down_grad_ref.shape[0]
    keys_own_t = rows_of(own_ref, blocks, tok, tok).T
    keys_other_t = rows_of(other_ref, blocks, 0, tok).T
    tiles = blocks // step
    down_total = jnp.zeros((low_rank, HD), jnp.float32)
    for tile in reversed(range(tiles)):
        upto = (tile + 1) * step
        width = upto * tok
        at = tile * TILE
        queries = own_ref[tile * step : upto, 0:tok, :].reshape(TILE, HD)
        douts_t = jnp.concatenate(
            [dout_ref[block, 0:HD, :] for block in range(tile * step, upto)], axis=1
        )
        highest = stat_ref[0:1, at : at + TILE]
        inverse = stat_ref[1:2, at : at + TILE]
        own = scores_of(rows_of(own_ref, upto, tok, tok), queries, own_visible())
        other = scores_of(
            rows_of(other_ref, upto, 0, tok), queries, other_visible(sub, tok)
        )
        own = jnp.exp2((own - highest) * LOG2_SCALE) * inverse
        other = jnp.exp2((other - highest) * LOG2_SCALE) * inverse
        dprob_own = dot_nn(rows_of(own_ref, upto, 2 * tok, tok), douts_t)
        dprob_other = dot_nn(rows_of(other_ref, upto, tok, tok), douts_t)
        delta = jnp.sum(own * dprob_own, axis=0, keepdims=True) + jnp.sum(
            other * dprob_other, axis=0, keepdims=True
        )
        ds_own = (own * (dprob_own - delta)).astype(jnp.bfloat16)
        ds_other = (other * (dprob_other - delta)).astype(jnp.bfloat16)
        dq = dot_nn(keys_own_t[:, :width], ds_own) + dot_nn(keys_other_t[:, :width], ds_other)
        dq = (dq * SCALE).T.astype(jnp.bfloat16)
        dq_ref[tile * step : upto] = dq.reshape(step, tok, HD)
        terms = (
            (dk_own, dot_nn(ds_own, queries)),
            (dk_other, dot_nn(ds_other, queries)),
            (dv_own, dot_nt(own.astype(jnp.bfloat16), douts_t)),
            (dv_other, dot_nt(other.astype(jnp.bfloat16), douts_t)),
        )
        for total, term in terms:
            if tile == tiles - 1:
                total[...] = term
            else:
                total[0:width] += term
        for i in range(step):
            lora = dout_ref[tile * step + i, HD : HD + low_rank, :]
            attn = attn_ref[:, at + i * tok : at + (i + 1) * tok]
            down_total += dot_nt(lora, attn)
    shape = (blocks, tok, HD)
    dk_own_ref[...] = (dk_own[...] * SCALE).reshape(shape)
    dv_own_ref[...] = dv_own[...].reshape(shape)
    pair_other_ref[:, 0:tok, :] = (dk_other[...] * SCALE).astype(jnp.bfloat16).reshape(shape)
    pair_other_ref[:, tok : 2 * tok, :] = dv_other[...].astype(jnp.bfloat16).reshape(shape)
    down_grad_ref[...] = 2.0 * down_total


def call_kernel(body, outs, scratch, flops, exps, *operands, declared=None, limit=48):
    in_bytes = sum(x.size * x.dtype.itemsize for x in operands)
    out_bytes = sum(x.size * x.dtype.itemsize for x in outs)
    specs = [pl.BlockSpec(memory_space=pltpu.SMEM)]
    specs += [pl.BlockSpec(memory_space=pltpu.VMEM)] * (len(operands) - 1)
    return pl.pallas_call(
        body,
        out_shape=outs,
        in_specs=specs,
        out_specs=[pl.BlockSpec(memory_space=pltpu.VMEM)] * len(outs),
        scratch_shapes=scratch,
        compiler_params=pltpu.CompilerParams(vmem_limit_bytes=limit * 1024 * 1024),
        cost_estimate=pl.CostEstimate(
            flops=flops,
            bytes_accessed=declared or in_bytes + out_bytes,
            transcendentals=exps,
        ),
    )(*operands)


def shape_of(shape, dtype):
    return jax.ShapeDtypeStruct(shape, dtype)


def butterfly_sum(value, axis, bits, count):
    for bit in bits:
        pairs = [(i, i ^ bit) for i in range(count)]
        value = value.astype(jnp.bfloat16)
        taken = lax.ppermute(value, axis, pairs)
        value = value.astype(jnp.float32) + taken.astype(jnp.float32)
    return value


def powers_below(count):
    return [1 << n for n in range(count.bit_length() - 1)]


def message_kernel(copies, *refs):
    count = (len(refs) - 3) // 2
    operands, message_ref = refs[:count], refs[count]
    held, in_sems, out_sems = refs[count + 1 : -2], refs[-2], refs[-1]
    tok = operands[0].shape[0]
    arriving = [
        pltpu.make_async_copy(ref, to, in_sems.at[n])
        for n, (ref, to) in enumerate(zip(operands, held))
    ]
    for copy in arriving:
        copy.start()
    leaving = []
    for n, (copy, ref) in enumerate(zip(arriving, held)):
        copy.wait()
        for rank in range(message_ref.shape[0]):
            cols = pl.ds((rank // copies) * HD, HD)
            to = message_ref.at[rank, pl.ds(n * tok, tok), :]
            leaving.append(pltpu.make_async_copy(ref.at[:, cols], to, out_sems.at[len(leaving)]))
            leaving[-1].start()
    for copy in leaving:
        copy.wait()


def message_of(copies, ranks, *operands):
    tok = operands[0].shape[0]
    count = len(operands)
    shape = (ranks, count * tok, HD)
    return pl.pallas_call(
        functools.partial(message_kernel, copies),
        out_shape=shape_of(shape, operands[0].dtype),
        in_specs=[pl.BlockSpec(memory_space=pltpu.HBM)] * count,
        out_specs=pl.BlockSpec(memory_space=pltpu.HBM),
        scratch_shapes=[pltpu.VMEM(x.shape, x.dtype) for x in operands]
        + [pltpu.SemaphoreType.DMA((count,)), pltpu.SemaphoreType.DMA((ranks * count,))],
        cost_estimate=pl.CostEstimate(
            flops=0, bytes_accessed=4 * math.prod(shape), transcendentals=0
        ),
    )(*operands)


def unpack_kernel(copies, back_ref, *refs):
    out_refs, down_ref = refs[:3], refs[3] if len(refs) > 3 else None
    tok = out_refs[0].shape[0]
    for at_head in range(out_refs[0].shape[1] // HD):
        cols = slice(at_head * HD, (at_head + 1) * HD)
        for n, ref in enumerate(out_refs):
            ref[:, cols] = back_ref[at_head * copies, n * tok : (n + 1) * tok, :]
        if down_ref is not None:
            down_ref[:, cols] = back_ref[at_head * copies, 3 * tok :, :].astype(jnp.float32)


def in_vmem(body, outs, *operands):
    whole = pl.BlockSpec(memory_space=pltpu.VMEM)
    size = sum(x.size * x.dtype.itemsize for x in operands)
    size += sum(x.size * x.dtype.itemsize for x in outs)
    return pl.pallas_call(
        body,
        out_shape=outs,
        in_specs=[whole] * len(operands),
        out_specs=[whole] * len(outs),
        compiler_params=pltpu.CompilerParams(vmem_limit_bytes=16 * 1024 * 1024),
        cost_estimate=pl.CostEstimate(flops=0, bytes_accessed=size, transcendentals=0),
    )(*operands)


def cotangent_kernel(chunks, plan_ref, *refs):
    pieces, (matrix_ref, up_ref, own_ref, sent_ref) = refs[:-4], refs[-4:]
    tok, cols = pieces[0].shape
    feats, low_rank = matrix_ref.shape[0], up_ref.shape[0]
    count = len(pieces)
    if chunks == 1:
        stacks = [(jnp.concatenate([p[...] for p in pieces], axis=0), pl.ds(0, cols))]
    else:
        stacks = [
            (p[...], pl.ds(pl.multiple_of(plan_ref[count + k], HD), cols))
            for k, p in enumerate(pieces)
        ]
    mine = [plan_ref[k] == 1 for k in range(count)]
    for ref, here in ((matrix_ref, pl.ds(0, feats)), (up_ref, pl.ds(feats, low_rank))):
        terms = [dot_nt(ref[:, at], rows) for rows, at in stacks]
        parts = [t[:, i : i + tok] for t in terms for i in range(0, t.shape[1], tok)]
        own_ref[here, :] = summed([jnp.where(m, p, 0.0) for m, p in zip(mine, parts)])
        sent = summed([jnp.where(m, 0.0, p) for m, p in zip(mine, parts)])
        sent_ref[here, :] = sent.astype(jnp.bfloat16)


def dout_kernel(copies, own_ref, taken_ref, mid_ref, message_ref):
    low_rank = mid_ref.shape[1]
    feats = own_ref.shape[0] - low_rank
    lora = own_ref[feats:, :] + taken_ref[feats:, :].astype(jnp.float32)
    for rank in range(message_ref.shape[0]):
        at = pl.ds((rank // copies) * HD, HD)
        part = own_ref[at, :] + taken_ref[at, :].astype(jnp.float32)
        message_ref[rank, 0:HD, :] = part.astype(jnp.bfloat16)
        message_ref[rank, HD : HD + low_rank, :] = lora.astype(jnp.bfloat16)
        message_ref[rank, HD + low_rank : HD + 2 * low_rank, :] = mid_ref[rank]


def on_device(
    sizes,
    head_query_rows,
    head_key_rows,
    head_value_rows,
    output_gradient,
    output_matrix,
    adapter_down_weight,
    adapter_up_weight,
):
    seqs, heads, subs = sizes
    tok, feats = head_query_rows.shape
    cols = output_gradient.shape[1]
    low_rank = adapter_up_weight.shape[0]
    local_heads = feats // HD
    block_rows = tok * subs
    ranks = GROUP // block_rows
    copies = ranks // local_heads
    shift_blocks = GROUP // 2 // block_rows

    seq = lax.axis_index("seq")
    head = lax.axis_index("head")
    sub = lax.axis_index("sub")
    shifted = head >= heads // 2
    rank = (seq + shift_blocks) % ranks
    my_head = rank // copies

    groups = []
    for at_head in range(heads):
        for first in range(0, seqs, ranks):
            members = [first + shift_blocks + i for i in range(ranks)]
            if at_head < heads // 2:
                members = [first + (m - first) % ranks for m in members]
            members = [m % seqs for m in members]
            groups.append([m * heads + at_head for m in members])
    scalars = jnp.full((1,), sub, jnp.int32)

    def in_order(blocks):
        half = ranks // 2
        turned = jnp.concatenate((blocks[half:], blocks[:half]), axis=0)
        return jnp.where(shifted, blocks, turned)


    def exchange(parts):
        return lax.all_to_all(
            parts, ("seq", "head"), 0, 0, axis_index_groups=groups, tiled=True
        )

    def swap(value):
        if subs == 1:
            return value
        return lax.ppermute(value, "sub", [(0, 1), (1, 0)])

    sent = message_of(copies, ranks, head_query_rows, head_key_rows, head_value_rows)
    sent, output_gradient, output_matrix = lax.optimization_barrier(
        (sent, output_gradient, output_matrix)
    )
    own = exchange(sent)

    chunks = heads // subs
    pieces = []
    for k in range(heads):
        pairs = []
        for src_head in range(heads):
            for src_sub in range(subs):
                j = (src_head % chunks) * subs + src_sub
                dst = ((j + k) % heads) * subs + src_head // chunks
                pairs.append((src_head * subs + src_sub, dst))
        pieces.append(lax.ppermute(output_gradient, ("head", "sub"), pairs))

    up_half = lax.dynamic_slice_in_dim(adapter_up_weight, sub * chunks * cols, chunks * cols, 1)
    folded = dot_nn(adapter_down_weight, up_half)
    folded = (output_matrix.astype(jnp.float32) + 2.0 * folded).astype(jnp.bfloat16)
    sources = [(head - k + heads) % heads for k in range(heads)]
    plan = [(j % subs == sub).astype(jnp.int32) for j in sources]
    plan += [(j // subs * cols).astype(jnp.int32) for j in sources]
    packed_own, packed_sent = call_kernel(
        functools.partial(cotangent_kernel, chunks),
        [
            shape_of((feats + low_rank, tok), jnp.float32),
            shape_of((feats + low_rank, tok), jnp.bfloat16),
        ],
        [],
        0,
        0,
        jnp.stack(plan),
        *pieces,
        folded,
        up_half,
        declared=1024,
        limit=16,
    )
    received = swap(packed_sent)
    down_head = lax.dynamic_slice_in_dim(adapter_down_weight, my_head * HD, HD, 0).T
    own, down_head, _ = lax.optimization_barrier((own, down_head, packed_sent))
    own = in_order(own)
    other = swap(own[:, tok:])

    rows = ranks * tok
    pair_count = rows * (rows + TILE)
    own_total, own_stats = call_kernel(
        functools.partial(forward_own_kernel, tok),
        [shape_of((HD, rows), jnp.float32), shape_of((8, rows), jnp.float32)],
        [],
        2 * pair_count * HD,
        pair_count // 2,
        scalars,
        own,
        limit=16,
    )
    attn_t, middle_rows, stats = call_kernel(
        functools.partial(forward_kernel, tok),
        [
            shape_of((HD, rows), jnp.bfloat16),
            shape_of((low_rank, rows), jnp.float32),
            shape_of((8, rows), jnp.float32),
        ],
        [],
        2 * pair_count * HD,
        pair_count // 2,
        scalars,
        own,
        other,
        own_total,
        own_stats,
        down_head,
        limit=16,
    )

    first_copy = rank % copies == 0
    middle_rows = middle_rows.astype(jnp.bfloat16).reshape(low_rank, ranks, tok)
    middle_rows = in_order(middle_rows.transpose(1, 0, 2))
    if copies > 1:
        middle_rows = jnp.where(first_copy, middle_rows, 0.0)
    (message,) = in_vmem(
        functools.partial(dout_kernel, copies),
        [shape_of((ranks, HD + 2 * low_rank, tok), jnp.bfloat16)],
        packed_own,
        received,
        middle_rows,
    )
    arrived = exchange(message)
    middle = jnp.sum(arrived[:, HD + low_rank :].astype(jnp.float32), axis=0)
    bit = 1
    while bit < heads:
        middle += lax.ppermute(middle, "head", [(i, i ^ bit) for i in range(heads)])
        bit *= 2
    up_part = 2.0 * dot_nn(middle.astype(jnp.bfloat16), output_gradient)

    dq, dk_own, dv_own, pair_other, down_part = call_kernel(
        functools.partial(backward_kernel, tok),
        [
            shape_of((ranks, tok, HD), jnp.bfloat16),
            shape_of((ranks, tok, HD), jnp.float32),
            shape_of((ranks, tok, HD), jnp.float32),
            shape_of((ranks, 2 * tok, HD), jnp.bfloat16),
            shape_of((low_rank, HD), jnp.float32),
        ],
        [pltpu.VMEM((rows, HD), jnp.float32)] * 4,
        10 * pair_count * HD,
        pair_count,
        scalars,
        own,
        other,
        in_order(arrived[:, : HD + low_rank]),
        attn_t,
        stats,
        limit=28,
    )
    pair_other, _ = lax.optimization_barrier((pair_other, middle))
    pair_received = swap(pair_other).astype(jnp.float32)
    down_rows = jnp.where(first_copy, down_part + swap(down_part), 0.0)
    dk = (dk_own + pair_received[:, :tok]).astype(jnp.bfloat16)
    dv = (dv_own + pair_received[:, tok:]).astype(jnp.bfloat16)
    down_rows = jnp.broadcast_to(down_rows.astype(jnp.bfloat16), (ranks, low_rank, HD))
    back_message = jnp.concatenate([*map(in_order, (dq, dk, dv)), down_rows], axis=1)
    back = exchange(back_message)
    outs = [shape_of((tok, feats), back.dtype)] * 3
    if seqs == ranks:
        outs.append(shape_of((low_rank, feats), jnp.float32))
    outs = list(in_vmem(functools.partial(unpack_kernel, copies), outs, back))
    if seqs > ranks:
        bits = [bit for bit in powers_below(seqs) if bit >= ranks]
        down_terms = back[::copies, 3 * tok :].astype(jnp.float32)
        down_terms = butterfly_sum(down_terms, "seq", bits, seqs)
        outs.append(down_terms.transpose(1, 0, 2).reshape(low_rank, feats))
    query_gradient, key_gradient, value_gradient, down_gradient = outs

    up_sum = butterfly_sum(up_part, "seq", powers_below(seqs), seqs)
    _, up_sum = lax.optimization_barrier((back, up_sum))
    up_gradient = butterfly_sum(up_sum, "sub", powers_below(subs), subs)
    return (query_gradient, key_gradient, value_gradient, down_gradient.T, up_gradient)


def solution(mesh):
    rows = P(("rep", "seq", "sub"), "head")
    sizes = (mesh.shape["seq"], mesh.shape["head"], mesh.shape["sub"])
    return jax.shard_map(
        functools.partial(on_device, sizes),
        mesh=mesh,
        in_specs=(rows, rows, rows, rows, P("head", "sub"), P("head", None), P()),
        out_specs=(rows, rows, rows, P(("rep", "head"), None), P("rep", "head")),
        check_vma=False,
    )
```

```python
import functools
import math

import jax
import jax.numpy as jnp
from jax import lax
from jax.experimental import pallas as pl
from jax.experimental.pallas import tpu as pltpu
from jax.sharding import PartitionSpec as P

HD = 128
GROUP = 2048
TILE = 256
HIDDEN = -1e30
SCALE = HD ** (-0.5)
LOG2_SCALE = SCALE * math.log2(math.e)


def dot_nt(left, right):
    return lax.dot_general(
        left, right, (((1,), (1,)), ((), ())), preferred_element_type=jnp.float32
    )


def dot_nn(left, right):
    return jnp.dot(left, right, preferred_element_type=jnp.float32)


def rows_of(ref, blocks, first, count):
    return ref[0:blocks, first : first + count, :].reshape(blocks * count, HD)


def scores_of(keys, queries, visible):
    scores = dot_nt(keys, queries)
    head = scores.shape[0] - TILE
    tail = jnp.where(visible, scores[head:], HIDDEN)
    return tail if head == 0 else jnp.concatenate((scores[:head], tail), axis=0)


def tile_index(dimension):
    shape = (TILE, 1) if dimension == 0 else (1, TILE)
    return lax.broadcasted_iota(jnp.int32, shape, dimension)


def own_visible():
    return tile_index(0) <= tile_index(1)


def other_visible(sub, tok):
    return tile_index(0) // tok < tile_index(1) // tok + sub


def summed(terms):
    return functools.reduce(jnp.add, terms)


def forward_own_kernel(tok, scalar_ref, own_ref, total_ref, stat_ref):
    blocks = own_ref.shape[0]
    step = TILE // tok
    values_t = rows_of(own_ref, blocks, 2 * tok, tok).T
    for tile in range(blocks // step):
        upto = (tile + 1) * step
        at = tile * TILE
        queries = own_ref[tile * step : upto, 0:tok, :].reshape(TILE, HD)
        scores = scores_of(rows_of(own_ref, upto, tok, tok), queries, own_visible())
        highest = jnp.max(scores, axis=0, keepdims=True)
        powers = jnp.exp2((scores - highest) * LOG2_SCALE)
        total_ref[:, at : at + TILE] = dot_nn(
            values_t[:, : upto * tok], powers.astype(jnp.bfloat16)
        )
        stat_ref[0:1, at : at + TILE] = highest
        stat_ref[1:2, at : at + TILE] = jnp.sum(powers, axis=0, keepdims=True)


def forward_kernel(
    tok,
    scalar_ref,
    own_ref,
    other_ref,
    total_ref,
    own_stat_ref,
    down_t_ref,
    attn_ref,
    mid_ref,
    stat_ref,
):
    blocks = own_ref.shape[0]
    step = TILE // tok
    sub = scalar_ref[0]
    values_t = rows_of(other_ref, blocks, tok, tok).T
    for tile in range(blocks // step):
        upto = (tile + 1) * step
        at = tile * TILE
        here = pl.ds(at, TILE)
        queries = own_ref[tile * step : upto, 0:tok, :].reshape(TILE, HD)
        scores = scores_of(
            rows_of(other_ref, upto, 0, tok), queries, other_visible(sub, tok)
        )
        own_highest = own_stat_ref[0:1, here]
        highest = jnp.maximum(own_highest, jnp.max(scores, axis=0, keepdims=True))
        powers = jnp.exp2((scores - highest) * LOG2_SCALE)
        share = jnp.exp2((own_highest - highest) * LOG2_SCALE)
        inverse = 1.0 / (
            own_stat_ref[1:2, here] * share + jnp.sum(powers, axis=0, keepdims=True)
        )
        attn = dot_nn(values_t[:, : upto * tok], powers.astype(jnp.bfloat16))
        attn = ((attn + total_ref[:, here] * share) * inverse).astype(jnp.bfloat16)
        attn_ref[:, here] = attn
        stat_ref[0:1, here] = highest
        stat_ref[1:2, here] = inverse
    mid_ref[...] = dot_nn(down_t_ref[...], attn_ref[...])


def tile_rows(tile):
    return pl.ds(tile * (tile + 1) // 2 * TILE, (tile + 1) * TILE)


def prob_kernel(tok, scalar_ref, own_ref, other_ref, stat_ref, prob_ref, keys_t_ref):
    blocks = own_ref.shape[0]
    step = TILE // tok
    visible = (own_visible(), other_visible(scalar_ref[0], tok))
    for tile in range(blocks // step):
        upto = (tile + 1) * step
        here = pl.ds(tile * TILE, TILE)
        queries = own_ref[tile * step : upto, 0:tok, :].reshape(TILE, HD)
        for side, (ref, first) in enumerate(((own_ref, tok), (other_ref, 0))):
            scores = scores_of(rows_of(ref, upto, first, tok), queries, visible[side])
            powers = jnp.exp2((scores - stat_ref[0:1, here]) * LOG2_SCALE)
            prob_ref[side, tile_rows(tile), :] = powers * stat_ref[1:2, here]
    keys_t_ref[0] = rows_of(own_ref, blocks, tok, tok).T
    keys_t_ref[1] = rows_of(other_ref, blocks, 0, tok).T


def backward_kernel(
    tok,
    scalar_ref,
    own_ref,
    other_ref,
    dout_ref,
    attn_ref,
    prob_ref,
    keys_t_ref,
    dq_ref,
    dk_own_ref,
    dv_own_ref,
    pair_other_ref,
    down_grad_ref,
    dk_own,
    dv_own,
    dk_other,
    dv_other,
):
    blocks = own_ref.shape[0]
    step = TILE // tok
    low_rank = down_grad_ref.shape[0]
    tiles = blocks // step
    lora = jnp.concatenate(
        [dout_ref[block, HD : HD + low_rank, :] for block in range(blocks)], axis=1
    )
    down_grad_ref[...] = 2.0 * dot_nt(lora, attn_ref[...])
    for tile in reversed(range(tiles)):
        upto = (tile + 1) * step
        width = upto * tok
        queries = own_ref[tile * step : upto, 0:tok, :].reshape(TILE, HD)
        douts_t = jnp.concatenate(
            [dout_ref[block, 0:HD, :] for block in range(tile * step, upto)], axis=1
        )
        own = prob_ref[0, tile_rows(tile), :]
        other = prob_ref[1, tile_rows(tile), :]
        dprob_own = dot_nn(rows_of(own_ref, upto, 2 * tok, tok), douts_t)
        dprob_other = dot_nn(rows_of(other_ref, upto, tok, tok), douts_t)
        delta = jnp.sum(own * dprob_own, axis=0, keepdims=True) + jnp.sum(
            other * dprob_other, axis=0, keepdims=True
        )
        ds_own = (own * (dprob_own - delta)).astype(jnp.bfloat16)
        ds_other = (other * (dprob_other - delta)).astype(jnp.bfloat16)
        dq = dot_nn(keys_t_ref[0, :, 0:width], ds_own)
        dq += dot_nn(keys_t_ref[1, :, 0:width], ds_other)
        dq = (dq * SCALE).T.astype(jnp.bfloat16)
        dq_ref[tile * step : upto] = dq.reshape(step, tok, HD)
        terms = (
            (dk_own, dot_nn(ds_own, queries)),
            (dk_other, dot_nn(ds_other, queries)),
            (dv_own, dot_nt(own.astype(jnp.bfloat16), douts_t)),
            (dv_other, dot_nt(other.astype(jnp.bfloat16), douts_t)),
        )
        for total, term in terms:
            if tile == tiles - 1:
                total[...] = term
            else:
                total[0:width] += term
    shape = (blocks, tok, HD)
    dk_own_ref[...] = (dk_own[...] * SCALE).reshape(shape)
    dv_own_ref[...] = dv_own[...].reshape(shape)
    pair_other_ref[:, 0:tok, :] = (dk_other[...] * SCALE).astype(jnp.bfloat16).reshape(shape)
    pair_other_ref[:, tok : 2 * tok, :] = dv_other[...].astype(jnp.bfloat16).reshape(shape)


def call_kernel(body, outs, scratch, flops, exps, *operands, declared=None, limit=48):
    in_bytes = sum(x.size * x.dtype.itemsize for x in operands)
    out_bytes = sum(x.size * x.dtype.itemsize for x in outs)
    specs = [pl.BlockSpec(memory_space=pltpu.SMEM)]
    specs += [pl.BlockSpec(memory_space=pltpu.VMEM)] * (len(operands) - 1)
    return pl.pallas_call(
        body,
        out_shape=outs,
        in_specs=specs,
        out_specs=[pl.BlockSpec(memory_space=pltpu.VMEM)] * len(outs),
        scratch_shapes=scratch,
        compiler_params=pltpu.CompilerParams(vmem_limit_bytes=limit * 1024 * 1024),
        cost_estimate=pl.CostEstimate(
            flops=flops,
            bytes_accessed=declared or in_bytes + out_bytes,
            transcendentals=exps,
        ),
    )(*operands)


def shape_of(shape, dtype):
    return jax.ShapeDtypeStruct(shape, dtype)


def butterfly_sum(value, axis, bits, count):
    for bit in bits:
        pairs = [(i, i ^ bit) for i in range(count)]
        value = value.astype(jnp.bfloat16)
        taken = lax.ppermute(value, axis, pairs)
        value = value.astype(jnp.float32) + taken.astype(jnp.float32)
    return value


def powers_below(count):
    return [1 << n for n in range(count.bit_length() - 1)]


def message_kernel(copies, *refs):
    count = (len(refs) - 3) // 2
    operands, message_ref = refs[:count], refs[count]
    held, in_sems, out_sems = refs[count + 1 : -2], refs[-2], refs[-1]
    tok = operands[0].shape[0]
    arriving = [
        pltpu.make_async_copy(ref, to, in_sems.at[n])
        for n, (ref, to) in enumerate(zip(operands, held))
    ]
    for copy in arriving:
        copy.start()
    leaving = []
    for n, (copy, ref) in enumerate(zip(arriving, held)):
        copy.wait()
        for rank in range(message_ref.shape[0]):
            cols = pl.ds((rank // copies) * HD, HD)
            to = message_ref.at[rank, pl.ds(n * tok, tok), :]
            leaving.append(pltpu.make_async_copy(ref.at[:, cols], to, out_sems.at[len(leaving)]))
            leaving[-1].start()
    for copy in leaving:
        copy.wait()


def message_of(copies, ranks, *operands):
    tok = operands[0].shape[0]
    count = len(operands)
    shape = (ranks, count * tok, HD)
    return pl.pallas_call(
        functools.partial(message_kernel, copies),
        out_shape=shape_of(shape, operands[0].dtype),
        in_specs=[pl.BlockSpec(memory_space=pltpu.HBM)] * count,
        out_specs=pl.BlockSpec(memory_space=pltpu.HBM),
        scratch_shapes=[pltpu.VMEM(x.shape, x.dtype) for x in operands]
        + [pltpu.SemaphoreType.DMA((count,)), pltpu.SemaphoreType.DMA((ranks * count,))],
        cost_estimate=pl.CostEstimate(
            flops=0, bytes_accessed=4 * math.prod(shape), transcendentals=0
        ),
    )(*operands)


def unpack_kernel(copies, back_ref, *refs):
    (*out_refs, sems), down_ref = (refs[:3] + refs[-1:]), refs[3] if len(refs) > 4 else None
    tok = out_refs[0].shape[0]
    moves = []
    for at_head in range(out_refs[0].shape[1] // HD):
        cols = pl.ds(at_head * HD, HD)
        for n, ref in enumerate(out_refs):
            block = back_ref.at[at_head * copies, pl.ds(n * tok, tok), :]
            moves.append(pltpu.make_async_copy(block, ref.at[:, cols], sems.at[len(moves)]))
            moves[-1].start()
    if down_ref is not None:
        for at_head in range(out_refs[0].shape[1] // HD):
            cols = slice(at_head * HD, (at_head + 1) * HD)
            down_ref[:, cols] = back_ref[at_head * copies, 3 * tok :, :].astype(jnp.float32)
    for move in moves:
        move.wait()


def in_vmem(body, outs, *operands):
    whole = pl.BlockSpec(memory_space=pltpu.VMEM)
    size = sum(x.size * x.dtype.itemsize for x in operands)
    size += sum(x.size * x.dtype.itemsize for x in outs)
    return pl.pallas_call(
        body,
        out_shape=outs,
        in_specs=[whole] * len(operands),
        out_specs=[whole] * len(outs),
        compiler_params=pltpu.CompilerParams(vmem_limit_bytes=16 * 1024 * 1024),
        cost_estimate=pl.CostEstimate(flops=0, bytes_accessed=size, transcendentals=0),
    )(*operands)


def cotangent_kernel(chunks, plan_ref, *refs):
    pieces, (matrix_ref, up_ref, own_ref, sent_ref) = refs[:-4], refs[-4:]
    tok, cols = pieces[0].shape
    feats, low_rank = matrix_ref.shape[0], up_ref.shape[0]
    count = len(pieces)
    if chunks == 1:
        stacks = [(jnp.concatenate([p[...] for p in pieces], axis=0), pl.ds(0, cols))]
    else:
        stacks = [
            (p[...], pl.ds(pl.multiple_of(plan_ref[count + k], HD), cols))
            for k, p in enumerate(pieces)
        ]
    mine = [plan_ref[k] == 1 for k in range(count)]
    for ref, here in ((matrix_ref, pl.ds(0, feats)), (up_ref, pl.ds(feats, low_rank))):
        terms = [dot_nt(ref[:, at], rows) for rows, at in stacks]
        parts = [t[:, i : i + tok] for t in terms for i in range(0, t.shape[1], tok)]
        own_ref[here, :] = summed([jnp.where(m, p, 0.0) for m, p in zip(mine, parts)])
        sent = summed([jnp.where(m, 0.0, p) for m, p in zip(mine, parts)])
        sent_ref[here, :] = sent.astype(jnp.bfloat16)


def dout_kernel(copies, own_ref, taken_ref, mid_ref, message_ref):
    low_rank = mid_ref.shape[1]
    feats = own_ref.shape[0] - low_rank
    lora = own_ref[feats:, :] + taken_ref[feats:, :].astype(jnp.float32)
    for rank in range(message_ref.shape[0]):
        at = pl.ds((rank // copies) * HD, HD)
        part = own_ref[at, :] + taken_ref[at, :].astype(jnp.float32)
        message_ref[rank, 0:HD, :] = part.astype(jnp.bfloat16)
        message_ref[rank, HD : HD + low_rank, :] = lora.astype(jnp.bfloat16)
        message_ref[rank, HD + low_rank : HD + 2 * low_rank, :] = mid_ref[rank]


def on_device(
    sizes,
    head_query_rows,
    head_key_rows,
    head_value_rows,
    output_gradient,
    output_matrix,
    adapter_down_weight,
    adapter_up_weight,
):
    seqs, heads, subs = sizes
    tok, feats = head_query_rows.shape
    cols = output_gradient.shape[1]
    low_rank = adapter_up_weight.shape[0]
    local_heads = feats // HD
    block_rows = tok * subs
    ranks = GROUP // block_rows
    copies = ranks // local_heads
    shift_blocks = GROUP // 2 // block_rows

    seq = lax.axis_index("seq")
    head = lax.axis_index("head")
    sub = lax.axis_index("sub")
    shifted = head >= heads // 2
    rank = (seq + shift_blocks) % ranks
    my_head = rank // copies

    groups = []
    for at_head in range(heads):
        for first in range(0, seqs, ranks):
            members = [first + shift_blocks + i for i in range(ranks)]
            if at_head < heads // 2:
                members = [first + (m - first) % ranks for m in members]
            members = [m % seqs for m in members]
            groups.append([m * heads + at_head for m in members])
    scalars = jnp.full((1,), sub, jnp.int32)

    def in_order(blocks):
        half = ranks // 2
        turned = jnp.concatenate((blocks[half:], blocks[:half]), axis=0)
        return jnp.where(shifted, blocks, turned)


    def exchange(parts):
        return lax.all_to_all(
            parts, ("seq", "head"), 0, 0, axis_index_groups=groups, tiled=True
        )

    def swap(value):
        if subs == 1:
            return value
        return lax.ppermute(value, "sub", [(0, 1), (1, 0)])

    sent = message_of(copies, ranks, head_query_rows, head_key_rows, head_value_rows)
    sent, output_gradient, output_matrix = lax.optimization_barrier(
        (sent, output_gradient, output_matrix)
    )
    own = exchange(sent)

    chunks = heads // subs
    pieces = []
    for k in range(heads):
        pairs = []
        for src_head in range(heads):
            for src_sub in range(subs):
                j = (src_head % chunks) * subs + src_sub
                dst = ((j + k) % heads) * subs + src_head // chunks
                pairs.append((src_head * subs + src_sub, dst))
        pieces.append(lax.ppermute(output_gradient, ("head", "sub"), pairs))

    up_half = lax.dynamic_slice_in_dim(adapter_up_weight, sub * chunks * cols, chunks * cols, 1)
    folded = dot_nn(adapter_down_weight, up_half)
    folded = (output_matrix.astype(jnp.float32) + 2.0 * folded).astype(jnp.bfloat16)
    sources = [(head - k + heads) % heads for k in range(heads)]
    plan = [(j % subs == sub).astype(jnp.int32) for j in sources]
    plan += [(j // subs * cols).astype(jnp.int32) for j in sources]
    packed_own, packed_sent = call_kernel(
        functools.partial(cotangent_kernel, chunks),
        [
            shape_of((feats + low_rank, tok), jnp.float32),
            shape_of((feats + low_rank, tok), jnp.bfloat16),
        ],
        [],
        0,
        0,
        jnp.stack(plan),
        *pieces,
        folded,
        up_half,
        declared=1024,
        limit=16,
    )
    received = swap(packed_sent)
    down_head = lax.dynamic_slice_in_dim(adapter_down_weight, my_head * HD, HD, 0).T
    own, down_head, _ = lax.optimization_barrier((own, down_head, packed_sent))
    own = in_order(own)
    other = swap(own[:, tok:])

    rows = ranks * tok
    pair_count = rows * (rows + TILE)
    own_total, own_stats = call_kernel(
        functools.partial(forward_own_kernel, tok),
        [shape_of((HD, rows), jnp.float32), shape_of((8, rows), jnp.float32)],
        [],
        2 * pair_count * HD,
        pair_count // 2,
        scalars,
        own,
        limit=16,
    )
    attn_t, middle_rows, stats = call_kernel(
        functools.partial(forward_kernel, tok),
        [
            shape_of((HD, rows), jnp.bfloat16),
            shape_of((low_rank, rows), jnp.float32),
            shape_of((8, rows), jnp.float32),
        ],
        [],
        2 * pair_count * HD,
        pair_count // 2,
        scalars,
        own,
        other,
        own_total,
        own_stats,
        down_head,
        limit=16,
    )

    first_copy = rank % copies == 0
    middle_rows = middle_rows.astype(jnp.bfloat16).reshape(low_rank, ranks, tok)
    middle_rows = in_order(middle_rows.transpose(1, 0, 2))
    if copies > 1:
        middle_rows = jnp.where(first_copy, middle_rows, 0.0)
    (message,) = in_vmem(
        functools.partial(dout_kernel, copies),
        [shape_of((ranks, HD + 2 * low_rank, tok), jnp.bfloat16)],
        packed_own,
        received,
        middle_rows,
    )
    arrived = exchange(message)
    tiles = rows // TILE
    probs, keys_t = call_kernel(
        functools.partial(prob_kernel, tok),
        [
            shape_of((2, tiles * (tiles + 1) // 2 * TILE, TILE), jnp.float32),
            shape_of((2, HD, rows), jnp.bfloat16),
        ],
        [],
        2 * pair_count * HD,
        pair_count,
        scalars,
        own,
        other,
        stats,
        limit=16,
    )
    middle = jnp.sum(arrived[:, HD + low_rank :].astype(jnp.float32), axis=0)
    bit = 1
    while bit < heads:
        middle += lax.ppermute(middle, "head", [(i, i ^ bit) for i in range(heads)])
        bit *= 2
    up_part = 2.0 * dot_nn(middle.astype(jnp.bfloat16), output_gradient)

    dq, dk_own, dv_own, pair_other, down_part = call_kernel(
        functools.partial(backward_kernel, tok),
        [
            shape_of((ranks, tok, HD), jnp.bfloat16),
            shape_of((ranks, tok, HD), jnp.float32),
            shape_of((ranks, tok, HD), jnp.float32),
            shape_of((ranks, 2 * tok, HD), jnp.bfloat16),
            shape_of((low_rank, HD), jnp.float32),
        ],
        [pltpu.VMEM((rows, HD), jnp.float32)] * 4,
        8 * pair_count * HD,
        0,
        scalars,
        own,
        other,
        in_order(arrived[:, : HD + low_rank]),
        attn_t,
        probs,
        keys_t,
        limit=24,
    )
    pair_other, _ = lax.optimization_barrier((pair_other, middle))
    pair_received = swap(pair_other).astype(jnp.float32)
    down_rows = jnp.where(first_copy, down_part + swap(down_part), 0.0)
    dk = (dk_own + pair_received[:, :tok]).astype(jnp.bfloat16)
    dv = (dv_own + pair_received[:, tok:]).astype(jnp.bfloat16)
    down_rows = jnp.broadcast_to(down_rows.astype(jnp.bfloat16), (ranks, low_rank, HD))
    back_message = jnp.concatenate([*map(in_order, (dq, dk, dv)), down_rows], axis=1)
    back = exchange(back_message)
    outs = [shape_of((tok, feats), back.dtype)] * 3
    if seqs == ranks:
        outs.append(shape_of((low_rank, feats), jnp.float32))
    whole = pl.BlockSpec(memory_space=pltpu.VMEM)
    outs = list(
        pl.pallas_call(
            functools.partial(unpack_kernel, copies),
            out_shape=outs,
            in_specs=[whole],
            out_specs=[pl.BlockSpec(memory_space=pltpu.HBM)] * 3 + [whole] * (len(outs) - 3),
            scratch_shapes=[pltpu.SemaphoreType.DMA((3 * local_heads,))],
            compiler_params=pltpu.CompilerParams(vmem_limit_bytes=16 * 1024 * 1024),
            cost_estimate=pl.CostEstimate(
                flops=0, bytes_accessed=4 * back.size, transcendentals=0
            ),
        )(back)
    )
    if seqs > ranks:
        bits = [bit for bit in powers_below(seqs) if bit >= ranks]
        down_terms = back[::copies, 3 * tok :].astype(jnp.float32)
        down_terms = butterfly_sum(down_terms, "seq", bits, seqs)
        outs.append(down_terms.transpose(1, 0, 2).reshape(low_rank, feats))
    query_gradient, key_gradient, value_gradient, down_gradient = outs

    up_sum = butterfly_sum(up_part, "seq", powers_below(seqs), seqs)
    _, up_sum = lax.optimization_barrier((back, up_sum))
    up_gradient = butterfly_sum(up_sum, "sub", powers_below(subs), subs)
    return (query_gradient, key_gradient, value_gradient, down_gradient.T, up_gradient)


def solution(mesh):
    rows = P(("rep", "seq", "sub"), "head")
    sizes = (mesh.shape["seq"], mesh.shape["head"], mesh.shape["sub"])
    return jax.shard_map(
        functools.partial(on_device, sizes),
        mesh=mesh,
        in_specs=(rows, rows, rows, rows, P("head", "sub"), P("head", None), P()),
        out_specs=(rows, rows, rows, P(("rep", "head"), None), P("rep", "head")),
        check_vma=False,
    )
```

```python
import functools
import math

import jax
import jax.numpy as jnp
from jax import lax
from jax.experimental import pallas as pl
from jax.experimental.pallas import tpu as pltpu
from jax.sharding import PartitionSpec as P

HD = 128
GROUP = 2048
TILE = 256
HIDDEN = -1e30
SCALE = HD ** (-0.5)
LOG2_SCALE = SCALE * math.log2(math.e)


def dot_nt(left, right):
    return lax.dot_general(
        left, right, (((1,), (1,)), ((), ())), preferred_element_type=jnp.float32
    )


def dot_nn(left, right):
    return jnp.dot(left, right, preferred_element_type=jnp.float32)


def rows_of(ref, blocks, first, count):
    return ref[0:blocks, first : first + count, :].reshape(blocks * count, HD)


def scores_of(keys, queries, visible):
    scores = dot_nt(keys, queries)
    head = scores.shape[0] - TILE
    tail = jnp.where(visible, scores[head:], HIDDEN)
    return tail if head == 0 else jnp.concatenate((scores[:head], tail), axis=0)


def tile_index(dimension):
    shape = (TILE, 1) if dimension == 0 else (1, TILE)
    return lax.broadcasted_iota(jnp.int32, shape, dimension)


def own_visible():
    return tile_index(0) <= tile_index(1)


def other_visible(sub, tok):
    return tile_index(0) // tok < tile_index(1) // tok + sub


def summed(terms):
    return functools.reduce(jnp.add, terms)


def forward_own_kernel(tok, scalar_ref, own_ref, total_ref, stat_ref):
    blocks = own_ref.shape[0]
    step = TILE // tok
    values_t = rows_of(own_ref, blocks, 2 * tok, tok).T
    for tile in range(blocks // step):
        upto = (tile + 1) * step
        at = tile * TILE
        queries = own_ref[tile * step : upto, 0:tok, :].reshape(TILE, HD)
        scores = scores_of(rows_of(own_ref, upto, tok, tok), queries, own_visible())
        highest = jnp.max(scores, axis=0, keepdims=True)
        powers = jnp.exp2((scores - highest) * LOG2_SCALE)
        total_ref[:, at : at + TILE] = dot_nn(
            values_t[:, : upto * tok], powers.astype(jnp.bfloat16)
        )
        stat_ref[0:1, at : at + TILE] = highest
        stat_ref[1:2, at : at + TILE] = jnp.sum(powers, axis=0, keepdims=True)


def forward_kernel(
    tok,
    scalar_ref,
    own_ref,
    other_ref,
    total_ref,
    own_stat_ref,
    down_t_ref,
    attn_ref,
    mid_ref,
    stat_ref,
):
    blocks = own_ref.shape[0]
    step = TILE // tok
    sub = scalar_ref[0]
    values_t = rows_of(other_ref, blocks, tok, tok).T
    for tile in range(blocks // step):
        upto = (tile + 1) * step
        at = tile * TILE
        here = pl.ds(at, TILE)
        queries = own_ref[tile * step : upto, 0:tok, :].reshape(TILE, HD)
        scores = scores_of(
            rows_of(other_ref, upto, 0, tok), queries, other_visible(sub, tok)
        )
        own_highest = own_stat_ref[0:1, here]
        highest = jnp.maximum(own_highest, jnp.max(scores, axis=0, keepdims=True))
        powers = jnp.exp2((scores - highest) * LOG2_SCALE)
        share = jnp.exp2((own_highest - highest) * LOG2_SCALE)
        inverse = 1.0 / (
            own_stat_ref[1:2, here] * share + jnp.sum(powers, axis=0, keepdims=True)
        )
        attn = dot_nn(values_t[:, : upto * tok], powers.astype(jnp.bfloat16))
        attn = ((attn + total_ref[:, here] * share) * inverse).astype(jnp.bfloat16)
        attn_ref[:, here] = attn
        stat_ref[0:1, here] = highest
        stat_ref[1:2, here] = inverse
    mid_ref[...] = dot_nn(down_t_ref[...], attn_ref[...])


def backward_kernel(
    tok,
    scalar_ref,
    own_ref,
    other_ref,
    dout_ref,
    attn_ref,
    stat_ref,
    dq_ref,
    dk_own_ref,
    dv_own_ref,
    pair_other_ref,
    down_grad_ref,
    dk_own,
    dv_own,
    dk_other,
    dv_other,
):
    blocks = own_ref.shape[0]
    step = TILE // tok
    sub = scalar_ref[0]
    low_rank = down_grad_ref.shape[0]
    keys_own_t = rows_of(own_ref, blocks, tok, tok).T
    keys_other_t = rows_of(other_ref, blocks, 0, tok).T
    tiles = blocks // step
    lora = jnp.concatenate(
        [dout_ref[block, HD : HD + low_rank, :] for block in range(blocks)], axis=1
    )
    down_grad_ref[...] = 2.0 * dot_nt(lora, attn_ref[...])
    for tile in reversed(range(tiles)):
        upto = (tile + 1) * step
        width = upto * tok
        at = tile * TILE
        queries = own_ref[tile * step : upto, 0:tok, :].reshape(TILE, HD)
        douts_t = jnp.concatenate(
            [dout_ref[block, 0:HD, :] for block in range(tile * step, upto)], axis=1
        )
        highest = stat_ref[0:1, at : at + TILE]
        inverse = stat_ref[1:2, at : at + TILE]
        own = scores_of(rows_of(own_ref, upto, tok, tok), queries, own_visible())
        other = scores_of(
            rows_of(other_ref, upto, 0, tok), queries, other_visible(sub, tok)
        )
        own = jnp.exp2((own - highest) * LOG2_SCALE) * inverse
        other = jnp.exp2((other - highest) * LOG2_SCALE) * inverse
        dprob_own = dot_nn(rows_of(own_ref, upto, 2 * tok, tok), douts_t)
        dprob_other = dot_nn(rows_of(other_ref, upto, tok, tok), douts_t)
        delta = jnp.sum(own * dprob_own, axis=0, keepdims=True) + jnp.sum(
            other * dprob_other, axis=0, keepdims=True
        )
        ds_own = (own * (dprob_own - delta)).astype(jnp.bfloat16)
        ds_other = (other * (dprob_other - delta)).astype(jnp.bfloat16)
        dq = dot_nn(keys_own_t[:, :width], ds_own) + dot_nn(keys_other_t[:, :width], ds_other)
        dq = (dq * SCALE).T.astype(jnp.bfloat16)
        dq_ref[tile * step : upto] = dq.reshape(step, tok, HD)
        terms = (
            (dk_own, dot_nn(ds_own, queries)),
            (dk_other, dot_nn(ds_other, queries)),
            (dv_own, dot_nt(own.astype(jnp.bfloat16), douts_t)),
            (dv_other, dot_nt(other.astype(jnp.bfloat16), douts_t)),
        )
        for total, term in terms:
            if tile == tiles - 1:
                total[...] = term
            else:
                total[0:width] += term
    shape = (blocks, tok, HD)
    dk_own_ref[...] = (dk_own[...] * SCALE).reshape(shape)
    dv_own_ref[...] = dv_own[...].reshape(shape)
    pair_other_ref[:, 0:tok, :] = (dk_other[...] * SCALE).astype(jnp.bfloat16).reshape(shape)
    pair_other_ref[:, tok : 2 * tok, :] = dv_other[...].astype(jnp.bfloat16).reshape(shape)


def call_kernel(body, outs, scratch, flops, exps, *operands, declared=None, limit=48):
    in_bytes = sum(x.size * x.dtype.itemsize for x in operands)
    out_bytes = sum(x.size * x.dtype.itemsize for x in outs)
    specs = [pl.BlockSpec(memory_space=pltpu.SMEM)]
    specs += [pl.BlockSpec(memory_space=pltpu.VMEM)] * (len(operands) - 1)
    return pl.pallas_call(
        body,
        out_shape=outs,
        in_specs=specs,
        out_specs=[pl.BlockSpec(memory_space=pltpu.VMEM)] * len(outs),
        scratch_shapes=scratch,
        compiler_params=pltpu.CompilerParams(vmem_limit_bytes=limit * 1024 * 1024),
        cost_estimate=pl.CostEstimate(
            flops=flops,
            bytes_accessed=declared or in_bytes + out_bytes,
            transcendentals=exps,
        ),
    )(*operands)


def shape_of(shape, dtype):
    return jax.ShapeDtypeStruct(shape, dtype)


def butterfly_sum(value, axis, bits, count):
    for bit in bits:
        pairs = [(i, i ^ bit) for i in range(count)]
        value = value.astype(jnp.bfloat16)
        taken = lax.ppermute(value, axis, pairs)
        value = value.astype(jnp.float32) + taken.astype(jnp.float32)
    return value


def powers_below(count):
    return [1 << n for n in range(count.bit_length() - 1)]


def message_kernel(copies, *refs):
    count = (len(refs) - 3) // 2
    operands, message_ref = refs[:count], refs[count]
    held, in_sems, out_sems = refs[count + 1 : -2], refs[-2], refs[-1]
    tok = operands[0].shape[0]
    arriving = [
        pltpu.make_async_copy(ref, to, in_sems.at[n])
        for n, (ref, to) in enumerate(zip(operands, held))
    ]
    for copy in arriving:
        copy.start()
    leaving = []
    for n, (copy, ref) in enumerate(zip(arriving, held)):
        copy.wait()
        for rank in range(message_ref.shape[0]):
            cols = pl.ds((rank // copies) * HD, HD)
            to = message_ref.at[rank, pl.ds(n * tok, tok), :]
            leaving.append(pltpu.make_async_copy(ref.at[:, cols], to, out_sems.at[len(leaving)]))
            leaving[-1].start()
    for copy in leaving:
        copy.wait()


def message_of(copies, ranks, *operands):
    tok = operands[0].shape[0]
    count = len(operands)
    shape = (ranks, count * tok, HD)
    return pl.pallas_call(
        functools.partial(message_kernel, copies),
        out_shape=shape_of(shape, operands[0].dtype),
        in_specs=[pl.BlockSpec(memory_space=pltpu.HBM)] * count,
        out_specs=pl.BlockSpec(memory_space=pltpu.HBM),
        scratch_shapes=[pltpu.VMEM(x.shape, x.dtype) for x in operands]
        + [pltpu.SemaphoreType.DMA((count,)), pltpu.SemaphoreType.DMA((ranks * count,))],
        cost_estimate=pl.CostEstimate(
            flops=0, bytes_accessed=4 * math.prod(shape), transcendentals=0
        ),
    )(*operands)


def unpack_kernel(copies, back_ref, *refs):
    out_refs, down_ref = refs[:3], refs[3] if len(refs) > 3 else None
    tok = out_refs[0].shape[0]
    for at_head in range(out_refs[0].shape[1] // HD):
        cols = slice(at_head * HD, (at_head + 1) * HD)
        for n, ref in enumerate(out_refs):
            ref[:, cols] = back_ref[at_head * copies, n * tok : (n + 1) * tok, :]
        if down_ref is not None:
            down_ref[:, cols] = back_ref[at_head * copies, 3 * tok :, :].astype(jnp.float32)


def in_vmem(body, outs, *operands):
    whole = pl.BlockSpec(memory_space=pltpu.VMEM)
    size = sum(x.size * x.dtype.itemsize for x in operands)
    size += sum(x.size * x.dtype.itemsize for x in outs)
    return pl.pallas_call(
        body,
        out_shape=outs,
        in_specs=[whole] * len(operands),
        out_specs=[whole] * len(outs),
        compiler_params=pltpu.CompilerParams(vmem_limit_bytes=16 * 1024 * 1024),
        cost_estimate=pl.CostEstimate(flops=0, bytes_accessed=size, transcendentals=0),
    )(*operands)


def cotangent_kernel(chunks, plan_ref, *refs):
    pieces, (matrix_ref, up_ref, own_ref, sent_ref) = refs[:-4], refs[-4:]
    tok, cols = pieces[0].shape
    feats, low_rank = matrix_ref.shape[0], up_ref.shape[0]
    count = len(pieces)
    if chunks == 1:
        stacks = [(jnp.concatenate([p[...] for p in pieces], axis=0), pl.ds(0, cols))]
    else:
        stacks = [
            (p[...], pl.ds(pl.multiple_of(plan_ref[count + k], HD), cols))
            for k, p in enumerate(pieces)
        ]
    mine = [plan_ref[k] == 1 for k in range(count)]
    for ref, here in ((matrix_ref, pl.ds(0, feats)), (up_ref, pl.ds(feats, low_rank))):
        terms = [dot_nt(ref[:, at], rows) for rows, at in stacks]
        parts = [t[:, i : i + tok] for t in terms for i in range(0, t.shape[1], tok)]
        own_ref[here, :] = summed([jnp.where(m, p, 0.0) for m, p in zip(mine, parts)])
        sent = summed([jnp.where(m, 0.0, p) for m, p in zip(mine, parts)])
        sent_ref[here, :] = sent.astype(jnp.bfloat16)


def dout_kernel(copies, own_ref, taken_ref, mid_ref, message_ref):
    low_rank = mid_ref.shape[1]
    feats = own_ref.shape[0] - low_rank
    lora = own_ref[feats:, :] + taken_ref[feats:, :].astype(jnp.float32)
    for rank in range(message_ref.shape[0]):
        at = pl.ds((rank // copies) * HD, HD)
        part = own_ref[at, :] + taken_ref[at, :].astype(jnp.float32)
        message_ref[rank, 0:HD, :] = part.astype(jnp.bfloat16)
        message_ref[rank, HD : HD + low_rank, :] = lora.astype(jnp.bfloat16)
        message_ref[rank, HD + low_rank : HD + 2 * low_rank, :] = mid_ref[rank]


def on_device(
    sizes,
    head_query_rows,
    head_key_rows,
    head_value_rows,
    output_gradient,
    output_matrix,
    adapter_down_weight,
    adapter_up_weight,
):
    seqs, heads, subs = sizes
    tok, feats = head_query_rows.shape
    cols = output_gradient.shape[1]
    low_rank = adapter_up_weight.shape[0]
    local_heads = feats // HD
    block_rows = tok * subs
    ranks = GROUP // block_rows
    copies = ranks // local_heads
    shift_blocks = GROUP // 2 // block_rows

    seq = lax.axis_index("seq")
    head = lax.axis_index("head")
    sub = lax.axis_index("sub")
    shifted = head >= heads // 2
    rank = (seq + shift_blocks) % ranks
    my_head = rank // copies

    groups = []
    for at_head in range(heads):
        for first in range(0, seqs, ranks):
            members = [first + shift_blocks + i for i in range(ranks)]
            if at_head < heads // 2:
                members = [first + (m - first) % ranks for m in members]
            members = [m % seqs for m in members]
            groups.append([m * heads + at_head for m in members])
    scalars = jnp.full((1,), sub, jnp.int32)

    def in_order(blocks):
        half = ranks // 2
        turned = jnp.concatenate((blocks[half:], blocks[:half]), axis=0)
        return jnp.where(shifted, blocks, turned)


    def exchange(parts):
        return lax.all_to_all(
            parts, ("seq", "head"), 0, 0, axis_index_groups=groups, tiled=True
        )

    def swap(value):
        if subs == 1:
            return value
        return lax.ppermute(value, "sub", [(0, 1), (1, 0)])

    sent = message_of(copies, ranks, head_query_rows, head_key_rows, head_value_rows)
    sent, output_gradient, output_matrix = lax.optimization_barrier(
        (sent, output_gradient, output_matrix)
    )
    own = exchange(sent)

    chunks = heads // subs
    pieces = []
    for k in range(heads):
        pairs = []
        for src_head in range(heads):
            for src_sub in range(subs):
                j = (src_head % chunks) * subs + src_sub
                dst = ((j + k) % heads) * subs + src_head // chunks
                pairs.append((src_head * subs + src_sub, dst))
        pieces.append(lax.ppermute(output_gradient, ("head", "sub"), pairs))

    up_half = lax.dynamic_slice_in_dim(adapter_up_weight, sub * chunks * cols, chunks * cols, 1)
    folded = dot_nn(adapter_down_weight, up_half)
    folded = (output_matrix.astype(jnp.float32) + 2.0 * folded).astype(jnp.bfloat16)
    sources = [(head - k + heads) % heads for k in range(heads)]
    plan = [(j % subs == sub).astype(jnp.int32) for j in sources]
    plan += [(j // subs * cols).astype(jnp.int32) for j in sources]
    packed_own, packed_sent = call_kernel(
        functools.partial(cotangent_kernel, chunks),
        [
            shape_of((feats + low_rank, tok), jnp.float32),
            shape_of((feats + low_rank, tok), jnp.bfloat16),
        ],
        [],
        0,
        0,
        jnp.stack(plan),
        *pieces,
        folded,
        up_half,
        declared=1024,
        limit=16,
    )
    received = swap(packed_sent)
    down_head = lax.dynamic_slice_in_dim(adapter_down_weight, my_head * HD, HD, 0).T
    own, down_head, _ = lax.optimization_barrier((own, down_head, packed_sent))
    own = in_order(own)
    other = swap(own[:, tok:])

    rows = ranks * tok
    pair_count = rows * (rows + TILE)
    own_total, own_stats = call_kernel(
        functools.partial(forward_own_kernel, tok),
        [shape_of((HD, rows), jnp.float32), shape_of((8, rows), jnp.float32)],
        [],
        2 * pair_count * HD,
        pair_count // 2,
        scalars,
        own,
        limit=16,
    )
    attn_t, middle_rows, stats = call_kernel(
        functools.partial(forward_kernel, tok),
        [
            shape_of((HD, rows), jnp.bfloat16),
            shape_of((low_rank, rows), jnp.float32),
            shape_of((8, rows), jnp.float32),
        ],
        [],
        2 * pair_count * HD,
        pair_count // 2,
        scalars,
        own,
        other,
        own_total,
        own_stats,
        down_head,
        limit=16,
    )

    first_copy = rank % copies == 0
    middle_rows = middle_rows.astype(jnp.bfloat16).reshape(low_rank, ranks, tok)
    middle_rows = in_order(middle_rows.transpose(1, 0, 2))
    if copies > 1:
        middle_rows = jnp.where(first_copy, middle_rows, 0.0)
    (message,) = in_vmem(
        functools.partial(dout_kernel, copies),
        [shape_of((ranks, HD + 2 * low_rank, tok), jnp.bfloat16)],
        packed_own,
        received,
        middle_rows,
    )
    arrived = exchange(message)
    middle = jnp.sum(arrived[:, HD + low_rank :].astype(jnp.float32), axis=0)
    bit = 1
    while bit < heads:
        middle += lax.ppermute(middle, "head", [(i, i ^ bit) for i in range(heads)])
        bit *= 2
    up_part = 2.0 * dot_nn(middle.astype(jnp.bfloat16), output_gradient)

    dq, dk_own, dv_own, pair_other, down_part = call_kernel(
        functools.partial(backward_kernel, tok),
        [
            shape_of((ranks, tok, HD), jnp.bfloat16),
            shape_of((ranks, tok, HD), jnp.float32),
            shape_of((ranks, tok, HD), jnp.float32),
            shape_of((ranks, 2 * tok, HD), jnp.bfloat16),
            shape_of((low_rank, HD), jnp.float32),
        ],
        [pltpu.VMEM((rows, HD), jnp.float32)] * 4,
        10 * pair_count * HD,
        pair_count,
        scalars,
        own,
        other,
        in_order(arrived[:, : HD + low_rank]),
        attn_t,
        stats,
        limit=28,
    )
    pair_other, _ = lax.optimization_barrier((pair_other, middle))
    pair_received = swap(pair_other).astype(jnp.float32)
    down_rows = jnp.where(first_copy, down_part + swap(down_part), 0.0)
    dk = (dk_own + pair_received[:, :tok]).astype(jnp.bfloat16)
    dv = (dv_own + pair_received[:, tok:]).astype(jnp.bfloat16)
    down_rows = jnp.broadcast_to(down_rows.astype(jnp.bfloat16), (ranks, low_rank, HD))
    back_message = jnp.concatenate([*map(in_order, (dq, dk, dv)), down_rows], axis=1)
    back = exchange(back_message)
    outs = [shape_of((tok, feats), back.dtype)] * 3
    if seqs == ranks:
        outs.append(shape_of((low_rank, feats), jnp.float32))
    outs = list(in_vmem(functools.partial(unpack_kernel, copies), outs, back))
    if seqs > ranks:
        bits = [bit for bit in powers_below(seqs) if bit >= ranks]
        down_terms = back[::copies, 3 * tok :].astype(jnp.float32)
        down_terms = butterfly_sum(down_terms, "seq", bits, seqs)
        outs.append(down_terms.transpose(1, 0, 2).reshape(low_rank, feats))
    query_gradient, key_gradient, value_gradient, down_gradient = outs

    up_sum = butterfly_sum(up_part, "seq", powers_below(seqs), seqs)
    _, up_sum = lax.optimization_barrier((back, up_sum))
    up_gradient = butterfly_sum(up_sum, "sub", powers_below(subs), subs)
    return (query_gradient, key_gradient, value_gradient, down_gradient.T, up_gradient)


def solution(mesh):
    rows = P(("rep", "seq", "sub"), "head")
    sizes = (mesh.shape["seq"], mesh.shape["head"], mesh.shape["sub"])
    return jax.shard_map(
        functools.partial(on_device, sizes),
        mesh=mesh,
        in_specs=(rows, rows, rows, rows, P("head", "sub"), P("head", None), P()),
        out_specs=(rows, rows, rows, P(("rep", "head"), None), P("rep", "head")),
        check_vma=False,
    )
```

```python
import functools
import math

import jax
import jax.numpy as jnp
from jax import lax
from jax.experimental import pallas as pl
from jax.experimental.pallas import tpu as pltpu
from jax.sharding import PartitionSpec as P

HD = 128
GROUP = 2048
TILE = 256
HIDDEN = -1e30
SCALE = HD ** (-0.5)
LOG2_SCALE = SCALE * math.log2(math.e)


def dot_nt(left, right):
    return lax.dot_general(
        left, right, (((1,), (1,)), ((), ())), preferred_element_type=jnp.float32
    )


def dot_tn(left, right):
    return lax.dot_general(
        left, right, (((0,), (0,)), ((), ())), preferred_element_type=jnp.float32
    )


def dot_nn(left, right):
    return jnp.dot(left, right, preferred_element_type=jnp.float32)


def rows_of(ref, blocks, first, count):
    return ref[0:blocks, first : first + count, :].reshape(blocks * count, HD)


def scores_of(keys, queries, visible):
    scores = dot_nt(keys, queries)
    head = scores.shape[0] - TILE
    tail = jnp.where(visible, scores[head:], HIDDEN)
    return tail if head == 0 else jnp.concatenate((scores[:head], tail), axis=0)


def tile_index(dimension):
    shape = (TILE, 1) if dimension == 0 else (1, TILE)
    return lax.broadcasted_iota(jnp.int32, shape, dimension)


def own_visible():
    return tile_index(0) <= tile_index(1)


def other_visible(sub, tok):
    return tile_index(0) // tok < tile_index(1) // tok + sub


def summed(terms):
    return functools.reduce(jnp.add, terms)


def forward_own_kernel(tok, scalar_ref, own_ref, total_ref, stat_ref):
    blocks = own_ref.shape[0]
    step = TILE // tok
    values_t = rows_of(own_ref, blocks, 2 * tok, tok).T
    for tile in range(blocks // step):
        upto = (tile + 1) * step
        at = tile * TILE
        queries = own_ref[tile * step : upto, 0:tok, :].reshape(TILE, HD)
        scores = scores_of(rows_of(own_ref, upto, tok, tok), queries, own_visible())
        highest = jnp.max(scores, axis=0, keepdims=True)
        powers = jnp.exp2((scores - highest) * LOG2_SCALE)
        total_ref[:, at : at + TILE] = dot_nn(
            values_t[:, : upto * tok], powers.astype(jnp.bfloat16)
        )
        stat_ref[0:1, at : at + TILE] = highest
        stat_ref[1:2, at : at + TILE] = jnp.sum(powers, axis=0, keepdims=True)


def forward_kernel(
    tok,
    scalar_ref,
    own_ref,
    other_ref,
    total_ref,
    own_stat_ref,
    down_t_ref,
    attn_ref,
    mid_ref,
    stat_ref,
):
    blocks = own_ref.shape[0]
    step = TILE // tok
    sub = scalar_ref[0]
    values_t = rows_of(other_ref, blocks, tok, tok).T
    for tile in range(blocks // step):
        upto = (tile + 1) * step
        at = tile * TILE
        here = pl.ds(at, TILE)
        queries = own_ref[tile * step : upto, 0:tok, :].reshape(TILE, HD)
        scores = scores_of(
            rows_of(other_ref, upto, 0, tok), queries, other_visible(sub, tok)
        )
        own_highest = own_stat_ref[0:1, here]
        highest = jnp.maximum(own_highest, jnp.max(scores, axis=0, keepdims=True))
        powers = jnp.exp2((scores - highest) * LOG2_SCALE)
        share = jnp.exp2((own_highest - highest) * LOG2_SCALE)
        inverse = 1.0 / (
            own_stat_ref[1:2, here] * share + jnp.sum(powers, axis=0, keepdims=True)
        )
        attn = dot_nn(values_t[:, : upto * tok], powers.astype(jnp.bfloat16))
        attn = ((attn + total_ref[:, here] * share) * inverse).astype(jnp.bfloat16)
        attn_ref[:, here] = attn
        stat_ref[0:1, here] = highest
        stat_ref[1:2, here] = inverse
    mid_ref[...] = dot_nn(down_t_ref[...], attn_ref[...])


def backward_kernel(
    tok,
    scalar_ref,
    own_ref,
    other_ref,
    dout_ref,
    attn_ref,
    stat_ref,
    dq_ref,
    dk_own_ref,
    dv_own_ref,
    pair_other_ref,
    down_grad_ref,
    dk_own,
    dv_own,
    dk_other,
    dv_other,
):
    blocks = own_ref.shape[0]
    step = TILE // tok
    sub = scalar_ref[0]
    low_rank = down_grad_ref.shape[0]
    tiles = blocks // step
    lora = jnp.concatenate(
        [dout_ref[block, HD : HD + low_rank, :] for block in range(blocks)], axis=1
    )
    down_grad_ref[...] = 2.0 * dot_nt(lora, attn_ref[...])
    for tile in reversed(range(tiles)):
        upto = (tile + 1) * step
        width = upto * tok
        at = tile * TILE
        queries = own_ref[tile * step : upto, 0:tok, :].reshape(TILE, HD)
        douts_t = jnp.concatenate(
            [dout_ref[block, 0:HD, :] for block in range(tile * step, upto)], axis=1
        )
        highest = stat_ref[0:1, at : at + TILE]
        inverse = stat_ref[1:2, at : at + TILE]
        keys_own = rows_of(own_ref, upto, tok, tok)
        keys_other = rows_of(other_ref, upto, 0, tok)
        own = scores_of(keys_own, queries, own_visible())
        other = scores_of(keys_other, queries, other_visible(sub, tok))
        own = jnp.exp2((own - highest) * LOG2_SCALE) * inverse
        other = jnp.exp2((other - highest) * LOG2_SCALE) * inverse
        dprob_own = dot_nn(rows_of(own_ref, upto, 2 * tok, tok), douts_t)
        dprob_other = dot_nn(rows_of(other_ref, upto, tok, tok), douts_t)
        delta = jnp.sum(own * dprob_own, axis=0, keepdims=True) + jnp.sum(
            other * dprob_other, axis=0, keepdims=True
        )
        ds_own = (own * (dprob_own - delta)).astype(jnp.bfloat16)
        ds_other = (other * (dprob_other - delta)).astype(jnp.bfloat16)
        dq = dot_tn(ds_own, keys_own) + dot_tn(ds_other, keys_other)
        dq = (dq * SCALE).astype(jnp.bfloat16)
        dq_ref[tile * step : upto] = dq.reshape(step, tok, HD)
        terms = (
            (dk_own, dot_nn(ds_own, queries)),
            (dk_other, dot_nn(ds_other, queries)),
            (dv_own, dot_nt(own.astype(jnp.bfloat16), douts_t)),
            (dv_other, dot_nt(other.astype(jnp.bfloat16), douts_t)),
        )
        for total, term in terms:
            if tile == tiles - 1:
                total[...] = term
            else:
                total[0:width] += term
    shape = (blocks, tok, HD)
    dk_own_ref[...] = (dk_own[...] * SCALE).reshape(shape)
    dv_own_ref[...] = dv_own[...].reshape(shape)
    pair_other_ref[:, 0:tok, :] = (dk_other[...] * SCALE).astype(jnp.bfloat16).reshape(shape)
    pair_other_ref[:, tok : 2 * tok, :] = dv_other[...].astype(jnp.bfloat16).reshape(shape)


def call_kernel(body, outs, scratch, flops, exps, *operands, declared=None, limit=48):
    in_bytes = sum(x.size * x.dtype.itemsize for x in operands)
    out_bytes = sum(x.size * x.dtype.itemsize for x in outs)
    specs = [pl.BlockSpec(memory_space=pltpu.SMEM)]
    specs += [pl.BlockSpec(memory_space=pltpu.VMEM)] * (len(operands) - 1)
    return pl.pallas_call(
        body,
        out_shape=outs,
        in_specs=specs,
        out_specs=[pl.BlockSpec(memory_space=pltpu.VMEM)] * len(outs),
        scratch_shapes=scratch,
        compiler_params=pltpu.CompilerParams(vmem_limit_bytes=limit * 1024 * 1024),
        cost_estimate=pl.CostEstimate(
            flops=flops,
            bytes_accessed=declared or in_bytes + out_bytes,
            transcendentals=exps,
        ),
    )(*operands)


def shape_of(shape, dtype):
    return jax.ShapeDtypeStruct(shape, dtype)


def butterfly_sum(value, axis, bits, count):
    for bit in bits:
        pairs = [(i, i ^ bit) for i in range(count)]
        value = value.astype(jnp.bfloat16)
        taken = lax.ppermute(value, axis, pairs)
        value = value.astype(jnp.float32) + taken.astype(jnp.float32)
    return value


def powers_below(count):
    return [1 << n for n in range(count.bit_length() - 1)]


def message_kernel(copies, *refs):
    count = (len(refs) - 3) // 2
    operands, message_ref = refs[:count], refs[count]
    held, in_sems, out_sems = refs[count + 1 : -2], refs[-2], refs[-1]
    tok = operands[0].shape[0]
    halves = [pl.ds(0, tok // 2), pl.ds(tok // 2, tok // 2)]
    arriving = [
        pltpu.make_async_copy(ref.at[half], to.at[half], in_sems.at[n, i])
        for n, (ref, to) in enumerate(zip(operands, held))
        for i, half in enumerate(halves)
    ]
    for copy in arriving:
        copy.start()
    leaving = []
    for at, copy in enumerate(arriving):
        copy.wait()
        n, i = divmod(at, 2)
        for rank in range(message_ref.shape[0]):
            cols = pl.ds((rank // copies) * HD, HD)
            to = message_ref.at[rank, pl.ds(n * tok + i * (tok // 2), tok // 2), :]
            block = held[n].at[halves[i], cols]
            leaving.append(pltpu.make_async_copy(block, to, out_sems.at[len(leaving)]))
            leaving[-1].start()
    for copy in leaving:
        copy.wait()


def message_of(copies, ranks, *operands):
    tok = operands[0].shape[0]
    count = len(operands)
    shape = (ranks, count * tok, HD)
    return pl.pallas_call(
        functools.partial(message_kernel, copies),
        out_shape=shape_of(shape, operands[0].dtype),
        in_specs=[pl.BlockSpec(memory_space=pltpu.HBM)] * count,
        out_specs=pl.BlockSpec(memory_space=pltpu.HBM),
        scratch_shapes=[pltpu.VMEM(x.shape, x.dtype) for x in operands]
        + [pltpu.SemaphoreType.DMA((count, 2)), pltpu.SemaphoreType.DMA((2 * ranks * count,))],
        cost_estimate=pl.CostEstimate(
            flops=0, bytes_accessed=4 * math.prod(shape), transcendentals=0
        ),
    )(*operands)


def unpack_kernel(copies, back_ref, *refs):
    out_refs, down_ref = refs[:3], refs[3] if len(refs) > 3 else None
    tok = out_refs[0].shape[0]
    for at_head in range(out_refs[0].shape[1] // HD):
        cols = slice(at_head * HD, (at_head + 1) * HD)
        for n, ref in enumerate(out_refs):
            ref[:, cols] = back_ref[at_head * copies, n * tok : (n + 1) * tok, :]
        if down_ref is not None:
            down_ref[:, cols] = back_ref[at_head * copies, 3 * tok :, :].astype(jnp.float32)


def in_vmem(body, outs, *operands):
    whole = pl.BlockSpec(memory_space=pltpu.VMEM)
    size = sum(x.size * x.dtype.itemsize for x in operands)
    size += sum(x.size * x.dtype.itemsize for x in outs)
    return pl.pallas_call(
        body,
        out_shape=outs,
        in_specs=[whole] * len(operands),
        out_specs=[whole] * len(outs),
        compiler_params=pltpu.CompilerParams(vmem_limit_bytes=16 * 1024 * 1024),
        cost_estimate=pl.CostEstimate(flops=0, bytes_accessed=size, transcendentals=0),
    )(*operands)


def cotangent_kernel(chunks, plan_ref, *refs):
    pieces, (matrix_ref, up_ref, own_ref, sent_ref) = refs[:-4], refs[-4:]
    tok, cols = pieces[0].shape
    feats, low_rank = matrix_ref.shape[0], up_ref.shape[0]
    count = len(pieces)
    if chunks == 1:
        stacks = [(jnp.concatenate([p[...] for p in pieces], axis=0), pl.ds(0, cols))]
    else:
        stacks = [
            (p[...], pl.ds(pl.multiple_of(plan_ref[count + k], HD), cols))
            for k, p in enumerate(pieces)
        ]
    mine = [plan_ref[k] == 1 for k in range(count)]
    for ref, here in ((matrix_ref, pl.ds(0, feats)), (up_ref, pl.ds(feats, low_rank))):
        terms = [dot_nt(ref[:, at], rows) for rows, at in stacks]
        parts = [t[:, i : i + tok] for t in terms for i in range(0, t.shape[1], tok)]
        own_ref[here, :] = summed([jnp.where(m, p, 0.0) for m, p in zip(mine, parts)])
        sent = summed([jnp.where(m, 0.0, p) for m, p in zip(mine, parts)])
        sent_ref[here, :] = sent.astype(jnp.bfloat16)


def dout_kernel(copies, own_ref, taken_ref, mid_ref, message_ref):
    low_rank = mid_ref.shape[1]
    feats = own_ref.shape[0] - low_rank
    lora = own_ref[feats:, :] + taken_ref[feats:, :].astype(jnp.float32)
    for rank in range(message_ref.shape[0]):
        at = pl.ds((rank // copies) * HD, HD)
        part = own_ref[at, :] + taken_ref[at, :].astype(jnp.float32)
        message_ref[rank, 0:HD, :] = part.astype(jnp.bfloat16)
        message_ref[rank, HD : HD + low_rank, :] = lora.astype(jnp.bfloat16)
        message_ref[rank, HD + low_rank : HD + 2 * low_rank, :] = mid_ref[rank]


def on_device(
    sizes,
    head_query_rows,
    head_key_rows,
    head_value_rows,
    output_gradient,
    output_matrix,
    adapter_down_weight,
    adapter_up_weight,
):
    seqs, heads, subs = sizes
    tok, feats = head_query_rows.shape
    cols = output_gradient.shape[1]
    low_rank = adapter_up_weight.shape[0]
    local_heads = feats // HD
    block_rows = tok * subs
    ranks = GROUP // block_rows
    copies = ranks // local_heads
    shift_blocks = GROUP // 2 // block_rows

    seq = lax.axis_index("seq")
    head = lax.axis_index("head")
    sub = lax.axis_index("sub")
    shifted = head >= heads // 2
    rank = (seq + shift_blocks) % ranks
    my_head = rank // copies

    groups = []
    for at_head in range(heads):
        for first in range(0, seqs, ranks):
            members = [first + shift_blocks + i for i in range(ranks)]
            if at_head < heads // 2:
                members = [first + (m - first) % ranks for m in members]
            members = [m % seqs for m in members]
            groups.append([m * heads + at_head for m in members])
    scalars = jnp.full((1,), sub, jnp.int32)

    def in_order(blocks):
        half = ranks // 2
        turned = jnp.concatenate((blocks[half:], blocks[:half]), axis=0)
        return jnp.where(shifted, blocks, turned)


    def exchange(parts):
        return lax.all_to_all(
            parts, ("seq", "head"), 0, 0, axis_index_groups=groups, tiled=True
        )

    def swap(value):
        if subs == 1:
            return value
        return lax.ppermute(value, "sub", [(0, 1), (1, 0)])

    sent = message_of(copies, ranks, head_query_rows, head_key_rows, head_value_rows)
    sent, output_gradient, output_matrix = lax.optimization_barrier(
        (sent, output_gradient, output_matrix)
    )
    own = exchange(sent)

    chunks = heads // subs
    pieces = []
    for k in range(heads):
        pairs = []
        for src_head in range(heads):
            for src_sub in range(subs):
                j = (src_head % chunks) * subs + src_sub
                dst = ((j + k) % heads) * subs + src_head // chunks
                pairs.append((src_head * subs + src_sub, dst))
        pieces.append(lax.ppermute(output_gradient, ("head", "sub"), pairs))

    up_half = lax.dynamic_slice_in_dim(adapter_up_weight, sub * chunks * cols, chunks * cols, 1)
    folded = dot_nn(adapter_down_weight, up_half)
    folded = (output_matrix.astype(jnp.float32) + 2.0 * folded).astype(jnp.bfloat16)
    sources = [(head - k + heads) % heads for k in range(heads)]
    plan = [(j % subs == sub).astype(jnp.int32) for j in sources]
    plan += [(j // subs * cols).astype(jnp.int32) for j in sources]
    packed_own, packed_sent = call_kernel(
        functools.partial(cotangent_kernel, chunks),
        [
            shape_of((feats + low_rank, tok), jnp.float32),
            shape_of((feats + low_rank, tok), jnp.bfloat16),
        ],
        [],
        0,
        0,
        jnp.stack(plan),
        *pieces,
        folded,
        up_half,
        declared=1024,
        limit=16,
    )
    received = swap(packed_sent)
    down_head = lax.dynamic_slice_in_dim(adapter_down_weight, my_head * HD, HD, 0).T
    own, down_head, _ = lax.optimization_barrier((own, down_head, packed_sent))
    own = in_order(own)
    other = swap(own[:, tok:])

    rows = ranks * tok
    pair_count = rows * (rows + TILE)
    own_total, own_stats = call_kernel(
        functools.partial(forward_own_kernel, tok),
        [shape_of((HD, rows), jnp.float32), shape_of((8, rows), jnp.float32)],
        [],
        2 * pair_count * HD,
        pair_count // 2,
        scalars,
        own,
        limit=16,
    )
    attn_t, middle_rows, stats = call_kernel(
        functools.partial(forward_kernel, tok),
        [
            shape_of((HD, rows), jnp.bfloat16),
            shape_of((low_rank, rows), jnp.float32),
            shape_of((8, rows), jnp.float32),
        ],
        [],
        2 * pair_count * HD,
        pair_count // 2,
        scalars,
        own,
        other,
        own_total,
        own_stats,
        down_head,
        limit=16,
    )

    first_copy = rank % copies == 0
    middle_rows = middle_rows.astype(jnp.bfloat16).reshape(low_rank, ranks, tok)
    middle_rows = in_order(middle_rows.transpose(1, 0, 2))
    if copies > 1:
        middle_rows = jnp.where(first_copy, middle_rows, 0.0)
    (message,) = in_vmem(
        functools.partial(dout_kernel, copies),
        [shape_of((ranks, HD + 2 * low_rank, tok), jnp.bfloat16)],
        packed_own,
        received,
        middle_rows,
    )
    arrived = exchange(message)
    middle = jnp.sum(arrived[:, HD + low_rank :].astype(jnp.float32), axis=0)
    bit = 1
    while bit < heads:
        middle += lax.ppermute(middle, "head", [(i, i ^ bit) for i in range(heads)])
        bit *= 2
    up_part = 2.0 * dot_nn(middle.astype(jnp.bfloat16), output_gradient)

    dq, dk_own, dv_own, pair_other, down_part = call_kernel(
        functools.partial(backward_kernel, tok),
        [
            shape_of((ranks, tok, HD), jnp.bfloat16),
            shape_of((ranks, tok, HD), jnp.float32),
            shape_of((ranks, tok, HD), jnp.float32),
            shape_of((ranks, 2 * tok, HD), jnp.bfloat16),
            shape_of((low_rank, HD), jnp.float32),
        ],
        [pltpu.VMEM((rows, HD), jnp.float32)] * 4,
        10 * pair_count * HD,
        pair_count,
        scalars,
        own,
        other,
        in_order(arrived[:, : HD + low_rank]),
        attn_t,
        stats,
        limit=28,
    )
    pair_other, _ = lax.optimization_barrier((pair_other, middle))
    pair_received = swap(pair_other).astype(jnp.float32)
    down_rows = jnp.where(first_copy, down_part + swap(down_part), 0.0)
    dk = (dk_own + pair_received[:, :tok]).astype(jnp.bfloat16)
    dv = (dv_own + pair_received[:, tok:]).astype(jnp.bfloat16)
    down_rows = jnp.broadcast_to(down_rows.astype(jnp.bfloat16), (ranks, low_rank, HD))
    back_message = jnp.concatenate([*map(in_order, (dq, dk, dv)), down_rows], axis=1)
    back = exchange(back_message)
    outs = [shape_of((tok, feats), back.dtype)] * 3
    if seqs == ranks:
        outs.append(shape_of((low_rank, feats), jnp.float32))
    outs = list(in_vmem(functools.partial(unpack_kernel, copies), outs, back))
    if seqs > ranks:
        bits = [bit for bit in powers_below(seqs) if bit >= ranks]
        down_terms = back[::copies, 3 * tok :].astype(jnp.float32)
        down_terms = butterfly_sum(down_terms, "seq", bits, seqs)
        outs.append(down_terms.transpose(1, 0, 2).reshape(low_rank, feats))
    query_gradient, key_gradient, value_gradient, down_gradient = outs

    up_sum = butterfly_sum(up_part, "seq", powers_below(seqs), seqs)
    _, up_sum = lax.optimization_barrier((back, up_sum))
    up_gradient = butterfly_sum(up_sum, "sub", powers_below(subs), subs)
    return (query_gradient, key_gradient, value_gradient, down_gradient.T, up_gradient)


def solution(mesh):
    rows = P(("rep", "seq", "sub"), "head")
    sizes = (mesh.shape["seq"], mesh.shape["head"], mesh.shape["sub"])
    return jax.shard_map(
        functools.partial(on_device, sizes),
        mesh=mesh,
        in_specs=(rows, rows, rows, rows, P("head", "sub"), P("head", None), P()),
        out_specs=(rows, rows, rows, P(("rep", "head"), None), P("rep", "head")),
        check_vma=False,
    )
```

```python
import functools
import math

import jax
import jax.numpy as jnp
from jax import lax
from jax.experimental import pallas as pl
from jax.experimental.pallas import tpu as pltpu
from jax.sharding import PartitionSpec as P

HD = 128
GROUP = 2048
TILE = 256
HIDDEN = -1e30
SCALE = HD ** (-0.5)
LOG2_SCALE = SCALE * math.log2(math.e)


def dot_nt(left, right):
    return lax.dot_general(
        left, right, (((1,), (1,)), ((), ())), preferred_element_type=jnp.float32
    )


def dot_nn(left, right):
    return jnp.dot(left, right, preferred_element_type=jnp.float32)


def rows_of(ref, blocks, first, count):
    return ref[0:blocks, first : first + count, :].reshape(blocks * count, HD)


def scores_of(keys, queries, visible):
    scores = dot_nt(keys, queries)
    head = scores.shape[0] - TILE
    tail = jnp.where(visible, scores[head:], HIDDEN)
    return tail if head == 0 else jnp.concatenate((scores[:head], tail), axis=0)


def tile_index(dimension):
    shape = (TILE, 1) if dimension == 0 else (1, TILE)
    return lax.broadcasted_iota(jnp.int32, shape, dimension)


def own_visible():
    return tile_index(0) <= tile_index(1)


def other_visible(sub, tok):
    return tile_index(0) // tok < tile_index(1) // tok + sub


def summed(terms):
    return functools.reduce(jnp.add, terms)


def forward_own_kernel(tok, scalar_ref, own_ref, total_ref, stat_ref):
    blocks = own_ref.shape[0]
    step = TILE // tok
    values_t = rows_of(own_ref, blocks, 2 * tok, tok).T
    for tile in range(blocks // step):
        upto = (tile + 1) * step
        at = tile * TILE
        queries = own_ref[tile * step : upto, 0:tok, :].reshape(TILE, HD)
        scores = scores_of(rows_of(own_ref, upto, tok, tok), queries, own_visible())
        highest = jnp.max(scores, axis=0, keepdims=True)
        powers = jnp.exp2((scores - highest) * LOG2_SCALE)
        total_ref[:, at : at + TILE] = dot_nn(
            values_t[:, : upto * tok], powers.astype(jnp.bfloat16)
        )
        stat_ref[0:1, at : at + TILE] = highest
        stat_ref[1:2, at : at + TILE] = jnp.sum(powers, axis=0, keepdims=True)


def forward_kernel(
    tok,
    scalar_ref,
    own_ref,
    other_ref,
    total_ref,
    own_stat_ref,
    down_t_ref,
    attn_ref,
    mid_ref,
    stat_ref,
):
    blocks = own_ref.shape[0]
    step = TILE // tok
    sub = scalar_ref[0]
    values_t = rows_of(other_ref, blocks, tok, tok).T
    for tile in range(blocks // step):
        upto = (tile + 1) * step
        at = tile * TILE
        here = pl.ds(at, TILE)
        queries = own_ref[tile * step : upto, 0:tok, :].reshape(TILE, HD)
        scores = scores_of(
            rows_of(other_ref, upto, 0, tok), queries, other_visible(sub, tok)
        )
        own_highest = own_stat_ref[0:1, here]
        highest = jnp.maximum(own_highest, jnp.max(scores, axis=0, keepdims=True))
        powers = jnp.exp2((scores - highest) * LOG2_SCALE)
        share = jnp.exp2((own_highest - highest) * LOG2_SCALE)
        inverse = 1.0 / (
            own_stat_ref[1:2, here] * share + jnp.sum(powers, axis=0, keepdims=True)
        )
        attn = dot_nn(values_t[:, : upto * tok], powers.astype(jnp.bfloat16))
        attn = ((attn + total_ref[:, here] * share) * inverse).astype(jnp.bfloat16)
        attn_ref[:, here] = attn
        stat_ref[0:1, here] = highest
        stat_ref[1:2, here] = inverse
    mid_ref[...] = dot_nn(down_t_ref[...], attn_ref[...])


def backward_kernel(
    tok,
    scalar_ref,
    own_ref,
    other_ref,
    dout_ref,
    attn_ref,
    stat_ref,
    dq_ref,
    dk_own_ref,
    dv_own_ref,
    pair_other_ref,
    down_grad_ref,
    dk_own,
    dv_own,
    dk_other,
    dv_other,
):
    blocks = own_ref.shape[0]
    step = TILE // tok
    sub = scalar_ref[0]
    low_rank = down_grad_ref.shape[0]
    keys_own_t = rows_of(own_ref, blocks, tok, tok).T
    keys_other_t = rows_of(other_ref, blocks, 0, tok).T
    tiles = blocks // step
    lora = jnp.concatenate(
        [dout_ref[block, HD : HD + low_rank, :] for block in range(blocks)], axis=1
    )
    down_grad_ref[...] = 2.0 * dot_nt(lora, attn_ref[...])
    for tile in reversed(range(tiles)):
        upto = (tile + 1) * step
        width = upto * tok
        at = tile * TILE
        queries = own_ref[tile * step : upto, 0:tok, :].reshape(TILE, HD)
        douts_t = jnp.concatenate(
            [dout_ref[block, 0:HD, :] for block in range(tile * step, upto)], axis=1
        )
        highest = stat_ref[0:1, at : at + TILE]
        inverse = stat_ref[1:2, at : at + TILE]
        own = scores_of(rows_of(own_ref, upto, tok, tok), queries, own_visible())
        other = scores_of(
            rows_of(other_ref, upto, 0, tok), queries, other_visible(sub, tok)
        )
        own = jnp.exp2((own - highest) * LOG2_SCALE) * inverse
        other = jnp.exp2((other - highest) * LOG2_SCALE) * inverse
        dprob_own = dot_nn(rows_of(own_ref, upto, 2 * tok, tok), douts_t)
        dprob_other = dot_nn(rows_of(other_ref, upto, tok, tok), douts_t)
        delta = jnp.sum(own * dprob_own, axis=0, keepdims=True) + jnp.sum(
            other * dprob_other, axis=0, keepdims=True
        )
        ds_own = (own * (dprob_own - delta)).astype(jnp.bfloat16)
        ds_other = (other * (dprob_other - delta)).astype(jnp.bfloat16)
        dq = dot_nn(keys_own_t[:, :width], ds_own) + dot_nn(keys_other_t[:, :width], ds_other)
        dq = (dq * SCALE).T.astype(jnp.bfloat16)
        dq_ref[tile * step : upto] = dq.reshape(step, tok, HD)
        terms = (
            (dk_own, dot_nn(ds_own, queries)),
            (dk_other, dot_nn(ds_other, queries)),
            (dv_own, dot_nt(own.astype(jnp.bfloat16), douts_t)),
            (dv_other, dot_nt(other.astype(jnp.bfloat16), douts_t)),
        )
        for total, term in terms:
            if tile == tiles - 1:
                total[...] = term
            else:
                total[0:width] += term
    shape = (blocks, tok, HD)
    dk_own_ref[...] = (dk_own[...] * SCALE).reshape(shape)
    dv_own_ref[...] = dv_own[...].reshape(shape)
    pair_other_ref[:, 0:tok, :] = (dk_other[...] * SCALE).astype(jnp.bfloat16).reshape(shape)
    pair_other_ref[:, tok : 2 * tok, :] = dv_other[...].astype(jnp.bfloat16).reshape(shape)


def call_kernel(body, outs, scratch, flops, exps, *operands, declared=None, limit=48):
    in_bytes = sum(x.size * x.dtype.itemsize for x in operands)
    out_bytes = sum(x.size * x.dtype.itemsize for x in outs)
    specs = [pl.BlockSpec(memory_space=pltpu.SMEM)]
    specs += [pl.BlockSpec(memory_space=pltpu.VMEM)] * (len(operands) - 1)
    return pl.pallas_call(
        body,
        out_shape=outs,
        in_specs=specs,
        out_specs=[pl.BlockSpec(memory_space=pltpu.VMEM)] * len(outs),
        scratch_shapes=scratch,
        compiler_params=pltpu.CompilerParams(vmem_limit_bytes=limit * 1024 * 1024),
        cost_estimate=pl.CostEstimate(
            flops=flops,
            bytes_accessed=declared or in_bytes + out_bytes,
            transcendentals=exps,
        ),
    )(*operands)


def shape_of(shape, dtype):
    return jax.ShapeDtypeStruct(shape, dtype)


def butterfly_sum(value, axis, bits, count):
    for bit in bits:
        pairs = [(i, i ^ bit) for i in range(count)]
        value = value.astype(jnp.bfloat16)
        taken = lax.ppermute(value, axis, pairs)
        value = value.astype(jnp.float32) + taken.astype(jnp.float32)
    return value


def powers_below(count):
    return [1 << n for n in range(count.bit_length() - 1)]


def message_kernel(copies, *refs):
    count = (len(refs) - 3) // 3
    operands, message_ref = refs[:count], refs[count]
    held, grouped = refs[count + 1 : 2 * count + 1], refs[2 * count + 1 : 3 * count + 1]
    in_sems, out_sems = refs[-2], refs[-1]
    tok = operands[0].shape[0]
    arriving = [
        pltpu.make_async_copy(ref, to, in_sems.at[n])
        for n, (ref, to) in enumerate(zip(operands, held))
    ]
    for copy in arriving:
        copy.start()
    leaving = []
    for n, copy in enumerate(arriving):
        copy.wait()
        for rank in range(message_ref.shape[0]):
            at = (rank // copies) * HD
            grouped[n][rank] = held[n][:, at : at + HD]
        to = message_ref.at[:, pl.ds(n * tok, tok), :]
        leaving.append(pltpu.make_async_copy(grouped[n], to, out_sems.at[n]))
        leaving[-1].start()
    for copy in leaving:
        copy.wait()


def message_of(copies, ranks, *operands):
    tok = operands[0].shape[0]
    count = len(operands)
    shape = (ranks, count * tok, HD)
    return pl.pallas_call(
        functools.partial(message_kernel, copies),
        out_shape=shape_of(shape, operands[0].dtype),
        in_specs=[pl.BlockSpec(memory_space=pltpu.HBM)] * count,
        out_specs=pl.BlockSpec(memory_space=pltpu.HBM),
        scratch_shapes=[pltpu.VMEM(x.shape, x.dtype) for x in operands]
        + [pltpu.VMEM((ranks, tok, HD), x.dtype) for x in operands]
        + [pltpu.SemaphoreType.DMA((count,))] * 2,
        cost_estimate=pl.CostEstimate(
            flops=0, bytes_accessed=4 * math.prod(shape), transcendentals=0
        ),
    )(*operands)


def return_kernel(turn_ref, dq_ref, dk_ref, dv_ref, pair_ref, down_ref, taken_ref, *refs):
    message_ref, held, sems = refs
    blocks, tok, _ = dq_ref.shape
    down = (down_ref[...] + taken_ref[...]).astype(held.dtype)
    copies = []
    for slot in range(blocks):
        block = (slot + turn_ref[0]) % blocks
        held[slot, 0:tok, :] = dq_ref[block]
        dk = dk_ref[block] + pair_ref[block, 0:tok, :].astype(jnp.float32)
        dv = dv_ref[block] + pair_ref[block, tok : 2 * tok, :].astype(jnp.float32)
        held[slot, tok : 2 * tok, :] = dk.astype(held.dtype)
        held[slot, 2 * tok : 3 * tok, :] = dv.astype(held.dtype)
        held[slot, 3 * tok :, :] = down
        copies.append(pltpu.make_async_copy(held.at[slot], message_ref.at[slot], sems.at[slot]))
        copies[-1].start()
    for copy in copies:
        copy.wait()


def return_message(turn, dq, *operands):
    blocks, tok, _ = dq.shape
    shape = (blocks, 3 * tok + operands[-1].shape[0], HD)
    return pl.pallas_call(
        return_kernel,
        out_shape=shape_of(shape, dq.dtype),
        in_specs=[pl.BlockSpec(memory_space=pltpu.SMEM)]
        + [pl.BlockSpec(memory_space=pltpu.VMEM)] * (len(operands) + 1),
        out_specs=pl.BlockSpec(memory_space=pltpu.HBM),
        scratch_shapes=[pltpu.VMEM(shape, dq.dtype), pltpu.SemaphoreType.DMA((blocks,))],
        compiler_params=pltpu.CompilerParams(vmem_limit_bytes=16 * 1024 * 1024),
        cost_estimate=pl.CostEstimate(
            flops=0, bytes_accessed=4 * math.prod(shape), transcendentals=0
        ),
    )(turn, dq, *operands)


def unpack_kernel(copies, back_ref, *refs):
    out_refs, held, sems = refs[:3], refs[-4:-1], refs[-1]
    down_ref = refs[3] if len(refs) > 7 else None
    tok = out_refs[0].shape[0]
    heads = out_refs[0].shape[1] // HD
    leaving = []
    for n, ref in enumerate(out_refs):
        for at_head in range(heads):
            cols = slice(at_head * HD, (at_head + 1) * HD)
            held[n][:, cols] = back_ref[at_head * copies, n * tok : (n + 1) * tok, :]
        leaving.append(pltpu.make_async_copy(held[n], ref, sems.at[n]))
        leaving[-1].start()
    if down_ref is not None:
        for at_head in range(heads):
            cols = slice(at_head * HD, (at_head + 1) * HD)
            down_ref[:, cols] = back_ref[at_head * copies, 3 * tok :, :].astype(jnp.float32)
    for copy in leaving:
        copy.wait()


def in_vmem(body, outs, *operands):
    whole = pl.BlockSpec(memory_space=pltpu.VMEM)
    size = sum(x.size * x.dtype.itemsize for x in operands)
    size += sum(x.size * x.dtype.itemsize for x in outs)
    return pl.pallas_call(
        body,
        out_shape=outs,
        in_specs=[whole] * len(operands),
        out_specs=[whole] * len(outs),
        compiler_params=pltpu.CompilerParams(vmem_limit_bytes=16 * 1024 * 1024),
        cost_estimate=pl.CostEstimate(flops=0, bytes_accessed=size, transcendentals=0),
    )(*operands)


def cotangent_kernel(chunks, plan_ref, *refs):
    pieces, (matrix_ref, up_ref, own_ref, sent_ref) = refs[:-4], refs[-4:]
    tok, cols = pieces[0].shape
    feats, low_rank = matrix_ref.shape[0], up_ref.shape[0]
    count = len(pieces)
    if chunks == 1:
        stacks = [(jnp.concatenate([p[...] for p in pieces], axis=0), pl.ds(0, cols))]
    else:
        stacks = [
            (p[...], pl.ds(pl.multiple_of(plan_ref[count + k], HD), cols))
            for k, p in enumerate(pieces)
        ]
    mine = [plan_ref[k] == 1 for k in range(count)]
    for ref, here in ((matrix_ref, pl.ds(0, feats)), (up_ref, pl.ds(feats, low_rank))):
        terms = [dot_nt(ref[:, at], rows) for rows, at in stacks]
        parts = [t[:, i : i + tok] for t in terms for i in range(0, t.shape[1], tok)]
        own_ref[here, :] = summed([jnp.where(m, p, 0.0) for m, p in zip(mine, parts)])
        sent = summed([jnp.where(m, 0.0, p) for m, p in zip(mine, parts)])
        sent_ref[here, :] = sent.astype(jnp.bfloat16)


def dout_kernel(copies, own_ref, taken_ref, mid_ref, message_ref):
    low_rank = mid_ref.shape[1]
    feats = own_ref.shape[0] - low_rank
    lora = own_ref[feats:, :] + taken_ref[feats:, :].astype(jnp.float32)
    for rank in range(message_ref.shape[0]):
        at = pl.ds((rank // copies) * HD, HD)
        part = own_ref[at, :] + taken_ref[at, :].astype(jnp.float32)
        message_ref[rank, 0:HD, :] = part.astype(jnp.bfloat16)
        message_ref[rank, HD : HD + low_rank, :] = lora.astype(jnp.bfloat16)
        message_ref[rank, HD + low_rank : HD + 2 * low_rank, :] = mid_ref[rank]


def on_device(
    sizes,
    head_query_rows,
    head_key_rows,
    head_value_rows,
    output_gradient,
    output_matrix,
    adapter_down_weight,
    adapter_up_weight,
):
    seqs, heads, subs = sizes
    tok, feats = head_query_rows.shape
    cols = output_gradient.shape[1]
    low_rank = adapter_up_weight.shape[0]
    local_heads = feats // HD
    block_rows = tok * subs
    ranks = GROUP // block_rows
    copies = ranks // local_heads
    shift_blocks = GROUP // 2 // block_rows

    seq = lax.axis_index("seq")
    head = lax.axis_index("head")
    sub = lax.axis_index("sub")
    shifted = head >= heads // 2
    rank = (seq + shift_blocks) % ranks
    my_head = rank // copies

    groups = []
    for at_head in range(heads):
        for first in range(0, seqs, ranks):
            members = [first + shift_blocks + i for i in range(ranks)]
            if at_head < heads // 2:
                members = [first + (m - first) % ranks for m in members]
            members = [m % seqs for m in members]
            groups.append([m * heads + at_head for m in members])
    scalars = jnp.full((1,), sub, jnp.int32)

    def in_order(blocks):
        half = ranks // 2
        turned = jnp.concatenate((blocks[half:], blocks[:half]), axis=0)
        return jnp.where(shifted, blocks, turned)


    def exchange(parts):
        return lax.all_to_all(
            parts, ("seq", "head"), 0, 0, axis_index_groups=groups, tiled=True
        )

    def swap(value):
        if subs == 1:
            return value
        return lax.ppermute(value, "sub", [(0, 1), (1, 0)])

    sent = message_of(copies, ranks, head_query_rows, head_key_rows, head_value_rows)
    sent, output_gradient, output_matrix = lax.optimization_barrier(
        (sent, output_gradient, output_matrix)
    )
    own = exchange(sent)

    chunks = heads // subs
    pieces = []
    for k in range(heads):
        pairs = []
        for src_head in range(heads):
            for src_sub in range(subs):
                j = (src_head % chunks) * subs + src_sub
                dst = ((j + k) % heads) * subs + src_head // chunks
                pairs.append((src_head * subs + src_sub, dst))
        pieces.append(lax.ppermute(output_gradient, ("head", "sub"), pairs))

    up_half = lax.dynamic_slice_in_dim(adapter_up_weight, sub * chunks * cols, chunks * cols, 1)
    folded = dot_nn(adapter_down_weight, up_half)
    folded = (output_matrix.astype(jnp.float32) + 2.0 * folded).astype(jnp.bfloat16)
    sources = [(head - k + heads) % heads for k in range(heads)]
    plan = [(j % subs == sub).astype(jnp.int32) for j in sources]
    plan += [(j // subs * cols).astype(jnp.int32) for j in sources]
    packed_own, packed_sent = call_kernel(
        functools.partial(cotangent_kernel, chunks),
        [
            shape_of((feats + low_rank, tok), jnp.float32),
            shape_of((feats + low_rank, tok), jnp.bfloat16),
        ],
        [],
        0,
        0,
        jnp.stack(plan),
        *pieces,
        folded,
        up_half,
        declared=1024,
        limit=16,
    )
    received = swap(packed_sent)
    down_head = lax.dynamic_slice_in_dim(adapter_down_weight, my_head * HD, HD, 0).T
    own, down_head, _ = lax.optimization_barrier((own, down_head, packed_sent))
    own = in_order(own)
    other = swap(own[:, tok:])

    rows = ranks * tok
    pair_count = rows * (rows + TILE)
    own_total, own_stats = call_kernel(
        functools.partial(forward_own_kernel, tok),
        [shape_of((HD, rows), jnp.float32), shape_of((8, rows), jnp.float32)],
        [],
        2 * pair_count * HD,
        pair_count // 2,
        scalars,
        own,
        limit=16,
    )
    attn_t, middle_rows, stats = call_kernel(
        functools.partial(forward_kernel, tok),
        [
            shape_of((HD, rows), jnp.bfloat16),
            shape_of((low_rank, rows), jnp.float32),
            shape_of((8, rows), jnp.float32),
        ],
        [],
        2 * pair_count * HD,
        pair_count // 2,
        scalars,
        own,
        other,
        own_total,
        own_stats,
        down_head,
        limit=16,
    )

    first_copy = rank % copies == 0
    middle_rows = middle_rows.astype(jnp.bfloat16).reshape(low_rank, ranks, tok)
    middle_rows = in_order(middle_rows.transpose(1, 0, 2))
    if copies > 1:
        middle_rows = jnp.where(first_copy, middle_rows, 0.0)
    (message,) = in_vmem(
        functools.partial(dout_kernel, copies),
        [shape_of((ranks, HD + 2 * low_rank, tok), jnp.bfloat16)],
        packed_own,
        received,
        middle_rows,
    )
    arrived = exchange(message)
    middle = jnp.sum(arrived[:, HD + low_rank :].astype(jnp.float32), axis=0)
    bit = 1
    while bit < heads:
        middle += lax.ppermute(middle, "head", [(i, i ^ bit) for i in range(heads)])
        bit *= 2
    up_part = 2.0 * dot_nn(middle.astype(jnp.bfloat16), output_gradient)

    dq, dk_own, dv_own, pair_other, down_part = call_kernel(
        functools.partial(backward_kernel, tok),
        [
            shape_of((ranks, tok, HD), jnp.bfloat16),
            shape_of((ranks, tok, HD), jnp.float32),
            shape_of((ranks, tok, HD), jnp.float32),
            shape_of((ranks, 2 * tok, HD), jnp.bfloat16),
            shape_of((low_rank, HD), jnp.float32),
        ],
        [pltpu.VMEM((rows, HD), jnp.float32)] * 4,
        10 * pair_count * HD,
        pair_count,
        scalars,
        own,
        other,
        in_order(arrived[:, : HD + low_rank]),
        attn_t,
        stats,
        limit=28,
    )
    pair_other, _ = lax.optimization_barrier((pair_other, middle))
    turn = jnp.full((1,), jnp.where(shifted, 0, ranks // 2), jnp.int32)
    back_message = return_message(
        turn, dq, dk_own, dv_own, swap(pair_other), down_part, swap(down_part)
    )
    back = exchange(back_message)
    outs = [shape_of((tok, feats), back.dtype)] * 3
    if seqs == ranks:
        outs.append(shape_of((low_rank, feats), jnp.float32))
    whole = pl.BlockSpec(memory_space=pltpu.VMEM)
    outs = list(
        pl.pallas_call(
            functools.partial(unpack_kernel, copies),
            out_shape=outs,
            in_specs=[whole],
            out_specs=[pl.BlockSpec(memory_space=pltpu.HBM)] * 3 + [whole] * (len(outs) - 3),
            scratch_shapes=[pltpu.VMEM((tok, feats), back.dtype)] * 3
            + [pltpu.SemaphoreType.DMA((3,))],
            compiler_params=pltpu.CompilerParams(vmem_limit_bytes=16 * 1024 * 1024),
            cost_estimate=pl.CostEstimate(
                flops=0, bytes_accessed=4 * back.size, transcendentals=0
            ),
        )(back)
    )
    if seqs > ranks:
        bits = [bit for bit in powers_below(seqs) if bit >= ranks]
        down_terms = back[::copies, 3 * tok :].astype(jnp.float32)
        down_terms = butterfly_sum(down_terms, "seq", bits, seqs)
        outs.append(down_terms.transpose(1, 0, 2).reshape(low_rank, feats))
    query_gradient, key_gradient, value_gradient, down_gradient = outs

    up_sum = butterfly_sum(up_part, "seq", powers_below(seqs), seqs)
    _, up_sum = lax.optimization_barrier((back, up_sum))
    up_gradient = butterfly_sum(up_sum, "sub", powers_below(subs), subs)
    return (query_gradient, key_gradient, value_gradient, down_gradient.T, up_gradient)


def solution(mesh):
    rows = P(("rep", "seq", "sub"), "head")
    sizes = (mesh.shape["seq"], mesh.shape["head"], mesh.shape["sub"])
    return jax.shard_map(
        functools.partial(on_device, sizes),
        mesh=mesh,
        in_specs=(rows, rows, rows, rows, P("head", "sub"), P("head", None), P()),
        out_specs=(rows, rows, rows, P(("rep", "head"), None), P("rep", "head")),
        check_vma=False,
    )
```

```python
import functools
import math

import jax
import jax.numpy as jnp
from jax import lax
from jax.experimental import pallas as pl
from jax.experimental.pallas import tpu as pltpu
from jax.sharding import PartitionSpec as P

HD = 128
GROUP = 2048
TILE = 256
HIDDEN = -1e30
SCALE = HD ** (-0.5)
LOG2_SCALE = SCALE * math.log2(math.e)


def dot_nt(left, right):
    return lax.dot_general(
        left, right, (((1,), (1,)), ((), ())), preferred_element_type=jnp.float32
    )


def dot_nn(left, right):
    return jnp.dot(left, right, preferred_element_type=jnp.float32)


def rows_of(ref, blocks, first, count):
    return ref[0:blocks, first : first + count, :].reshape(blocks * count, HD)


def scores_of(keys, queries, visible):
    scores = dot_nt(keys, queries)
    head = scores.shape[0] - TILE
    tail = jnp.where(visible, scores[head:], HIDDEN)
    return tail if head == 0 else jnp.concatenate((scores[:head], tail), axis=0)


def tile_index(dimension):
    shape = (TILE, 1) if dimension == 0 else (1, TILE)
    return lax.broadcasted_iota(jnp.int32, shape, dimension)


def own_visible():
    return tile_index(0) <= tile_index(1)


def other_visible(sub, tok):
    return tile_index(0) // tok < tile_index(1) // tok + sub


def summed(terms):
    return functools.reduce(jnp.add, terms)


def ahead(prepare, tiles):
    tiles = list(tiles)
    ready = prepare(tiles[0])
    for tile, following in zip(tiles, tiles[1:] + [None]):
        present, ready = ready, None if following is None else prepare(following)
        yield tile, present


def forward_own_kernel(tok, scalar_ref, own_ref, total_ref, stat_ref):
    blocks = own_ref.shape[0]
    step = TILE // tok
    values_t = rows_of(own_ref, blocks, 2 * tok, tok).T

    def prepare(tile):
        upto = (tile + 1) * step
        queries = own_ref[tile * step : upto, 0:tok, :].reshape(TILE, HD)
        return scores_of(rows_of(own_ref, upto, tok, tok), queries, own_visible())

    for tile, scores in ahead(prepare, range(blocks // step)):
        upto = (tile + 1) * step
        at = tile * TILE
        highest = jnp.max(scores, axis=0, keepdims=True)
        powers = jnp.exp2((scores - highest) * LOG2_SCALE)
        total_ref[:, at : at + TILE] = dot_nn(
            values_t[:, : upto * tok], powers.astype(jnp.bfloat16)
        )
        stat_ref[0:1, at : at + TILE] = highest
        stat_ref[1:2, at : at + TILE] = jnp.sum(powers, axis=0, keepdims=True)


def forward_kernel(
    tok,
    scalar_ref,
    own_ref,
    other_ref,
    total_ref,
    own_stat_ref,
    down_t_ref,
    attn_ref,
    mid_ref,
    stat_ref,
):
    blocks = own_ref.shape[0]
    step = TILE // tok
    sub = scalar_ref[0]
    values_t = rows_of(other_ref, blocks, tok, tok).T

    def prepare(tile):
        upto = (tile + 1) * step
        queries = own_ref[tile * step : upto, 0:tok, :].reshape(TILE, HD)
        keys = rows_of(other_ref, upto, 0, tok)
        return scores_of(keys, queries, other_visible(sub, tok))

    for tile, scores in ahead(prepare, range(blocks // step)):
        upto = (tile + 1) * step
        here = pl.ds(tile * TILE, TILE)
        own_highest = own_stat_ref[0:1, here]
        highest = jnp.maximum(own_highest, jnp.max(scores, axis=0, keepdims=True))
        powers = jnp.exp2((scores - highest) * LOG2_SCALE)
        share = jnp.exp2((own_highest - highest) * LOG2_SCALE)
        inverse = 1.0 / (
            own_stat_ref[1:2, here] * share + jnp.sum(powers, axis=0, keepdims=True)
        )
        attn = dot_nn(values_t[:, : upto * tok], powers.astype(jnp.bfloat16))
        attn = ((attn + total_ref[:, here] * share) * inverse).astype(jnp.bfloat16)
        attn_ref[:, here] = attn
        stat_ref[0:1, here] = highest
        stat_ref[1:2, here] = inverse
    mid_ref[...] = dot_nn(down_t_ref[...], attn_ref[...])


def backward_kernel(
    tok,
    scalar_ref,
    own_ref,
    other_ref,
    dout_ref,
    attn_ref,
    stat_ref,
    dq_ref,
    dk_own_ref,
    dv_own_ref,
    pair_other_ref,
    down_grad_ref,
    dk_own,
    dv_own,
    dk_other,
    dv_other,
):
    blocks = own_ref.shape[0]
    step = TILE // tok
    sub = scalar_ref[0]
    low_rank = down_grad_ref.shape[0]
    keys_own_t = rows_of(own_ref, blocks, tok, tok).T
    keys_other_t = rows_of(other_ref, blocks, 0, tok).T
    tiles = blocks // step
    lora = jnp.concatenate(
        [dout_ref[block, HD : HD + low_rank, :] for block in range(blocks)], axis=1
    )
    down_grad_ref[...] = 2.0 * dot_nt(lora, attn_ref[...])

    def prepare(tile):
        upto = (tile + 1) * step
        queries = own_ref[tile * step : upto, 0:tok, :].reshape(TILE, HD)
        douts_t = jnp.concatenate(
            [dout_ref[block, 0:HD, :] for block in range(tile * step, upto)], axis=1
        )
        own = scores_of(rows_of(own_ref, upto, tok, tok), queries, own_visible())
        other = scores_of(
            rows_of(other_ref, upto, 0, tok), queries, other_visible(sub, tok)
        )
        dprob_own = dot_nn(rows_of(own_ref, upto, 2 * tok, tok), douts_t)
        dprob_other = dot_nn(rows_of(other_ref, upto, tok, tok), douts_t)
        return queries, douts_t, own, other, dprob_own, dprob_other

    for tile, prepared in ahead(prepare, reversed(range(tiles))):
        queries, douts_t, own, other, dprob_own, dprob_other = prepared
        upto = (tile + 1) * step
        width = upto * tok
        at = tile * TILE
        highest = stat_ref[0:1, at : at + TILE]
        inverse = stat_ref[1:2, at : at + TILE]
        own = jnp.exp2((own - highest) * LOG2_SCALE) * inverse
        other = jnp.exp2((other - highest) * LOG2_SCALE) * inverse
        delta = jnp.sum(own * dprob_own, axis=0, keepdims=True) + jnp.sum(
            other * dprob_other, axis=0, keepdims=True
        )
        ds_own = (own * (dprob_own - delta)).astype(jnp.bfloat16)
        ds_other = (other * (dprob_other - delta)).astype(jnp.bfloat16)
        dq = dot_nn(keys_own_t[:, :width], ds_own) + dot_nn(keys_other_t[:, :width], ds_other)
        dq = (dq * SCALE).T.astype(jnp.bfloat16)
        dq_ref[tile * step : upto] = dq.reshape(step, tok, HD)
        terms = (
            (dk_own, dot_nn(ds_own, queries)),
            (dk_other, dot_nn(ds_other, queries)),
            (dv_own, dot_nt(own.astype(jnp.bfloat16), douts_t)),
            (dv_other, dot_nt(other.astype(jnp.bfloat16), douts_t)),
        )
        for total, term in terms:
            if tile == tiles - 1:
                total[...] = term
            else:
                total[0:width] += term
    shape = (blocks, tok, HD)
    dk_own_ref[...] = (dk_own[...] * SCALE).reshape(shape)
    dv_own_ref[...] = dv_own[...].reshape(shape)
    pair_other_ref[:, 0:tok, :] = (dk_other[...] * SCALE).astype(jnp.bfloat16).reshape(shape)
    pair_other_ref[:, tok : 2 * tok, :] = dv_other[...].astype(jnp.bfloat16).reshape(shape)


def call_kernel(body, outs, scratch, flops, exps, *operands, declared=None, limit=48):
    in_bytes = sum(x.size * x.dtype.itemsize for x in operands)
    out_bytes = sum(x.size * x.dtype.itemsize for x in outs)
    specs = [pl.BlockSpec(memory_space=pltpu.SMEM)]
    specs += [pl.BlockSpec(memory_space=pltpu.VMEM)] * (len(operands) - 1)
    return pl.pallas_call(
        body,
        out_shape=outs,
        in_specs=specs,
        out_specs=[pl.BlockSpec(memory_space=pltpu.VMEM)] * len(outs),
        scratch_shapes=scratch,
        compiler_params=pltpu.CompilerParams(vmem_limit_bytes=limit * 1024 * 1024),
        cost_estimate=pl.CostEstimate(
            flops=flops,
            bytes_accessed=declared or in_bytes + out_bytes,
            transcendentals=exps,
        ),
    )(*operands)


def shape_of(shape, dtype):
    return jax.ShapeDtypeStruct(shape, dtype)


def butterfly_sum(value, axis, bits, count):
    for bit in bits:
        pairs = [(i, i ^ bit) for i in range(count)]
        value = value.astype(jnp.bfloat16)
        taken = lax.ppermute(value, axis, pairs)
        value = value.astype(jnp.float32) + taken.astype(jnp.float32)
    return value


def powers_below(count):
    return [1 << n for n in range(count.bit_length() - 1)]


def message_kernel(copies, *refs):
    count = (len(refs) - 3) // 3
    operands, message_ref = refs[:count], refs[count]
    held, grouped = refs[count + 1 : 2 * count + 1], refs[2 * count + 1 : 3 * count + 1]
    in_sems, out_sems = refs[-2], refs[-1]
    tok = operands[0].shape[0]
    arriving = [
        pltpu.make_async_copy(ref, to, in_sems.at[n])
        for n, (ref, to) in enumerate(zip(operands, held))
    ]
    for copy in arriving:
        copy.start()
    leaving = []
    for n, copy in enumerate(arriving):
        copy.wait()
        for rank in range(message_ref.shape[0]):
            at = (rank // copies) * HD
            grouped[n][rank] = held[n][:, at : at + HD]
        to = message_ref.at[:, pl.ds(n * tok, tok), :]
        leaving.append(pltpu.make_async_copy(grouped[n], to, out_sems.at[n]))
        leaving[-1].start()
    for copy in leaving:
        copy.wait()


def message_of(copies, ranks, *operands):
    tok = operands[0].shape[0]
    count = len(operands)
    shape = (ranks, count * tok, HD)
    return pl.pallas_call(
        functools.partial(message_kernel, copies),
        out_shape=shape_of(shape, operands[0].dtype),
        in_specs=[pl.BlockSpec(memory_space=pltpu.HBM)] * count,
        out_specs=pl.BlockSpec(memory_space=pltpu.HBM),
        scratch_shapes=[pltpu.VMEM(x.shape, x.dtype) for x in operands]
        + [pltpu.VMEM((ranks, tok, HD), x.dtype) for x in operands]
        + [pltpu.SemaphoreType.DMA((count,))] * 2,
        cost_estimate=pl.CostEstimate(
            flops=0, bytes_accessed=4 * math.prod(shape), transcendentals=0
        ),
    )(*operands)


def return_kernel(turn_ref, dq_ref, dk_ref, dv_ref, pair_ref, down_ref, taken_ref, *refs):
    message_ref, held, sems = refs
    blocks, tok, _ = dq_ref.shape
    down = (down_ref[...] + taken_ref[...]).astype(held.dtype)
    copies = []
    for slot in range(blocks):
        block = (slot + turn_ref[0]) % blocks
        held[slot, 0:tok, :] = dq_ref[block]
        dk = dk_ref[block] + pair_ref[block, 0:tok, :].astype(jnp.float32)
        dv = dv_ref[block] + pair_ref[block, tok : 2 * tok, :].astype(jnp.float32)
        held[slot, tok : 2 * tok, :] = dk.astype(held.dtype)
        held[slot, 2 * tok : 3 * tok, :] = dv.astype(held.dtype)
        held[slot, 3 * tok :, :] = down
        copies.append(pltpu.make_async_copy(held.at[slot], message_ref.at[slot], sems.at[slot]))
        copies[-1].start()
    for copy in copies:
        copy.wait()


def return_message(turn, dq, *operands):
    blocks, tok, _ = dq.shape
    shape = (blocks, 3 * tok + operands[-1].shape[0], HD)
    return pl.pallas_call(
        return_kernel,
        out_shape=shape_of(shape, dq.dtype),
        in_specs=[pl.BlockSpec(memory_space=pltpu.SMEM)]
        + [pl.BlockSpec(memory_space=pltpu.VMEM)] * (len(operands) + 1),
        out_specs=pl.BlockSpec(memory_space=pltpu.HBM),
        scratch_shapes=[pltpu.VMEM(shape, dq.dtype), pltpu.SemaphoreType.DMA((blocks,))],
        compiler_params=pltpu.CompilerParams(vmem_limit_bytes=16 * 1024 * 1024),
        cost_estimate=pl.CostEstimate(
            flops=0, bytes_accessed=4 * math.prod(shape), transcendentals=0
        ),
    )(turn, dq, *operands)


def unpack_kernel(copies, back_ref, *refs):
    out_refs, down_ref = refs[:3], refs[3] if len(refs) > 3 else None
    tok = out_refs[0].shape[0]
    for at_head in range(out_refs[0].shape[1] // HD):
        cols = slice(at_head * HD, (at_head + 1) * HD)
        for n, ref in enumerate(out_refs):
            ref[:, cols] = back_ref[at_head * copies, n * tok : (n + 1) * tok, :]
        if down_ref is not None:
            down_ref[:, cols] = back_ref[at_head * copies, 3 * tok :, :].astype(jnp.float32)


def in_vmem(body, outs, *operands):
    whole = pl.BlockSpec(memory_space=pltpu.VMEM)
    size = sum(x.size * x.dtype.itemsize for x in operands)
    size += sum(x.size * x.dtype.itemsize for x in outs)
    return pl.pallas_call(
        body,
        out_shape=outs,
        in_specs=[whole] * len(operands),
        out_specs=[whole] * len(outs),
        compiler_params=pltpu.CompilerParams(vmem_limit_bytes=16 * 1024 * 1024),
        cost_estimate=pl.CostEstimate(flops=0, bytes_accessed=size, transcendentals=0),
    )(*operands)


def cotangent_kernel(chunks, plan_ref, *refs):
    pieces, (matrix_ref, up_ref, own_ref, sent_ref) = refs[:-4], refs[-4:]
    tok, cols = pieces[0].shape
    feats, low_rank = matrix_ref.shape[0], up_ref.shape[0]
    count = len(pieces)
    if chunks == 1:
        stacks = [(jnp.concatenate([p[...] for p in pieces], axis=0), pl.ds(0, cols))]
    else:
        stacks = [
            (p[...], pl.ds(pl.multiple_of(plan_ref[count + k], HD), cols))
            for k, p in enumerate(pieces)
        ]
    mine = [plan_ref[k] == 1 for k in range(count)]
    for ref, here in ((matrix_ref, pl.ds(0, feats)), (up_ref, pl.ds(feats, low_rank))):
        terms = [dot_nt(ref[:, at], rows) for rows, at in stacks]
        parts = [t[:, i : i + tok] for t in terms for i in range(0, t.shape[1], tok)]
        own_ref[here, :] = summed([jnp.where(m, p, 0.0) for m, p in zip(mine, parts)])
        sent = summed([jnp.where(m, 0.0, p) for m, p in zip(mine, parts)])
        sent_ref[here, :] = sent.astype(jnp.bfloat16)


def dout_kernel(copies, own_ref, taken_ref, mid_ref, message_ref):
    low_rank = mid_ref.shape[1]
    feats = own_ref.shape[0] - low_rank
    lora = own_ref[feats:, :] + taken_ref[feats:, :].astype(jnp.float32)
    for rank in range(message_ref.shape[0]):
        at = pl.ds((rank // copies) * HD, HD)
        part = own_ref[at, :] + taken_ref[at, :].astype(jnp.float32)
        message_ref[rank, 0:HD, :] = part.astype(jnp.bfloat16)
        message_ref[rank, HD : HD + low_rank, :] = lora.astype(jnp.bfloat16)
        message_ref[rank, HD + low_rank : HD + 2 * low_rank, :] = mid_ref[rank]


def on_device(
    sizes,
    head_query_rows,
    head_key_rows,
    head_value_rows,
    output_gradient,
    output_matrix,
    adapter_down_weight,
    adapter_up_weight,
):
    seqs, heads, subs = sizes
    tok, feats = head_query_rows.shape
    cols = output_gradient.shape[1]
    low_rank = adapter_up_weight.shape[0]
    local_heads = feats // HD
    block_rows = tok * subs
    ranks = GROUP // block_rows
    copies = ranks // local_heads
    shift_blocks = GROUP // 2 // block_rows

    seq = lax.axis_index("seq")
    head = lax.axis_index("head")
    sub = lax.axis_index("sub")
    shifted = head >= heads // 2
    rank = (seq + shift_blocks) % ranks
    my_head = rank // copies

    groups = []
    for at_head in range(heads):
        for first in range(0, seqs, ranks):
            members = [first + shift_blocks + i for i in range(ranks)]
            if at_head < heads // 2:
                members = [first + (m - first) % ranks for m in members]
            members = [m % seqs for m in members]
            groups.append([m * heads + at_head for m in members])
    scalars = jnp.full((1,), sub, jnp.int32)

    def in_order(blocks):
        half = ranks // 2
        turned = jnp.concatenate((blocks[half:], blocks[:half]), axis=0)
        return jnp.where(shifted, blocks, turned)


    def exchange(parts):
        return lax.all_to_all(
            parts, ("seq", "head"), 0, 0, axis_index_groups=groups, tiled=True
        )

    def swap(value):
        if subs == 1:
            return value
        return lax.ppermute(value, "sub", [(0, 1), (1, 0)])

    sent = message_of(copies, ranks, head_query_rows, head_key_rows, head_value_rows)
    sent, output_gradient, output_matrix = lax.optimization_barrier(
        (sent, output_gradient, output_matrix)
    )
    own = exchange(sent)

    chunks = heads // subs
    pieces = []
    for k in range(heads):
        pairs = []
        for src_head in range(heads):
            for src_sub in range(subs):
                j = (src_head % chunks) * subs + src_sub
                dst = ((j + k) % heads) * subs + src_head // chunks
                pairs.append((src_head * subs + src_sub, dst))
        pieces.append(lax.ppermute(output_gradient, ("head", "sub"), pairs))

    up_half = lax.dynamic_slice_in_dim(adapter_up_weight, sub * chunks * cols, chunks * cols, 1)
    folded = dot_nn(adapter_down_weight, up_half)
    folded = (output_matrix.astype(jnp.float32) + 2.0 * folded).astype(jnp.bfloat16)
    sources = [(head - k + heads) % heads for k in range(heads)]
    plan = [(j % subs == sub).astype(jnp.int32) for j in sources]
    plan += [(j // subs * cols).astype(jnp.int32) for j in sources]
    packed_own, packed_sent = call_kernel(
        functools.partial(cotangent_kernel, chunks),
        [
            shape_of((feats + low_rank, tok), jnp.float32),
            shape_of((feats + low_rank, tok), jnp.bfloat16),
        ],
        [],
        0,
        0,
        jnp.stack(plan),
        *pieces,
        folded,
        up_half,
        declared=1024,
        limit=16,
    )
    received = swap(packed_sent)
    down_head = lax.dynamic_slice_in_dim(adapter_down_weight, my_head * HD, HD, 0).T
    own, down_head, _ = lax.optimization_barrier((own, down_head, packed_sent))
    own = in_order(own)
    other = swap(own[:, tok:])

    rows = ranks * tok
    pair_count = rows * (rows + TILE)
    own_total, own_stats = call_kernel(
        functools.partial(forward_own_kernel, tok),
        [shape_of((HD, rows), jnp.float32), shape_of((8, rows), jnp.float32)],
        [],
        2 * pair_count * HD,
        pair_count // 2,
        scalars,
        own,
        limit=16,
    )
    attn_t, middle_rows, stats = call_kernel(
        functools.partial(forward_kernel, tok),
        [
            shape_of((HD, rows), jnp.bfloat16),
            shape_of((low_rank, rows), jnp.float32),
            shape_of((8, rows), jnp.float32),
        ],
        [],
        2 * pair_count * HD,
        pair_count // 2,
        scalars,
        own,
        other,
        own_total,
        own_stats,
        down_head,
        limit=16,
    )

    first_copy = rank % copies == 0
    middle_rows = middle_rows.astype(jnp.bfloat16).reshape(low_rank, ranks, tok)
    middle_rows = in_order(middle_rows.transpose(1, 0, 2))
    if copies > 1:
        middle_rows = jnp.where(first_copy, middle_rows, 0.0)
    (message,) = in_vmem(
        functools.partial(dout_kernel, copies),
        [shape_of((ranks, HD + 2 * low_rank, tok), jnp.bfloat16)],
        packed_own,
        received,
        middle_rows,
    )
    arrived = exchange(message)
    middle = jnp.sum(arrived[:, HD + low_rank :].astype(jnp.float32), axis=0)
    bit = 1
    while bit < heads:
        middle += lax.ppermute(middle, "head", [(i, i ^ bit) for i in range(heads)])
        bit *= 2
    up_part = 2.0 * dot_nn(middle.astype(jnp.bfloat16), output_gradient)

    dq, dk_own, dv_own, pair_other, down_part = call_kernel(
        functools.partial(backward_kernel, tok),
        [
            shape_of((ranks, tok, HD), jnp.bfloat16),
            shape_of((ranks, tok, HD), jnp.float32),
            shape_of((ranks, tok, HD), jnp.float32),
            shape_of((ranks, 2 * tok, HD), jnp.bfloat16),
            shape_of((low_rank, HD), jnp.float32),
        ],
        [pltpu.VMEM((rows, HD), jnp.float32)] * 4,
        10 * pair_count * HD,
        pair_count,
        scalars,
        own,
        other,
        in_order(arrived[:, : HD + low_rank]),
        attn_t,
        stats,
        limit=28,
    )
    pair_other, _ = lax.optimization_barrier((pair_other, middle))
    turn = jnp.full((1,), jnp.where(shifted, 0, ranks // 2), jnp.int32)
    back_message = return_message(
        turn, dq, dk_own, dv_own, swap(pair_other), down_part, swap(down_part)
    )
    back = exchange(back_message)
    outs = [shape_of((tok, feats), back.dtype)] * 3
    if seqs == ranks:
        outs.append(shape_of((low_rank, feats), jnp.float32))
    outs = list(in_vmem(functools.partial(unpack_kernel, copies), outs, back))
    if seqs > ranks:
        bits = [bit for bit in powers_below(seqs) if bit >= ranks]
        down_terms = back[::copies, 3 * tok :].astype(jnp.float32)
        down_terms = butterfly_sum(down_terms, "seq", bits, seqs)
        outs.append(down_terms.transpose(1, 0, 2).reshape(low_rank, feats))
    query_gradient, key_gradient, value_gradient, down_gradient = outs

    up_sum = butterfly_sum(up_part, "seq", powers_below(seqs), seqs)
    _, up_sum = lax.optimization_barrier((back, up_sum))
    up_gradient = butterfly_sum(up_sum, "sub", powers_below(subs), subs)
    return (query_gradient, key_gradient, value_gradient, down_gradient.T, up_gradient)


def solution(mesh):
    rows = P(("rep", "seq", "sub"), "head")
    sizes = (mesh.shape["seq"], mesh.shape["head"], mesh.shape["sub"])
    return jax.shard_map(
        functools.partial(on_device, sizes),
        mesh=mesh,
        in_specs=(rows, rows, rows, rows, P("head", "sub"), P("head", None), P()),
        out_specs=(rows, rows, rows, P(("rep", "head"), None), P("rep", "head")),
        check_vma=False,
    )
```

```python
import functools
import math

import jax
import jax.numpy as jnp
from jax import lax
from jax.experimental import pallas as pl
from jax.experimental.pallas import tpu as pltpu
from jax.sharding import PartitionSpec as P

HD = 128
GROUP = 2048
TILE = 256
HIDDEN = -1e30
SCALE = HD ** (-0.5)
LOG2_SCALE = SCALE * math.log2(math.e)


def dot_nt(left, right):
    return lax.dot_general(
        left, right, (((1,), (1,)), ((), ())), preferred_element_type=jnp.float32
    )


def dot_nn(left, right):
    return jnp.dot(left, right, preferred_element_type=jnp.float32)


def rows_of(ref, blocks, first, count):
    return ref[0:blocks, first : first + count, :].reshape(blocks * count, HD)


def scores_of(keys, queries, visible):
    scores = dot_nt(keys, queries)
    head = scores.shape[0] - TILE
    tail = jnp.where(visible, scores[head:], HIDDEN)
    return tail if head == 0 else jnp.concatenate((scores[:head], tail), axis=0)


def tile_index(dimension):
    shape = (TILE, 1) if dimension == 0 else (1, TILE)
    return lax.broadcasted_iota(jnp.int32, shape, dimension)


def own_visible():
    return tile_index(0) <= tile_index(1)


def other_visible(sub, tok):
    return tile_index(0) // tok < tile_index(1) // tok + sub


def summed(terms):
    return functools.reduce(jnp.add, terms)


def in_stages(prepare, work, finish, tiles):
    tiles = list(tiles)
    ready, worked = prepare(tiles[0]), None
    for n, tile in enumerate(tiles):
        present = ready
        if n + 1 < len(tiles):
            ready = prepare(tiles[n + 1])
        now = work(tile, present)
        if worked is not None:
            finish(tiles[n - 1], worked)
        worked = now
    finish(tiles[-1], worked)


def forward_own_kernel(tok, scalar_ref, own_ref, total_ref, stat_ref):
    blocks = own_ref.shape[0]
    step = TILE // tok
    values_t = rows_of(own_ref, blocks, 2 * tok, tok).T

    def prepare(tile):
        upto = (tile + 1) * step
        queries = own_ref[tile * step : upto, 0:tok, :].reshape(TILE, HD)
        return scores_of(rows_of(own_ref, upto, tok, tok), queries, own_visible())

    def work(tile, scores):
        here = pl.ds(tile * TILE, TILE)
        highest = jnp.max(scores, axis=0, keepdims=True)
        powers = jnp.exp2((scores - highest) * LOG2_SCALE)
        stat_ref[0:1, here] = highest
        stat_ref[1:2, here] = jnp.sum(powers, axis=0, keepdims=True)
        return powers.astype(jnp.bfloat16)

    def finish(tile, powers):
        total_ref[:, pl.ds(tile * TILE, TILE)] = dot_nn(
            values_t[:, : (tile + 1) * TILE], powers
        )

    in_stages(prepare, work, finish, range(blocks // step))


def forward_kernel(
    tok,
    scalar_ref,
    own_ref,
    other_ref,
    total_ref,
    own_stat_ref,
    down_t_ref,
    attn_ref,
    mid_ref,
    stat_ref,
):
    blocks = own_ref.shape[0]
    step = TILE // tok
    sub = scalar_ref[0]
    values_t = rows_of(other_ref, blocks, tok, tok).T

    def prepare(tile):
        upto = (tile + 1) * step
        queries = own_ref[tile * step : upto, 0:tok, :].reshape(TILE, HD)
        keys = rows_of(other_ref, upto, 0, tok)
        return scores_of(keys, queries, other_visible(sub, tok))

    def work(tile, scores):
        here = pl.ds(tile * TILE, TILE)
        own_highest = own_stat_ref[0:1, here]
        highest = jnp.maximum(own_highest, jnp.max(scores, axis=0, keepdims=True))
        powers = jnp.exp2((scores - highest) * LOG2_SCALE)
        share = jnp.exp2((own_highest - highest) * LOG2_SCALE)
        inverse = 1.0 / (
            own_stat_ref[1:2, here] * share + jnp.sum(powers, axis=0, keepdims=True)
        )
        stat_ref[0:1, here] = highest
        stat_ref[1:2, here] = inverse
        return powers.astype(jnp.bfloat16), share, inverse

    def finish(tile, worked):
        powers, share, inverse = worked
        here = pl.ds(tile * TILE, TILE)
        attn = dot_nn(values_t[:, : (tile + 1) * TILE], powers)
        attn = (attn + total_ref[:, here] * share) * inverse
        attn_ref[:, here] = attn.astype(jnp.bfloat16)

    in_stages(prepare, work, finish, range(blocks // step))
    mid_ref[...] = dot_nn(down_t_ref[...], attn_ref[...])


def backward_kernel(
    tok,
    scalar_ref,
    own_ref,
    other_ref,
    dout_ref,
    attn_ref,
    stat_ref,
    dq_ref,
    dk_own_ref,
    dv_own_ref,
    pair_other_ref,
    down_grad_ref,
    dk_own,
    dv_own,
    dk_other,
    dv_other,
):
    blocks = own_ref.shape[0]
    step = TILE // tok
    sub = scalar_ref[0]
    low_rank = down_grad_ref.shape[0]
    keys_own_t = rows_of(own_ref, blocks, tok, tok).T
    keys_other_t = rows_of(other_ref, blocks, 0, tok).T
    tiles = blocks // step
    lora = jnp.concatenate(
        [dout_ref[block, HD : HD + low_rank, :] for block in range(blocks)], axis=1
    )
    down_grad_ref[...] = 2.0 * dot_nt(lora, attn_ref[...])

    def prepare(tile):
        upto = (tile + 1) * step
        queries = own_ref[tile * step : upto, 0:tok, :].reshape(TILE, HD)
        douts_t = jnp.concatenate(
            [dout_ref[block, 0:HD, :] for block in range(tile * step, upto)], axis=1
        )
        own = scores_of(rows_of(own_ref, upto, tok, tok), queries, own_visible())
        other = scores_of(
            rows_of(other_ref, upto, 0, tok), queries, other_visible(sub, tok)
        )
        dprob_own = dot_nn(rows_of(own_ref, upto, 2 * tok, tok), douts_t)
        dprob_other = dot_nn(rows_of(other_ref, upto, tok, tok), douts_t)
        return queries, douts_t, own, other, dprob_own, dprob_other

    def work(tile, prepared):
        queries, douts_t, own, other, dprob_own, dprob_other = prepared
        here = pl.ds(tile * TILE, TILE)
        highest = stat_ref[0:1, here]
        inverse = stat_ref[1:2, here]
        own = jnp.exp2((own - highest) * LOG2_SCALE) * inverse
        other = jnp.exp2((other - highest) * LOG2_SCALE) * inverse
        delta = jnp.sum(own * dprob_own, axis=0, keepdims=True) + jnp.sum(
            other * dprob_other, axis=0, keepdims=True
        )
        ds_own = (own * (dprob_own - delta)).astype(jnp.bfloat16)
        ds_other = (other * (dprob_other - delta)).astype(jnp.bfloat16)
        probs = own.astype(jnp.bfloat16), other.astype(jnp.bfloat16)
        return queries, douts_t, ds_own, ds_other, *probs

    def finish(tile, worked):
        queries, douts_t, ds_own, ds_other, own, other = worked
        upto = (tile + 1) * step
        width = upto * tok
        dq = dot_nn(keys_own_t[:, :width], ds_own) + dot_nn(keys_other_t[:, :width], ds_other)
        dq = (dq * SCALE).T.astype(jnp.bfloat16)
        dq_ref[tile * step : upto] = dq.reshape(step, tok, HD)
        terms = (
            (dk_own, dot_nn(ds_own, queries)),
            (dk_other, dot_nn(ds_other, queries)),
            (dv_own, dot_nt(own, douts_t)),
            (dv_other, dot_nt(other, douts_t)),
        )
        for total, term in terms:
            if tile == tiles - 1:
                total[...] = term
            else:
                total[0:width] += term

    in_stages(prepare, work, finish, reversed(range(tiles)))
    shape = (blocks, tok, HD)
    dk_own_ref[...] = (dk_own[...] * SCALE).reshape(shape)
    dv_own_ref[...] = dv_own[...].reshape(shape)
    pair_other_ref[:, 0:tok, :] = (dk_other[...] * SCALE).astype(jnp.bfloat16).reshape(shape)
    pair_other_ref[:, tok : 2 * tok, :] = dv_other[...].astype(jnp.bfloat16).reshape(shape)


def call_kernel(body, outs, scratch, flops, exps, *operands, declared=None, limit=48):
    in_bytes = sum(x.size * x.dtype.itemsize for x in operands)
    out_bytes = sum(x.size * x.dtype.itemsize for x in outs)
    specs = [pl.BlockSpec(memory_space=pltpu.SMEM)]
    specs += [pl.BlockSpec(memory_space=pltpu.VMEM)] * (len(operands) - 1)
    return pl.pallas_call(
        body,
        out_shape=outs,
        in_specs=specs,
        out_specs=[pl.BlockSpec(memory_space=pltpu.VMEM)] * len(outs),
        scratch_shapes=scratch,
        compiler_params=pltpu.CompilerParams(vmem_limit_bytes=limit * 1024 * 1024),
        cost_estimate=pl.CostEstimate(
            flops=flops,
            bytes_accessed=declared or in_bytes + out_bytes,
            transcendentals=exps,
        ),
    )(*operands)


def shape_of(shape, dtype):
    return jax.ShapeDtypeStruct(shape, dtype)


def butterfly_sum(value, axis, bits, count):
    for bit in bits:
        pairs = [(i, i ^ bit) for i in range(count)]
        value = value.astype(jnp.bfloat16)
        taken = lax.ppermute(value, axis, pairs)
        value = value.astype(jnp.float32) + taken.astype(jnp.float32)
    return value


def powers_below(count):
    return [1 << n for n in range(count.bit_length() - 1)]


def message_kernel(copies, *refs):
    count = (len(refs) - 3) // 3
    operands, message_ref = refs[:count], refs[count]
    held, grouped = refs[count + 1 : 2 * count + 1], refs[2 * count + 1 : 3 * count + 1]
    in_sems, out_sems = refs[-2], refs[-1]
    tok = operands[0].shape[0]
    arriving = [
        pltpu.make_async_copy(ref, to, in_sems.at[n])
        for n, (ref, to) in enumerate(zip(operands, held))
    ]
    for copy in arriving:
        copy.start()
    leaving = []
    for n, copy in enumerate(arriving):
        copy.wait()
        for rank in range(message_ref.shape[0]):
            at = (rank // copies) * HD
            grouped[n][rank] = held[n][:, at : at + HD]
        to = message_ref.at[:, pl.ds(n * tok, tok), :]
        leaving.append(pltpu.make_async_copy(grouped[n], to, out_sems.at[n]))
        leaving[-1].start()
    for copy in leaving:
        copy.wait()


def message_of(copies, ranks, *operands):
    tok = operands[0].shape[0]
    count = len(operands)
    shape = (ranks, count * tok, HD)
    return pl.pallas_call(
        functools.partial(message_kernel, copies),
        out_shape=shape_of(shape, operands[0].dtype),
        in_specs=[pl.BlockSpec(memory_space=pltpu.HBM)] * count,
        out_specs=pl.BlockSpec(memory_space=pltpu.HBM),
        scratch_shapes=[pltpu.VMEM(x.shape, x.dtype) for x in operands]
        + [pltpu.VMEM((ranks, tok, HD), x.dtype) for x in operands]
        + [pltpu.SemaphoreType.DMA((count,))] * 2,
        cost_estimate=pl.CostEstimate(
            flops=0, bytes_accessed=4 * math.prod(shape), transcendentals=0
        ),
    )(*operands)


def return_kernel(turn_ref, dq_ref, dk_ref, dv_ref, pair_ref, down_ref, taken_ref, *refs):
    message_ref, held, sems = refs
    blocks, tok, _ = dq_ref.shape
    down = (down_ref[...] + taken_ref[...]).astype(held.dtype)
    copies = []
    for slot in range(blocks):
        block = (slot + turn_ref[0]) % blocks
        held[slot, 0:tok, :] = dq_ref[block]
        dk = dk_ref[block] + pair_ref[block, 0:tok, :].astype(jnp.float32)
        dv = dv_ref[block] + pair_ref[block, tok : 2 * tok, :].astype(jnp.float32)
        held[slot, tok : 2 * tok, :] = dk.astype(held.dtype)
        held[slot, 2 * tok : 3 * tok, :] = dv.astype(held.dtype)
        held[slot, 3 * tok :, :] = down
        copies.append(pltpu.make_async_copy(held.at[slot], message_ref.at[slot], sems.at[slot]))
        copies[-1].start()
    for copy in copies:
        copy.wait()


def return_message(turn, dq, *operands):
    blocks, tok, _ = dq.shape
    shape = (blocks, 3 * tok + operands[-1].shape[0], HD)
    return pl.pallas_call(
        return_kernel,
        out_shape=shape_of(shape, dq.dtype),
        in_specs=[pl.BlockSpec(memory_space=pltpu.SMEM)]
        + [pl.BlockSpec(memory_space=pltpu.VMEM)] * (len(operands) + 1),
        out_specs=pl.BlockSpec(memory_space=pltpu.HBM),
        scratch_shapes=[pltpu.VMEM(shape, dq.dtype), pltpu.SemaphoreType.DMA((blocks,))],
        compiler_params=pltpu.CompilerParams(vmem_limit_bytes=16 * 1024 * 1024),
        cost_estimate=pl.CostEstimate(
            flops=0, bytes_accessed=4 * math.prod(shape), transcendentals=0
        ),
    )(turn, dq, *operands)


def unpack_kernel(copies, back_ref, *refs):
    out_refs, down_ref = refs[:3], refs[3] if len(refs) > 3 else None
    tok = out_refs[0].shape[0]
    for at_head in range(out_refs[0].shape[1] // HD):
        cols = slice(at_head * HD, (at_head + 1) * HD)
        for n, ref in enumerate(out_refs):
            ref[:, cols] = back_ref[at_head * copies, n * tok : (n + 1) * tok, :]
        if down_ref is not None:
            down_ref[:, cols] = back_ref[at_head * copies, 3 * tok :, :].astype(jnp.float32)


def in_vmem(body, outs, *operands):
    whole = pl.BlockSpec(memory_space=pltpu.VMEM)
    size = sum(x.size * x.dtype.itemsize for x in operands)
    size += sum(x.size * x.dtype.itemsize for x in outs)
    return pl.pallas_call(
        body,
        out_shape=outs,
        in_specs=[whole] * len(operands),
        out_specs=[whole] * len(outs),
        compiler_params=pltpu.CompilerParams(vmem_limit_bytes=16 * 1024 * 1024),
        cost_estimate=pl.CostEstimate(flops=0, bytes_accessed=size, transcendentals=0),
    )(*operands)


def cotangent_kernel(chunks, plan_ref, *refs):
    pieces, (matrix_ref, up_ref, own_ref, sent_ref) = refs[:-4], refs[-4:]
    tok, cols = pieces[0].shape
    feats, low_rank = matrix_ref.shape[0], up_ref.shape[0]
    count = len(pieces)
    if chunks == 1:
        stacks = [(jnp.concatenate([p[...] for p in pieces], axis=0), pl.ds(0, cols))]
    else:
        stacks = [
            (p[...], pl.ds(pl.multiple_of(plan_ref[count + k], HD), cols))
            for k, p in enumerate(pieces)
        ]
    mine = [plan_ref[k] == 1 for k in range(count)]
    for ref, here in ((matrix_ref, pl.ds(0, feats)), (up_ref, pl.ds(feats, low_rank))):
        terms = [dot_nt(ref[:, at], rows) for rows, at in stacks]
        parts = [t[:, i : i + tok] for t in terms for i in range(0, t.shape[1], tok)]
        own_ref[here, :] = summed([jnp.where(m, p, 0.0) for m, p in zip(mine, parts)])
        sent = summed([jnp.where(m, 0.0, p) for m, p in zip(mine, parts)])
        sent_ref[here, :] = sent.astype(jnp.bfloat16)


def dout_kernel(copies, own_ref, taken_ref, mid_ref, message_ref):
    low_rank = mid_ref.shape[1]
    feats = own_ref.shape[0] - low_rank
    lora = own_ref[feats:, :] + taken_ref[feats:, :].astype(jnp.float32)
    for rank in range(message_ref.shape[0]):
        at = pl.ds((rank // copies) * HD, HD)
        part = own_ref[at, :] + taken_ref[at, :].astype(jnp.float32)
        message_ref[rank, 0:HD, :] = part.astype(jnp.bfloat16)
        message_ref[rank, HD : HD + low_rank, :] = lora.astype(jnp.bfloat16)
        message_ref[rank, HD + low_rank : HD + 2 * low_rank, :] = mid_ref[rank]


def on_device(
    sizes,
    head_query_rows,
    head_key_rows,
    head_value_rows,
    output_gradient,
    output_matrix,
    adapter_down_weight,
    adapter_up_weight,
):
    seqs, heads, subs = sizes
    tok, feats = head_query_rows.shape
    cols = output_gradient.shape[1]
    low_rank = adapter_up_weight.shape[0]
    local_heads = feats // HD
    block_rows = tok * subs
    ranks = GROUP // block_rows
    copies = ranks // local_heads
    shift_blocks = GROUP // 2 // block_rows

    seq = lax.axis_index("seq")
    head = lax.axis_index("head")
    sub = lax.axis_index("sub")
    shifted = head >= heads // 2
    rank = (seq + shift_blocks) % ranks
    my_head = rank // copies

    groups = []
    for at_head in range(heads):
        for first in range(0, seqs, ranks):
            members = [first + shift_blocks + i for i in range(ranks)]
            if at_head < heads // 2:
                members = [first + (m - first) % ranks for m in members]
            members = [m % seqs for m in members]
            groups.append([m * heads + at_head for m in members])
    scalars = jnp.full((1,), sub, jnp.int32)

    def in_order(blocks):
        half = ranks // 2
        turned = jnp.concatenate((blocks[half:], blocks[:half]), axis=0)
        return jnp.where(shifted, blocks, turned)


    def exchange(parts):
        return lax.all_to_all(
            parts, ("seq", "head"), 0, 0, axis_index_groups=groups, tiled=True
        )

    def swap(value):
        if subs == 1:
            return value
        return lax.ppermute(value, "sub", [(0, 1), (1, 0)])

    sent = message_of(copies, ranks, head_query_rows, head_key_rows, head_value_rows)
    sent, output_gradient, output_matrix = lax.optimization_barrier(
        (sent, output_gradient, output_matrix)
    )
    own = exchange(sent)

    chunks = heads // subs
    pieces = []
    for k in range(heads):
        pairs = []
        for src_head in range(heads):
            for src_sub in range(subs):
                j = (src_head % chunks) * subs + src_sub
                dst = ((j + k) % heads) * subs + src_head // chunks
                pairs.append((src_head * subs + src_sub, dst))
        pieces.append(lax.ppermute(output_gradient, ("head", "sub"), pairs))

    up_half = lax.dynamic_slice_in_dim(adapter_up_weight, sub * chunks * cols, chunks * cols, 1)
    folded = dot_nn(adapter_down_weight, up_half)
    folded = (output_matrix.astype(jnp.float32) + 2.0 * folded).astype(jnp.bfloat16)
    sources = [(head - k + heads) % heads for k in range(heads)]
    plan = [(j % subs == sub).astype(jnp.int32) for j in sources]
    plan += [(j // subs * cols).astype(jnp.int32) for j in sources]
    packed_own, packed_sent = call_kernel(
        functools.partial(cotangent_kernel, chunks),
        [
            shape_of((feats + low_rank, tok), jnp.float32),
            shape_of((feats + low_rank, tok), jnp.bfloat16),
        ],
        [],
        0,
        0,
        jnp.stack(plan),
        *pieces,
        folded,
        up_half,
        declared=1024,
        limit=16,
    )
    received = swap(packed_sent)
    down_head = lax.dynamic_slice_in_dim(adapter_down_weight, my_head * HD, HD, 0).T
    own, down_head, _ = lax.optimization_barrier((own, down_head, packed_sent))
    own = in_order(own)
    other = swap(own[:, tok:])

    rows = ranks * tok
    pair_count = rows * (rows + TILE)
    own_total, own_stats = call_kernel(
        functools.partial(forward_own_kernel, tok),
        [shape_of((HD, rows), jnp.float32), shape_of((8, rows), jnp.float32)],
        [],
        2 * pair_count * HD,
        pair_count // 2,
        scalars,
        own,
        limit=16,
    )
    attn_t, middle_rows, stats = call_kernel(
        functools.partial(forward_kernel, tok),
        [
            shape_of((HD, rows), jnp.bfloat16),
            shape_of((low_rank, rows), jnp.float32),
            shape_of((8, rows), jnp.float32),
        ],
        [],
        2 * pair_count * HD,
        pair_count // 2,
        scalars,
        own,
        other,
        own_total,
        own_stats,
        down_head,
        limit=16,
    )

    first_copy = rank % copies == 0
    middle_rows = middle_rows.astype(jnp.bfloat16).reshape(low_rank, ranks, tok)
    middle_rows = in_order(middle_rows.transpose(1, 0, 2))
    if copies > 1:
        middle_rows = jnp.where(first_copy, middle_rows, 0.0)
    (message,) = in_vmem(
        functools.partial(dout_kernel, copies),
        [shape_of((ranks, HD + 2 * low_rank, tok), jnp.bfloat16)],
        packed_own,
        received,
        middle_rows,
    )
    arrived = exchange(message)
    middle = jnp.sum(arrived[:, HD + low_rank :].astype(jnp.float32), axis=0)
    bit = 1
    while bit < heads:
        middle += lax.ppermute(middle, "head", [(i, i ^ bit) for i in range(heads)])
        bit *= 2
    up_part = 2.0 * dot_nn(middle.astype(jnp.bfloat16), output_gradient)

    dq, dk_own, dv_own, pair_other, down_part = call_kernel(
        functools.partial(backward_kernel, tok),
        [
            shape_of((ranks, tok, HD), jnp.bfloat16),
            shape_of((ranks, tok, HD), jnp.float32),
            shape_of((ranks, tok, HD), jnp.float32),
            shape_of((ranks, 2 * tok, HD), jnp.bfloat16),
            shape_of((low_rank, HD), jnp.float32),
        ],
        [pltpu.VMEM((rows, HD), jnp.float32)] * 4,
        10 * pair_count * HD,
        pair_count,
        scalars,
        own,
        other,
        in_order(arrived[:, : HD + low_rank]),
        attn_t,
        stats,
        limit=28,
    )
    pair_other, _ = lax.optimization_barrier((pair_other, middle))
    turn = jnp.full((1,), jnp.where(shifted, 0, ranks // 2), jnp.int32)
    back_message = return_message(
        turn, dq, dk_own, dv_own, swap(pair_other), down_part, swap(down_part)
    )
    back = exchange(back_message)
    outs = [shape_of((tok, feats), back.dtype)] * 3
    if seqs == ranks:
        outs.append(shape_of((low_rank, feats), jnp.float32))
    outs = list(in_vmem(functools.partial(unpack_kernel, copies), outs, back))
    if seqs > ranks:
        bits = [bit for bit in powers_below(seqs) if bit >= ranks]
        down_terms = back[::copies, 3 * tok :].astype(jnp.float32)
        down_terms = butterfly_sum(down_terms, "seq", bits, seqs)
        outs.append(down_terms.transpose(1, 0, 2).reshape(low_rank, feats))
    query_gradient, key_gradient, value_gradient, down_gradient = outs

    up_sum = butterfly_sum(up_part, "seq", powers_below(seqs), seqs)
    _, up_sum = lax.optimization_barrier((back, up_sum))
    up_gradient = butterfly_sum(up_sum, "sub", powers_below(subs), subs)
    return (query_gradient, key_gradient, value_gradient, down_gradient.T, up_gradient)


def solution(mesh):
    rows = P(("rep", "seq", "sub"), "head")
    sizes = (mesh.shape["seq"], mesh.shape["head"], mesh.shape["sub"])
    return jax.shard_map(
        functools.partial(on_device, sizes),
        mesh=mesh,
        in_specs=(rows, rows, rows, rows, P("head", "sub"), P("head", None), P()),
        out_specs=(rows, rows, rows, P(("rep", "head"), None), P("rep", "head")),
        check_vma=False,
    )
```

```python
import functools
import math

import jax
import jax.numpy as jnp
from jax import lax
from jax.experimental import pallas as pl
from jax.experimental.pallas import tpu as pltpu
from jax.sharding import PartitionSpec as P

HD = 128
GROUP = 2048
TILE = 256
HIDDEN = -1e30
SCALE = HD ** (-0.5)
LOG2_SCALE = SCALE * math.log2(math.e)


def dot_nt(left, right):
    return lax.dot_general(
        left, right, (((1,), (1,)), ((), ())), preferred_element_type=jnp.float32
    )


def dot_nn(left, right):
    return jnp.dot(left, right, preferred_element_type=jnp.float32)


def rows_of(ref, blocks, first, count):
    return ref[0:blocks, first : first + count, :].reshape(blocks * count, HD)


def scores_of(keys, queries, visible):
    scores = dot_nt(keys, queries)
    head = scores.shape[0] - TILE
    tail = jnp.where(visible, scores[head:], HIDDEN)
    return tail if head == 0 else jnp.concatenate((scores[:head], tail), axis=0)


def tile_index(dimension):
    shape = (TILE, 1) if dimension == 0 else (1, TILE)
    return lax.broadcasted_iota(jnp.int32, shape, dimension)


def own_visible():
    return tile_index(0) <= tile_index(1)


def other_visible(sub, tok):
    return tile_index(0) // tok < tile_index(1) // tok + sub


def summed(terms):
    return functools.reduce(jnp.add, terms)


def in_stages(prepare, work, finish, tiles):
    tiles = list(tiles)
    ready, worked = prepare(tiles[0]), None
    for n, tile in enumerate(tiles):
        present = ready
        if n + 1 < len(tiles):
            ready = prepare(tiles[n + 1])
        now = work(tile, present)
        if worked is not None:
            finish(tiles[n - 1], worked)
        worked = now
    finish(tiles[-1], worked)


def forward_own_kernel(tok, scalar_ref, own_ref, total_ref, stat_ref, keys_t_ref):
    blocks = own_ref.shape[0]
    step = TILE // tok
    values_t = rows_of(own_ref, blocks, 2 * tok, tok).T

    def prepare(tile):
        upto = (tile + 1) * step
        queries = own_ref[tile * step : upto, 0:tok, :].reshape(TILE, HD)
        return scores_of(rows_of(own_ref, upto, tok, tok), queries, own_visible())

    def work(tile, scores):
        here = pl.ds(tile * TILE, TILE)
        highest = jnp.max(scores, axis=0, keepdims=True)
        powers = jnp.exp2((scores - highest) * LOG2_SCALE)
        stat_ref[0:1, here] = highest
        stat_ref[1:2, here] = jnp.sum(powers, axis=0, keepdims=True)
        return powers.astype(jnp.bfloat16)

    def finish(tile, powers):
        total_ref[:, pl.ds(tile * TILE, TILE)] = dot_nn(
            values_t[:, : (tile + 1) * TILE], powers
        )

    in_stages(prepare, work, finish, reversed(range(blocks // step)))
    keys_t_ref[...] = rows_of(own_ref, blocks, tok, tok).T


def forward_kernel(
    tok,
    scalar_ref,
    own_ref,
    other_ref,
    total_ref,
    own_stat_ref,
    down_t_ref,
    attn_ref,
    mid_ref,
    stat_ref,
):
    blocks = own_ref.shape[0]
    step = TILE // tok
    sub = scalar_ref[0]
    values_t = rows_of(other_ref, blocks, tok, tok).T

    def prepare(tile):
        upto = (tile + 1) * step
        queries = own_ref[tile * step : upto, 0:tok, :].reshape(TILE, HD)
        keys = rows_of(other_ref, upto, 0, tok)
        return scores_of(keys, queries, other_visible(sub, tok))

    def work(tile, scores):
        here = pl.ds(tile * TILE, TILE)
        own_highest = own_stat_ref[0:1, here]
        highest = jnp.maximum(own_highest, jnp.max(scores, axis=0, keepdims=True))
        powers = jnp.exp2((scores - highest) * LOG2_SCALE)
        share = jnp.exp2((own_highest - highest) * LOG2_SCALE)
        inverse = 1.0 / (
            own_stat_ref[1:2, here] * share + jnp.sum(powers, axis=0, keepdims=True)
        )
        stat_ref[0:1, here] = highest
        stat_ref[1:2, here] = inverse
        return powers.astype(jnp.bfloat16), share, inverse

    def finish(tile, worked):
        powers, share, inverse = worked
        here = pl.ds(tile * TILE, TILE)
        attn = dot_nn(values_t[:, : (tile + 1) * TILE], powers)
        attn = (attn + total_ref[:, here] * share) * inverse
        attn_ref[:, here] = attn.astype(jnp.bfloat16)

    in_stages(prepare, work, finish, reversed(range(blocks // step)))
    mid_ref[...] = dot_nn(down_t_ref[...], attn_ref[...])


def backward_kernel(
    tok,
    scalar_ref,
    own_ref,
    other_ref,
    dout_ref,
    attn_ref,
    stat_ref,
    keys_t_ref,
    dq_ref,
    dk_own_ref,
    dv_own_ref,
    pair_other_ref,
    down_grad_ref,
    dk_own,
    dv_own,
    dk_other,
    dv_other,
):
    blocks = own_ref.shape[0]
    step = TILE // tok
    sub = scalar_ref[0]
    low_rank = down_grad_ref.shape[0]
    keys_own_t = keys_t_ref[...]
    keys_other_t = rows_of(other_ref, blocks, 0, tok).T
    tiles = blocks // step
    lora = jnp.concatenate(
        [dout_ref[block, HD : HD + low_rank, :] for block in range(blocks)], axis=1
    )
    down_grad_ref[...] = 2.0 * dot_nt(lora, attn_ref[...])

    def prepare(tile):
        upto = (tile + 1) * step
        queries = own_ref[tile * step : upto, 0:tok, :].reshape(TILE, HD)
        douts_t = jnp.concatenate(
            [dout_ref[block, 0:HD, :] for block in range(tile * step, upto)], axis=1
        )
        own = scores_of(rows_of(own_ref, upto, tok, tok), queries, own_visible())
        other = scores_of(
            rows_of(other_ref, upto, 0, tok), queries, other_visible(sub, tok)
        )
        dprob_own = dot_nn(rows_of(own_ref, upto, 2 * tok, tok), douts_t)
        dprob_other = dot_nn(rows_of(other_ref, upto, tok, tok), douts_t)
        return queries, douts_t, own, other, dprob_own, dprob_other

    def work(tile, prepared):
        queries, douts_t, own, other, dprob_own, dprob_other = prepared
        here = pl.ds(tile * TILE, TILE)
        highest = stat_ref[0:1, here]
        inverse = stat_ref[1:2, here]
        own = jnp.exp2((own - highest) * LOG2_SCALE) * inverse
        other = jnp.exp2((other - highest) * LOG2_SCALE) * inverse
        delta = jnp.sum(own * dprob_own, axis=0, keepdims=True) + jnp.sum(
            other * dprob_other, axis=0, keepdims=True
        )
        ds_own = (own * (dprob_own - delta)).astype(jnp.bfloat16)
        ds_other = (other * (dprob_other - delta)).astype(jnp.bfloat16)
        probs = own.astype(jnp.bfloat16), other.astype(jnp.bfloat16)
        return queries, douts_t, ds_own, ds_other, *probs

    def finish(tile, worked):
        queries, douts_t, ds_own, ds_other, own, other = worked
        upto = (tile + 1) * step
        width = upto * tok
        dq = dot_nn(keys_own_t[:, :width], ds_own) + dot_nn(keys_other_t[:, :width], ds_other)
        dq = (dq * SCALE).T.astype(jnp.bfloat16)
        dq_ref[tile * step : upto] = dq.reshape(step, tok, HD)
        terms = (
            (dk_own, dot_nn(ds_own, queries)),
            (dk_other, dot_nn(ds_other, queries)),
            (dv_own, dot_nt(own, douts_t)),
            (dv_other, dot_nt(other, douts_t)),
        )
        for total, term in terms:
            if tile == tiles - 1:
                total[...] = term
            else:
                total[0:width] += term

    in_stages(prepare, work, finish, reversed(range(tiles)))
    shape = (blocks, tok, HD)
    dk_own_ref[...] = (dk_own[...] * SCALE).reshape(shape)
    dv_own_ref[...] = dv_own[...].reshape(shape)
    pair_other_ref[:, 0:tok, :] = (dk_other[...] * SCALE).astype(jnp.bfloat16).reshape(shape)
    pair_other_ref[:, tok : 2 * tok, :] = dv_other[...].astype(jnp.bfloat16).reshape(shape)


def call_kernel(body, outs, scratch, flops, exps, *operands, declared=None, limit=48):
    in_bytes = sum(x.size * x.dtype.itemsize for x in operands)
    out_bytes = sum(x.size * x.dtype.itemsize for x in outs)
    specs = [pl.BlockSpec(memory_space=pltpu.SMEM)]
    specs += [pl.BlockSpec(memory_space=pltpu.VMEM)] * (len(operands) - 1)
    return pl.pallas_call(
        body,
        out_shape=outs,
        in_specs=specs,
        out_specs=[pl.BlockSpec(memory_space=pltpu.VMEM)] * len(outs),
        scratch_shapes=scratch,
        compiler_params=pltpu.CompilerParams(vmem_limit_bytes=limit * 1024 * 1024),
        cost_estimate=pl.CostEstimate(
            flops=flops,
            bytes_accessed=declared or in_bytes + out_bytes,
            transcendentals=exps,
        ),
    )(*operands)


def shape_of(shape, dtype):
    return jax.ShapeDtypeStruct(shape, dtype)


def butterfly_sum(value, axis, bits, count):
    for bit in bits:
        pairs = [(i, i ^ bit) for i in range(count)]
        value = value.astype(jnp.bfloat16)
        taken = lax.ppermute(value, axis, pairs)
        value = value.astype(jnp.float32) + taken.astype(jnp.float32)
    return value


def powers_below(count):
    return [1 << n for n in range(count.bit_length() - 1)]


def message_kernel(copies, *refs):
    count = (len(refs) - 3) // 3
    operands, message_ref = refs[:count], refs[count]
    held, grouped = refs[count + 1 : 2 * count + 1], refs[2 * count + 1 : 3 * count + 1]
    in_sems, out_sems = refs[-2], refs[-1]
    tok = operands[0].shape[0]
    arriving = [
        pltpu.make_async_copy(ref, to, in_sems.at[n])
        for n, (ref, to) in enumerate(zip(operands, held))
    ]
    for copy in arriving:
        copy.start()
    leaving = []
    for n, copy in enumerate(arriving):
        copy.wait()
        for rank in range(message_ref.shape[0]):
            at = (rank // copies) * HD
            grouped[n][rank] = held[n][:, at : at + HD]
        to = message_ref.at[:, pl.ds(n * tok, tok), :]
        leaving.append(pltpu.make_async_copy(grouped[n], to, out_sems.at[n]))
        leaving[-1].start()
    for copy in leaving:
        copy.wait()


def message_of(copies, ranks, *operands):
    tok = operands[0].shape[0]
    count = len(operands)
    shape = (ranks, count * tok, HD)
    return pl.pallas_call(
        functools.partial(message_kernel, copies),
        out_shape=shape_of(shape, operands[0].dtype),
        in_specs=[pl.BlockSpec(memory_space=pltpu.HBM)] * count,
        out_specs=pl.BlockSpec(memory_space=pltpu.HBM),
        scratch_shapes=[pltpu.VMEM(x.shape, x.dtype) for x in operands]
        + [pltpu.VMEM((ranks, tok, HD), x.dtype) for x in operands]
        + [pltpu.SemaphoreType.DMA((count,))] * 2,
        cost_estimate=pl.CostEstimate(
            flops=0, bytes_accessed=4 * math.prod(shape), transcendentals=0
        ),
    )(*operands)


def return_kernel(turn_ref, dq_ref, dk_ref, dv_ref, pair_ref, down_ref, taken_ref, *refs):
    message_ref, held, sems = refs
    blocks, tok, _ = dq_ref.shape
    down = (down_ref[...] + taken_ref[...]).astype(held.dtype)
    copies = []
    for slot in range(blocks):
        block = (slot + turn_ref[0]) % blocks
        held[slot, 0:tok, :] = dq_ref[block]
        dk = dk_ref[block] + pair_ref[block, 0:tok, :].astype(jnp.float32)
        dv = dv_ref[block] + pair_ref[block, tok : 2 * tok, :].astype(jnp.float32)
        held[slot, tok : 2 * tok, :] = dk.astype(held.dtype)
        held[slot, 2 * tok : 3 * tok, :] = dv.astype(held.dtype)
        held[slot, 3 * tok :, :] = down
        copies.append(pltpu.make_async_copy(held.at[slot], message_ref.at[slot], sems.at[slot]))
        copies[-1].start()
    for copy in copies:
        copy.wait()


def return_message(turn, dq, *operands):
    blocks, tok, _ = dq.shape
    shape = (blocks, 3 * tok + operands[-1].shape[0], HD)
    return pl.pallas_call(
        return_kernel,
        out_shape=shape_of(shape, dq.dtype),
        in_specs=[pl.BlockSpec(memory_space=pltpu.SMEM)]
        + [pl.BlockSpec(memory_space=pltpu.VMEM)] * (len(operands) + 1),
        out_specs=pl.BlockSpec(memory_space=pltpu.HBM),
        scratch_shapes=[pltpu.VMEM(shape, dq.dtype), pltpu.SemaphoreType.DMA((blocks,))],
        compiler_params=pltpu.CompilerParams(vmem_limit_bytes=16 * 1024 * 1024),
        cost_estimate=pl.CostEstimate(
            flops=0, bytes_accessed=4 * math.prod(shape), transcendentals=0
        ),
    )(turn, dq, *operands)


def unpack_kernel(copies, back_ref, *refs):
    out_refs, down_ref = refs[:3], refs[3] if len(refs) > 3 else None
    tok = out_refs[0].shape[0]
    for at_head in range(out_refs[0].shape[1] // HD):
        cols = slice(at_head * HD, (at_head + 1) * HD)
        for n, ref in enumerate(out_refs):
            ref[:, cols] = back_ref[at_head * copies, n * tok : (n + 1) * tok, :]
        if down_ref is not None:
            down_ref[:, cols] = back_ref[at_head * copies, 3 * tok :, :].astype(jnp.float32)


def in_vmem(body, outs, *operands):
    whole = pl.BlockSpec(memory_space=pltpu.VMEM)
    size = sum(x.size * x.dtype.itemsize for x in operands)
    size += sum(x.size * x.dtype.itemsize for x in outs)
    return pl.pallas_call(
        body,
        out_shape=outs,
        in_specs=[whole] * len(operands),
        out_specs=[whole] * len(outs),
        compiler_params=pltpu.CompilerParams(vmem_limit_bytes=16 * 1024 * 1024),
        cost_estimate=pl.CostEstimate(flops=0, bytes_accessed=size, transcendentals=0),
    )(*operands)


def cotangent_kernel(chunks, plan_ref, *refs):
    pieces, (matrix_ref, up_ref, own_ref, sent_ref) = refs[:-4], refs[-4:]
    tok, cols = pieces[0].shape
    feats, low_rank = matrix_ref.shape[0], up_ref.shape[0]
    count = len(pieces)
    if chunks == 1:
        stacks = [(jnp.concatenate([p[...] for p in pieces], axis=0), pl.ds(0, cols))]
    else:
        stacks = [
            (p[...], pl.ds(pl.multiple_of(plan_ref[count + k], HD), cols))
            for k, p in enumerate(pieces)
        ]
    mine = [plan_ref[k] == 1 for k in range(count)]
    for ref, here in ((matrix_ref, pl.ds(0, feats)), (up_ref, pl.ds(feats, low_rank))):
        terms = [dot_nt(ref[:, at], rows) for rows, at in stacks]
        parts = [t[:, i : i + tok] for t in terms for i in range(0, t.shape[1], tok)]
        own_ref[here, :] = summed([jnp.where(m, p, 0.0) for m, p in zip(mine, parts)])
        sent = summed([jnp.where(m, 0.0, p) for m, p in zip(mine, parts)])
        sent_ref[here, :] = sent.astype(jnp.bfloat16)


def dout_kernel(copies, own_ref, taken_ref, mid_ref, message_ref):
    low_rank = mid_ref.shape[1]
    feats = own_ref.shape[0] - low_rank
    lora = own_ref[feats:, :] + taken_ref[feats:, :].astype(jnp.float32)
    for rank in range(message_ref.shape[0]):
        at = pl.ds((rank // copies) * HD, HD)
        part = own_ref[at, :] + taken_ref[at, :].astype(jnp.float32)
        message_ref[rank, 0:HD, :] = part.astype(jnp.bfloat16)
        message_ref[rank, HD : HD + low_rank, :] = lora.astype(jnp.bfloat16)
        message_ref[rank, HD + low_rank : HD + 2 * low_rank, :] = mid_ref[rank]


def on_device(
    sizes,
    head_query_rows,
    head_key_rows,
    head_value_rows,
    output_gradient,
    output_matrix,
    adapter_down_weight,
    adapter_up_weight,
):
    seqs, heads, subs = sizes
    tok, feats = head_query_rows.shape
    cols = output_gradient.shape[1]
    low_rank = adapter_up_weight.shape[0]
    local_heads = feats // HD
    block_rows = tok * subs
    ranks = GROUP // block_rows
    copies = ranks // local_heads
    shift_blocks = GROUP // 2 // block_rows

    seq = lax.axis_index("seq")
    head = lax.axis_index("head")
    sub = lax.axis_index("sub")
    shifted = head >= heads // 2
    rank = (seq + shift_blocks) % ranks
    my_head = rank // copies

    groups = []
    for at_head in range(heads):
        for first in range(0, seqs, ranks):
            members = [first + shift_blocks + i for i in range(ranks)]
            if at_head < heads // 2:
                members = [first + (m - first) % ranks for m in members]
            members = [m % seqs for m in members]
            groups.append([m * heads + at_head for m in members])
    scalars = jnp.full((1,), sub, jnp.int32)

    def in_order(blocks):
        half = ranks // 2
        turned = jnp.concatenate((blocks[half:], blocks[:half]), axis=0)
        return jnp.where(shifted, blocks, turned)


    def exchange(parts):
        return lax.all_to_all(
            parts, ("seq", "head"), 0, 0, axis_index_groups=groups, tiled=True
        )

    def swap(value):
        if subs == 1:
            return value
        return lax.ppermute(value, "sub", [(0, 1), (1, 0)])

    sent = message_of(copies, ranks, head_query_rows, head_key_rows, head_value_rows)
    sent, output_gradient, output_matrix = lax.optimization_barrier(
        (sent, output_gradient, output_matrix)
    )
    own = exchange(sent)

    chunks = heads // subs
    pieces = []
    for k in range(heads):
        pairs = []
        for src_head in range(heads):
            for src_sub in range(subs):
                j = (src_head % chunks) * subs + src_sub
                dst = ((j + k) % heads) * subs + src_head // chunks
                pairs.append((src_head * subs + src_sub, dst))
        pieces.append(lax.ppermute(output_gradient, ("head", "sub"), pairs))

    up_half = lax.dynamic_slice_in_dim(adapter_up_weight, sub * chunks * cols, chunks * cols, 1)
    folded = dot_nn(adapter_down_weight, up_half)
    folded = (output_matrix.astype(jnp.float32) + 2.0 * folded).astype(jnp.bfloat16)
    sources = [(head - k + heads) % heads for k in range(heads)]
    plan = [(j % subs == sub).astype(jnp.int32) for j in sources]
    plan += [(j // subs * cols).astype(jnp.int32) for j in sources]
    packed_own, packed_sent = call_kernel(
        functools.partial(cotangent_kernel, chunks),
        [
            shape_of((feats + low_rank, tok), jnp.float32),
            shape_of((feats + low_rank, tok), jnp.bfloat16),
        ],
        [],
        0,
        0,
        jnp.stack(plan),
        *pieces,
        folded,
        up_half,
        declared=1024,
        limit=16,
    )
    received = swap(packed_sent)
    down_head = lax.dynamic_slice_in_dim(adapter_down_weight, my_head * HD, HD, 0).T
    own, down_head, _ = lax.optimization_barrier((own, down_head, packed_sent))
    own = in_order(own)
    other = swap(own[:, tok:])

    rows = ranks * tok
    pair_count = rows * (rows + TILE)
    own_total, own_stats, own_keys_t = call_kernel(
        functools.partial(forward_own_kernel, tok),
        [
            shape_of((HD, rows), jnp.float32),
            shape_of((8, rows), jnp.float32),
            shape_of((HD, rows), jnp.bfloat16),
        ],
        [],
        2 * pair_count * HD,
        pair_count // 2,
        scalars,
        own,
        limit=16,
    )
    attn_t, middle_rows, stats = call_kernel(
        functools.partial(forward_kernel, tok),
        [
            shape_of((HD, rows), jnp.bfloat16),
            shape_of((low_rank, rows), jnp.float32),
            shape_of((8, rows), jnp.float32),
        ],
        [],
        2 * pair_count * HD,
        pair_count // 2,
        scalars,
        own,
        other,
        own_total,
        own_stats,
        down_head,
        limit=16,
    )

    first_copy = rank % copies == 0
    middle_rows = middle_rows.astype(jnp.bfloat16).reshape(low_rank, ranks, tok)
    middle_rows = in_order(middle_rows.transpose(1, 0, 2))
    if copies > 1:
        middle_rows = jnp.where(first_copy, middle_rows, 0.0)
    (message,) = in_vmem(
        functools.partial(dout_kernel, copies),
        [shape_of((ranks, HD + 2 * low_rank, tok), jnp.bfloat16)],
        packed_own,
        received,
        middle_rows,
    )
    arrived = exchange(message)
    middle = jnp.sum(arrived[:, HD + low_rank :].astype(jnp.float32), axis=0)
    bit = 1
    while bit < heads:
        middle += lax.ppermute(middle, "head", [(i, i ^ bit) for i in range(heads)])
        bit *= 2
    up_part = 2.0 * dot_nn(middle.astype(jnp.bfloat16), output_gradient)

    dq, dk_own, dv_own, pair_other, down_part = call_kernel(
        functools.partial(backward_kernel, tok),
        [
            shape_of((ranks, tok, HD), jnp.bfloat16),
            shape_of((ranks, tok, HD), jnp.float32),
            shape_of((ranks, tok, HD), jnp.float32),
            shape_of((ranks, 2 * tok, HD), jnp.bfloat16),
            shape_of((low_rank, HD), jnp.float32),
        ],
        [pltpu.VMEM((rows, HD), jnp.float32)] * 4,
        10 * pair_count * HD,
        pair_count,
        scalars,
        own,
        other,
        in_order(arrived[:, : HD + low_rank]),
        attn_t,
        stats,
        own_keys_t,
        limit=28,
    )
    pair_other, _ = lax.optimization_barrier((pair_other, middle))
    turn = jnp.full((1,), jnp.where(shifted, 0, ranks // 2), jnp.int32)
    back_message = return_message(
        turn, dq, dk_own, dv_own, swap(pair_other), down_part, swap(down_part)
    )
    back = exchange(back_message)
    outs = [shape_of((tok, feats), back.dtype)] * 3
    if seqs == ranks:
        outs.append(shape_of((low_rank, feats), jnp.float32))
    outs = list(in_vmem(functools.partial(unpack_kernel, copies), outs, back))
    if seqs > ranks:
        bits = [bit for bit in powers_below(seqs) if bit >= ranks]
        down_terms = back[::copies, 3 * tok :].astype(jnp.float32)
        down_terms = butterfly_sum(down_terms, "seq", bits, seqs)
        outs.append(down_terms.transpose(1, 0, 2).reshape(low_rank, feats))
    query_gradient, key_gradient, value_gradient, down_gradient = outs

    up_sum = butterfly_sum(up_part, "seq", powers_below(seqs), seqs)
    _, up_sum = lax.optimization_barrier((back, up_sum))
    up_gradient = butterfly_sum(up_sum, "sub", powers_below(subs), subs)
    return (query_gradient, key_gradient, value_gradient, down_gradient.T, up_gradient)


def solution(mesh):
    rows = P(("rep", "seq", "sub"), "head")
    sizes = (mesh.shape["seq"], mesh.shape["head"], mesh.shape["sub"])
    return jax.shard_map(
        functools.partial(on_device, sizes),
        mesh=mesh,
        in_specs=(rows, rows, rows, rows, P("head", "sub"), P("head", None), P()),
        out_specs=(rows, rows, rows, P(("rep", "head"), None), P("rep", "head")),
        check_vma=False,
    )
```

```python
import functools
import math

import jax
import jax.numpy as jnp
from jax import lax
from jax.experimental import pallas as pl
from jax.experimental.pallas import tpu as pltpu
from jax.sharding import PartitionSpec as P

HD = 128
GROUP = 2048
TILE = 256
HIDDEN = -1e30
SCALE = HD ** (-0.5)
LOG2_SCALE = SCALE * math.log2(math.e)


def dot_nt(left, right):
    return lax.dot_general(
        left, right, (((1,), (1,)), ((), ())), preferred_element_type=jnp.float32
    )


def dot_nn(left, right):
    return jnp.dot(left, right, preferred_element_type=jnp.float32)


def rows_of(ref, blocks, first, count):
    return ref[0:blocks, first : first + count, :].reshape(blocks * count, HD)


def scores_of(keys, queries, visible):
    scores = dot_nt(keys, queries)
    head = scores.shape[0] - TILE
    tail = jnp.where(visible, scores[head:], HIDDEN)
    return tail if head == 0 else jnp.concatenate((scores[:head], tail), axis=0)


def tile_index(dimension):
    shape = (TILE, 1) if dimension == 0 else (1, TILE)
    return lax.broadcasted_iota(jnp.int32, shape, dimension)


def own_visible():
    return tile_index(0) <= tile_index(1)


def other_visible(sub, tok):
    return tile_index(0) // tok < tile_index(1) // tok + sub


def summed(terms):
    return functools.reduce(jnp.add, terms)


def in_stages(prepare, work, finish, tiles):
    tiles = list(tiles)
    ready, worked = prepare(tiles[0]), None
    for n, tile in enumerate(tiles):
        present = ready
        if n + 1 < len(tiles):
            ready = prepare(tiles[n + 1])
        now = work(tile, present)
        if worked is not None:
            finish(tiles[n - 1], worked)
        worked = now
    finish(tiles[-1], worked)


def forward_own_kernel(tok, scalar_ref, own_ref, total_ref, stat_ref, keys_t_ref):
    blocks = own_ref.shape[0]
    step = TILE // tok
    values_t = rows_of(own_ref, blocks, 2 * tok, tok).T

    def prepare(tile):
        upto = (tile + 1) * step
        queries = own_ref[tile * step : upto, 0:tok, :].reshape(TILE, HD)
        return scores_of(rows_of(own_ref, upto, tok, tok), queries, own_visible())

    def work(tile, scores):
        here = pl.ds(tile * TILE, TILE)
        highest = jnp.max(scores, axis=0, keepdims=True)
        powers = jnp.exp2((scores - highest) * LOG2_SCALE)
        stat_ref[0:1, here] = highest
        stat_ref[1:2, here] = jnp.sum(powers, axis=0, keepdims=True)
        return powers.astype(jnp.bfloat16)

    def finish(tile, powers):
        total_ref[:, pl.ds(tile * TILE, TILE)] = dot_nn(
            values_t[:, : (tile + 1) * TILE], powers
        )

    in_stages(prepare, work, finish, reversed(range(blocks // step)))
    keys_t_ref[...] = rows_of(own_ref, blocks, tok, tok).T


def forward_kernel(
    tok,
    scalar_ref,
    own_ref,
    other_ref,
    total_ref,
    own_stat_ref,
    down_t_ref,
    attn_ref,
    mid_ref,
    stat_ref,
):
    blocks = own_ref.shape[0]
    step = TILE // tok
    sub = scalar_ref[0]
    values_t = rows_of(other_ref, blocks, tok, tok).T

    def prepare(tile):
        upto = (tile + 1) * step
        queries = own_ref[tile * step : upto, 0:tok, :].reshape(TILE, HD)
        keys = rows_of(other_ref, upto, 0, tok)
        return scores_of(keys, queries, other_visible(sub, tok))

    def work(tile, scores):
        here = pl.ds(tile * TILE, TILE)
        own_highest = own_stat_ref[0:1, here]
        highest = jnp.maximum(own_highest, jnp.max(scores, axis=0, keepdims=True))
        powers = jnp.exp2((scores - highest) * LOG2_SCALE)
        share = jnp.exp2((own_highest - highest) * LOG2_SCALE)
        inverse = 1.0 / (
            own_stat_ref[1:2, here] * share + jnp.sum(powers, axis=0, keepdims=True)
        )
        stat_ref[0:1, here] = highest
        stat_ref[1:2, here] = inverse
        return powers.astype(jnp.bfloat16), share, inverse

    def finish(tile, worked):
        powers, share, inverse = worked
        here = pl.ds(tile * TILE, TILE)
        attn = dot_nn(values_t[:, : (tile + 1) * TILE], powers)
        attn = (attn + total_ref[:, here] * share) * inverse
        attn_ref[:, here] = attn.astype(jnp.bfloat16)

    in_stages(prepare, work, finish, reversed(range(blocks // step)))
    mid_ref[...] = dot_nn(down_t_ref[...], attn_ref[...])


def backward_kernel(
    tok,
    scalar_ref,
    own_ref,
    other_ref,
    dout_ref,
    attn_ref,
    stat_ref,
    keys_t_ref,
    dq_ref,
    dk_own_ref,
    dv_own_ref,
    pair_other_ref,
    down_grad_ref,
    dk_own,
    dv_own,
    dk_other,
    dv_other,
):
    blocks = own_ref.shape[0]
    step = TILE // tok
    sub = scalar_ref[0]
    low_rank = down_grad_ref.shape[0]
    keys_own_t = keys_t_ref[...]
    keys_other_t = rows_of(other_ref, blocks, 0, tok).T
    tiles = blocks // step
    lora = jnp.concatenate(
        [dout_ref[block, HD : HD + low_rank, :] for block in range(blocks)], axis=1
    )
    down_grad_ref[...] = 2.0 * dot_nt(lora, attn_ref[...])

    def prepare(tile):
        upto = (tile + 1) * step
        queries = own_ref[tile * step : upto, 0:tok, :].reshape(TILE, HD)
        douts_t = jnp.concatenate(
            [dout_ref[block, 0:HD, :] for block in range(tile * step, upto)], axis=1
        )
        own = scores_of(rows_of(own_ref, upto, tok, tok), queries, own_visible())
        other = scores_of(
            rows_of(other_ref, upto, 0, tok), queries, other_visible(sub, tok)
        )
        dprob_own = dot_nn(rows_of(own_ref, upto, 2 * tok, tok), douts_t)
        dprob_other = dot_nn(rows_of(other_ref, upto, tok, tok), douts_t)
        return queries, douts_t, own, other, dprob_own, dprob_other

    def work(tile, prepared):
        queries, douts_t, own, other, dprob_own, dprob_other = prepared
        here = pl.ds(tile * TILE, TILE)
        highest = stat_ref[0:1, here]
        inverse = stat_ref[1:2, here]
        own = jnp.exp2((own - highest) * LOG2_SCALE) * inverse
        other = jnp.exp2((other - highest) * LOG2_SCALE) * inverse
        delta = jnp.sum(own * dprob_own, axis=0, keepdims=True) + jnp.sum(
            other * dprob_other, axis=0, keepdims=True
        )
        ds_own = (own * (dprob_own - delta)).astype(jnp.bfloat16)
        ds_other = (other * (dprob_other - delta)).astype(jnp.bfloat16)
        probs = own.astype(jnp.bfloat16), other.astype(jnp.bfloat16)
        return queries, douts_t, ds_own, ds_other, *probs

    def finish(tile, worked):
        queries, douts_t, ds_own, ds_other, own, other = worked
        upto = (tile + 1) * step
        width = upto * tok
        dq = dot_nn(keys_own_t[:, :width], ds_own) + dot_nn(keys_other_t[:, :width], ds_other)
        dq = (dq * SCALE).T.astype(jnp.bfloat16)
        dq_ref[tile * step : upto] = dq.reshape(step, tok, HD)
        terms = (
            (dk_own, dot_nn(ds_own, queries)),
            (dk_other, dot_nn(ds_other, queries)),
            (dv_own, dot_nt(own, douts_t)),
            (dv_other, dot_nt(other, douts_t)),
        )
        for total, term in terms:
            if tile == tiles - 1:
                total[...] = term
            else:
                total[0:width] += term

    in_stages(prepare, work, finish, reversed(range(tiles)))
    shape = (blocks, tok, HD)
    dk_own_ref[...] = (dk_own[...] * SCALE).reshape(shape)
    dv_own_ref[...] = dv_own[...].reshape(shape)
    pair_other_ref[:, 0:tok, :] = (dk_other[...] * SCALE).astype(jnp.bfloat16).reshape(shape)
    pair_other_ref[:, tok : 2 * tok, :] = dv_other[...].astype(jnp.bfloat16).reshape(shape)


def call_kernel(body, outs, scratch, flops, exps, *operands, declared=None, limit=48):
    in_bytes = sum(x.size * x.dtype.itemsize for x in operands)
    out_bytes = sum(x.size * x.dtype.itemsize for x in outs)
    specs = [pl.BlockSpec(memory_space=pltpu.SMEM)]
    specs += [pl.BlockSpec(memory_space=pltpu.VMEM)] * (len(operands) - 1)
    return pl.pallas_call(
        body,
        out_shape=outs,
        in_specs=specs,
        out_specs=[pl.BlockSpec(memory_space=pltpu.VMEM)] * len(outs),
        scratch_shapes=scratch,
        compiler_params=pltpu.CompilerParams(vmem_limit_bytes=limit * 1024 * 1024),
        cost_estimate=pl.CostEstimate(
            flops=flops,
            bytes_accessed=declared or in_bytes + out_bytes,
            transcendentals=exps,
        ),
    )(*operands)


def shape_of(shape, dtype):
    return jax.ShapeDtypeStruct(shape, dtype)


def butterfly_sum(value, axis, bits, count):
    for bit in bits:
        pairs = [(i, i ^ bit) for i in range(count)]
        value = value.astype(jnp.bfloat16)
        taken = lax.ppermute(value, axis, pairs)
        value = value.astype(jnp.float32) + taken.astype(jnp.float32)
    return value


def powers_below(count):
    return [1 << n for n in range(count.bit_length() - 1)]


def message_kernel(copies, *refs):
    count = (len(refs) - 3) // 3
    operands, message_ref = refs[:count], refs[count]
    held, grouped = refs[count + 1 : 2 * count + 1], refs[2 * count + 1 : 3 * count + 1]
    in_sems, out_sems = refs[-2], refs[-1]
    tok = operands[0].shape[0]
    arriving = [
        pltpu.make_async_copy(ref, to, in_sems.at[n])
        for n, (ref, to) in enumerate(zip(operands, held))
    ]
    for copy in arriving:
        copy.start()
    leaving = []
    for n, copy in enumerate(arriving):
        copy.wait()
        for rank in range(message_ref.shape[0]):
            at = (rank // copies) * HD
            grouped[n][rank] = held[n][:, at : at + HD]
        to = message_ref.at[:, pl.ds(n * tok, tok), :]
        leaving.append(pltpu.make_async_copy(grouped[n], to, out_sems.at[n]))
        leaving[-1].start()
    for copy in leaving:
        copy.wait()


def message_of(copies, ranks, *operands):
    tok = operands[0].shape[0]
    count = len(operands)
    shape = (ranks, count * tok, HD)
    return pl.pallas_call(
        functools.partial(message_kernel, copies),
        out_shape=shape_of(shape, operands[0].dtype),
        in_specs=[pl.BlockSpec(memory_space=pltpu.HBM)] * count,
        out_specs=pl.BlockSpec(memory_space=pltpu.HBM),
        scratch_shapes=[pltpu.VMEM(x.shape, x.dtype) for x in operands]
        + [pltpu.VMEM((ranks, tok, HD), x.dtype) for x in operands]
        + [pltpu.SemaphoreType.DMA((count,))] * 2,
        cost_estimate=pl.CostEstimate(
            flops=0, bytes_accessed=4 * math.prod(shape), transcendentals=0
        ),
    )(*operands)


def return_kernel(turn_ref, dq_ref, dk_ref, dv_ref, pair_ref, down_ref, taken_ref, *refs):
    message_ref, held, sems = refs
    blocks, tok, _ = dq_ref.shape
    down = (down_ref[...] + taken_ref[...]).astype(held.dtype)
    copies = []
    for slot in range(blocks):
        block = (slot + turn_ref[0]) % blocks
        held[slot, 0:tok, :] = dq_ref[block]
        dk = dk_ref[block] + pair_ref[block, 0:tok, :].astype(jnp.float32)
        dv = dv_ref[block] + pair_ref[block, tok : 2 * tok, :].astype(jnp.float32)
        held[slot, tok : 2 * tok, :] = dk.astype(held.dtype)
        held[slot, 2 * tok : 3 * tok, :] = dv.astype(held.dtype)
        held[slot, 3 * tok :, :] = down
        copies.append(pltpu.make_async_copy(held.at[slot], message_ref.at[slot], sems.at[slot]))
        copies[-1].start()
    for copy in copies:
        copy.wait()


def return_message(turn, dq, *operands):
    blocks, tok, _ = dq.shape
    shape = (blocks, 3 * tok + operands[-1].shape[0], HD)
    return pl.pallas_call(
        return_kernel,
        out_shape=shape_of(shape, dq.dtype),
        in_specs=[pl.BlockSpec(memory_space=pltpu.SMEM)]
        + [pl.BlockSpec(memory_space=pltpu.VMEM)] * (len(operands) + 1),
        out_specs=pl.BlockSpec(memory_space=pltpu.HBM),
        scratch_shapes=[pltpu.VMEM(shape, dq.dtype), pltpu.SemaphoreType.DMA((blocks,))],
        compiler_params=pltpu.CompilerParams(vmem_limit_bytes=16 * 1024 * 1024),
        cost_estimate=pl.CostEstimate(
            flops=0, bytes_accessed=4 * math.prod(shape), transcendentals=0
        ),
    )(turn, dq, *operands)


def unpack_kernel(copies, back_ref, *refs):
    out_refs, down_ref = refs[:3], refs[3] if len(refs) > 3 else None
    tok = out_refs[0].shape[0]
    for at_head in range(out_refs[0].shape[1] // HD):
        cols = slice(at_head * HD, (at_head + 1) * HD)
        for n, ref in enumerate(out_refs):
            ref[:, cols] = back_ref[at_head * copies, n * tok : (n + 1) * tok, :]
        if down_ref is not None:
            down_ref[:, cols] = back_ref[at_head * copies, 3 * tok :, :].astype(jnp.float32)


def in_vmem(body, outs, *operands):
    whole = pl.BlockSpec(memory_space=pltpu.VMEM)
    size = sum(x.size * x.dtype.itemsize for x in operands)
    size += sum(x.size * x.dtype.itemsize for x in outs)
    return pl.pallas_call(
        body,
        out_shape=outs,
        in_specs=[whole] * len(operands),
        out_specs=[whole] * len(outs),
        compiler_params=pltpu.CompilerParams(vmem_limit_bytes=16 * 1024 * 1024),
        cost_estimate=pl.CostEstimate(flops=0, bytes_accessed=size, transcendentals=0),
    )(*operands)


def cotangent_kernel(chunks, plan_ref, *refs):
    pieces, (matrix_ref, up_ref, own_ref, sent_ref) = refs[:-4], refs[-4:]
    tok, cols = pieces[0].shape
    feats, low_rank = matrix_ref.shape[0], up_ref.shape[0]
    count = len(pieces)
    if chunks == 1:
        stacks = [(jnp.concatenate([p[...] for p in pieces], axis=0), pl.ds(0, cols))]
    else:
        stacks = [
            (p[...], pl.ds(pl.multiple_of(plan_ref[count + k], HD), cols))
            for k, p in enumerate(pieces)
        ]
    mine = [plan_ref[k] == 1 for k in range(count)]
    for ref, here in ((matrix_ref, pl.ds(0, feats)), (up_ref, pl.ds(feats, low_rank))):
        terms = [dot_nt(ref[:, at], rows) for rows, at in stacks]
        parts = [t[:, i : i + tok] for t in terms for i in range(0, t.shape[1], tok)]
        own_ref[here, :] = summed([jnp.where(m, p, 0.0) for m, p in zip(mine, parts)])
        sent = summed([jnp.where(m, 0.0, p) for m, p in zip(mine, parts)])
        sent_ref[here, :] = sent.astype(jnp.bfloat16)


def dout_kernel(copies, own_ref, taken_ref, mid_ref, message_ref):
    low_rank = mid_ref.shape[1]
    feats = own_ref.shape[0] - low_rank
    lora = own_ref[feats:, :] + taken_ref[feats:, :].astype(jnp.float32)
    for rank in range(message_ref.shape[0]):
        at = pl.ds((rank // copies) * HD, HD)
        part = own_ref[at, :] + taken_ref[at, :].astype(jnp.float32)
        message_ref[rank, 0:HD, :] = part.astype(jnp.bfloat16)
        message_ref[rank, HD : HD + low_rank, :] = lora.astype(jnp.bfloat16)
        message_ref[rank, HD + low_rank : HD + 2 * low_rank, :] = mid_ref[rank]


def on_device(
    sizes,
    head_query_rows,
    head_key_rows,
    head_value_rows,
    output_gradient,
    output_matrix,
    adapter_down_weight,
    adapter_up_weight,
):
    seqs, heads, subs = sizes
    tok, feats = head_query_rows.shape
    cols = output_gradient.shape[1]
    low_rank = adapter_up_weight.shape[0]
    local_heads = feats // HD
    block_rows = tok * subs
    ranks = GROUP // block_rows
    copies = ranks // local_heads
    shift_blocks = GROUP // 2 // block_rows

    seq = lax.axis_index("seq")
    head = lax.axis_index("head")
    sub = lax.axis_index("sub")
    shifted = head >= heads // 2
    rank = (seq + shift_blocks) % ranks
    my_head = rank // copies

    groups = []
    for at_head in range(heads):
        for first in range(0, seqs, ranks):
            members = [first + shift_blocks + i for i in range(ranks)]
            if at_head < heads // 2:
                members = [first + (m - first) % ranks for m in members]
            members = [m % seqs for m in members]
            groups.append([m * heads + at_head for m in members])
    scalars = jnp.full((1,), sub, jnp.int32)

    def in_order(blocks):
        half = ranks // 2
        turned = jnp.concatenate((blocks[half:], blocks[:half]), axis=0)
        return jnp.where(shifted, blocks, turned)


    def exchange(parts):
        return lax.all_to_all(
            parts, ("seq", "head"), 0, 0, axis_index_groups=groups, tiled=True
        )

    def swap(value):
        if subs == 1:
            return value
        return lax.ppermute(value, "sub", [(0, 1), (1, 0)])

    sent = message_of(copies, ranks, head_query_rows, head_key_rows, head_value_rows)
    sent, output_gradient, output_matrix = lax.optimization_barrier(
        (sent, output_gradient, output_matrix)
    )
    own = exchange(sent)

    chunks = heads // subs
    pieces = []
    for k in range(heads):
        pairs = []
        for src_head in range(heads):
            for src_sub in range(subs):
                j = (src_head % chunks) * subs + src_sub
                dst = ((j + k) % heads) * subs + src_head // chunks
                pairs.append((src_head * subs + src_sub, dst))
        pieces.append(lax.ppermute(output_gradient, ("head", "sub"), pairs))

    up_half = lax.dynamic_slice_in_dim(adapter_up_weight, sub * chunks * cols, chunks * cols, 1)
    folded = dot_nn(adapter_down_weight, up_half)
    folded = (output_matrix.astype(jnp.float32) + 2.0 * folded).astype(jnp.bfloat16)
    sources = [(head - k + heads) % heads for k in range(heads)]
    plan = [(j % subs == sub).astype(jnp.int32) for j in sources]
    plan += [(j // subs * cols).astype(jnp.int32) for j in sources]
    packed_own, packed_sent = call_kernel(
        functools.partial(cotangent_kernel, chunks),
        [
            shape_of((feats + low_rank, tok), jnp.float32),
            shape_of((feats + low_rank, tok), jnp.bfloat16),
        ],
        [],
        0,
        0,
        jnp.stack(plan),
        *pieces,
        folded,
        up_half,
        declared=1024,
        limit=16,
    )
    received = swap(packed_sent)
    down_head = lax.dynamic_slice_in_dim(adapter_down_weight, my_head * HD, HD, 0).T
    own, down_head, _ = lax.optimization_barrier((own, down_head, packed_sent))
    own = in_order(own)
    other = swap(own[:, tok:])

    rows = ranks * tok
    pair_count = rows * (rows + TILE)
    own_total, own_stats, own_keys_t = call_kernel(
        functools.partial(forward_own_kernel, tok),
        [
            shape_of((HD, rows), jnp.float32),
            shape_of((8, rows), jnp.float32),
            shape_of((HD, rows), jnp.bfloat16),
        ],
        [],
        2 * pair_count * HD,
        pair_count // 2,
        scalars,
        own,
        limit=16,
    )
    attn_t, middle_rows, stats = call_kernel(
        functools.partial(forward_kernel, tok),
        [
            shape_of((HD, rows), jnp.bfloat16),
            shape_of((low_rank, rows), jnp.float32),
            shape_of((8, rows), jnp.float32),
        ],
        [],
        2 * pair_count * HD,
        pair_count // 2,
        scalars,
        own,
        other,
        own_total,
        own_stats,
        down_head,
        limit=16,
    )

    first_copy = rank % copies == 0
    middle_rows = middle_rows.astype(jnp.bfloat16).reshape(low_rank, ranks, tok)
    middle_rows = in_order(middle_rows.transpose(1, 0, 2))
    if copies > 1:
        middle_rows = jnp.where(first_copy, middle_rows, 0.0)
    (message,) = in_vmem(
        functools.partial(dout_kernel, copies),
        [shape_of((ranks, HD + 2 * low_rank, tok), jnp.bfloat16)],
        packed_own,
        received,
        middle_rows,
    )
    arrived = exchange(message)
    middle = jnp.sum(arrived[:, HD + low_rank :].astype(jnp.float32), axis=0)
    bit = 1
    while bit < heads:
        middle += lax.ppermute(middle, "head", [(i, i ^ bit) for i in range(heads)])
        bit *= 2
    up_part = 2.0 * dot_nn(middle.astype(jnp.bfloat16), output_gradient)

    dq, dk_own, dv_own, pair_other, down_part = call_kernel(
        functools.partial(backward_kernel, tok),
        [
            shape_of((ranks, tok, HD), jnp.bfloat16),
            shape_of((ranks, tok, HD), jnp.float32),
            shape_of((ranks, tok, HD), jnp.float32),
            shape_of((ranks, 2 * tok, HD), jnp.bfloat16),
            shape_of((low_rank, HD), jnp.float32),
        ],
        [pltpu.VMEM((rows, HD), jnp.float32)] * 4,
        10 * pair_count * HD,
        pair_count,
        scalars,
        own,
        other,
        in_order(arrived[:, : HD + low_rank]),
        attn_t,
        stats,
        own_keys_t,
        limit=28,
    )
    pair_other, _ = lax.optimization_barrier((pair_other, middle))
    turn = jnp.full((1,), jnp.where(shifted, 0, ranks // 2), jnp.int32)
    back_message = return_message(
        turn, dq, dk_own, dv_own, swap(pair_other), down_part, swap(down_part)
    )
    back = exchange(back_message)
    outs = [shape_of((tok, feats), back.dtype)] * 3
    if seqs == ranks:
        outs.append(shape_of((low_rank, feats), jnp.float32))
    outs = list(in_vmem(functools.partial(unpack_kernel, copies), outs, back))
    if seqs > ranks:
        bits = [bit for bit in powers_below(seqs) if bit >= ranks]
        down_terms = back[::copies, 3 * tok :].astype(jnp.float32)
        down_terms = butterfly_sum(down_terms, "seq", bits, seqs)
        outs.append(down_terms.transpose(1, 0, 2).reshape(low_rank, feats))
    query_gradient, key_gradient, value_gradient, down_gradient = outs

    bits = powers_below(seqs)
    up_sum = butterfly_sum(up_part, "seq", bits[1:2] + bits[:1] + bits[2:], seqs)
    _, up_sum = lax.optimization_barrier((back, up_sum))
    up_gradient = butterfly_sum(up_sum, "sub", powers_below(subs), subs)
    return (query_gradient, key_gradient, value_gradient, down_gradient.T, up_gradient)


def solution(mesh):
    rows = P(("rep", "seq", "sub"), "head")
    sizes = (mesh.shape["seq"], mesh.shape["head"], mesh.shape["sub"])
    return jax.shard_map(
        functools.partial(on_device, sizes),
        mesh=mesh,
        in_specs=(rows, rows, rows, rows, P("head", "sub"), P("head", None), P()),
        out_specs=(rows, rows, rows, P(("rep", "head"), None), P("rep", "head")),
        check_vma=False,
    )
```
